32 devices in a mesh: seq: 8 (over z, x), ch: 4 (over y, core).
Axes of the slice: x: 2, y: 2, z: 4, core: 2. Of those that a mesh axis runs over, the one named last changes fastest.
Arguments:
- stream: bfloat16 [1024, 2048], P(('seq', 'ch')), may hold values from -6 to 6
- cotangent: bfloat16 [1024, 2048], P(('seq', 'ch')), may hold values from -6 to 6
- mix_gain: float32 [2048], replicated, may hold values from 0.1 to 1.9
- gelu_weight: bfloat16 [2048, 3072], P(None, 'ch'), may hold values from -0.125 to 0.125
- recur_weight: bfloat16 [2048, 3072], P(None, 'ch'), may hold values from -0.125 to 0.125
- conv_taps: float32 [4, 12, 256], P(None, 'ch'), may hold values from -3 to 3
- conv_bias: float32 [12, 256], P('ch'), may hold values from -3 to 3
- rate_weight: bfloat16 [12, 256, 256], P('ch'), may hold values from -0.375 to 0.375
- rate_bias: float32 [12, 256], P('ch'), may hold values from -4 to 4
- inlet_weight: bfloat16 [12, 256, 256], P('ch'), may hold values from -0.375 to 0.375
- inlet_bias: float32 [12, 256], P('ch'), may hold values from -4 to 4
- decay_param: float32 [12, 256], P('ch'), may hold values from -21 to -1.2
- init_states: float32 [5, 3072], P(None, 'ch'), may hold values from -5 to 5
- out_weight: bfloat16 [3072, 2048], P('ch'), may hold values from -0.375 to 0.375
- ffn_gain: float32 [2048], replicated, may hold values from 0.1 to 1.9
- gate_weight: bfloat16 [2048, 6144], P('seq', 'ch'), may hold values from -0.125 to 0.125
- up_weight: bfloat16 [2048, 6144], P('seq', 'ch'), may hold values from -0.125 to 0.125
- down_weight: bfloat16 [6144, 2048], P('ch', 'seq'), may hold values from -0.078125 to 0.078125
- doc_lengths: int32 [5], replicated, may hold values from 16 to 896, as said below
- block_counts: int32 [4], P('ch'), may hold values from 2 to 3, as said below
Outputs:
- final_states: float32 [5, 3072], replicated
- mixed_out: bfloat16 [1024, 2048], P(('seq', 'ch'))
- stream_grad: float32 [1024, 2048], P(('seq', 'ch'))
- mix_gain_grad: float32 [2048], replicated
- gelu_weight_grad: float32 [2048, 3072], P('seq', 'ch')
- recur_weight_grad: float32 [2048, 3072], P('seq', 'ch')
- conv_taps_grad: float32 [4, 12, 256], P(None, 'ch', 'seq')
- conv_bias_grad: float32 [12, 256], P('ch', 'seq')
- rate_weight_grad: float32 [12, 256, 256], P('ch', 'seq')
- rate_bias_grad: float32 [12, 256], P('ch', 'seq')
- inlet_weight_grad: float32 [12, 256, 256], P('ch', 'seq')
- inlet_bias_grad: float32 [12, 256], P('ch', 'seq')
- decay_grad: float32 [12, 256], P('ch', 'seq')
- out_weight_grad: float32 [3072, 2048], P('ch', 'seq')
- ffn_gain_grad: float32 [2048], replicated
- gate_weight_grad: float32 [2048, 6144], P('seq', 'ch')
- up_weight_grad: float32 [2048, 6144], P('seq', 'ch')
- down_weight_grad: float32 [6144, 2048], P('ch', 'seq')
The draws below stay inside these ranges and needn't reach their ends.
Inputs may be any that keep to these rules, and one draw needn't show every extreme that they name: `doc_lengths`: 2 short documents, then one long document, then 2 more short ones; the i-th short one after the long one and the i-th before it together hold 64 tokens, so the long one holds 896; the lengths sum to 1024. Index c of ch owns gate-block slots c * 3 to c * 3 + 2, of which the first block_counts[c] are live; the entries sum to 10.
All inputs are finite; a program needn't handle non-finite values.
Results may differ from the reference program's by a relative error of at most 0.009.
Values may be sent and summed in bfloat16 or wider, within the bound.
A program may use at most 256 MiB of HBM per device.

```python
import jax
import jax.numpy as jnp
from jax import lax

D = 2048
FF = 6144
BW = 256
BLOCKS = 10
CONV = 4
SIDE_DOCS = 2
TOK_DEV = 128
SLOTS = 3
BLOCKS_P = 12
WP = 3072
TOKENS = 1024
DOCS = 5
N_SEQ = 8


def draw_doc_lengths(key, part):
    key = jax.random.fold_in(key, 11)
    shortest = TOK_DEV // 8
    pair_total = TOK_DEV // 2
    before = jax.random.randint(key, (SIDE_DOCS,), shortest, pair_total - shortest + 1).astype(jnp.int32)
    after = (pair_total - jnp.flip(before, 0)).astype(jnp.int32)
    middle_doc = jnp.full((1,), TOKENS - SIDE_DOCS * pair_total, jnp.int32)
    return jnp.concatenate([before, middle_doc, after]).astype(jnp.int32)


def draw_block_counts(key, part):
    key = jax.random.fold_in(key, 12)
    groups = BLOCKS_P // SLOTS
    order = jax.random.permutation(key, groups)
    extra = BLOCKS - (SLOTS - 1) * groups
    return (SLOTS - 1 + (order < extra).astype(jnp.int32)).astype(jnp.int32)


def draw_decay_param(key, part):
    key = jax.random.fold_in(key, 13)
    lowest = -21.0
    highest = -1.2
    spread = jax.random.uniform(key, (BLOCKS_P, BW), jnp.float32)
    return (lowest + (highest - lowest) * spread).astype(jnp.float32)


def block_scale(stream_key, extent, cuts, smallest, high):
    def one(axis_at, blocks):
        heights = jax.random.uniform(jax.random.fold_in(jax.random.fold_in(stream_key, 6), axis_at), (blocks,), jnp.float32, smallest / len(cuts), high / len(cuts))
        return jnp.repeat(jnp.exp(heights), extent[axis_at] // blocks).reshape((-1,) + (1,) * (len(extent) - axis_at - 1))

    level = one(*cuts[0])
    for cut in cuts[1:]:
        level = level * one(*cut)
    return level


def noise(rng, extent, scale, limit, split=(), kind=jnp.bfloat16):
    values = jax.random.normal(rng, extent, jnp.float32) * scale
    if len(split) > 0:
        values = block_scale(rng, extent, split, -0.22, 0.18) * values
    return jnp.clip(values, min=-limit, max=limit).astype(kind)


def setup_inputs(seed: int = 0) -> dict:
    key_list = jax.random.split(jax.random.key(seed), 21)
    stream = noise(key_list[0], (TOKENS, D), 1.0, 6.0, ((0, 32),))
    cotangent = noise(key_list[1], (TOKENS, D), 1.0, 6.0, ((0, 32),))
    mix_gain = jnp.clip(1.0 + 0.18 * jax.random.normal(key_list[2], (D,), jnp.float32), 0.1, 1.9)
    gelu_weight = noise(key_list[3], (D, WP), D ** -0.5, 0.125, ((1, 4),))
    recur_weight = noise(key_list[4], (D, WP), D ** -0.5, 0.125, ((1, 4),))
    conv_taps = noise(key_list[5], (CONV, BLOCKS_P, BW), 0.5, 3.0, ((1, 4),), jnp.float32)
    conv_bias = noise(key_list[6], (BLOCKS_P, BW), 0.5, 3.0, ((0, 4),), jnp.float32)
    rate_weight = noise(key_list[7], (BLOCKS_P, BW, BW), BW ** -0.5, 0.375, ((0, 4),))
    rate_bias = noise(key_list[8], (BLOCKS_P, BW), 1.0, 4.0, ((0, 4),), jnp.float32)
    inlet_weight = noise(key_list[9], (BLOCKS_P, BW, BW), BW ** -0.5, 0.375, ((0, 4),))
    inlet_bias = noise(key_list[10], (BLOCKS_P, BW), 1.0, 4.0, ((0, 4),), jnp.float32)
    decay_param = draw_decay_param(jax.random.fold_in(key_list[20], 71), 0)
    init_states = noise(key_list[12], (DOCS, WP), 1.0, 5.0, ((1, 4),), jnp.float32)
    out_weight = noise(key_list[13], (WP, D), BW ** -0.5, 0.375, ((0, 4),))
    ffn_gain = jnp.clip(1.0 + 0.18 * jax.random.normal(key_list[14], (D,), jnp.float32), 0.1, 1.9)
    gate_weight = noise(key_list[15], (D, FF), D ** -0.5, 0.125, ((0, 8), (1, 4)))
    up_weight = noise(key_list[16], (D, FF), D ** -0.5, 0.125, ((0, 8), (1, 4)))
    down_weight = noise(key_list[17], (FF, D), FF ** -0.5, 0.078125, ((0, 4), (1, 8)))
    doc_lengths = draw_doc_lengths(jax.random.fold_in(key_list[20], 71), 0)
    block_counts = draw_block_counts(jax.random.fold_in(key_list[20], 71), 0)
    return dict(stream=stream, cotangent=cotangent, mix_gain=mix_gain, gelu_weight=gelu_weight, recur_weight=recur_weight, conv_taps=conv_taps, conv_bias=conv_bias, rate_weight=rate_weight, rate_bias=rate_bias, inlet_weight=inlet_weight, inlet_bias=inlet_bias, decay_param=decay_param, init_states=init_states, out_weight=out_weight, ffn_gain=ffn_gain, gate_weight=gate_weight, up_weight=up_weight, down_weight=down_weight, doc_lengths=doc_lengths, block_counts=block_counts)


EPS = 1e-06
HIGH = lax.Precision.HIGHEST

@jax.custom_vjp
def low(v):
    return lax.optimization_barrier(v.astype(jnp.bfloat16)).astype(jnp.float32)

@jax.custom_vjp
def low_back(v):
    return v

def low_keep(v):
    return (low(v), None)

def low_pass(kept, grad):
    return (grad,)

def back_keep(v):
    return (v, None)

def back_low(kept, grad):
    return (low(grad),)
low.defvjp(low_keep, low_pass)
low_back.defvjp(back_keep, back_low)

def normalize(values, gain):
    return values * lax.rsqrt(lax.optimization_barrier(jnp.mean(values * values, axis=-1, keepdims=True)) + EPS) * gain

def smooth(values):
    return jax.nn.gelu(values, approximate=True)

def affine(earlier, later):
    return (earlier[0] * later[0], later[0] * earlier[1] + later[1])

def doc_view(lengths, first, count):
    ends = jnp.cumsum(lengths).astype(jnp.int32)
    starts = (ends - lengths).astype(jnp.int32)
    position = (first + jnp.arange(count, dtype=jnp.int32)).astype(jnp.int32)
    owner = (position[:, None] >= starts[None, :]) & (position[:, None] < ends[None, :])
    start_of = lax.optimization_barrier(jnp.sum(jnp.where(owner, starts[None, :], 0), axis=1)).astype(jnp.int32)
    offset = (position - start_of).astype(jnp.int32)
    opening = (owner & (offset[:, None] == 0)).astype(jnp.float32)
    closing = (owner & (position[:, None] == ends[None, :] - 1)).astype(jnp.float32)
    return (offset, opening, closing)

def coefficients(rate_pre, inlet_pre, conv_value, decay, init_rows, keep):
    rate = jax.nn.sigmoid(rate_pre)
    inlet = jax.nn.sigmoid(inlet_pre)
    log_decay = -8.0 * rate * jax.nn.softplus(decay)
    factor = jnp.exp(log_decay)
    scale = jnp.sqrt(-jnp.expm1(2.0 * log_decay))
    carry_factor = keep * factor
    source = scale * inlet * conv_value + (1.0 - keep) * factor * init_rows
    return (carry_factor, source)

def reference(stream, cotangent, mix_gain, gelu_weight, recur_weight, conv_taps, conv_bias, rate_weight, rate_bias, inlet_weight, inlet_bias, decay_param, init_states, out_weight, ffn_gain, gate_weight, up_weight, down_weight, doc_lengths, block_counts):
    slot_live = (jnp.arange(SLOTS, dtype=jnp.int32)[None, :] < block_counts[:, None]).astype(jnp.float32)
    live = jnp.repeat(slot_live.reshape(-1), BW)[None, :]
    weights = (mix_gain, gelu_weight, recur_weight, conv_taps, conv_bias, rate_weight, rate_bias, inlet_weight, inlet_bias, decay_param, out_weight, ffn_gain, gate_weight, up_weight, down_weight)
    weights = tuple((item.astype(jnp.float32) for item in weights))
    init_float = init_states.astype(jnp.float32)

    def forward(inputs, params):
        mix_g, gelu_w, recur_w, taps_w, taps_b, rate_w, rate_b, inlet_w, inlet_b, decay_w, out_w, ffn_g, gate_w, up_w, down_w = params

        def step(carry, piece):
            state_in, tail, finals = carry
            rows, number = piece
            base = (number * TOK_DEV).astype(jnp.int32)
            offset, opening, closing = doc_view(doc_lengths, base, TOK_DEV)
            keep = (offset > 0).astype(jnp.float32)[:, None]
            mix_low = low(normalize(rows, mix_g))
            gelu_pre = low_back(jnp.dot(mix_low, gelu_w, precision=HIGH))
            recur_low = low_back(low(jnp.dot(mix_low, recur_w, precision=HIGH)))
            extended = jnp.concatenate([tail, recur_low], axis=0)
            conv_pre = taps_b.reshape(-1)[None, :]
            for tap_index in range(CONV):
                valid = (offset >= tap_index).astype(jnp.float32)[:, None]
                lead = CONV - 1 - tap_index
                conv_pre = conv_pre + taps_w[tap_index].reshape(-1)[None, :] * extended[lead:lead + TOK_DEV] * valid
            conv_low = low_back(low(conv_pre))
            grouped = conv_low.reshape(TOK_DEV, BLOCKS_P, BW)
            rate_pre = low_back((jnp.einsum('rsi,sio->rso', grouped, rate_w, precision=HIGH) + rate_b[None]).reshape(TOK_DEV, WP))
            inlet_pre = low_back((jnp.einsum('rsi,sio->rso', grouped, inlet_w, precision=HIGH) + inlet_b[None]).reshape(TOK_DEV, WP))
            init_rows = jnp.dot(opening, init_float, precision=HIGH)
            carry_factor, source = coefficients(rate_pre, inlet_pre, conv_low, decay_w.reshape(-1)[None, :], init_rows, keep)
            cumulative, local_state = lax.associative_scan(affine, (carry_factor, source), axis=0)
            state = local_state + cumulative * state_in[None, :]
            product_low = low(smooth(gelu_pre) * state * live)
            branch = low_back(jnp.dot(product_low, out_w, precision=HIGH))
            middle = rows + branch
            ffn_low = low(normalize(middle, ffn_g))
            gate = low_back(jnp.dot(ffn_low, gate_w, precision=HIGH))
            upward = low_back(jnp.dot(ffn_low, up_w, precision=HIGH))
            hidden = low(smooth(gate) * upward)
            result = middle + jnp.dot(hidden, down_w, precision=HIGH)
            finals = finals + jnp.dot(closing.T, state * live, precision=HIGH)
            return ((state[-1], recur_low[TOK_DEV - CONV + 1:], finals), result)
        start_carry = (jnp.zeros((WP,), jnp.float32), jnp.zeros((CONV - 1, WP), jnp.float32), jnp.zeros((DOCS, WP), jnp.float32))
        pieces = (inputs.reshape(N_SEQ, TOK_DEV, D), jnp.arange(N_SEQ, dtype=jnp.int32))
        (state_end, tail_end, finals), results = lax.scan(jax.checkpoint(step), start_carry, pieces)
        return (results.reshape(TOKENS, D), finals)
    result, pullback, finals = jax.vjp(forward, stream.astype(jnp.float32), weights, has_aux=True)
    stream_grad, grads = pullback(cotangent.astype(jnp.float32))
    return (finals, result.astype(jnp.bfloat16), stream_grad, grads[0], grads[1], grads[2], grads[3], grads[4], grads[5], grads[6], grads[7], grads[8], grads[9], grads[10], grads[11], grads[12], grads[13], grads[14])
```

```python
import functools

import jax
import jax.numpy as jnp
from jax import lax
from jax.experimental import pallas as pl
from jax.experimental.pallas import tpu as pltpu
from jax.sharding import PartitionSpec as P

EPS = 1e-06
HIGH = lax.Precision.HIGHEST
MESH = pl.DeviceIdType.MESH
K1 = 0.7978845608028654
K2 = 0.044715
VMEM_BYTES = 56 * 2**20


def passed_along(shard, axis, by):
    length = lax.axis_size(axis)
    pairs = [(i, i + by) for i in range(length) if 0 <= i + by < length]
    return lax.ppermute(shard, axis, pairs)


def entering_2(shard, axis, combine, identity, reverse):
    length, here = (lax.axis_size(axis), lax.axis_index(axis))
    everything = jax.tree.map(lambda part: lax.all_gather(part, axis), shard)
    start = jax.tree.map(
        lambda part, zero: jnp.broadcast_to(jnp.asarray(zero, part.dtype), part.shape),
        shard,
        identity,
    )

    def turn(k, before):
        at = length - 1 - k if reverse else k
        reached = at > here if reverse else at < here
        new = combine(before, jax.tree.map(lambda part: part[at], everything))
        return jax.tree.map(lambda a, b: jnp.where(reached, a, b), new, before)

    return lax.fori_loop(0, length, turn, start)


def normalize(values, gain):
    return values * lax.rsqrt(jnp.mean(values * values, axis=-1, keepdims=True) + EPS) * gain


def smooth(values):
    return jax.nn.gelu(values, approximate=True)


def affine(earlier, later):
    return (earlier[0] * later[0], later[0] * earlier[1] + later[1])


def doc_view(lengths, first, count):
    ends = jnp.cumsum(lengths)
    starts = ends - lengths
    position = first + jnp.arange(count, dtype=jnp.int32)
    owner = (position[:, None] >= starts[None, :]) & (position[:, None] < ends[None, :])
    start_of = jnp.sum(jnp.where(owner, starts[None, :], 0), axis=1)
    offset = position - start_of
    opening = (owner & (offset[:, None] == 0)).astype(jnp.float32)
    closing = (owner & (position[:, None] == ends[None, :] - 1)).astype(jnp.float32)
    return (offset, opening, closing)


def coefficients(rate_pre, inlet_pre, conv_value, decay, init_rows, keep):
    rate = jax.nn.sigmoid(rate_pre)
    inlet = jax.nn.sigmoid(inlet_pre)
    log_decay = -8.0 * rate * jax.nn.softplus(decay)
    factor = jnp.exp(log_decay)
    scale = jnp.sqrt(-jnp.expm1(2.0 * log_decay))
    carry_factor = keep * factor
    source = scale * inlet * conv_value + (1.0 - keep) * factor * init_rows
    return (carry_factor, source)


def spread(values):
    return lax.all_gather(values, "ch", axis=0, tiled=True)


def collect(terms):
    return lax.psum_scatter(terms, "ch", scatter_dimension=0, tiled=True)


def contract_last(left, right):
    return lax.dot_general(
        left, right, (((1,), (1,)), ((), ())), preferred_element_type=jnp.float32
    )


def contract_first(left, right):
    return lax.dot_general(
        left, right, (((0,), (0,)), ((), ())), preferred_element_type=jnp.float32
    )


def body(
    stream,
    cotangent,
    mix_gain,
    gelu_weight,
    recur_weight,
    conv_taps,
    conv_bias,
    rate_weight,
    rate_bias,
    inlet_weight,
    inlet_bias,
    decay_param,
    init_states,
    out_weight,
    ffn_gain,
    gate_weight,
    up_weight,
    down_weight,
    doc_lengths,
    block_counts,
):
    slot_count = rate_weight.shape[0]
    block_width = rate_weight.shape[1]
    local_width = slot_count * block_width
    taps = conv_taps.shape[0]
    token_count = stream.shape[0] * lax.axis_size("ch")
    hidden_width = gate_weight.shape[1]
    base = lax.axis_index("seq") * token_count
    offset_all, opening, closing = doc_view(doc_lengths, base, token_count + taps - 1)
    offset = offset_all[:token_count]
    opening = opening[:token_count]
    closing = closing[:token_count]
    keep = (offset > 0).astype(jnp.float32)[:, None]
    slot_live = (jnp.arange(slot_count, dtype=jnp.int32) < block_counts[0]).astype(jnp.float32)
    live = jnp.repeat(slot_live, block_width)[None, :]
    taps_flat = conv_taps.reshape(taps, local_width)
    decay_flat = decay_param.reshape(1, local_width)
    stream_float = stream.astype(jnp.float32)
    mix_low = normalize(stream_float, mix_gain).astype(jnp.bfloat16)
    mix_full = spread(mix_low)
    gelu_pre = jnp.dot(mix_full, gelu_weight, preferred_element_type=jnp.float32)
    recur_low = jnp.dot(mix_full, recur_weight, preferred_element_type=jnp.float32).astype(
        jnp.bfloat16
    )
    rim = passed_along(recur_low[token_count - taps + 1 :], "seq", 1)
    extended = jnp.concatenate([rim, recur_low], axis=0).astype(jnp.float32)
    conv_pre = conv_bias.reshape(1, local_width)
    for tap_index in range(taps):
        valid = (offset >= tap_index).astype(jnp.float32)[:, None]
        lead = taps - 1 - tap_index
        conv_pre = (
            conv_pre + taps_flat[tap_index][None, :] * extended[lead : lead + token_count] * valid
        )
    conv_low = conv_pre.astype(jnp.bfloat16)
    conv_value = conv_low.astype(jnp.float32)
    grouped = conv_low.reshape(token_count, slot_count, block_width)
    rate_pre = (
        jnp.einsum("rsi,sio->rso", grouped, rate_weight, preferred_element_type=jnp.float32)
        + rate_bias[None]
    ).reshape(token_count, local_width)
    inlet_pre = (
        jnp.einsum("rsi,sio->rso", grouped, inlet_weight, preferred_element_type=jnp.float32)
        + inlet_bias[None]
    ).reshape(token_count, local_width)
    init_rows = jnp.dot(opening, init_states, precision=HIGH)
    carry_factor, source = coefficients(
        rate_pre, inlet_pre, conv_value, decay_flat, init_rows, keep
    )
    cumulative, local_state = lax.associative_scan(affine, (carry_factor, source), axis=0)
    summary = (cumulative[-1], local_state[-1])
    entering = entering_2(
        summary, "seq", affine, (jnp.ones_like(summary[0]), jnp.zeros_like(summary[1])), False
    )
    state_in = entering[1]
    state = local_state + cumulative * state_in[None, :]
    gelu_value = smooth(gelu_pre)
    product_low = (gelu_value * state * live).astype(jnp.bfloat16)
    branch = collect(jnp.dot(product_low, out_weight, preferred_element_type=jnp.float32))
    middle = stream_float + branch
    ffn_low = normalize(middle, ffn_gain).astype(jnp.bfloat16)
    ffn_full = spread(ffn_low)
    stacked = jnp.concatenate([gate_weight, up_weight], axis=1)
    columns = ffn_full
    gate_up = jnp.dot(
        columns,
        lax.all_gather(stacked, "seq", axis=0, tiled=True),
        preferred_element_type=jnp.float32,
    )
    gate = gate_up[:, :hidden_width]
    upward = gate_up[:, hidden_width:]
    hidden = (smooth(gate) * upward).astype(jnp.bfloat16)
    ffn_terms = jnp.dot(
        hidden,
        lax.all_gather(down_weight, "seq", axis=1, tiled=True),
        preferred_element_type=jnp.float32,
    )
    mixed_out = (middle + collect(ffn_terms)).astype(jnp.bfloat16)
    out_grad_full = spread(cotangent)
    columns = out_grad_full
    hidden_grad = contract_last(columns, lax.all_gather(down_weight, "seq", axis=1, tiled=True))
    down_weight_grad = contract_first(hidden, out_grad_full)
    unused, pair_pull = jax.vjp(lambda left, right: smooth(left) * right, gate, upward)
    gate_grad, up_grad = pair_pull(hidden_grad)
    pair_low = jnp.concatenate([gate_grad, up_grad], axis=1).astype(jnp.bfloat16)
    pair_weight_grad = contract_first(ffn_full, pair_low)
    norm_ffn_part = contract_last(pair_low, lax.all_gather(stacked, "seq", axis=0, tiled=True))
    norm_ffn_grad = collect(norm_ffn_part)
    unused, ffn_norm_pull = jax.vjp(normalize, middle, ffn_gain)
    middle_norm_grad, ffn_gain_part = ffn_norm_pull(norm_ffn_grad)
    middle_grad = cotangent.astype(jnp.float32) + middle_norm_grad
    branch_full = spread(middle_grad.astype(jnp.bfloat16))
    out_weight_grad = contract_first(product_low, branch_full)
    product_grad = contract_last(branch_full, out_weight)
    state_grad = product_grad * gelu_value * live
    unused, gelu_pull = jax.vjp(smooth, gelu_pre)
    gelu_low = gelu_pull(product_grad * state * live)[0].astype(jnp.bfloat16)
    following = jnp.concatenate([carry_factor[1:], jnp.ones_like(carry_factor[:1])], axis=0)
    cum_back, adjoint_local = lax.associative_scan(
        affine, (jnp.flip(following, 0), jnp.flip(state_grad, 0)), axis=0
    )
    cum_back = jnp.flip(cum_back, 0)
    adjoint_local = jnp.flip(adjoint_local, 0)
    summary_back = (carry_factor[0] * cum_back[0], carry_factor[0] * adjoint_local[0])
    arriving = entering_2(
        summary_back,
        "seq",
        affine,
        (jnp.ones_like(summary_back[0]), jnp.zeros_like(summary_back[1])),
        True,
    )
    adjoint_in = arriving[1]
    adjoint = adjoint_local + cum_back * adjoint_in[None, :]
    previous_state = jnp.concatenate([state_in[None, :], state[:-1]], axis=0)

    def local_coefficients(rate_value, inlet_value, conv_part, decay_value):
        return coefficients(rate_value, inlet_value, conv_part, decay_value, init_rows, keep)

    unused, coefficient_pull = jax.vjp(
        local_coefficients, rate_pre, inlet_pre, conv_value, decay_flat
    )
    rate_grad, inlet_grad, conv_direct, decay_part = coefficient_pull(
        (adjoint * previous_state, adjoint)
    )
    rate_low = rate_grad.astype(jnp.bfloat16).reshape(token_count, slot_count, block_width)
    inlet_low = inlet_grad.astype(jnp.bfloat16).reshape(token_count, slot_count, block_width)
    rate_weight_grad = jnp.einsum(
        "rsi,rso->sio", grouped, rate_low, preferred_element_type=jnp.float32
    )
    inlet_weight_grad = jnp.einsum(
        "rsi,rso->sio", grouped, inlet_low, preferred_element_type=jnp.float32
    )
    rate_bias_grad = jnp.sum(rate_low.astype(jnp.float32), axis=0)
    inlet_bias_grad = jnp.sum(inlet_low.astype(jnp.float32), axis=0)
    conv_back = jnp.einsum(
        "rso,sio->rsi", rate_low, rate_weight, preferred_element_type=jnp.float32
    )
    conv_back = conv_back + jnp.einsum(
        "rso,sio->rsi", inlet_low, inlet_weight, preferred_element_type=jnp.float32
    )
    conv_low_grad = (conv_direct + conv_back.reshape(token_count, local_width)).astype(jnp.bfloat16)
    rim_back = passed_along(conv_low_grad[: taps - 1], "seq", -1)
    ahead = jnp.concatenate([conv_low_grad, rim_back], axis=0).astype(jnp.float32)
    own_grad = ahead[:token_count]
    recur_grad = jnp.zeros((token_count, local_width), jnp.float32)
    tap_grads = []
    for tap_index in range(taps):
        lead = taps - 1 - tap_index
        valid_here = (offset >= tap_index).astype(jnp.float32)[:, None]
        tap_grads.append(
            jnp.sum(own_grad * extended[lead : lead + token_count] * valid_here, axis=0)
        )
        valid_ahead = (offset_all[tap_index : tap_index + token_count] >= tap_index).astype(
            jnp.float32
        )[:, None]
        recur_grad = (
            recur_grad
            + taps_flat[tap_index][None, :]
            * ahead[tap_index : tap_index + token_count]
            * valid_ahead
        )
    conv_taps_grad = jnp.stack(tap_grads, axis=0).reshape(taps, slot_count, block_width)
    conv_bias_grad = jnp.sum(own_grad, axis=0).reshape(slot_count, block_width)
    recur_low_grad = recur_grad.astype(jnp.bfloat16)
    gelu_weight_grad = contract_first(mix_full, gelu_low)
    recur_weight_grad = contract_first(mix_full, recur_low_grad)
    norm_mix_part = contract_last(gelu_low, gelu_weight) + contract_last(
        recur_low_grad, recur_weight
    )
    norm_mix_grad = collect(norm_mix_part)
    unused, mix_norm_pull = jax.vjp(normalize, stream_float, mix_gain)
    stream_norm_grad, mix_gain_part = mix_norm_pull(norm_mix_grad)
    stream_grad = middle_grad + stream_norm_grad
    finals_local = lax.dot_general(closing, state * live, (((0,), (0,)), ((), ())), precision=HIGH)
    finals_wide = jnp.zeros((finals_local.shape[0], local_width * lax.axis_size("ch")), jnp.float32)
    finals_wide = lax.dynamic_update_slice(
        finals_wide, finals_local, (jnp.int32(0), lax.axis_index("ch") * local_width)
    )
    final_states, mix_gain_grad, ffn_gain_grad = lax.psum(
        (finals_wide, mix_gain_part, ffn_gain_part), ("seq", "ch")
    )
    summed = (
        lax.psum_scatter(gelu_weight_grad, "seq", scatter_dimension=0, tiled=True),
        lax.psum_scatter(recur_weight_grad, "seq", scatter_dimension=0, tiled=True),
        lax.psum_scatter(conv_taps_grad, "seq", scatter_dimension=2, tiled=True),
        lax.psum_scatter(conv_bias_grad, "seq", scatter_dimension=1, tiled=True),
        lax.psum_scatter(rate_weight_grad, "seq", scatter_dimension=1, tiled=True),
        lax.psum_scatter(rate_bias_grad, "seq", scatter_dimension=1, tiled=True),
        lax.psum_scatter(inlet_weight_grad, "seq", scatter_dimension=1, tiled=True),
        lax.psum_scatter(inlet_bias_grad, "seq", scatter_dimension=1, tiled=True),
        lax.psum_scatter(
            decay_part.reshape(slot_count, block_width), "seq", scatter_dimension=1, tiled=True
        ),
        lax.psum_scatter(out_weight_grad, "seq", scatter_dimension=1, tiled=True),
        lax.psum_scatter(
            pair_weight_grad[:, :hidden_width], "seq", scatter_dimension=0, tiled=True
        ),
        lax.psum_scatter(
            pair_weight_grad[:, hidden_width:], "seq", scatter_dimension=0, tiled=True
        ),
        lax.psum_scatter(down_weight_grad, "seq", scatter_dimension=1, tiled=True),
    )
    return (
        final_states,
        mixed_out,
        stream_grad,
        mix_gain_grad,
        summed[0],
        summed[1],
        summed[2],
        summed[3],
        summed[4],
        summed[5],
        summed[6],
        summed[7],
        summed[8],
        summed[9],
        ffn_gain_grad,
        summed[10],
        summed[11],
        summed[12],
    )


def ffn_kernel(
    sizes, low_ref, cot_ref, weight_ref, out_ref, grad_ref, dw_ref,
    wt, full, cfull, hid, gat, upg, part, sib, psum_buf, pl_in, zsum, z_in, dwl,
    ws, wr, zs, zr, ps, pr, cs, cr, rs1, rr1, rs2, rr2, rs3, rr3, ds_, dr_,
):
    n_seq, n_ch, rows, width, sl = sizes
    n_z = n_seq // 2
    s, c = lax.axis_index("seq"), lax.axis_index("ch")
    z, x = s // 2, s % 2
    y, core = c // 2, c % 2

    def dev(zz, xx, yy, cc):
        return (zz * 2 + xx, yy * 2 + cc)

    def block(zz, xx, yy, cc):
        return pl.multiple_of(((zz * 2 + xx) * n_ch + yy * 2 + cc) * rows, rows)

    plane = [(1 - x, y), (x, 1 - y), (1 - x, 1 - y)]
    z_to = [(z + k) % n_z for k in range(n_z)]
    z_from = [(z + n_z - k) % n_z for k in range(n_z)]
    s_to = [(s + k) % n_seq for k in range(n_seq)]
    s_from = [(s + n_seq - k) % n_seq for k in range(n_seq)]

    barrier = pltpu.get_barrier_semaphore()
    peers = [(s_to[k], c) for k in range(1, n_seq)]
    peers += [dev(z, x, y, 1 - core)] + [dev(z, x, 1 - y, core), dev(z, 1 - x, 1 - y, core)]
    for peer in peers:
        pl.semaphore_signal(barrier, inc=1, device_id=peer, device_id_type=MESH)
    pl.semaphore_wait(barrier, len(peers))

    def send(src, dst, ssem, rsem, to):
        copy = pltpu.make_async_remote_copy(
            src_ref=src, dst_ref=dst, send_sem=ssem, recv_sem=rsem,
            device_id=to, device_id_type=MESH,
        )
        copy.start()
        return copy

    sent = []
    arrays = [(low_ref, full), (cot_ref, cfull)]
    mine = block(z, x, y, core)
    for a, (src, dst) in enumerate(arrays):
        for k in range(1, n_z):
            sent.append(send(src, dst.at[pl.ds(mine, rows)], zs.at[a, k], zr.at[a, k], dev(z_to[k], x, y, core)))
    own_cols = pl.multiple_of(s * width, width)
    for k in range(1, n_seq):
        sent.append(send(
            weight_ref.at[:, pl.ds(pl.multiple_of(s_to[k] * sl, sl), sl), :],
            wt.at[:, :, pl.ds(own_cols, width)], ws.at[k], wr.at[k], (s_to[k], c),
        ))
    for src, dst in arrays:
        dst[pl.ds(mine, rows), :] = src[...]
    wt[:, :, pl.ds(own_cols, width)] = weight_ref[:, pl.ds(pl.multiple_of(s * sl, sl), sl), :]

    sibling = dev(z, x, y, 1 - core)

    def rows_of(dst, zz, p):
        xx, yy = ((x, y) if p is None else plane[p])
        return dst.at[pl.ds(block(zz, xx, yy, core), rows)]

    def recv(dst_view, ssem, rsem):
        pltpu.make_async_remote_copy(
            src_ref=dst_view, dst_ref=dst_view, send_sem=ssem, recv_sem=rsem,
            device_id=(s, c), device_id_type=MESH,
        ).wait_recv()

    def spread_plane(a, j):
        dst = arrays[a][1]
        view = rows_of(dst, z_from[j], None)
        for p, (xx, yy) in enumerate(plane):
            sent.append(send(view, view, ps.at[a, j, p], pr.at[a, j, p], dev(z, xx, yy, core)))
        sent.append(send(view, view, cs.at[a, j, 3], cr.at[a, j, 3], sibling))

    def pass_to_sibling(a, j):
        dst = arrays[a][1]
        for p in range(3):
            view = rows_of(dst, z_from[j], p)
            recv(view, ps.at[a, j, p], pr.at[a, j, p])
            sent.append(send(view, view, cs.at[a, j, p], cr.at[a, j, p], sibling))

    def from_sibling(a, j):
        dst = arrays[a][1]
        for p in range(4):
            xx, yy = (x, y) if p == 3 else plane[p]
            view = dst.at[pl.ds(block(z_from[j], xx, yy, 1 - core), rows)]
            recv(view, cs.at[a, j, p], cr.at[a, j, p])

    for a in (0, 1):
        spread_plane(a, 0)
    for j in range(1, n_z):
        for a in (0, 1):
            view = rows_of(arrays[a][1], z_from[j], None)
            recv(view, zs.at[a, j], zr.at[a, j])
            spread_plane(a, j)
    for j in range(n_z):
        for a in (0, 1):
            pass_to_sibling(a, j)
    for k in range(1, n_seq):
        view = wt.at[:, :, pl.ds(pl.multiple_of(s_from[k] * width, width), width)]
        recv(view, ws.at[k], wr.at[k])

    group = n_ch * 2 * rows
    per = 2 * 2 * rows

    def compute(j):
        for a in (0, 1):
            from_sibling(a, j)
        at = pl.multiple_of(z_from[j] * group, group)
        rows_in = full[pl.ds(at, group), :]
        gate = contract_last(rows_in, wt[0])
        up = contract_last(rows_in, wt[1])
        hg = contract_last(cfull[pl.ds(at, group), :], wt[2])
        inner = K1 * (gate + K2 * gate * gate * gate)
        t = jnp.tanh(inner)
        sm = 0.5 * gate * (1.0 + t)
        dsm = 0.5 * (1.0 + t) + 0.5 * gate * (1.0 - t * t) * K1 * (1.0 + 3.0 * K2 * gate * gate)
        hidden = (sm * up).astype(jnp.bfloat16)
        gg = (hg * up * dsm).astype(jnp.bfloat16)
        ug = (hg * sm).astype(jnp.bfloat16)
        hid[pl.ds(at, group), :] = hidden
        gat[pl.ds(at, group), :] = gg
        upg[pl.ds(at, group), :] = ug

        def tile(i, _):
            cols = pl.ds(pl.multiple_of(i * 256, 256), 256)
            nf = jnp.dot(gg, wt[0, :, cols], preferred_element_type=jnp.float32)
            nf = nf + jnp.dot(ug, wt[1, :, cols], preferred_element_type=jnp.float32)
            ot = jnp.dot(hidden, wt[2, :, cols], preferred_element_type=jnp.float32)
            for b, value in ((0, nf), (1, ot)):
                value = value.astype(jnp.bfloat16)
                for xx in range(2):
                    for yy in range(2):
                        for cc in range(2):
                            at_row = (xx * 4 + yy * 2 + cc) * rows
                            part[j, b, cc, xx * 2 + yy, :, cols] = value[at_row : at_row + rows]
            return 0

        lax.fori_loop(0, full.shape[1] // 256, tile, 0)
        for b in (0, 1):
            sent.append(send(part.at[j, b, 1 - core], sib.at[j, b], rs1.at[j, b], rr1.at[j, b], sibling))

    def second(j, b):
        recv(sib.at[j, b], rs1.at[j, b], rr1.at[j, b])

        def add(i, _):
            psum_buf[j, b, i] = (part[j, b, core, i].astype(jnp.float32) + sib[j, b, i].astype(jnp.float32)).astype(jnp.bfloat16)
            return 0

        lax.fori_loop(0, 4, add, 0)
        for p, (xx, yy) in enumerate(plane):
            sent.append(send(psum_buf.at[j, b, xx * 2 + yy], pl_in.at[j, b, p], rs2.at[j, b, p], rr2.at[j, b, p], dev(z, xx, yy, core)))

    def third(j, b):
        total = psum_buf[j, b, x * 2 + y].astype(jnp.float32)
        for p in range(3):
            recv(pl_in.at[j, b, p], rs2.at[j, b, p], rr2.at[j, b, p])
            total = total + pl_in[j, b, p].astype(jnp.float32)
        if j == 0:
            (grad_ref, out_ref)[b][...] = total
        else:
            zsum[j, b] = total.astype(jnp.bfloat16)
            sent.append(send(zsum.at[j, b], z_in.at[j, b], rs3.at[j, b], rr3.at[j, b], dev(z_from[j], x, y, core)))

    for j in range(n_z):
        compute(j)
        for b in (0, 1):
            if j >= 1:
                second(j - 1, b)
            if j >= 2:
                third(j - 2, b)
    for b in (0, 1):
        second(n_z - 1, b)
    for b in (0, 1):
        third(n_z - 2, b)

    def grads(i, _):
        cols = pl.ds(pl.multiple_of(i * 256, 256), 256)
        dwl[0, :, cols] = contract_first(gat[...], full[:, cols]).astype(jnp.bfloat16)
        dwl[1, :, cols] = contract_first(upg[...], full[:, cols]).astype(jnp.bfloat16)
        dwl[2, :, cols] = contract_first(hid[...], cfull[:, cols]).astype(jnp.bfloat16)
        return 0

    lax.fori_loop(0, full.shape[1] // 256, grads, 0)
    own_rows = pl.multiple_of(s * sl, sl)
    for k in range(1, n_seq):
        cols = pl.ds(pl.multiple_of(s_to[k] * width, width), width)
        sent.append(send(dwl.at[:, :, cols], dw_ref.at[:, pl.ds(own_rows, sl), :], ds_.at[k], dr_.at[k], (s_to[k], c)))
    dw_ref[:, pl.ds(own_rows, sl), :] = dwl[:, :, pl.ds(own_cols, width)]
    for b in (0, 1):
        third(n_z - 1, b)
    for b in (0, 1):
        for j in range(1, n_z):
            recv(z_in.at[j, b], rs3.at[j, b], rr3.at[j, b])
            ref = (grad_ref, out_ref)[b]
            ref[...] += z_in[j, b].astype(jnp.float32)
    for k in range(1, n_seq):
        view = dw_ref.at[:, pl.ds(pl.multiple_of(s_from[k] * sl, sl), sl), :]
        recv(view, ds_.at[k], dr_.at[k])
    for copy in sent:
        copy.wait_send()


def ffn(low, cot, weights):
    n_seq, n_ch = lax.axis_size("seq"), lax.axis_size("ch")
    rows, d = low.shape
    width = weights.shape[2]
    sl = weights.shape[1] // n_seq
    n_z = n_seq // 2
    tokens = n_seq * n_ch * rows
    bf, f32 = jnp.bfloat16, jnp.float32
    dma = pltpu.SemaphoreType.DMA
    vmem = pl.BlockSpec(memory_space=pltpu.VMEM)
    return pl.pallas_call(
        functools.partial(ffn_kernel, (n_seq, n_ch, rows, width, sl)),
        out_shape=[
            jax.ShapeDtypeStruct((rows, d), f32),
            jax.ShapeDtypeStruct((rows, d), f32),
            jax.ShapeDtypeStruct(weights.shape, bf),
        ],
        in_specs=[vmem] * 3,
        out_specs=[vmem] * 3,
        scratch_shapes=[
            pltpu.VMEM((3, sl, d), bf),
            pltpu.VMEM((tokens, d), bf),
            pltpu.VMEM((tokens, d), bf),
            pltpu.VMEM((tokens, sl), bf),
            pltpu.VMEM((tokens, sl), bf),
            pltpu.VMEM((tokens, sl), bf),
            pltpu.VMEM((n_z, 2, 2, 4, rows, d), bf),
            pltpu.VMEM((n_z, 2, 4, rows, d), bf),
            pltpu.VMEM((n_z, 2, 4, rows, d), bf),
            pltpu.VMEM((n_z, 2, 3, rows, d), bf),
            pltpu.VMEM((n_z, 2, rows, d), bf),
            pltpu.VMEM((n_z, 2, rows, d), bf),
            pltpu.VMEM((3, sl, d), bf),
            dma((n_seq,)), dma((n_seq,)),
            dma((2, n_z)), dma((2, n_z)),
            dma((2, n_z, 3)), dma((2, n_z, 3)),
            dma((2, n_z, 4)), dma((2, n_z, 4)),
            dma((n_z, 2)), dma((n_z, 2)),
            dma((n_z, 2, 3)), dma((n_z, 2, 3)),
            dma((n_z, 2)), dma((n_z, 2)),
            dma((n_seq,)), dma((n_seq,)),
        ],
        compiler_params=pltpu.CompilerParams(
            collective_id=1, has_side_effects=True, vmem_limit_bytes=VMEM_BYTES
        ),
    )(low, cot, weights)


def small_body(
    stream,
    cotangent,
    mix_gain,
    gelu_weight,
    recur_weight,
    conv_taps,
    conv_bias,
    rate_weight,
    rate_bias,
    inlet_weight,
    inlet_bias,
    decay_param,
    init_states,
    out_weight,
    ffn_gain,
    gate_weight,
    up_weight,
    down_weight,
    doc_lengths,
    block_counts,
):
    slot_count = rate_weight.shape[0]
    block_width = rate_weight.shape[1]
    local_width = slot_count * block_width
    taps = conv_taps.shape[0]
    token_count = stream.shape[0] * lax.axis_size("ch")
    hidden_width = gate_weight.shape[1]
    base = lax.axis_index("seq") * token_count
    offset_all, opening, closing = doc_view(doc_lengths, base, token_count + taps - 1)
    offset = offset_all[:token_count]
    opening = opening[:token_count]
    closing = closing[:token_count]
    keep = (offset > 0).astype(jnp.float32)[:, None]
    slot_live = (jnp.arange(slot_count, dtype=jnp.int32) < block_counts[0]).astype(jnp.float32)
    live = jnp.repeat(slot_live, block_width)[None, :]
    taps_flat = conv_taps.reshape(taps, local_width)
    decay_flat = decay_param.reshape(1, local_width)
    stream_float = stream.astype(jnp.float32)
    mix_low = normalize(stream_float, mix_gain).astype(jnp.bfloat16)
    mix_full = spread(mix_low)
    gelu_pre = jnp.dot(mix_full, gelu_weight, preferred_element_type=jnp.float32)
    recur_low = jnp.dot(mix_full, recur_weight, preferred_element_type=jnp.float32).astype(
        jnp.bfloat16
    )
    rim = passed_along(recur_low[token_count - taps + 1 :], "seq", 1)
    extended = jnp.concatenate([rim, recur_low], axis=0).astype(jnp.float32)
    conv_pre = conv_bias.reshape(1, local_width)
    for tap_index in range(taps):
        valid = (offset >= tap_index).astype(jnp.float32)[:, None]
        lead = taps - 1 - tap_index
        conv_pre = (
            conv_pre + taps_flat[tap_index][None, :] * extended[lead : lead + token_count] * valid
        )
    conv_low = conv_pre.astype(jnp.bfloat16)
    conv_value = conv_low.astype(jnp.float32)
    grouped = conv_low.reshape(token_count, slot_count, block_width)
    rate_pre = (
        jnp.einsum("rsi,sio->rso", grouped, rate_weight, preferred_element_type=jnp.float32)
        + rate_bias[None]
    ).reshape(token_count, local_width)
    inlet_pre = (
        jnp.einsum("rsi,sio->rso", grouped, inlet_weight, preferred_element_type=jnp.float32)
        + inlet_bias[None]
    ).reshape(token_count, local_width)
    init_rows = jnp.dot(opening, init_states, precision=HIGH)
    carry_factor, source = coefficients(
        rate_pre, inlet_pre, conv_value, decay_flat, init_rows, keep
    )
    cumulative, local_state = lax.associative_scan(affine, (carry_factor, source), axis=0)
    summary = (cumulative[-1], local_state[-1])
    entering = entering_2(
        summary, "seq", affine, (jnp.ones_like(summary[0]), jnp.zeros_like(summary[1])), False
    )
    state_in = entering[1]
    state = local_state + cumulative * state_in[None, :]
    gelu_value = smooth(gelu_pre)
    product_low = (gelu_value * state * live).astype(jnp.bfloat16)
    branch = collect(jnp.dot(product_low, out_weight, preferred_element_type=jnp.float32))
    middle = stream_float + branch
    ffn_low = normalize(middle, ffn_gain).astype(jnp.bfloat16)
    weights = jnp.stack([gate_weight.T, up_weight.T, down_weight])
    ffn_sum, norm_ffn_grad, dw = ffn(ffn_low, cotangent, weights)
    mixed_out = (middle + ffn_sum).astype(jnp.bfloat16)
    unused, ffn_norm_pull = jax.vjp(normalize, middle, ffn_gain)
    middle_norm_grad, ffn_gain_part = ffn_norm_pull(norm_ffn_grad)
    middle_grad = cotangent.astype(jnp.float32) + middle_norm_grad
    branch_full = spread(middle_grad.astype(jnp.bfloat16))
    out_weight_grad = contract_first(product_low, branch_full)
    product_grad = contract_last(branch_full, out_weight)
    state_grad = product_grad * gelu_value * live
    unused, gelu_pull = jax.vjp(smooth, gelu_pre)
    gelu_low = gelu_pull(product_grad * state * live)[0].astype(jnp.bfloat16)
    following = jnp.concatenate([carry_factor[1:], jnp.ones_like(carry_factor[:1])], axis=0)
    cum_back, adjoint_local = lax.associative_scan(
        affine, (jnp.flip(following, 0), jnp.flip(state_grad, 0)), axis=0
    )
    cum_back = jnp.flip(cum_back, 0)
    adjoint_local = jnp.flip(adjoint_local, 0)
    summary_back = (carry_factor[0] * cum_back[0], carry_factor[0] * adjoint_local[0])
    arriving = entering_2(
        summary_back,
        "seq",
        affine,
        (jnp.ones_like(summary_back[0]), jnp.zeros_like(summary_back[1])),
        True,
    )
    adjoint_in = arriving[1]
    adjoint = adjoint_local + cum_back * adjoint_in[None, :]
    previous_state = jnp.concatenate([state_in[None, :], state[:-1]], axis=0)

    def local_coefficients(rate_value, inlet_value, conv_part, decay_value):
        return coefficients(rate_value, inlet_value, conv_part, decay_value, init_rows, keep)

    unused, coefficient_pull = jax.vjp(
        local_coefficients, rate_pre, inlet_pre, conv_value, decay_flat
    )
    rate_grad, inlet_grad, conv_direct, decay_part = coefficient_pull(
        (adjoint * previous_state, adjoint)
    )
    rate_low = rate_grad.astype(jnp.bfloat16).reshape(token_count, slot_count, block_width)
    inlet_low = inlet_grad.astype(jnp.bfloat16).reshape(token_count, slot_count, block_width)
    rate_weight_grad = jnp.einsum(
        "rsi,rso->sio", grouped, rate_low, preferred_element_type=jnp.float32
    )
    inlet_weight_grad = jnp.einsum(
        "rsi,rso->sio", grouped, inlet_low, preferred_element_type=jnp.float32
    )
    rate_bias_grad = jnp.sum(rate_low.astype(jnp.float32), axis=0)
    inlet_bias_grad = jnp.sum(inlet_low.astype(jnp.float32), axis=0)
    conv_back = jnp.einsum(
        "rso,sio->rsi", rate_low, rate_weight, preferred_element_type=jnp.float32
    )
    conv_back = conv_back + jnp.einsum(
        "rso,sio->rsi", inlet_low, inlet_weight, preferred_element_type=jnp.float32
    )
    conv_low_grad = (conv_direct + conv_back.reshape(token_count, local_width)).astype(jnp.bfloat16)
    rim_back = passed_along(conv_low_grad[: taps - 1], "seq", -1)
    ahead = jnp.concatenate([conv_low_grad, rim_back], axis=0).astype(jnp.float32)
    own_grad = ahead[:token_count]
    recur_grad = jnp.zeros((token_count, local_width), jnp.float32)
    tap_grads = []
    for tap_index in range(taps):
        lead = taps - 1 - tap_index
        valid_here = (offset >= tap_index).astype(jnp.float32)[:, None]
        tap_grads.append(
            jnp.sum(own_grad * extended[lead : lead + token_count] * valid_here, axis=0)
        )
        valid_ahead = (offset_all[tap_index : tap_index + token_count] >= tap_index).astype(
            jnp.float32
        )[:, None]
        recur_grad = (
            recur_grad
            + taps_flat[tap_index][None, :]
            * ahead[tap_index : tap_index + token_count]
            * valid_ahead
        )
    conv_taps_grad = jnp.stack(tap_grads, axis=0).reshape(taps, slot_count, block_width)
    conv_bias_grad = jnp.sum(own_grad, axis=0).reshape(slot_count, block_width)
    recur_low_grad = recur_grad.astype(jnp.bfloat16)
    gelu_weight_grad = contract_first(mix_full, gelu_low)
    recur_weight_grad = contract_first(mix_full, recur_low_grad)
    norm_mix_part = contract_last(gelu_low, gelu_weight) + contract_last(
        recur_low_grad, recur_weight
    )
    norm_mix_grad = collect(norm_mix_part)
    unused, mix_norm_pull = jax.vjp(normalize, stream_float, mix_gain)
    stream_norm_grad, mix_gain_part = mix_norm_pull(norm_mix_grad)
    stream_grad = middle_grad + stream_norm_grad
    finals_local = lax.dot_general(closing, state * live, (((0,), (0,)), ((), ())), precision=HIGH)
    finals_wide = jnp.zeros((finals_local.shape[0], local_width * lax.axis_size("ch")), jnp.float32)
    finals_wide = lax.dynamic_update_slice(
        finals_wide, finals_local, (jnp.int32(0), lax.axis_index("ch") * local_width)
    )
    final_states, mix_gain_grad, ffn_gain_grad = lax.psum(
        (finals_wide, mix_gain_part, ffn_gain_part), ("seq", "ch")
    )
    summed = (
        lax.psum_scatter(gelu_weight_grad, "seq", scatter_dimension=0, tiled=True),
        lax.psum_scatter(recur_weight_grad, "seq", scatter_dimension=0, tiled=True),
        lax.psum_scatter(conv_taps_grad, "seq", scatter_dimension=2, tiled=True),
        lax.psum_scatter(conv_bias_grad, "seq", scatter_dimension=1, tiled=True),
        lax.psum_scatter(rate_weight_grad, "seq", scatter_dimension=1, tiled=True),
        lax.psum_scatter(rate_bias_grad, "seq", scatter_dimension=1, tiled=True),
        lax.psum_scatter(inlet_weight_grad, "seq", scatter_dimension=1, tiled=True),
        lax.psum_scatter(inlet_bias_grad, "seq", scatter_dimension=1, tiled=True),
        lax.psum_scatter(
            decay_part.reshape(slot_count, block_width), "seq", scatter_dimension=1, tiled=True
        ),
        lax.psum_scatter(out_weight_grad, "seq", scatter_dimension=1, tiled=True),
        dw[0].T.astype(jnp.float32),
        dw[1].T.astype(jnp.float32),
        dw[2].astype(jnp.float32),
    )
    return (
        final_states,
        mixed_out,
        stream_grad,
        mix_gain_grad,
        summed[0],
        summed[1],
        summed[2],
        summed[3],
        summed[4],
        summed[5],
        summed[6],
        summed[7],
        summed[8],
        summed[9],
        ffn_gain_grad,
        summed[10],
        summed[11],
        summed[12],
    )


def solution(mesh):
    in_specs = (
        P(("seq", "ch"), None),
        P(("seq", "ch"), None),
        P(),
        P(None, "ch"),
        P(None, "ch"),
        P(None, "ch", None),
        P("ch", None),
        P("ch", None, None),
        P("ch", None),
        P("ch", None, None),
        P("ch", None),
        P("ch", None),
        P(None, "ch"),
        P("ch", None),
        P(),
        P("seq", "ch"),
        P("seq", "ch"),
        P("ch", "seq"),
        P(),
        P("ch"),
    )
    out_specs = (
        P(),
        P(("seq", "ch"), None),
        P(("seq", "ch"), None),
        P(),
        P("seq", "ch"),
        P("seq", "ch"),
        P(None, "ch", "seq"),
        P("ch", "seq"),
        P("ch", "seq", None),
        P("ch", "seq"),
        P("ch", "seq", None),
        P("ch", "seq"),
        P("ch", "seq"),
        P("ch", "seq"),
        P(),
        P("seq", "ch"),
        P("seq", "ch"),
        P("ch", "seq"),
    )
    return jax.shard_map(small_body if mesh.shape['seq'] == 8 else body, mesh=mesh, in_specs=in_specs, out_specs=out_specs, check_vma=False)
```

```python
import functools

import jax
import jax.numpy as jnp
from jax import lax
from jax.experimental import pallas as pl
from jax.experimental.pallas import tpu as pltpu
from jax.sharding import PartitionSpec as P

EPS = 1e-06
HIGH = lax.Precision.HIGHEST
MESH = pl.DeviceIdType.MESH
K1 = 0.7978845608028654
K2 = 0.044715
VMEM_BYTES = 56 * 2**20


def passed_along(shard, axis, by):
    length = lax.axis_size(axis)
    pairs = [(i, i + by) for i in range(length) if 0 <= i + by < length]
    return lax.ppermute(shard, axis, pairs)


def entering_2(shard, axis, combine, identity, reverse):
    length, here = (lax.axis_size(axis), lax.axis_index(axis))
    everything = jax.tree.map(lambda part: lax.all_gather(part, axis), shard)
    start = jax.tree.map(
        lambda part, zero: jnp.broadcast_to(jnp.asarray(zero, part.dtype), part.shape),
        shard,
        identity,
    )

    def turn(k, before):
        at = length - 1 - k if reverse else k
        reached = at > here if reverse else at < here
        new = combine(before, jax.tree.map(lambda part: part[at], everything))
        return jax.tree.map(lambda a, b: jnp.where(reached, a, b), new, before)

    return lax.fori_loop(0, length, turn, start)


def normalize(values, gain):
    return values * lax.rsqrt(jnp.mean(values * values, axis=-1, keepdims=True) + EPS) * gain


def smooth(values):
    return jax.nn.gelu(values, approximate=True)


def affine(earlier, later):
    return (earlier[0] * later[0], later[0] * earlier[1] + later[1])


def doc_view(lengths, first, count):
    ends = jnp.cumsum(lengths)
    starts = ends - lengths
    position = first + jnp.arange(count, dtype=jnp.int32)
    owner = (position[:, None] >= starts[None, :]) & (position[:, None] < ends[None, :])
    start_of = jnp.sum(jnp.where(owner, starts[None, :], 0), axis=1)
    offset = position - start_of
    opening = (owner & (offset[:, None] == 0)).astype(jnp.float32)
    closing = (owner & (position[:, None] == ends[None, :] - 1)).astype(jnp.float32)
    return (offset, opening, closing)


def coefficients(rate_pre, inlet_pre, conv_value, decay, init_rows, keep):
    rate = jax.nn.sigmoid(rate_pre)
    inlet = jax.nn.sigmoid(inlet_pre)
    log_decay = -8.0 * rate * jax.nn.softplus(decay)
    factor = jnp.exp(log_decay)
    scale = jnp.sqrt(-jnp.expm1(2.0 * log_decay))
    carry_factor = keep * factor
    source = scale * inlet * conv_value + (1.0 - keep) * factor * init_rows
    return (carry_factor, source)


def spread(values):
    return lax.all_gather(values, "ch", axis=0, tiled=True)


def collect(terms):
    return lax.psum_scatter(terms, "ch", scatter_dimension=0, tiled=True)


def contract_last(left, right):
    return lax.dot_general(
        left, right, (((1,), (1,)), ((), ())), preferred_element_type=jnp.float32
    )


def contract_first(left, right):
    return lax.dot_general(
        left, right, (((0,), (0,)), ((), ())), preferred_element_type=jnp.float32
    )


def body(
    stream,
    cotangent,
    mix_gain,
    gelu_weight,
    recur_weight,
    conv_taps,
    conv_bias,
    rate_weight,
    rate_bias,
    inlet_weight,
    inlet_bias,
    decay_param,
    init_states,
    out_weight,
    ffn_gain,
    gate_weight,
    up_weight,
    down_weight,
    doc_lengths,
    block_counts,
):
    slot_count = rate_weight.shape[0]
    block_width = rate_weight.shape[1]
    local_width = slot_count * block_width
    taps = conv_taps.shape[0]
    token_count = stream.shape[0] * lax.axis_size("ch")
    hidden_width = gate_weight.shape[1]
    base = lax.axis_index("seq") * token_count
    offset_all, opening, closing = doc_view(doc_lengths, base, token_count + taps - 1)
    offset = offset_all[:token_count]
    opening = opening[:token_count]
    closing = closing[:token_count]
    keep = (offset > 0).astype(jnp.float32)[:, None]
    slot_live = (jnp.arange(slot_count, dtype=jnp.int32) < block_counts[0]).astype(jnp.float32)
    live = jnp.repeat(slot_live, block_width)[None, :]
    taps_flat = conv_taps.reshape(taps, local_width)
    decay_flat = decay_param.reshape(1, local_width)
    stream_float = stream.astype(jnp.float32)
    mix_low = normalize(stream_float, mix_gain).astype(jnp.bfloat16)
    mix_full = spread(mix_low)
    gelu_pre = jnp.dot(mix_full, gelu_weight, preferred_element_type=jnp.float32)
    recur_low = jnp.dot(mix_full, recur_weight, preferred_element_type=jnp.float32).astype(
        jnp.bfloat16
    )
    rim = passed_along(recur_low[token_count - taps + 1 :], "seq", 1)
    extended = jnp.concatenate([rim, recur_low], axis=0).astype(jnp.float32)
    conv_pre = conv_bias.reshape(1, local_width)
    for tap_index in range(taps):
        valid = (offset >= tap_index).astype(jnp.float32)[:, None]
        lead = taps - 1 - tap_index
        conv_pre = (
            conv_pre + taps_flat[tap_index][None, :] * extended[lead : lead + token_count] * valid
        )
    conv_low = conv_pre.astype(jnp.bfloat16)
    conv_value = conv_low.astype(jnp.float32)
    grouped = conv_low.reshape(token_count, slot_count, block_width)
    rate_pre = (
        jnp.einsum("rsi,sio->rso", grouped, rate_weight, preferred_element_type=jnp.float32)
        + rate_bias[None]
    ).reshape(token_count, local_width)
    inlet_pre = (
        jnp.einsum("rsi,sio->rso", grouped, inlet_weight, preferred_element_type=jnp.float32)
        + inlet_bias[None]
    ).reshape(token_count, local_width)
    init_rows = jnp.dot(opening, init_states, precision=HIGH)
    carry_factor, source = coefficients(
        rate_pre, inlet_pre, conv_value, decay_flat, init_rows, keep
    )
    cumulative, local_state = lax.associative_scan(affine, (carry_factor, source), axis=0)
    summary = (cumulative[-1], local_state[-1])
    entering = entering_2(
        summary, "seq", affine, (jnp.ones_like(summary[0]), jnp.zeros_like(summary[1])), False
    )
    state_in = entering[1]
    state = local_state + cumulative * state_in[None, :]
    gelu_value = smooth(gelu_pre)
    product_low = (gelu_value * state * live).astype(jnp.bfloat16)
    branch = collect(jnp.dot(product_low, out_weight, preferred_element_type=jnp.float32))
    middle = stream_float + branch
    ffn_low = normalize(middle, ffn_gain).astype(jnp.bfloat16)
    ffn_full = spread(ffn_low)
    stacked = jnp.concatenate([gate_weight, up_weight], axis=1)
    columns = ffn_full
    gate_up = jnp.dot(
        columns,
        lax.all_gather(stacked, "seq", axis=0, tiled=True),
        preferred_element_type=jnp.float32,
    )
    gate = gate_up[:, :hidden_width]
    upward = gate_up[:, hidden_width:]
    hidden = (smooth(gate) * upward).astype(jnp.bfloat16)
    ffn_terms = jnp.dot(
        hidden,
        lax.all_gather(down_weight, "seq", axis=1, tiled=True),
        preferred_element_type=jnp.float32,
    )
    mixed_out = (middle + collect(ffn_terms)).astype(jnp.bfloat16)
    out_grad_full = spread(cotangent)
    columns = out_grad_full
    hidden_grad = contract_last(columns, lax.all_gather(down_weight, "seq", axis=1, tiled=True))
    down_weight_grad = contract_first(hidden, out_grad_full)
    unused, pair_pull = jax.vjp(lambda left, right: smooth(left) * right, gate, upward)
    gate_grad, up_grad = pair_pull(hidden_grad)
    pair_low = jnp.concatenate([gate_grad, up_grad], axis=1).astype(jnp.bfloat16)
    pair_weight_grad = contract_first(ffn_full, pair_low)
    norm_ffn_part = contract_last(pair_low, lax.all_gather(stacked, "seq", axis=0, tiled=True))
    norm_ffn_grad = collect(norm_ffn_part)
    unused, ffn_norm_pull = jax.vjp(normalize, middle, ffn_gain)
    middle_norm_grad, ffn_gain_part = ffn_norm_pull(norm_ffn_grad)
    middle_grad = cotangent.astype(jnp.float32) + middle_norm_grad
    branch_full = spread(middle_grad.astype(jnp.bfloat16))
    out_weight_grad = contract_first(product_low, branch_full)
    product_grad = contract_last(branch_full, out_weight)
    state_grad = product_grad * gelu_value * live
    unused, gelu_pull = jax.vjp(smooth, gelu_pre)
    gelu_low = gelu_pull(product_grad * state * live)[0].astype(jnp.bfloat16)
    following = jnp.concatenate([carry_factor[1:], jnp.ones_like(carry_factor[:1])], axis=0)
    cum_back, adjoint_local = lax.associative_scan(
        affine, (jnp.flip(following, 0), jnp.flip(state_grad, 0)), axis=0
    )
    cum_back = jnp.flip(cum_back, 0)
    adjoint_local = jnp.flip(adjoint_local, 0)
    summary_back = (carry_factor[0] * cum_back[0], carry_factor[0] * adjoint_local[0])
    arriving = entering_2(
        summary_back,
        "seq",
        affine,
        (jnp.ones_like(summary_back[0]), jnp.zeros_like(summary_back[1])),
        True,
    )
    adjoint_in = arriving[1]
    adjoint = adjoint_local + cum_back * adjoint_in[None, :]
    previous_state = jnp.concatenate([state_in[None, :], state[:-1]], axis=0)

    def local_coefficients(rate_value, inlet_value, conv_part, decay_value):
        return coefficients(rate_value, inlet_value, conv_part, decay_value, init_rows, keep)

    unused, coefficient_pull = jax.vjp(
        local_coefficients, rate_pre, inlet_pre, conv_value, decay_flat
    )
    rate_grad, inlet_grad, conv_direct, decay_part = coefficient_pull(
        (adjoint * previous_state, adjoint)
    )
    rate_low = rate_grad.astype(jnp.bfloat16).reshape(token_count, slot_count, block_width)
    inlet_low = inlet_grad.astype(jnp.bfloat16).reshape(token_count, slot_count, block_width)
    rate_weight_grad = jnp.einsum(
        "rsi,rso->sio", grouped, rate_low, preferred_element_type=jnp.float32
    )
    inlet_weight_grad = jnp.einsum(
        "rsi,rso->sio", grouped, inlet_low, preferred_element_type=jnp.float32
    )
    rate_bias_grad = jnp.sum(rate_low.astype(jnp.float32), axis=0)
    inlet_bias_grad = jnp.sum(inlet_low.astype(jnp.float32), axis=0)
    conv_back = jnp.einsum(
        "rso,sio->rsi", rate_low, rate_weight, preferred_element_type=jnp.float32
    )
    conv_back = conv_back + jnp.einsum(
        "rso,sio->rsi", inlet_low, inlet_weight, preferred_element_type=jnp.float32
    )
    conv_low_grad = (conv_direct + conv_back.reshape(token_count, local_width)).astype(jnp.bfloat16)
    rim_back = passed_along(conv_low_grad[: taps - 1], "seq", -1)
    ahead = jnp.concatenate([conv_low_grad, rim_back], axis=0).astype(jnp.float32)
    own_grad = ahead[:token_count]
    recur_grad = jnp.zeros((token_count, local_width), jnp.float32)
    tap_grads = []
    for tap_index in range(taps):
        lead = taps - 1 - tap_index
        valid_here = (offset >= tap_index).astype(jnp.float32)[:, None]
        tap_grads.append(
            jnp.sum(own_grad * extended[lead : lead + token_count] * valid_here, axis=0)
        )
        valid_ahead = (offset_all[tap_index : tap_index + token_count] >= tap_index).astype(
            jnp.float32
        )[:, None]
        recur_grad = (
            recur_grad
            + taps_flat[tap_index][None, :]
            * ahead[tap_index : tap_index + token_count]
            * valid_ahead
        )
    conv_taps_grad = jnp.stack(tap_grads, axis=0).reshape(taps, slot_count, block_width)
    conv_bias_grad = jnp.sum(own_grad, axis=0).reshape(slot_count, block_width)
    recur_low_grad = recur_grad.astype(jnp.bfloat16)
    gelu_weight_grad = contract_first(mix_full, gelu_low)
    recur_weight_grad = contract_first(mix_full, recur_low_grad)
    norm_mix_part = contract_last(gelu_low, gelu_weight) + contract_last(
        recur_low_grad, recur_weight
    )
    norm_mix_grad = collect(norm_mix_part)
    unused, mix_norm_pull = jax.vjp(normalize, stream_float, mix_gain)
    stream_norm_grad, mix_gain_part = mix_norm_pull(norm_mix_grad)
    stream_grad = middle_grad + stream_norm_grad
    finals_local = lax.dot_general(closing, state * live, (((0,), (0,)), ((), ())), precision=HIGH)
    finals_wide = jnp.zeros((finals_local.shape[0], local_width * lax.axis_size("ch")), jnp.float32)
    finals_wide = lax.dynamic_update_slice(
        finals_wide, finals_local, (jnp.int32(0), lax.axis_index("ch") * local_width)
    )
    final_states, mix_gain_grad, ffn_gain_grad = lax.psum(
        (finals_wide, mix_gain_part, ffn_gain_part), ("seq", "ch")
    )
    summed = (
        lax.psum_scatter(gelu_weight_grad, "seq", scatter_dimension=0, tiled=True),
        lax.psum_scatter(recur_weight_grad, "seq", scatter_dimension=0, tiled=True),
        lax.psum_scatter(conv_taps_grad, "seq", scatter_dimension=2, tiled=True),
        lax.psum_scatter(conv_bias_grad, "seq", scatter_dimension=1, tiled=True),
        lax.psum_scatter(rate_weight_grad, "seq", scatter_dimension=1, tiled=True),
        lax.psum_scatter(rate_bias_grad, "seq", scatter_dimension=1, tiled=True),
        lax.psum_scatter(inlet_weight_grad, "seq", scatter_dimension=1, tiled=True),
        lax.psum_scatter(inlet_bias_grad, "seq", scatter_dimension=1, tiled=True),
        lax.psum_scatter(
            decay_part.reshape(slot_count, block_width), "seq", scatter_dimension=1, tiled=True
        ),
        lax.psum_scatter(out_weight_grad, "seq", scatter_dimension=1, tiled=True),
        lax.psum_scatter(
            pair_weight_grad[:, :hidden_width], "seq", scatter_dimension=0, tiled=True
        ),
        lax.psum_scatter(
            pair_weight_grad[:, hidden_width:], "seq", scatter_dimension=0, tiled=True
        ),
        lax.psum_scatter(down_weight_grad, "seq", scatter_dimension=1, tiled=True),
    )
    return (
        final_states,
        mixed_out,
        stream_grad,
        mix_gain_grad,
        summed[0],
        summed[1],
        summed[2],
        summed[3],
        summed[4],
        summed[5],
        summed[6],
        summed[7],
        summed[8],
        summed[9],
        ffn_gain_grad,
        summed[10],
        summed[11],
        summed[12],
    )


class Net:
    def __init__(self, n_seq, n_ch, rows, send_sems, recv_sems):
        self.n_seq, self.n_ch, self.rows = n_seq, n_ch, rows
        self.n_z = n_seq // 2
        self.send_sems, self.recv_sems = send_sems, recv_sems
        self.tags, self.sent = {}, []
        self.s, self.c = lax.axis_index("seq"), lax.axis_index("ch")
        s, c, n_z = self.s, self.c, self.n_z
        self.z, self.x, self.y, self.core = s // 2, s % 2, c // 2, c % 2
        x, y = self.x, self.y
        self.plane = [(1 - x, y), (x, 1 - y), (1 - x, 1 - y)]
        self.z_to = [(self.z + k) % n_z for k in range(n_z)]
        self.z_from = [(self.z + n_z - k) % n_z for k in range(n_z)]
        self.s_to = [(s + k) % n_seq for k in range(n_seq)]
        self.s_from = [(s + n_seq - k) % n_seq for k in range(n_seq)]
        self.sibling = self.dev(self.z, x, y, 1 - self.core)
        self.across = self.dev(self.z, x, 1 - y, self.core)

    def dev(self, z, x, y, core):
        return (z * 2 + x, y * 2 + core)

    def block(self, z, x, y, core):
        rows = self.rows
        return pl.multiple_of(((z * 2 + x) * self.n_ch + y * 2 + core) * rows, rows)

    def seq_peers(self):
        return [(self.s_to[k], self.c) for k in range(1, self.n_seq)]

    def plane_peers(self):
        return [self.dev(self.z, xx, yy, self.core) for xx, yy in self.plane]

    def meet(self, peers):
        barrier = pltpu.get_barrier_semaphore()
        for peer in peers:
            pl.semaphore_signal(barrier, inc=1, device_id=peer, device_id_type=MESH)
        pl.semaphore_wait(barrier, len(peers))

    def sems(self, tag):
        at = self.tags.setdefault(tag, len(self.tags))
        return self.send_sems.at[at], self.recv_sems.at[at]

    def copy(self, src, dst, tag, to):
        ssem, rsem = self.sems(tag)
        return pltpu.make_async_remote_copy(
            src_ref=src, dst_ref=dst, send_sem=ssem, recv_sem=rsem,
            device_id=to, device_id_type=MESH,
        )

    def send(self, src, dst, tag, to):
        copy = self.copy(src, dst, tag, to)
        copy.start()
        self.sent.append(copy)

    def recv(self, view, tag):
        self.copy(view, view, tag, (self.s, self.c)).wait_recv()

    def drain(self):
        for copy in self.sent:
            copy.wait_send()
        self.sent = []

    def ch_gather_start(self, view_of, tag):
        mine = view_of(self.c)
        self.send(mine, mine, (tag, "y"), self.across)
        self.send(mine, mine, (tag, "core"), self.sibling)

    def ch_gather_finish(self, view_of, tag):
        y, core = self.y, self.core
        theirs = view_of((1 - y) * 2 + core)
        self.recv(theirs, (tag, "y"))
        self.send(theirs, theirs, (tag, "fwd"), self.sibling)
        self.recv(view_of(y * 2 + 1 - core), (tag, "core"))
        self.recv(view_of((1 - y) * 2 + 1 - core), (tag, "fwd"))

    def ch_sum(self, part, mid, low, far, tag):
        y, core = self.y, self.core
        self.send(part.at[1 - core], mid, (tag, "core"), self.sibling)
        self.recv(mid, (tag, "core"))
        low[...] = (part[core, 1 - y] + mid[1 - y]).astype(jnp.bfloat16)
        self.send(low, far, (tag, "y"), self.across)
        total = part[core, y] + mid[y]
        self.recv(far, (tag, "y"))
        return total + far[...].astype(jnp.float32)


def stack_rows(rows):
    return jnp.concatenate(rows, axis=0)


def smooth_pair(v):
    t = jnp.tanh(K1 * (v + K2 * v * v * v))
    value = 0.5 * v * (1.0 + t)
    slope = 0.5 * (1.0 + t) + 0.5 * v * (1.0 - t * t) * K1 * (1.0 + 3.0 * K2 * v * v)
    return value, slope


def sigmoid(v):
    return 1.0 / (1.0 + jnp.exp(-v))


def softplus_exact(d):
    u = jnp.exp(-jnp.abs(d))
    r = u / (2.0 + u)
    q = r * r
    series = 1.0 / 15.0
    for k in (13, 11, 9, 7, 5, 3, 1):
        series = series * q + 1.0 / k
    return jnp.maximum(d, 0.0) + 2.0 * r * series


def minus_expm1(v):
    series = 1.0 / 362880.0
    for k in (40320.0, 5040.0, 720.0, 120.0, 24.0, 6.0, 2.0, 1.0):
        series = series * v + 1.0 / k
    return jnp.where(v > -0.5, -v * series, 1.0 - jnp.exp(v))


class Docs:
    def __init__(self, lengths, first, count, before=0):
        position = first - before + lax.broadcasted_iota(jnp.int32, (count, 1), 0)
        self.opening, self.closing = [], []
        start_of = jnp.zeros((count, 1), jnp.int32)
        start = jnp.int32(0)
        for e in range(lengths.shape[0]):
            end = start + lengths[e]
            owner = (position >= start) & (position < end)
            start_of = jnp.where(owner, start, start_of)
            self.opening.append((position == start).astype(jnp.float32))
            self.closing.append((position == end - 1).astype(jnp.float32))
            start = end
        self.offset = position - start_of
        self.keep = (self.offset > 0).astype(jnp.float32)

    def valid(self, k):
        return (self.offset >= k).astype(jnp.float32)


def prefix(a, b, count):
    row = lax.broadcasted_iota(jnp.int32, a.shape, 0)
    k = 1
    while k < count:
        inside = row >= k
        a_far = jnp.where(inside, pltpu.roll(a, k, 0), 1.0)
        b_far = jnp.where(inside, pltpu.roll(b, k, 0), 0.0)
        b = a * b_far + b
        a = a * a_far
        k *= 2
    return a, b


def suffix(a, b, count):
    row = lax.broadcasted_iota(jnp.int32, a.shape, 0)
    k = 1
    while k < count:
        inside = row < count - k
        a_far = jnp.where(inside, pltpu.roll(a, count - k, 0), 1.0)
        b_far = jnp.where(inside, pltpu.roll(b, count - k, 0), 0.0)
        b = a * b_far + b
        a = a * a_far
        k *= 2
    return a, b


def coefficient_parts(rate_pre, inlet_pre, decay):
    rate = sigmoid(rate_pre)
    inlet = sigmoid(inlet_pre)
    sp = softplus_exact(decay)
    log_decay = -8.0 * rate * sp
    factor = jnp.exp(log_decay)
    scale = jnp.sqrt(minus_expm1(2.0 * log_decay))
    return rate, inlet, sp, log_decay, factor, scale


def opening_rows(docs, init):
    total = docs.opening[0] * init[0:1]
    for e in range(1, len(docs.opening)):
        total = total + docs.opening[e] * init[e : e + 1]
    return total


RIM = 16


def recur_kernel(
    sizes, stream_ref, mix_gain_ref, gelu_w, recur_w, taps_ref, bias_ref, rate_w, rate_b, inlet_w, inlet_b,
    decay_ref, init_ref, out_w, ffn_gain_ref, lengths_ref, counts_ref,
    low_ref, middle_ref, mix_ref, gelu_ref, recur_ref, conv_ref, ratep_ref, inletp_ref, state_ref, enter_ref,
    product_ref, finals_ref,
    cum, loc, summary, part, mid, ylow, yfar, send_sems, recv_sems,
):
    n_seq, n_ch, rows, slots, bw = sizes
    count = rows * n_ch
    net = Net(n_seq, n_ch, rows, send_sems, recv_sems)
    s, c = net.s, net.c
    nxt = [(net.s_to[1], i) for i in range(n_ch)]
    net.meet(net.seq_peers() + [net.sibling, net.across] + [(net.s_to[k], (c + i) % n_ch) for k in (1, n_seq - 1) for i in range(1, n_ch)])
    values = stream_ref[...].astype(jnp.float32)
    scale = lax.rsqrt(jnp.mean(values * values, axis=-1, keepdims=True) + EPS)
    own = (values * scale * mix_gain_ref[...][None, :]).astype(jnp.bfloat16)
    mix_ref[pl.ds(pl.multiple_of(RIM + c * rows, 16), rows), :] = own

    def rows_of(cc):
        return mix_ref.at[pl.ds(pl.multiple_of(RIM + cc * rows, 16), rows)]

    last = mix_ref.at[pl.ds(count, RIM)]
    first = mix_ref.at[pl.ds(0, RIM)]
    rim_sends = [net.copy(last, first, ("rim", i), nxt[i]) for i in range(n_ch)]
    net.ch_gather_start(rows_of, "mix")

    @pl.when((c == n_ch - 1) & (s < n_seq - 1))
    def _():
        for copy in rim_sends:
            copy.start()

    @pl.when(s == 0)
    def _():
        mix_ref[pl.ds(0, RIM), :] = jnp.zeros((RIM, mix_ref.shape[1]), jnp.bfloat16)

    net.ch_gather_finish(rows_of, "mix")

    for i in range(n_ch):
        @pl.when((s > 0) & (c == i))
        def _(i=i):
            net.recv(first, ("rim", i))

    docs = Docs(lengths_ref, s * count, count)
    keep = docs.keep
    summary_cum, summary_loc = [], []
    for b in range(slots):
        cols = pl.ds(b * bw, bw)
        wide = mix_ref[...]
        gelu_ref[:, cols] = jnp.dot(wide[RIM:], gelu_w[:, cols], preferred_element_type=jnp.float32)
        recur = jnp.dot(wide, recur_w[:, cols], preferred_element_type=jnp.float32).astype(jnp.bfloat16)
        recur_ref[:, cols] = recur
        recur = recur.astype(jnp.float32)
        conv_pre = bias_ref[b : b + 1, :]
        for k in range(taps_ref.shape[0]):
            conv_pre = conv_pre + taps_ref[k, b : b + 1, :] * recur[RIM - k : RIM - k + count] * docs.valid(k)
        conv_low = conv_pre.astype(jnp.bfloat16)
        conv_ref[:, cols] = conv_low
        rate_pre = jnp.dot(conv_low, rate_w[b], preferred_element_type=jnp.float32) + rate_b[b : b + 1, :]
        inlet_pre = jnp.dot(conv_low, inlet_w[b], preferred_element_type=jnp.float32) + inlet_b[b : b + 1, :]
        ratep_ref[:, cols] = rate_pre
        inletp_ref[:, cols] = inlet_pre
        rate, inlet, sp, log_decay, factor, scale = coefficient_parts(rate_pre, inlet_pre, decay_ref[b : b + 1, :])
        carry = keep * factor
        source = scale * inlet * conv_low.astype(jnp.float32) + (1.0 - keep) * factor * opening_rows(docs, init_ref[:, cols])
        total, local = prefix(carry, source, count)
        cum[:, cols] = total
        loc[:, cols] = local
        summary_cum.append(total[count - 1 : count])
        summary_loc.append(local[count - 1 : count])
    fill = [jnp.zeros((8 - 2 * slots, bw), jnp.float32)]
    summary[s] = stack_rows(summary_cum + summary_loc + fill)
    for k in range(1, n_seq):
        net.send(summary.at[s], summary.at[s], ("sum", k), (net.s_to[k], c))
    for k in range(1, n_seq):
        net.recv(summary.at[net.s_from[k]], ("sum", k))
    enter = jnp.zeros((slots, bw), jnp.float32)
    for q in range(n_seq - 1):
        after = summary[q, 0:slots] * enter + summary[q, slots : 2 * slots]
        enter = jnp.where(s > q, after, enter)
    enter_ref[0:slots, :] = enter
    for b in range(slots):
        cols = pl.ds(b * bw, bw)
        live = jnp.where(counts_ref[0] > b, 1.0, 0.0)
        state = loc[:, cols] + cum[:, cols] * enter[b : b + 1]
        state_ref[:, cols] = state
        value, _ = smooth_pair(gelu_ref[:, cols])
        product_ref[:, cols] = (value * state * live).astype(jnp.bfloat16)
        ends = [jnp.sum(mark * state, axis=0, keepdims=True) * live for mark in docs.closing]
        finals_ref[:, cols] = stack_rows(ends + [jnp.zeros((8 - len(ends), bw), jnp.float32)])

    def tile(i, _):
        cols = pl.ds(pl.multiple_of(i * 256, 256), 256)
        value = jnp.dot(product_ref[...], out_w[:, cols], preferred_element_type=jnp.float32)
        for cc in range(n_ch):
            part[cc % 2, cc // 2, :, cols] = value[cc * rows : (cc + 1) * rows]
        return 0

    lax.fori_loop(0, out_w.shape[1] // 256, tile, 0)
    branch = net.ch_sum(part, mid, ylow, yfar, "branch")
    middle = values + branch
    middle_ref[...] = middle
    scale = lax.rsqrt(jnp.mean(middle * middle, axis=-1, keepdims=True) + EPS)
    low_ref[...] = (middle * scale * ffn_gain_ref[...][None, :]).astype(jnp.bfloat16)

    @pl.when((c == n_ch - 1) & (s < n_seq - 1))
    def _():
        for copy in rim_sends:
            copy.wait_send()

    net.drain()


def recur_forward(stream, mix_gain, gelu_w, recur_w, taps, bias, rate_w, rate_b, inlet_w, inlet_b, decay, init, out_w, ffn_gain, lengths, counts):
    n_seq, n_ch = lax.axis_size("seq"), lax.axis_size("ch")
    rows, d = stream.shape
    slots, bw = bias.shape
    count, wide = rows * n_ch, slots * bw
    bf, f32 = jnp.bfloat16, jnp.float32
    dma = pltpu.SemaphoreType.DMA
    vmem = pl.BlockSpec(memory_space=pltpu.VMEM)
    smem = pl.BlockSpec(memory_space=pltpu.SMEM)
    shape = jax.ShapeDtypeStruct
    return pl.pallas_call(
        functools.partial(recur_kernel, (n_seq, n_ch, rows, slots, bw)),
        out_shape=[
            shape((rows, d), bf), shape((rows, d), f32), shape((RIM + count, d), bf), shape((count, wide), f32),
            shape((RIM + count, wide), bf), shape((count, wide), bf), shape((count, wide), f32), shape((count, wide), f32),
            shape((count, wide), f32), shape((8, bw), f32), shape((count, wide), bf), shape((8, wide), f32),
        ],
        in_specs=[vmem] * 14 + [smem] * 2,
        out_specs=[vmem] * 12,
        scratch_shapes=[
            pltpu.VMEM((count, wide), f32), pltpu.VMEM((count, wide), f32), pltpu.VMEM((n_seq, 8, bw), f32),
            pltpu.VMEM((2, 2, rows, d), f32), pltpu.VMEM((2, rows, d), f32),
            pltpu.VMEM((rows, d), bf), pltpu.VMEM((rows, d), bf),
            dma((32,)), dma((32,)),
        ],
        compiler_params=pltpu.CompilerParams(
            collective_id=2, has_side_effects=True, vmem_limit_bytes=VMEM_BYTES
        ),
    )(stream, mix_gain, gelu_w, recur_w, taps, bias, rate_w, rate_b, inlet_w, inlet_b, decay, init, out_w, ffn_gain, lengths, counts)


def ffn_kernel(
    sizes, low_ref, cot_ref, weight_ref, out_ref, grad_ref, dw_ref,
    wt, full, cfull, hid, gat, upg, part, sib, psum_buf, pl_in, zsum, z_in, dwl,
    ws, wr, zs, zr, ps, pr, cs, cr, rs1, rr1, rs2, rr2, rs3, rr3, ds_, dr_,
):
    n_seq, n_ch, rows, width, sl = sizes
    n_z = n_seq // 2
    s, c = lax.axis_index("seq"), lax.axis_index("ch")
    z, x = s // 2, s % 2
    y, core = c // 2, c % 2

    def dev(zz, xx, yy, cc):
        return (zz * 2 + xx, yy * 2 + cc)

    def block(zz, xx, yy, cc):
        return pl.multiple_of(((zz * 2 + xx) * n_ch + yy * 2 + cc) * rows, rows)

    plane = [(1 - x, y), (x, 1 - y), (1 - x, 1 - y)]
    z_to = [(z + k) % n_z for k in range(n_z)]
    z_from = [(z + n_z - k) % n_z for k in range(n_z)]
    s_to = [(s + k) % n_seq for k in range(n_seq)]
    s_from = [(s + n_seq - k) % n_seq for k in range(n_seq)]

    barrier = pltpu.get_barrier_semaphore()
    peers = [(s_to[k], c) for k in range(1, n_seq)]
    peers += [dev(z, x, y, 1 - core)] + [dev(z, x, 1 - y, core), dev(z, 1 - x, 1 - y, core)]
    for peer in peers:
        pl.semaphore_signal(barrier, inc=1, device_id=peer, device_id_type=MESH)
    pl.semaphore_wait(barrier, len(peers))

    def send(src, dst, ssem, rsem, to):
        copy = pltpu.make_async_remote_copy(
            src_ref=src, dst_ref=dst, send_sem=ssem, recv_sem=rsem,
            device_id=to, device_id_type=MESH,
        )
        copy.start()
        return copy

    sent = []
    arrays = [(low_ref, full), (cot_ref, cfull)]
    mine = block(z, x, y, core)
    for a, (src, dst) in enumerate(arrays):
        for k in range(1, n_z):
            sent.append(send(src, dst.at[pl.ds(mine, rows)], zs.at[a, k], zr.at[a, k], dev(z_to[k], x, y, core)))
    own_cols = pl.multiple_of(s * width, width)
    for k in range(1, n_seq):
        sent.append(send(
            weight_ref.at[:, pl.ds(pl.multiple_of(s_to[k] * sl, sl), sl), :],
            wt.at[:, :, pl.ds(own_cols, width)], ws.at[k], wr.at[k], (s_to[k], c),
        ))
    for src, dst in arrays:
        dst[pl.ds(mine, rows), :] = src[...]
    wt[:, :, pl.ds(own_cols, width)] = weight_ref[:, pl.ds(pl.multiple_of(s * sl, sl), sl), :]

    sibling = dev(z, x, y, 1 - core)

    def rows_of(dst, zz, p):
        xx, yy = ((x, y) if p is None else plane[p])
        return dst.at[pl.ds(block(zz, xx, yy, core), rows)]

    def recv(dst_view, ssem, rsem):
        pltpu.make_async_remote_copy(
            src_ref=dst_view, dst_ref=dst_view, send_sem=ssem, recv_sem=rsem,
            device_id=(s, c), device_id_type=MESH,
        ).wait_recv()

    def spread_plane(a, j):
        dst = arrays[a][1]
        view = rows_of(dst, z_from[j], None)
        for p, (xx, yy) in enumerate(plane):
            sent.append(send(view, view, ps.at[a, j, p], pr.at[a, j, p], dev(z, xx, yy, core)))
        sent.append(send(view, view, cs.at[a, j, 3], cr.at[a, j, 3], sibling))

    def pass_to_sibling(a, j):
        dst = arrays[a][1]
        for p in range(3):
            view = rows_of(dst, z_from[j], p)
            recv(view, ps.at[a, j, p], pr.at[a, j, p])
            sent.append(send(view, view, cs.at[a, j, p], cr.at[a, j, p], sibling))

    def from_sibling(a, j):
        dst = arrays[a][1]
        for p in range(4):
            xx, yy = (x, y) if p == 3 else plane[p]
            view = dst.at[pl.ds(block(z_from[j], xx, yy, 1 - core), rows)]
            recv(view, cs.at[a, j, p], cr.at[a, j, p])

    for a in (0, 1):
        spread_plane(a, 0)
    for j in range(1, n_z):
        for a in (0, 1):
            view = rows_of(arrays[a][1], z_from[j], None)
            recv(view, zs.at[a, j], zr.at[a, j])
            spread_plane(a, j)
    for j in range(n_z):
        for a in (0, 1):
            pass_to_sibling(a, j)
    for k in range(1, n_seq):
        view = wt.at[:, :, pl.ds(pl.multiple_of(s_from[k] * width, width), width)]
        recv(view, ws.at[k], wr.at[k])

    group = n_ch * 2 * rows
    per = 2 * 2 * rows

    def compute(j):
        for a in (0, 1):
            from_sibling(a, j)
        at = pl.multiple_of(z_from[j] * group, group)
        rows_in = full[pl.ds(at, group), :]
        gate = contract_last(rows_in, wt[0])
        up = contract_last(rows_in, wt[1])
        hg = contract_last(cfull[pl.ds(at, group), :], wt[2])
        inner = K1 * (gate + K2 * gate * gate * gate)
        t = jnp.tanh(inner)
        sm = 0.5 * gate * (1.0 + t)
        dsm = 0.5 * (1.0 + t) + 0.5 * gate * (1.0 - t * t) * K1 * (1.0 + 3.0 * K2 * gate * gate)
        hidden = (sm * up).astype(jnp.bfloat16)
        gg = (hg * up * dsm).astype(jnp.bfloat16)
        ug = (hg * sm).astype(jnp.bfloat16)
        hid[pl.ds(at, group), :] = hidden
        gat[pl.ds(at, group), :] = gg
        upg[pl.ds(at, group), :] = ug

        def tile(i, _):
            cols = pl.ds(pl.multiple_of(i * 256, 256), 256)
            nf = jnp.dot(gg, wt[0, :, cols], preferred_element_type=jnp.float32)
            nf = nf + jnp.dot(ug, wt[1, :, cols], preferred_element_type=jnp.float32)
            ot = jnp.dot(hidden, wt[2, :, cols], preferred_element_type=jnp.float32)
            for b, value in ((0, nf), (1, ot)):
                value = value.astype(jnp.bfloat16)
                for xx in range(2):
                    for yy in range(2):
                        for cc in range(2):
                            at_row = (xx * 4 + yy * 2 + cc) * rows
                            part[j, b, cc, xx * 2 + yy, :, cols] = value[at_row : at_row + rows]
            return 0

        lax.fori_loop(0, full.shape[1] // 256, tile, 0)
        for b in (0, 1):
            sent.append(send(part.at[j, b, 1 - core], sib.at[j, b], rs1.at[j, b], rr1.at[j, b], sibling))

    def second(j, b):
        recv(sib.at[j, b], rs1.at[j, b], rr1.at[j, b])

        def add(i, _):
            psum_buf[j, b, i] = (part[j, b, core, i].astype(jnp.float32) + sib[j, b, i].astype(jnp.float32)).astype(jnp.bfloat16)
            return 0

        lax.fori_loop(0, 4, add, 0)
        for p, (xx, yy) in enumerate(plane):
            sent.append(send(psum_buf.at[j, b, xx * 2 + yy], pl_in.at[j, b, p], rs2.at[j, b, p], rr2.at[j, b, p], dev(z, xx, yy, core)))

    def third(j, b):
        total = psum_buf[j, b, x * 2 + y].astype(jnp.float32)
        for p in range(3):
            recv(pl_in.at[j, b, p], rs2.at[j, b, p], rr2.at[j, b, p])
            total = total + pl_in[j, b, p].astype(jnp.float32)
        if j == 0:
            (grad_ref, out_ref)[b][...] = total
        else:
            zsum[j, b] = total.astype(jnp.bfloat16)
            sent.append(send(zsum.at[j, b], z_in.at[j, b], rs3.at[j, b], rr3.at[j, b], dev(z_from[j], x, y, core)))

    for j in range(n_z):
        compute(j)
        for b in (0, 1):
            if j >= 1:
                second(j - 1, b)
            if j >= 2:
                third(j - 2, b)
    for b in (0, 1):
        second(n_z - 1, b)
    for b in (0, 1):
        third(n_z - 2, b)

    def grads(i, _):
        cols = pl.ds(pl.multiple_of(i * 256, 256), 256)
        dwl[0, :, cols] = contract_first(gat[...], full[:, cols]).astype(jnp.bfloat16)
        dwl[1, :, cols] = contract_first(upg[...], full[:, cols]).astype(jnp.bfloat16)
        dwl[2, :, cols] = contract_first(hid[...], cfull[:, cols]).astype(jnp.bfloat16)
        return 0

    lax.fori_loop(0, full.shape[1] // 256, grads, 0)
    own_rows = pl.multiple_of(s * sl, sl)
    for k in range(1, n_seq):
        cols = pl.ds(pl.multiple_of(s_to[k] * width, width), width)
        sent.append(send(dwl.at[:, :, cols], dw_ref.at[:, pl.ds(own_rows, sl), :], ds_.at[k], dr_.at[k], (s_to[k], c)))
    dw_ref[:, pl.ds(own_rows, sl), :] = dwl[:, :, pl.ds(own_cols, width)]
    for b in (0, 1):
        third(n_z - 1, b)
    for b in (0, 1):
        for j in range(1, n_z):
            recv(z_in.at[j, b], rs3.at[j, b], rr3.at[j, b])
            ref = (grad_ref, out_ref)[b]
            ref[...] += z_in[j, b].astype(jnp.float32)
    for k in range(1, n_seq):
        view = dw_ref.at[:, pl.ds(pl.multiple_of(s_from[k] * sl, sl), sl), :]
        recv(view, ds_.at[k], dr_.at[k])
    for copy in sent:
        copy.wait_send()


def ffn(low, cot, weights):
    n_seq, n_ch = lax.axis_size("seq"), lax.axis_size("ch")
    rows, d = low.shape
    width = weights.shape[2]
    sl = weights.shape[1] // n_seq
    n_z = n_seq // 2
    tokens = n_seq * n_ch * rows
    bf, f32 = jnp.bfloat16, jnp.float32
    dma = pltpu.SemaphoreType.DMA
    vmem = pl.BlockSpec(memory_space=pltpu.VMEM)
    return pl.pallas_call(
        functools.partial(ffn_kernel, (n_seq, n_ch, rows, width, sl)),
        out_shape=[
            jax.ShapeDtypeStruct((rows, d), f32),
            jax.ShapeDtypeStruct((rows, d), f32),
            jax.ShapeDtypeStruct(weights.shape, bf),
        ],
        in_specs=[vmem] * 3,
        out_specs=[vmem] * 3,
        scratch_shapes=[
            pltpu.VMEM((3, sl, d), bf),
            pltpu.VMEM((tokens, d), bf),
            pltpu.VMEM((tokens, d), bf),
            pltpu.VMEM((tokens, sl), bf),
            pltpu.VMEM((tokens, sl), bf),
            pltpu.VMEM((tokens, sl), bf),
            pltpu.VMEM((n_z, 2, 2, 4, rows, d), bf),
            pltpu.VMEM((n_z, 2, 4, rows, d), bf),
            pltpu.VMEM((n_z, 2, 4, rows, d), bf),
            pltpu.VMEM((n_z, 2, 3, rows, d), bf),
            pltpu.VMEM((n_z, 2, rows, d), bf),
            pltpu.VMEM((n_z, 2, rows, d), bf),
            pltpu.VMEM((3, sl, d), bf),
            dma((n_seq,)), dma((n_seq,)),
            dma((2, n_z)), dma((2, n_z)),
            dma((2, n_z, 3)), dma((2, n_z, 3)),
            dma((2, n_z, 4)), dma((2, n_z, 4)),
            dma((n_z, 2)), dma((n_z, 2)),
            dma((n_z, 2, 3)), dma((n_z, 2, 3)),
            dma((n_z, 2)), dma((n_z, 2)),
            dma((n_seq,)), dma((n_seq,)),
        ],
        compiler_params=pltpu.CompilerParams(
            collective_id=1, has_side_effects=True, vmem_limit_bytes=VMEM_BYTES
        ),
    )(low, cot, weights)


def pack_gain(row):
    tiles = [row[:, i * 128 : (i + 1) * 128] for i in range(row.shape[1] // 128)]
    return jnp.concatenate([stack_rows(tiles[i : i + 8]) for i in range(0, len(tiles), 8)], axis=1)


def norm_back(values, gain, grad):
    r = lax.rsqrt(jnp.mean(values * values, axis=-1, keepdims=True) + EPS)
    u = grad * gain
    to_values = r * u - values * (r * r * r) * jnp.mean(u * values, axis=-1, keepdims=True)
    to_gain = jnp.sum(grad * values * r, axis=0, keepdims=True)
    return to_values, to_gain


def recur_back_kernel(
    sizes, nfg_ref, middle_ref, cot_ref, stream_ref, mix_gain_ref, ffn_gain_ref, gelu_w, recur_w, out_w,
    taps_ref, rate_w, inlet_w, decay_ref, init_ref, mix_ref, gelu_ref, recur_ref, conv_ref, ratep_ref, inletp_ref,
    state_ref, enter_ref, product_ref, finals_ref, lengths_ref, counts_ref,
    sgrad_ref, gelu_wg, recur_wg, out_wg, rate_wg, inlet_wg, taps_g, bias_g, rate_bg, inlet_bg, decay_g,
    finals_out, mixg_out, ffng_out,
    branch, back_a, back_b, summary, cgrad, part, mid, ylow, yfar, gathered, left, early, late, gates, gates_in, shared,
    send_sems, recv_sems,
):
    n_seq, n_ch, rows, slots, bw, width = sizes
    count = rows * n_ch
    wide = slots * bw
    net = Net(n_seq, n_ch, rows, send_sems, recv_sems)
    s, c, z, x, y, core = net.s, net.c, net.z, net.x, net.y, net.core
    net.meet(net.seq_peers() + [net.sibling, net.across])
    own_s = pl.multiple_of(s * count, count)

    def gather_z(a):
        view = gathered.at[a, pl.ds(own_s, count)]
        for k in range(1, net.n_z):
            net.send(view, view, ("gz", a, k), net.dev(net.z_to[k], x, y, core))

    def gather_x_view(a, k, xx):
        return gathered.at[a, pl.ds(pl.multiple_of((net.z_from[k] * 2 + xx) * count, count), count)]

    def gather_x(a, k):
        view = gather_x_view(a, k, x)
        if k:
            net.recv(view, ("gz", a, k))
        net.send(view, view, ("gx", a, k), net.dev(z, 1 - x, y, core))

    def gather_done(a):
        for k in range(net.n_z):
            net.recv(gather_x_view(a, k, 1 - x), ("gx", a, k))

    def left_start(a, src):
        for k in range(1, n_seq):
            net.send(
                src(pl.ds(pl.multiple_of(net.s_to[k] * width, width), width)), left.at[a, s, c], ("left", a, k),
                (net.s_to[k], c),
            )

    def left_pass(a):
        for k in range(1, n_seq):
            net.recv(left.at[a, net.s_from[k], c], ("left", a, k))
        net.ch_gather_start(lambda cc: left.at[a, :, cc], ("leftch", a))

    def left_done(a):
        net.ch_gather_finish(lambda cc: left.at[a, :, cc], ("leftch", a))

    nfg = nfg_ref[...]
    middle = middle_ref[...]
    to_middle, ffn_part = norm_back(middle, ffn_gain_ref[...][None, :], nfg)
    middle_grad = cot_ref[...].astype(jnp.float32) + to_middle
    branch[c] = middle_grad.astype(jnp.bfloat16)
    net.ch_gather_start(lambda cc: branch.at[cc], "branch")
    own_cols = pl.ds(pl.multiple_of(s * width, width), width)
    mix_rows = pl.ds(pl.multiple_of(RIM + c * rows, 16), rows)
    left[0, s, c] = mix_ref[mix_rows, own_cols]
    left[1, s, c] = branch[c, :, own_cols]
    left_start(1, lambda cols: branch.at[c, :, cols])
    left_start(0, lambda cols: mix_ref.at[mix_rows, cols])
    gathered[0, pl.ds(own_s, count), :] = product_ref[...]
    gather_z(0)
    early[s] = jnp.concatenate([finals_ref[...], pack_gain(ffn_part)], axis=1)
    net.ch_gather_finish(lambda cc: branch.at[cc], "branch")

    docs = Docs(lengths_ref, s * count, count)
    keep = docs.keep
    ahead_docs = Docs(lengths_ref, s * count, count + RIM)
    one = jnp.ones((1, bw), jnp.float32)
    row = lax.broadcasted_iota(jnp.int32, (count, bw), 0)
    enter = enter_ref[...]
    first_carry, heads_a, heads_b = [], [], []
    for b in range(slots):
        cols = pl.ds(b * bw, bw)
        live = jnp.where(counts_ref[0] > b, 1.0, 0.0)
        product_grad = contract_last(branch[...].reshape(count, branch.shape[2]), out_w[b * bw : (b + 1) * bw, :])
        value, slope = smooth_pair(gelu_ref[:, cols])
        state = state_ref[:, cols]
        gathered[1, pl.ds(own_s, count), cols] = (product_grad * state * live * slope).astype(jnp.bfloat16)
        state_grad = product_grad * value * live
        rate, inlet, sp, log_decay, factor, scale = coefficient_parts(ratep_ref[:, cols], inletp_ref[:, cols], decay_ref[b : b + 1, :])
        carry = keep * factor
        following = jnp.where(row < count - 1, pltpu.roll(carry, count - 1, 0), 1.0)
        total, local = suffix(following, state_grad, count)
        back_a[:, cols] = total
        back_b[:, cols] = local
        heads_a.append(carry[0:1] * total[0:1])
        heads_b.append(carry[0:1] * local[0:1])
    summary[s] = stack_rows(heads_a + heads_b + [jnp.zeros((8 - 2 * slots, bw), jnp.float32)])
    for k in range(1, n_seq):
        net.send(summary.at[s], summary.at[s], ("sum", k), (net.s_to[k], c))
    for k in range(1, n_seq):
        net.recv(summary.at[net.s_from[k]], ("sum", k))
    enter_back = jnp.zeros((slots, bw), jnp.float32)
    for q in range(n_seq - 1, 0, -1):
        after = summary[q, 0:slots] * enter_back + summary[q, slots : 2 * slots]
        enter_back = jnp.where(s < q, after, enter_back)
    vec = []
    for b in range(slots):
        cols = pl.ds(b * bw, bw)
        adjoint = back_b[:, cols] + back_a[:, cols] * enter_back[b : b + 1]
        state = state_ref[:, cols]
        previous = jnp.where(row > 0, pltpu.roll(state, 1, 0), enter[b : b + 1])
        decay = decay_ref[b : b + 1, :]
        rate, inlet, sp, log_decay, factor, scale = coefficient_parts(ratep_ref[:, cols], inletp_ref[:, cols], decay)
        conv_low = conv_ref[:, cols]
        conv = conv_low.astype(jnp.float32)
        init_rows = opening_rows(docs, init_ref[:, cols])
        log_grad = adjoint * (
            factor * (keep * previous + (1.0 - keep) * init_rows) - inlet * conv * jnp.exp(2.0 * log_decay) / scale
        )
        rate_low = (log_grad * (-8.0 * sp) * rate * (1.0 - rate)).astype(jnp.bfloat16)
        direct = adjoint * scale
        inlet_low = (direct * conv * inlet * (1.0 - inlet)).astype(jnp.bfloat16)
        decay_row = jnp.sum(log_grad * (-8.0 * rate), axis=0, keepdims=True) * sigmoid(decay)
        back = direct * inlet + contract_last(rate_low, rate_w[b]) + contract_last(inlet_low, inlet_w[b])
        cgrad[0:count, cols] = back.astype(jnp.bfloat16)
        gates[0, b] = contract_first(conv_low, rate_low).astype(jnp.bfloat16)
        gates[1, b] = contract_first(conv_low, inlet_low).astype(jnp.bfloat16)
        vec.append([
            jnp.sum(rate_low.astype(jnp.float32), axis=0, keepdims=True),
            jnp.sum(inlet_low.astype(jnp.float32), axis=0, keepdims=True),
            decay_row,
        ])
    rim = cgrad.at[pl.ds(count, RIM)]
    rim_send = net.copy(cgrad.at[pl.ds(0, RIM)], rim, "rim", (net.s_to[n_seq - 1], c))

    @pl.when(s > 0)
    def _():
        rim_send.start()

    @pl.when(s == n_seq - 1)
    def _():
        cgrad[pl.ds(count, RIM), :] = jnp.zeros((RIM, wide), jnp.bfloat16)

    @pl.when(s < n_seq - 1)
    def _():
        net.recv(rim, "rim")

    gather_z(1)
    for k in range(net.n_z):
        gather_x(0, k)
    vectors = []
    for b in range(slots):
        cols = pl.ds(b * bw, bw)
        grad = cgrad[:, cols].astype(jnp.float32)
        own = grad[:count]
        recur = recur_ref[:, cols].astype(jnp.float32)
        total = jnp.zeros((count, bw), jnp.float32)
        tap_rows = []
        for k in range(taps_ref.shape[0]):
            tap_rows.append(jnp.sum(own * recur[RIM - k : RIM - k + count] * docs.valid(k), axis=0, keepdims=True))
            total = total + taps_ref[k, b : b + 1, :] * grad[k : k + count] * ahead_docs.valid(k)[k : k + count]
        gathered[2, pl.ds(own_s, count), cols] = total.astype(jnp.bfloat16)
        vectors.append(stack_rows(tap_rows + [jnp.sum(own, axis=0, keepdims=True)] + vec[b]))
    gather_z(2)

    def tile(i, _):
        cols = pl.ds(pl.multiple_of(i * 256, 256), 256)
        own_rows = pl.ds(own_s, count)
        value = contract_last(gathered[1, own_rows, :], gelu_w[cols, :]) + contract_last(gathered[2, own_rows, :], recur_w[cols, :])
        for cc in range(n_ch):
            part[cc % 2, cc // 2, :, cols] = value[cc * rows : (cc + 1) * rows]
        return 0

    lax.fori_loop(0, gelu_w.shape[0] // 256, tile, 0)
    gate_rows = rate_wg.shape[1]
    for k in range(1, n_seq):
        net.send(
            gates.at[:, :, pl.ds(pl.multiple_of(net.s_to[k] * gate_rows, gate_rows), gate_rows), :], gates_in.at[s],
            ("gates", k), (net.s_to[k], c),
        )
    gates_in[s] = gates[:, :, pl.ds(pl.multiple_of(s * gate_rows, gate_rows), gate_rows), :]
    for k in range(1, n_seq):
        net.send(early.at[s], early.at[s], ("early", k), (net.s_to[k], c))
    norm_grad = net.ch_sum(part, mid, ylow, yfar, "norm")
    to_stream, mix_part = norm_back(stream_ref[...].astype(jnp.float32), mix_gain_ref[...][None, :], norm_grad)
    sgrad_ref[...] = middle_grad + to_stream
    late[s] = jnp.concatenate(vectors + [pack_gain(mix_part)], axis=1)
    for k in range(1, n_seq):
        net.send(late.at[s], late.at[s], ("late", k), (net.s_to[k], c))
    for a in (0, 1):
        left_pass(a)
    for a in (0, 1):
        left_done(a)
    for k in range(net.n_z):
        gather_x(1, k)
    gather_done(0)

    def left_of(a):
        return left[a].reshape(n_seq * n_ch * rows, width)

    out_wg[...] = contract_first(gathered[0], left_of(1))
    for k in range(net.n_z):
        gather_x(2, k)
    gather_done(1)
    gelu_wg[...] = contract_first(left_of(0), gathered[1])
    for k in range(1, n_seq):
        net.recv(gates_in.at[net.s_from[k]], ("gates", k))
        net.recv(early.at[net.s_from[k]], ("early", k))
        net.recv(late.at[net.s_from[k]], ("late", k))
    total = gates_in[0].astype(jnp.float32)
    early_sum, late_sum = early[0], late[0]
    for q in range(1, n_seq):
        total = total + gates_in[q].astype(jnp.float32)
        early_sum = early_sum + early[q]
        late_sum = late_sum + late[q]
    rate_wg[...] = total[0]
    inlet_wg[...] = total[1]
    shared[c] = jnp.concatenate([early_sum, late_sum[:, wide:]], axis=1)
    net.ch_gather_start(lambda cc: shared.at[cc], "shared")
    piece = bw // n_seq
    for b in range(slots):
        mine = jnp.zeros((8, piece), jnp.float32)
        for q in range(n_seq):
            at = b * bw + q * piece
            mine = jnp.where(s == q, late_sum[:, at : at + piece], mine)
        n_taps = taps_ref.shape[0]
        for k in range(n_taps):
            taps_g[k, b : b + 1, :] = mine[k : k + 1]
        for k, ref in enumerate((bias_g, rate_bg, inlet_bg, decay_g)):
            ref[b : b + 1, :] = mine[n_taps + k : n_taps + k + 1]
    net.ch_gather_finish(lambda cc: shared.at[cc], "shared")
    gains = shared[0, :, wide:]
    for cc in range(1, n_ch):
        gains = gains + shared[cc, :, wide:]
    for cc in range(n_ch):
        finals_out[:, cc * wide : (cc + 1) * wide] = shared[cc, 0 : finals_out.shape[0], 0:wide]
    half = gains.shape[1] // 2
    for ref, at in ((ffng_out, 0), (mixg_out, half)):
        for i in range(half // 128):
            ref[i * 8 : (i + 1) * 8, :] = gains[:, at + i * 128 : at + (i + 1) * 128]
    gather_done(2)
    recur_wg[...] = contract_first(left_of(0), gathered[2])

    @pl.when(s > 0)
    def _():
        rim_send.wait_send()

    net.drain()


def recur_backward(nfg, middle, cot, stream, mix_gain, ffn_gain, gelu_w, recur_w, out_w, taps, rate_w, inlet_w, decay, init,
                   mix, gelu_pre, recur, conv_low, rate_pre, inlet_pre, state, enter, product, finals, lengths, counts):
    n_seq, n_ch = lax.axis_size("seq"), lax.axis_size("ch")
    rows, d = stream.shape
    slots, bw = decay.shape
    count, wide, width = rows * n_ch, slots * bw, d // n_seq
    bf, f32 = jnp.bfloat16, jnp.float32
    dma = pltpu.SemaphoreType.DMA
    vmem = pl.BlockSpec(memory_space=pltpu.VMEM)
    smem = pl.BlockSpec(memory_space=pltpu.SMEM)
    shape = jax.ShapeDtypeStruct
    piece = bw // n_seq
    vector = shape((slots, piece), f32)
    packed = wide + d // 8
    return pl.pallas_call(
        functools.partial(recur_back_kernel, (n_seq, n_ch, rows, slots, bw, width)),
        out_shape=[
            shape((rows, d), f32), shape((width, wide), f32), shape((width, wide), f32), shape((wide, width), f32),
            shape((slots, piece, bw), f32), shape((slots, piece, bw), f32), shape((taps.shape[0], slots, piece), f32),
            vector, vector, vector, vector,
            shape((lengths.shape[0], wide * n_ch), f32), shape((d // 128, 128), f32), shape((d // 128, 128), f32),
        ],
        in_specs=[vmem] * 24 + [smem] * 2,
        out_specs=[vmem] * 14,
        scratch_shapes=[
            pltpu.VMEM((n_ch, rows, d), bf), pltpu.VMEM((count, wide), f32), pltpu.VMEM((count, wide), f32),
            pltpu.VMEM((n_seq, 8, bw), f32), pltpu.VMEM((count + RIM, wide), bf),
            pltpu.VMEM((2, 2, rows, d), f32), pltpu.VMEM((2, rows, d), f32), pltpu.VMEM((rows, d), bf), pltpu.VMEM((rows, d), bf),
            pltpu.VMEM((3, n_seq * count, wide), bf), pltpu.VMEM((2, n_seq, n_ch, rows, width), bf),
            pltpu.VMEM((n_seq, 8, packed), f32), pltpu.VMEM((n_seq, 8, packed), f32),
            pltpu.VMEM((2, slots, bw, bw), bf), pltpu.VMEM((n_seq, 2, slots, piece, bw), bf),
            pltpu.VMEM((n_ch, 8, packed + d // 8), f32),
            dma((96,)), dma((96,)),
        ],
        compiler_params=pltpu.CompilerParams(
            collective_id=3, has_side_effects=True, vmem_limit_bytes=VMEM_BYTES
        ),
    )(nfg, middle, cot, stream, mix_gain, ffn_gain, gelu_w, recur_w, out_w, taps, rate_w, inlet_w, decay, init,
      mix, gelu_pre, recur, conv_low, rate_pre, inlet_pre, state, enter, product, finals, lengths, counts)


def small_body(
    stream,
    cotangent,
    mix_gain,
    gelu_weight,
    recur_weight,
    conv_taps,
    conv_bias,
    rate_weight,
    rate_bias,
    inlet_weight,
    inlet_bias,
    decay_param,
    init_states,
    out_weight,
    ffn_gain,
    gate_weight,
    up_weight,
    down_weight,
    doc_lengths,
    block_counts,
):
    (ffn_low, middle, mix_wide, gelu_pre, recur_wide, conv_low, rate_pre, inlet_pre, state, enter, product_low, finals) = recur_forward(
        stream, mix_gain, gelu_weight, recur_weight, conv_taps, conv_bias, rate_weight, rate_bias, inlet_weight,
        inlet_bias, decay_param, init_states, out_weight, ffn_gain, doc_lengths, block_counts,
    )
    weights = jnp.stack([gate_weight.T, up_weight.T, down_weight])
    ffn_sum, norm_ffn_grad, dw = ffn(ffn_low, cotangent, weights)
    mixed_out = (middle + ffn_sum).astype(jnp.bfloat16)
    (stream_grad, gelu_wg, recur_wg, out_wg, rate_wg, inlet_wg, taps_g, bias_g, rate_bg, inlet_bg, decay_g, final_states,
     mix_gain_grad, ffn_gain_grad) = recur_backward(
        norm_ffn_grad, middle, cotangent, stream, mix_gain, ffn_gain, gelu_weight, recur_weight, out_weight, conv_taps,
        rate_weight, inlet_weight, decay_param, init_states, mix_wide, gelu_pre, recur_wide, conv_low, rate_pre, inlet_pre,
        state, enter, product_low, finals, doc_lengths, block_counts,
    )
    return (
        final_states, mixed_out, stream_grad, mix_gain_grad.reshape(-1), gelu_wg, recur_wg, taps_g, bias_g, rate_wg, rate_bg,
        inlet_wg, inlet_bg, decay_g, out_wg, ffn_gain_grad.reshape(-1), dw[0].T.astype(jnp.float32),
        dw[1].T.astype(jnp.float32), dw[2].astype(jnp.float32),
    )


def solution(mesh):
    in_specs = (
        P(("seq", "ch"), None),
        P(("seq", "ch"), None),
        P(),
        P(None, "ch"),
        P(None, "ch"),
        P(None, "ch", None),
        P("ch", None),
        P("ch", None, None),
        P("ch", None),
        P("ch", None, None),
        P("ch", None),
        P("ch", None),
        P(None, "ch"),
        P("ch", None),
        P(),
        P("seq", "ch"),
        P("seq", "ch"),
        P("ch", "seq"),
        P(),
        P("ch"),
    )
    out_specs = (
        P(),
        P(("seq", "ch"), None),
        P(("seq", "ch"), None),
        P(),
        P("seq", "ch"),
        P("seq", "ch"),
        P(None, "ch", "seq"),
        P("ch", "seq"),
        P("ch", "seq", None),
        P("ch", "seq"),
        P("ch", "seq", None),
        P("ch", "seq"),
        P("ch", "seq"),
        P("ch", "seq"),
        P(),
        P("seq", "ch"),
        P("seq", "ch"),
        P("ch", "seq"),
    )
    return jax.shard_map(small_body if mesh.shape['seq'] == 8 else body, mesh=mesh, in_specs=in_specs, out_specs=out_specs, check_vma=False)
```

```python
import functools
import types

import jax
import jax.numpy as jnp
from jax import lax
from jax.experimental import pallas as pl
from jax.experimental.pallas import tpu as pltpu
from jax.sharding import PartitionSpec as P

EPS = 1e-06
HIGH = lax.Precision.HIGHEST
MESH = pl.DeviceIdType.MESH
K1 = 0.7978845608028654
K2 = 0.044715
VMEM_BYTES = 62 * 2**20
N_SEMS = 400


def passed_along(shard, axis, by):
    length = lax.axis_size(axis)
    pairs = [(i, i + by) for i in range(length) if 0 <= i + by < length]
    return lax.ppermute(shard, axis, pairs)


def entering_2(shard, axis, combine, identity, reverse):
    length, here = (lax.axis_size(axis), lax.axis_index(axis))
    everything = jax.tree.map(lambda part: lax.all_gather(part, axis), shard)
    start = jax.tree.map(
        lambda part, zero: jnp.broadcast_to(jnp.asarray(zero, part.dtype), part.shape),
        shard,
        identity,
    )

    def turn(k, before):
        at = length - 1 - k if reverse else k
        reached = at > here if reverse else at < here
        new = combine(before, jax.tree.map(lambda part: part[at], everything))
        return jax.tree.map(lambda a, b: jnp.where(reached, a, b), new, before)

    return lax.fori_loop(0, length, turn, start)


def normalize(values, gain):
    return values * lax.rsqrt(jnp.mean(values * values, axis=-1, keepdims=True) + EPS) * gain


def smooth(values):
    return jax.nn.gelu(values, approximate=True)


def affine(earlier, later):
    return (earlier[0] * later[0], later[0] * earlier[1] + later[1])


def doc_view(lengths, first, count):
    ends = jnp.cumsum(lengths)
    starts = ends - lengths
    position = first + jnp.arange(count, dtype=jnp.int32)
    owner = (position[:, None] >= starts[None, :]) & (position[:, None] < ends[None, :])
    start_of = jnp.sum(jnp.where(owner, starts[None, :], 0), axis=1)
    offset = position - start_of
    opening = (owner & (offset[:, None] == 0)).astype(jnp.float32)
    closing = (owner & (position[:, None] == ends[None, :] - 1)).astype(jnp.float32)
    return (offset, opening, closing)


def coefficients(rate_pre, inlet_pre, conv_value, decay, init_rows, keep):
    rate = jax.nn.sigmoid(rate_pre)
    inlet = jax.nn.sigmoid(inlet_pre)
    log_decay = -8.0 * rate * jax.nn.softplus(decay)
    factor = jnp.exp(log_decay)
    scale = jnp.sqrt(-jnp.expm1(2.0 * log_decay))
    carry_factor = keep * factor
    source = scale * inlet * conv_value + (1.0 - keep) * factor * init_rows
    return (carry_factor, source)


def spread(values):
    return lax.all_gather(values, "ch", axis=0, tiled=True)


def collect(terms):
    return lax.psum_scatter(terms, "ch", scatter_dimension=0, tiled=True)


def contract_last(left, right):
    return lax.dot_general(
        left, right, (((1,), (1,)), ((), ())), preferred_element_type=jnp.float32
    )


def contract_first(left, right):
    return lax.dot_general(
        left, right, (((0,), (0,)), ((), ())), preferred_element_type=jnp.float32
    )


def body(
    stream,
    cotangent,
    mix_gain,
    gelu_weight,
    recur_weight,
    conv_taps,
    conv_bias,
    rate_weight,
    rate_bias,
    inlet_weight,
    inlet_bias,
    decay_param,
    init_states,
    out_weight,
    ffn_gain,
    gate_weight,
    up_weight,
    down_weight,
    doc_lengths,
    block_counts,
):
    slot_count = rate_weight.shape[0]
    block_width = rate_weight.shape[1]
    local_width = slot_count * block_width
    taps = conv_taps.shape[0]
    token_count = stream.shape[0] * lax.axis_size("ch")
    hidden_width = gate_weight.shape[1]
    base = lax.axis_index("seq") * token_count
    offset_all, opening, closing = doc_view(doc_lengths, base, token_count + taps - 1)
    offset = offset_all[:token_count]
    opening = opening[:token_count]
    closing = closing[:token_count]
    keep = (offset > 0).astype(jnp.float32)[:, None]
    slot_live = (jnp.arange(slot_count, dtype=jnp.int32) < block_counts[0]).astype(jnp.float32)
    live = jnp.repeat(slot_live, block_width)[None, :]
    taps_flat = conv_taps.reshape(taps, local_width)
    decay_flat = decay_param.reshape(1, local_width)
    stream_float = stream.astype(jnp.float32)
    mix_low = normalize(stream_float, mix_gain).astype(jnp.bfloat16)
    mix_full = spread(mix_low)
    gelu_pre = jnp.dot(mix_full, gelu_weight, preferred_element_type=jnp.float32)
    recur_low = jnp.dot(mix_full, recur_weight, preferred_element_type=jnp.float32).astype(
        jnp.bfloat16
    )
    rim = passed_along(recur_low[token_count - taps + 1 :], "seq", 1)
    extended = jnp.concatenate([rim, recur_low], axis=0).astype(jnp.float32)
    conv_pre = conv_bias.reshape(1, local_width)
    for tap_index in range(taps):
        valid = (offset >= tap_index).astype(jnp.float32)[:, None]
        lead = taps - 1 - tap_index
        conv_pre = (
            conv_pre + taps_flat[tap_index][None, :] * extended[lead : lead + token_count] * valid
        )
    conv_low = conv_pre.astype(jnp.bfloat16)
    conv_value = conv_low.astype(jnp.float32)
    grouped = conv_low.reshape(token_count, slot_count, block_width)
    rate_pre = (
        jnp.einsum("rsi,sio->rso", grouped, rate_weight, preferred_element_type=jnp.float32)
        + rate_bias[None]
    ).reshape(token_count, local_width)
    inlet_pre = (
        jnp.einsum("rsi,sio->rso", grouped, inlet_weight, preferred_element_type=jnp.float32)
        + inlet_bias[None]
    ).reshape(token_count, local_width)
    init_rows = jnp.dot(opening, init_states, precision=HIGH)
    carry_factor, source = coefficients(
        rate_pre, inlet_pre, conv_value, decay_flat, init_rows, keep
    )
    cumulative, local_state = lax.associative_scan(affine, (carry_factor, source), axis=0)
    summary = (cumulative[-1], local_state[-1])
    entering = entering_2(
        summary, "seq", affine, (jnp.ones_like(summary[0]), jnp.zeros_like(summary[1])), False
    )
    state_in = entering[1]
    state = local_state + cumulative * state_in[None, :]
    gelu_value = smooth(gelu_pre)
    product_low = (gelu_value * state * live).astype(jnp.bfloat16)
    branch = collect(jnp.dot(product_low, out_weight, preferred_element_type=jnp.float32))
    middle = stream_float + branch
    ffn_low = normalize(middle, ffn_gain).astype(jnp.bfloat16)
    ffn_full = spread(ffn_low)
    stacked = jnp.concatenate([gate_weight, up_weight], axis=1)
    columns = ffn_full
    gate_up = jnp.dot(
        columns,
        lax.all_gather(stacked, "seq", axis=0, tiled=True),
        preferred_element_type=jnp.float32,
    )
    gate = gate_up[:, :hidden_width]
    upward = gate_up[:, hidden_width:]
    hidden = (smooth(gate) * upward).astype(jnp.bfloat16)
    ffn_terms = jnp.dot(
        hidden,
        lax.all_gather(down_weight, "seq", axis=1, tiled=True),
        preferred_element_type=jnp.float32,
    )
    mixed_out = (middle + collect(ffn_terms)).astype(jnp.bfloat16)
    out_grad_full = spread(cotangent)
    columns = out_grad_full
    hidden_grad = contract_last(columns, lax.all_gather(down_weight, "seq", axis=1, tiled=True))
    down_weight_grad = contract_first(hidden, out_grad_full)
    unused, pair_pull = jax.vjp(lambda left, right: smooth(left) * right, gate, upward)
    gate_grad, up_grad = pair_pull(hidden_grad)
    pair_low = jnp.concatenate([gate_grad, up_grad], axis=1).astype(jnp.bfloat16)
    pair_weight_grad = contract_first(ffn_full, pair_low)
    norm_ffn_part = contract_last(pair_low, lax.all_gather(stacked, "seq", axis=0, tiled=True))
    norm_ffn_grad = collect(norm_ffn_part)
    unused, ffn_norm_pull = jax.vjp(normalize, middle, ffn_gain)
    middle_norm_grad, ffn_gain_part = ffn_norm_pull(norm_ffn_grad)
    middle_grad = cotangent.astype(jnp.float32) + middle_norm_grad
    branch_full = spread(middle_grad.astype(jnp.bfloat16))
    out_weight_grad = contract_first(product_low, branch_full)
    product_grad = contract_last(branch_full, out_weight)
    state_grad = product_grad * gelu_value * live
    unused, gelu_pull = jax.vjp(smooth, gelu_pre)
    gelu_low = gelu_pull(product_grad * state * live)[0].astype(jnp.bfloat16)
    following = jnp.concatenate([carry_factor[1:], jnp.ones_like(carry_factor[:1])], axis=0)
    cum_back, adjoint_local = lax.associative_scan(
        affine, (jnp.flip(following, 0), jnp.flip(state_grad, 0)), axis=0
    )
    cum_back = jnp.flip(cum_back, 0)
    adjoint_local = jnp.flip(adjoint_local, 0)
    summary_back = (carry_factor[0] * cum_back[0], carry_factor[0] * adjoint_local[0])
    arriving = entering_2(
        summary_back,
        "seq",
        affine,
        (jnp.ones_like(summary_back[0]), jnp.zeros_like(summary_back[1])),
        True,
    )
    adjoint_in = arriving[1]
    adjoint = adjoint_local + cum_back * adjoint_in[None, :]
    previous_state = jnp.concatenate([state_in[None, :], state[:-1]], axis=0)

    def local_coefficients(rate_value, inlet_value, conv_part, decay_value):
        return coefficients(rate_value, inlet_value, conv_part, decay_value, init_rows, keep)

    unused, coefficient_pull = jax.vjp(
        local_coefficients, rate_pre, inlet_pre, conv_value, decay_flat
    )
    rate_grad, inlet_grad, conv_direct, decay_part = coefficient_pull(
        (adjoint * previous_state, adjoint)
    )
    rate_low = rate_grad.astype(jnp.bfloat16).reshape(token_count, slot_count, block_width)
    inlet_low = inlet_grad.astype(jnp.bfloat16).reshape(token_count, slot_count, block_width)
    rate_weight_grad = jnp.einsum(
        "rsi,rso->sio", grouped, rate_low, preferred_element_type=jnp.float32
    )
    inlet_weight_grad = jnp.einsum(
        "rsi,rso->sio", grouped, inlet_low, preferred_element_type=jnp.float32
    )
    rate_bias_grad = jnp.sum(rate_low.astype(jnp.float32), axis=0)
    inlet_bias_grad = jnp.sum(inlet_low.astype(jnp.float32), axis=0)
    conv_back = jnp.einsum(
        "rso,sio->rsi", rate_low, rate_weight, preferred_element_type=jnp.float32
    )
    conv_back = conv_back + jnp.einsum(
        "rso,sio->rsi", inlet_low, inlet_weight, preferred_element_type=jnp.float32
    )
    conv_low_grad = (conv_direct + conv_back.reshape(token_count, local_width)).astype(jnp.bfloat16)
    rim_back = passed_along(conv_low_grad[: taps - 1], "seq", -1)
    ahead = jnp.concatenate([conv_low_grad, rim_back], axis=0).astype(jnp.float32)
    own_grad = ahead[:token_count]
    recur_grad = jnp.zeros((token_count, local_width), jnp.float32)
    tap_grads = []
    for tap_index in range(taps):
        lead = taps - 1 - tap_index
        valid_here = (offset >= tap_index).astype(jnp.float32)[:, None]
        tap_grads.append(
            jnp.sum(own_grad * extended[lead : lead + token_count] * valid_here, axis=0)
        )
        valid_ahead = (offset_all[tap_index : tap_index + token_count] >= tap_index).astype(
            jnp.float32
        )[:, None]
        recur_grad = (
            recur_grad
            + taps_flat[tap_index][None, :]
            * ahead[tap_index : tap_index + token_count]
            * valid_ahead
        )
    conv_taps_grad = jnp.stack(tap_grads, axis=0).reshape(taps, slot_count, block_width)
    conv_bias_grad = jnp.sum(own_grad, axis=0).reshape(slot_count, block_width)
    recur_low_grad = recur_grad.astype(jnp.bfloat16)
    gelu_weight_grad = contract_first(mix_full, gelu_low)
    recur_weight_grad = contract_first(mix_full, recur_low_grad)
    norm_mix_part = contract_last(gelu_low, gelu_weight) + contract_last(
        recur_low_grad, recur_weight
    )
    norm_mix_grad = collect(norm_mix_part)
    unused, mix_norm_pull = jax.vjp(normalize, stream_float, mix_gain)
    stream_norm_grad, mix_gain_part = mix_norm_pull(norm_mix_grad)
    stream_grad = middle_grad + stream_norm_grad
    finals_local = lax.dot_general(closing, state * live, (((0,), (0,)), ((), ())), precision=HIGH)
    finals_wide = jnp.zeros((finals_local.shape[0], local_width * lax.axis_size("ch")), jnp.float32)
    finals_wide = lax.dynamic_update_slice(
        finals_wide, finals_local, (jnp.int32(0), lax.axis_index("ch") * local_width)
    )
    final_states, mix_gain_grad, ffn_gain_grad = lax.psum(
        (finals_wide, mix_gain_part, ffn_gain_part), ("seq", "ch")
    )
    summed = (
        lax.psum_scatter(gelu_weight_grad, "seq", scatter_dimension=0, tiled=True),
        lax.psum_scatter(recur_weight_grad, "seq", scatter_dimension=0, tiled=True),
        lax.psum_scatter(conv_taps_grad, "seq", scatter_dimension=2, tiled=True),
        lax.psum_scatter(conv_bias_grad, "seq", scatter_dimension=1, tiled=True),
        lax.psum_scatter(rate_weight_grad, "seq", scatter_dimension=1, tiled=True),
        lax.psum_scatter(rate_bias_grad, "seq", scatter_dimension=1, tiled=True),
        lax.psum_scatter(inlet_weight_grad, "seq", scatter_dimension=1, tiled=True),
        lax.psum_scatter(inlet_bias_grad, "seq", scatter_dimension=1, tiled=True),
        lax.psum_scatter(
            decay_part.reshape(slot_count, block_width), "seq", scatter_dimension=1, tiled=True
        ),
        lax.psum_scatter(out_weight_grad, "seq", scatter_dimension=1, tiled=True),
        lax.psum_scatter(
            pair_weight_grad[:, :hidden_width], "seq", scatter_dimension=0, tiled=True
        ),
        lax.psum_scatter(
            pair_weight_grad[:, hidden_width:], "seq", scatter_dimension=0, tiled=True
        ),
        lax.psum_scatter(down_weight_grad, "seq", scatter_dimension=1, tiled=True),
    )
    return (
        final_states,
        mixed_out,
        stream_grad,
        mix_gain_grad,
        summed[0],
        summed[1],
        summed[2],
        summed[3],
        summed[4],
        summed[5],
        summed[6],
        summed[7],
        summed[8],
        summed[9],
        ffn_gain_grad,
        summed[10],
        summed[11],
        summed[12],
    )


class Net:
    def __init__(self, n_seq, n_ch, rows, send_sems, recv_sems):
        self.n_seq, self.n_ch, self.rows = n_seq, n_ch, rows
        self.n_z = n_seq // 2
        self.send_sems, self.recv_sems = send_sems, recv_sems
        self.tags, self.used, self.sent = {}, 0, []
        self.s, self.c = lax.axis_index("seq"), lax.axis_index("ch")
        s, c, n_z = self.s, self.c, self.n_z
        self.z, self.x, self.y, self.core = s // 2, s % 2, c // 2, c % 2
        x, y = self.x, self.y
        self.s_to = [(s + k) % n_seq for k in range(n_seq)]
        self.s_from = [(s + n_seq - k) % n_seq for k in range(n_seq)]
        self.sibling = self.dev(self.z, x, y, 1 - self.core)
        self.across = self.dev(self.z, x, 1 - y, self.core)
        self.beside = self.dev(self.z, 1 - x, y, self.core)
        self.above = self.dev((self.z + 1) % n_z, x, y, self.core)
        self.below = self.dev((self.z + n_z - 1) % n_z, x, y, self.core)

    def dev(self, z, x, y, core):
        return (z * 2 + x, y * 2 + core)

    def block(self, z, x, y, core):
        rows = self.rows
        return pl.multiple_of(((z * 2 + x) * self.n_ch + y * 2 + core) * rows, rows)

    def z_of(self, slot):
        return (self.z + self.n_z - slot) % self.n_z

    def slot(self, at):
        if at == 0:
            return 0
        n_z, z = self.n_z, self.z
        low, high = (n_z - 1 - z) // (n_z - 1), z // (n_z - 1)
        inner = (at + 1) // 2 if at % 2 else n_z - at // 2
        return low * (n_z - at) + high * at + (1 - low - high) * inner

    def meet(self, peers):
        barrier = pltpu.get_barrier_semaphore()
        for peer in peers:
            pl.semaphore_signal(barrier, inc=1, device_id=peer, device_id_type=MESH)
        pl.semaphore_wait(barrier, len(peers))

    def sems(self, tag, at=0, size=1):
        if tag not in self.tags:
            self.tags[tag] = self.used
            self.used += size
        index = self.tags[tag] + at
        return self.send_sems.at[index], self.recv_sems.at[index]

    def copy(self, src, dst, sems, to):
        return pltpu.make_async_remote_copy(
            src_ref=src, dst_ref=dst, send_sem=sems[0], recv_sem=sems[1],
            device_id=to, device_id_type=MESH,
        )

    def send(self, src, dst, to, sems, when=None):
        copy = self.copy(src, dst, sems, to)
        if when is None:
            copy.start()
        else:
            @pl.when(when)
            def _():
                copy.start()
        self.sent.append((copy, when))

    def recv(self, view, sems):
        self.copy(view, view, sems, (self.s, self.c)).wait_recv()

    def local(self, src, dst, sems):
        copy = pltpu.make_async_copy(src, dst, sems[0])
        copy.start()
        return copy

    def drain(self):
        for copy, when in self.sent:
            if when is None:
                copy.wait_send()
            else:
                @pl.when(when)
                def _(copy=copy):
                    copy.wait_send()
        self.sent = []

    def ch_gather_start(self, view_of, tag):
        mine = view_of(self.c)
        self.send(mine, mine, self.across, self.sems((tag, "y")))
        self.send(mine, mine, self.sibling, self.sems((tag, "core")))

    def ch_gather_finish(self, view_of, tag):
        y, core = self.y, self.core
        theirs = view_of((1 - y) * 2 + core)
        self.recv(theirs, self.sems((tag, "y")))
        self.send(theirs, theirs, self.sibling, self.sems((tag, "fwd")))
        self.recv(view_of(y * 2 + 1 - core), self.sems((tag, "core")))
        self.recv(view_of((1 - y) * 2 + 1 - core), self.sems((tag, "fwd")))

    def ch_sum(self, part, mid, low, far, tag):
        y, core = self.y, self.core
        first = self.copy(part.at[1 - core], mid, self.sems((tag, "core")), self.sibling)
        first.start()
        first.wait()
        low[...] = (part[core, 1 - y] + mid[1 - y]).astype(jnp.bfloat16)
        second = self.copy(low, far, self.sems((tag, "y")), self.across)
        second.start()
        total = part[core, y] + mid[y]
        second.wait()
        return total + far[...].astype(jnp.float32)

    def chain_start(self, mine, target, tag):
        n_z, z = self.n_z, self.z
        self.send(mine, target, self.above, (self.sems((tag, "own"), 0, 2)[0], self.sems((tag, "z"), 1, n_z)[1]), z < n_z - 1)
        self.send(mine, target, self.below, (self.sems((tag, "own"), 1, 2)[0], self.sems((tag, "z"), n_z - 1, n_z)[1]), z > 0)

    def chain_arrive(self, view, slot, tag):
        n_z, z = self.n_z, self.z
        self.recv(view, self.sems((tag, "z"), slot, n_z))
        up = (self.sems((tag, "up"), slot, n_z)[0], self.sems((tag, "z"), (slot + 1) % n_z, n_z)[1])
        down = (self.sems((tag, "up"), slot, n_z)[0], self.sems((tag, "z"), (slot + n_z - 1) % n_z, n_z)[1])
        self.send(view, view, self.above, up, (z >= slot) & (z < n_z - 1))
        self.send(view, view, self.below, down, (z < slot) & (z > 0))


class Spread:
    def __init__(self, net, ref, tag):
        self.net, self.ref, self.tag = net, ref, tag

    def view(self, slot, x, y, core, half=None):
        net = self.net
        at, rows = net.block(net.z_of(slot), x, y, core), net.rows
        if half is not None:
            at, rows = pl.multiple_of(at + half * (rows // 2), rows // 2), rows // 2
        return self.ref.at[pl.ds(at, rows)]

    def sems(self, what, slot):
        return self.net.sems((self.tag, what), slot, self.net.n_z)

    def start(self):
        net = self.net
        mine = self.view(0, net.x, net.y, net.core)
        net.chain_start(mine, mine, self.tag)
        self.plane(0)

    def plane(self, slot):
        net = self.net
        view = self.view(slot, net.x, net.y, net.core)
        net.send(view, view, net.beside, self.sems("x", slot))
        net.send(view, view, net.across, self.sems("y", slot))
        net.send(view, view, net.sibling, self.sems("s0", slot))

    def arrive(self, slot):
        net = self.net
        net.chain_arrive(self.view(slot, net.x, net.y, net.core), slot, self.tag)
        self.plane(slot)

    def relay(self, slot):
        net = self.net
        x, y, core = net.x, net.y, net.core
        view = self.view(slot, 1 - x, y, core)
        net.recv(view, self.sems("x", slot))
        half = self.view(slot, 1 - x, y, core, 0)
        net.send(half, half, net.across, self.sems("d0", slot))
        net.send(view, view, net.sibling, self.sems("s1", slot))
        view = self.view(slot, x, 1 - y, core)
        net.recv(view, self.sems("y", slot))
        half = self.view(slot, x, 1 - y, core, 1)
        net.send(half, half, net.beside, self.sems("d1", slot))
        net.send(view, view, net.sibling, self.sems("s2", slot))

    def relay_far(self, slot):
        net = self.net
        for half in (0, 1):
            view = self.view(slot, 1 - net.x, 1 - net.y, net.core, half)
            net.recv(view, self.sems(f"d{half}", slot))
            net.send(view, view, net.sibling, self.sems(f"s{3 + half}", slot))

    def done(self, slot):
        net = self.net
        x, y, core = net.x, net.y, 1 - net.core
        net.recv(self.view(slot, x, y, core), self.sems("s0", slot))
        net.recv(self.view(slot, 1 - x, y, core), self.sems("s1", slot))
        net.recv(self.view(slot, x, 1 - y, core), self.sems("s2", slot))
        for half in (0, 1):
            net.recv(self.view(slot, 1 - x, 1 - y, core, half), self.sems(f"s{3 + half}", slot))


class Collect:
    def __init__(self, net, part, sib, far, side, along, tag):
        self.net, self.part, self.sib, self.far, self.side, self.along, self.tag = net, part, sib, far, side, along, tag

    def sems(self, what, at):
        return self.net.sems((self.tag, what), at, self.net.n_z)

    def first(self, at):
        net = self.net
        net.send(self.part.at[at, 1 - net.core], self.sib.at[at], net.sibling, self.sems("s", at))

    def second(self, at):
        net = self.net
        net.recv(self.sib.at[at], self.sems("s", at))
        core, part, sib = net.core, self.part, self.sib

        def add(i, _):
            part[at, core, i] = (part[at, core, i].astype(jnp.float32) + sib[at, i].astype(jnp.float32)).astype(jnp.bfloat16)
            return 0

        lax.fori_loop(0, 4, add, 0)
        half = net.rows // 2
        diagonal = part.at[at, core, (1 - net.x) * 2 + 1 - net.y]
        net.send(diagonal.at[pl.ds(0, half)], self.far.at[at, 0], net.beside, self.sems("f0", at))
        net.send(diagonal.at[pl.ds(half, half)], self.far.at[at, 1], net.across, self.sems("f1", at))

    def third(self, at):
        net, part, far = self.net, self.part, self.far
        half = net.rows // 2
        for which, index, first, to in (
            (0, net.x * 2 + 1 - net.y, 0, net.across),
            (1, (1 - net.x) * 2 + net.y, half, net.beside),
        ):
            net.recv(far.at[at, which], self.sems(f"f{which}", at))
            rows = pl.ds(first, half)
            value = part[at, net.core, index, rows, :].astype(jnp.float32) + far[at, which].astype(jnp.float32)
            part[at, net.core, index, rows, :] = value.astype(jnp.bfloat16)
            net.send(part.at[at, net.core, index], self.side.at[at, which], to, self.sems(f"p{which}", at))

    def fourth(self, at):
        net = self.net
        mine = net.x * 2 + net.y
        for which in (0, 1):
            net.recv(self.side.at[at, which], self.sems(f"p{which}", at))
        total = self.part[at, net.core, mine].astype(jnp.float32)
        total = total + self.side[at, 0].astype(jnp.float32) + self.side[at, 1].astype(jnp.float32)
        if at == 0:
            return total
        slot = net.slot(at)
        self.part[at, net.core, mine] = total.astype(jnp.bfloat16)
        net.send(
            self.part.at[at, net.core, mine], self.along.at[slot], net.dev(net.z_of(slot), net.x, net.y, net.core),
            self.sems("z", slot),
        )
        return None

    def total(self, own):
        net = self.net
        for slot in range(1, net.n_z):
            net.recv(self.along.at[slot], self.sems("z", slot))
            own = own + self.along[slot].astype(jnp.float32)
        return own


def stack_rows(rows):
    return jnp.concatenate(rows, axis=0)


def smooth_pair(v):
    t = jnp.tanh(K1 * (v + K2 * v * v * v))
    value = 0.5 * v * (1.0 + t)
    slope = 0.5 * (1.0 + t) + 0.5 * v * (1.0 - t * t) * K1 * (1.0 + 3.0 * K2 * v * v)
    return value, slope


def sigmoid(v):
    return 1.0 / (1.0 + jnp.exp(-v))


def softplus_exact(d):
    u = jnp.exp(-jnp.abs(d))
    r = u / (2.0 + u)
    q = r * r
    series = 1.0 / 15.0
    for k in (13, 11, 9, 7, 5, 3, 1):
        series = series * q + 1.0 / k
    return jnp.maximum(d, 0.0) + 2.0 * r * series


def minus_expm1(v):
    series = 1.0 / 362880.0
    for k in (40320.0, 5040.0, 720.0, 120.0, 24.0, 6.0, 2.0, 1.0):
        series = series * v + 1.0 / k
    return jnp.where(v > -0.5, -v * series, 1.0 - jnp.exp(v))


class Docs:
    def __init__(self, lengths, first, count, before=0):
        position = first - before + lax.broadcasted_iota(jnp.int32, (count, 1), 0)
        self.opening, self.closing = [], []
        start_of = jnp.zeros((count, 1), jnp.int32)
        start = jnp.int32(0)
        for e in range(lengths.shape[0]):
            end = start + lengths[e]
            owner = (position >= start) & (position < end)
            start_of = jnp.where(owner, start, start_of)
            self.opening.append((position == start).astype(jnp.float32))
            self.closing.append((position == end - 1).astype(jnp.float32))
            start = end
        self.offset = position - start_of
        self.keep = (self.offset > 0).astype(jnp.float32)

    def valid(self, k):
        return (self.offset >= k).astype(jnp.float32)


def prefix(a, b, count):
    row = lax.broadcasted_iota(jnp.int32, a.shape, 0)
    k = 1
    while k < count:
        inside = row >= k
        a_far = jnp.where(inside, pltpu.roll(a, k, 0), 1.0)
        b_far = jnp.where(inside, pltpu.roll(b, k, 0), 0.0)
        b = a * b_far + b
        a = a * a_far
        k *= 2
    return a, b


def suffix(a, b, count):
    row = lax.broadcasted_iota(jnp.int32, a.shape, 0)
    k = 1
    while k < count:
        inside = row < count - k
        a_far = jnp.where(inside, pltpu.roll(a, count - k, 0), 1.0)
        b_far = jnp.where(inside, pltpu.roll(b, count - k, 0), 0.0)
        b = a * b_far + b
        a = a * a_far
        k *= 2
    return a, b


def coefficient_parts(rate_pre, inlet_pre, decay):
    rate = sigmoid(rate_pre)
    inlet = sigmoid(inlet_pre)
    sp = softplus_exact(decay)
    log_decay = -8.0 * rate * sp
    factor = jnp.exp(log_decay)
    scale = jnp.sqrt(minus_expm1(2.0 * log_decay))
    return rate, inlet, sp, log_decay, factor, scale


def opening_rows(docs, init):
    total = docs.opening[0] * init[0:1]
    for e in range(1, len(docs.opening)):
        total = total + docs.opening[e] * init[e : e + 1]
    return total


def pack_gain(row):
    tiles = [row[:, i * 128 : (i + 1) * 128] for i in range(row.shape[1] // 128)]
    return jnp.concatenate([stack_rows(tiles[i : i + 8]) for i in range(0, len(tiles), 8)], axis=1)


def norm_back(values, gain, grad):
    r = lax.rsqrt(jnp.mean(values * values, axis=-1, keepdims=True) + EPS)
    u = grad * gain
    to_values = r * u - values * (r * r * r) * jnp.mean(u * values, axis=-1, keepdims=True)
    to_gain = jnp.sum(grad * values * r, axis=0, keepdims=True)
    return to_values, to_gain


RIM = 16


def block_kernel(sizes, names, *refs):
    n_seq, n_ch, rows, d, slots, bw, width, sl = sizes
    r = types.SimpleNamespace(**dict(zip(names, refs)))
    bf, f32 = jnp.bfloat16, jnp.float32
    net = Net(n_seq, n_ch, rows, r.send_sems, r.recv_sems)
    s, c, x, y, z, core, n_z = net.s, net.c, net.x, net.y, net.z, net.core, net.n_z
    count, wide, tokens = rows * n_ch, slots * bw, rows * n_ch * n_seq
    n_taps = r.taps.shape[0]
    seq_peers = [(net.s_to[k], c) for k in range(1, n_seq)]
    rim_peers = [(net.s_to[k], (c + i) % n_ch) for k in (1, n_seq - 1) for i in range(1, n_ch)]
    net.meet(seq_peers + rim_peers + [net.sibling, net.across])

    own_cols = pl.ds(pl.multiple_of(s * width, width), width)
    own_count = pl.ds(pl.multiple_of(s * count, count), count)
    own_slice = pl.ds(pl.multiple_of(s * sl, sl), sl)
    local = []

    values = r.stream[...].astype(f32)
    scale = lax.rsqrt(jnp.mean(values * values, axis=-1, keepdims=True) + EPS)
    mix_rows = pl.ds(pl.multiple_of(RIM + c * rows, 16), rows)
    r.mix[mix_rows, :] = (values * scale * r.mix_gain[...][None, :]).astype(bf)

    def mix_of(cc):
        return r.mix.at[pl.ds(pl.multiple_of(RIM + cc * rows, 16), rows)]

    last, first = r.mix.at[pl.ds(count, RIM)], r.mix.at[pl.ds(0, RIM)]
    net.ch_gather_start(mix_of, "mix")
    for i in range(n_ch):
        net.send(last, first, (net.s_to[1], i), net.sems("rim", i, n_ch), (c == n_ch - 1) & (s < n_seq - 1))

    @pl.when(s == 0)
    def _():
        r.mix[pl.ds(0, RIM), :] = jnp.zeros((RIM, d), bf)

    cots = Spread(net, r.cfull, "cot")
    lows = Spread(net, r.full, "low")
    mine = net.block(z, x, y, core)
    r.cfull[pl.ds(mine, rows), :] = r.cot[...]
    cots.start()

    def left_start(a, src):
        r.left[a, s, c] = src[:, own_cols]
        for k in range(1, n_seq):
            cols = pl.ds(pl.multiple_of(net.s_to[k] * width, width), width)
            net.send(src.at[:, cols], r.left.at[a, s, c], (net.s_to[k], c), net.sems(("left", a), k, n_seq))

    def left_pass(a):
        for k in range(1, n_seq):
            net.recv(r.left.at[a, net.s_from[k], c], net.sems(("left", a), k, n_seq))
        net.ch_gather_start(lambda cc: r.left.at[a, :, cc], ("leftch", a))

    def left_done(a):
        net.ch_gather_finish(lambda cc: r.left.at[a, :, cc], ("leftch", a))

    left_start(0, r.mix.at[mix_rows])

    def turn(a, src):
        for i in range(src.shape[1] // 256):
            r.turned[a, i * 256 : (i + 1) * 256, :] = src[:, i * 256 : (i + 1) * 256].T

    def weight_start(a):
        src = r.turned.at[a] if a < 2 else r.down
        for k in range(1, n_seq):
            net.send(
                src.at[pl.ds(pl.multiple_of(net.s_to[k] * sl, sl), sl)], r.wt.at[a, :, own_cols],
                (net.s_to[k], c), net.sems(("w", a), k, n_seq),
            )
        local.append(net.local(src.at[own_slice], r.wt.at[a, :, own_cols], net.sems(("w", a), 0, n_seq)))

    def weight_done(a):
        for k in range(1, n_seq):
            cols = pl.ds(pl.multiple_of(net.s_from[k] * width, width), width)
            net.recv(r.wt.at[a, :, cols], net.sems(("w", a), k, n_seq))
        local.pop(0).wait()

    turn(0, r.gate_w)
    weight_start(0)
    turn(1, r.up_w)

    net.ch_gather_finish(mix_of, "mix")
    for i in range(n_ch):
        @pl.when((s > 0) & (c == i))
        def _(i=i):
            net.recv(first, net.sems("rim", i, n_ch))

    docs = Docs(r.lengths, s * count, count)
    keep = docs.keep
    ends_a, ends_b = [], []
    for b in range(slots):
        cols = pl.ds(b * bw, bw)
        rowsof = r.mix[...]
        r.gelu[:, cols] = jnp.dot(rowsof[RIM:], r.gelu_w[:, cols], preferred_element_type=f32)
        recur = jnp.dot(rowsof, r.recur_w[:, cols], preferred_element_type=f32).astype(bf)
        r.recur[:, cols] = recur
        recur = recur.astype(f32)
        conv_pre = r.bias[b : b + 1, :]
        for k in range(n_taps):
            conv_pre = conv_pre + r.taps[k, b : b + 1, :] * recur[RIM - k : RIM - k + count] * docs.valid(k)
        conv_low = conv_pre.astype(bf)
        r.conv[:, cols] = conv_low
        rate_pre = jnp.dot(conv_low, r.rate_w[b], preferred_element_type=f32) + r.rate_b[b : b + 1, :]
        inlet_pre = jnp.dot(conv_low, r.inlet_w[b], preferred_element_type=f32) + r.inlet_b[b : b + 1, :]
        r.rate_pre[:, cols] = rate_pre
        r.inlet_pre[:, cols] = inlet_pre
        rate, inlet, sp, log_decay, factor, scale = coefficient_parts(rate_pre, inlet_pre, r.decay[b : b + 1, :])
        source = scale * inlet * conv_low.astype(f32) + (1.0 - keep) * factor * opening_rows(docs, r.init[:, cols])
        total, part = prefix(keep * factor, source, count)
        r.scan_a[:, cols] = total
        r.scan_b[:, cols] = part
        ends_a.append(total[count - 1 : count])
        ends_b.append(part[count - 1 : count])

    def exchange(summary, pieces, tag):
        summary[s] = stack_rows(pieces + [jnp.zeros((8 - 2 * slots, bw), f32)])
        for k in range(1, n_seq):
            net.send(summary.at[s], summary.at[s], (net.s_to[k], c), net.sems(tag, k, n_seq))

    def exchanged(summary, tag):
        for k in range(1, n_seq):
            net.recv(summary.at[net.s_from[k]], net.sems(tag, k, n_seq))

    exchange(r.summary, ends_a + ends_b, "sum")
    cots.arrive(net.slot(1))
    cots.arrive(net.slot(2))
    weight_start(1)
    cots.relay(0)
    exchanged(r.summary, "sum")
    enter = jnp.zeros((slots, bw), f32)
    for q in range(n_seq - 1):
        after = r.summary[q, 0:slots] * enter + r.summary[q, slots : 2 * slots]
        enter = jnp.where(s > q, after, enter)
    finals = []
    for b in range(slots):
        cols = pl.ds(b * bw, bw)
        live = jnp.where(r.counts[0] > b, 1.0, 0.0)
        state = r.scan_b[:, cols] + r.scan_a[:, cols] * enter[b : b + 1]
        r.state[:, cols] = state
        value, _ = smooth_pair(r.gelu[:, cols])
        r.own[0, :, cols] = (value * state * live).astype(bf)
        ends = [jnp.sum(mark * state, axis=0, keepdims=True) * live for mark in docs.closing]
        finals.append(stack_rows(ends + [jnp.zeros((8 - len(ends), bw), f32)]))

    def branch_tile(i, _):
        cols = pl.ds(pl.multiple_of(i * 256, 256), 256)
        value = jnp.dot(r.own[0], r.out_w[:, cols], preferred_element_type=f32)
        for cc in range(n_ch):
            r.part[cc % 2, cc // 2, :, cols] = value[cc * rows : (cc + 1) * rows]
        return 0

    lax.fori_loop(0, d // 256, branch_tile, 0)
    middle = values + net.ch_sum(r.part, r.mid, r.ylow, r.yfar, "branch")
    scale = lax.rsqrt(jnp.mean(middle * middle, axis=-1, keepdims=True) + EPS)
    r.full[pl.ds(mine, rows), :] = (middle * scale * r.ffn_gain[...][None, :]).astype(bf)
    r.middle[...] = middle

    lows.start()
    cots.arrive(net.slot(3))
    weight_start(2)
    cots.relay(net.slot(1))
    cots.relay(net.slot(2))
    cots.relay_far(0)
    lows.relay(0)
    lows.arrive(net.slot(1))
    lows.arrive(net.slot(2))
    lows.relay_far(0)
    lows.relay(net.slot(1))
    lows.relay(net.slot(2))
    lows.arrive(net.slot(3))
    cots.relay(net.slot(3))
    for at in (1, 2, 3):
        cots.relay_far(net.slot(at))
    group = n_ch * 2 * rows

    def chunk(at):
        return pl.ds(pl.multiple_of(net.z_of(net.slot(at)) * group, group), group)

    weight_done(0)
    weight_done(1)

    def forward(at):
        lows.done(net.slot(at))
        here = chunk(at)
        gate = contract_last(r.full[here, :], r.wt[0])
        up = contract_last(r.full[here, :], r.wt[1])
        value, slope = smooth_pair(gate)
        r.value[here, :] = value
        r.slope[here, :] = up * slope
        r.hid[here, :] = (value * up).astype(bf)

    forward(0)
    lows.relay_far(net.slot(1))
    lows.relay(net.slot(3))
    forward(1)
    lows.relay_far(net.slot(2))
    forward(2)
    lows.relay_far(net.slot(3))
    forward(3)
    for at in range(n_z):
        cots.done(net.slot(at))

    def weight_grad(a, left, right):
        def tile(i, _):
            cols = pl.ds(pl.multiple_of(i * 256, 256), 256)
            r.dwl[a, :, cols] = contract_first(left[...], right[:, cols]).astype(bf)
            return 0

        lax.fori_loop(0, d // 256, tile, 0)
        for k in range(1, n_seq):
            cols = pl.ds(pl.multiple_of(net.s_to[k] * width, width), width)
            net.send(r.dwl.at[a, :, cols], r.dw.at[a, own_slice], (net.s_to[k], c), net.sems(("dw", a), k, n_seq))
        local.append(net.local(r.dwl.at[a, :, own_cols], r.dw.at[a, own_slice], net.sems(("dw", a), 0, n_seq)))

    def weight_grad_done(a):
        for k in range(1, n_seq):
            rows_at = pl.ds(pl.multiple_of(net.s_from[k] * sl, sl), sl)
            net.recv(r.dw.at[a, rows_at], net.sems(("dw", a), k, n_seq))

    weight_grad(2, r.hid, r.cfull)
    down_local = local.pop()
    weight_done(2)
    local.append(down_local)

    def spread_out(ref, at, value, cols):
        value = value.astype(bf)
        for xx in range(2):
            for yy in range(2):
                for cc in range(2):
                    row = (xx * 4 + yy * 2 + cc) * rows
                    ref[at, cc, xx * 2 + yy, :, cols] = value[row : row + rows]

    def backward(at):
        here = chunk(at)
        grad = contract_last(r.cfull[here, :], r.wt[2])
        r.gat[here, :] = (grad * r.slope[here, :]).astype(bf)
        r.upg[here, :] = (grad * r.value[here, :]).astype(bf)

        def tile(i, _):
            cols = pl.ds(pl.multiple_of(i * 256, 256), 256)
            value = jnp.dot(r.gat[here, :], r.wt[0, :, cols], preferred_element_type=f32)
            value = value + jnp.dot(r.upg[here, :], r.wt[1, :, cols], preferred_element_type=f32)
            spread_out(r.npart, at, value, cols)
            return 0

        lax.fori_loop(0, d // 256, tile, 0)

    def output(at):
        here = chunk(at)

        def tile(i, _):
            cols = pl.ds(pl.multiple_of(i * 256, 256), 256)
            value = jnp.dot(r.hid[here, :], r.wt[2, :, cols], preferred_element_type=f32)
            spread_out(r.opart, at, value, cols)
            return 0

        lax.fori_loop(0, d // 256, tile, 0)

    norms = Collect(net, r.npart, r.nsib, r.nfar, r.nside, r.nalong, "norm")
    outs = Collect(net, r.opart, r.osib, r.ofar, r.oside, r.oalong, "out")
    backward(3)
    norms.first(3)
    backward(2)
    norms.first(2)
    norms.second(3)
    backward(1)
    norms.first(1)
    norms.second(2)
    norms.third(3)
    backward(0)
    norms.first(0)
    norms.second(1)
    norms.third(2)
    norms.fourth(3)
    norms.second(0)
    output(3)
    output(2)
    norms.third(1)
    norms.fourth(2)
    output(1)
    output(0)
    norms.third(0)
    norms.fourth(1)
    weight_grad(0, r.gat, r.full)
    nfg = norms.total(norms.fourth(0))

    to_middle, ffn_part = norm_back(middle, r.ffn_gain[...][None, :], nfg)
    middle_grad = r.cot[...].astype(f32) + to_middle
    r.branch[c] = middle_grad.astype(bf)
    net.ch_gather_start(lambda cc: r.branch.at[cc], "bgrad")
    left_start(1, r.branch.at[c])
    outs.first(3)
    outs.first(2)
    r.early[n_z] = jnp.concatenate(finals + [pack_gain(ffn_part)], axis=1)
    net.ch_gather_finish(lambda cc: r.branch.at[cc], "bgrad")

    ahead_docs = Docs(r.lengths, s * count, count + RIM)
    row = lax.broadcasted_iota(jnp.int32, (count, bw), 0)
    heads_a, heads_b = [], []
    for b in range(slots):
        cols = pl.ds(b * bw, bw)
        live = jnp.where(r.counts[0] > b, 1.0, 0.0)
        product_grad = contract_last(r.branch[...].reshape(count, d), r.out_w[b * bw : (b + 1) * bw, :])
        value, slope = smooth_pair(r.gelu[:, cols])
        r.own[1, :, cols] = (product_grad * r.state[:, cols] * live * slope).astype(bf)
        rate, inlet, sp, log_decay, factor, scale = coefficient_parts(r.rate_pre[:, cols], r.inlet_pre[:, cols], r.decay[b : b + 1, :])
        carry = keep * factor
        following = jnp.where(row < count - 1, pltpu.roll(carry, count - 1, 0), 1.0)
        total, part = suffix(following, product_grad * value * live, count)
        r.scan_a[:, cols] = total
        r.scan_b[:, cols] = part
        heads_a.append(carry[0:1] * total[0:1])
        heads_b.append(carry[0:1] * part[0:1])
    exchange(r.summary_back, heads_a + heads_b, "sumback")

    chains = [r.gathered.at[a] for a in range(3)]

    def gather_view(a, slot, xx):
        at = (net.z_of(slot) * 2 + xx) * count
        return r.gathered.at[a, pl.ds(pl.multiple_of(at, count), count)]

    def gather_start(a):
        view = gather_view(a, 0, x)
        net.chain_start(r.own.at[a], view, ("g", a))
        net.send(r.own.at[a], view, net.beside, net.sems(("gx", a), 0, n_z))
        local.append(net.local(r.own.at[a], view, net.sems(("glocal", a))))

    def gather_arrive(a, at):
        slot = net.slot(at)
        view = gather_view(a, slot, x)
        net.chain_arrive(view, slot, ("g", a))
        net.send(view, view, net.beside, net.sems(("gx", a), slot, n_z))

    def gather_done(a):
        for slot in range(n_z):
            net.recv(gather_view(a, slot, 1 - x), net.sems(("gx", a), slot, n_z))

    gather_start(0)
    outs.first(1)
    outs.first(0)
    for at in (3, 2, 1, 0):
        outs.second(at)
    exchanged(r.summary_back, "sumback")
    enter_back = jnp.zeros((slots, bw), f32)
    for q in range(n_seq - 1, 0, -1):
        after = r.summary_back[q, 0:slots] * enter_back + r.summary_back[q, slots : 2 * slots]
        enter_back = jnp.where(s < q, after, enter_back)
    vec = []
    for b in range(slots):
        cols = pl.ds(b * bw, bw)
        adjoint = r.scan_b[:, cols] + r.scan_a[:, cols] * enter_back[b : b + 1]
        previous = jnp.where(row > 0, pltpu.roll(r.state[:, cols], 1, 0), enter[b : b + 1])
        decay = r.decay[b : b + 1, :]
        rate, inlet, sp, log_decay, factor, scale = coefficient_parts(r.rate_pre[:, cols], r.inlet_pre[:, cols], decay)
        conv_low = r.conv[:, cols]
        conv = conv_low.astype(f32)
        init_rows = opening_rows(docs, r.init[:, cols])
        log_grad = adjoint * (
            factor * (keep * previous + (1.0 - keep) * init_rows) - inlet * conv * jnp.exp(2.0 * log_decay) / scale
        )
        rate_low = (log_grad * (-8.0 * sp) * rate * (1.0 - rate)).astype(bf)
        direct = adjoint * scale
        inlet_low = (direct * conv * inlet * (1.0 - inlet)).astype(bf)
        decay_row = jnp.sum(log_grad * (-8.0 * rate), axis=0, keepdims=True) * sigmoid(decay)
        back = direct * inlet + contract_last(rate_low, r.rate_w[b]) + contract_last(inlet_low, r.inlet_w[b])
        r.cgrad[0:count, cols] = back.astype(bf)
        for a, low in enumerate((rate_low, inlet_low)):
            part = contract_first(conv_low, low).astype(bf)
            r.gates[a, b] = part.reshape(r.gates.shape[2:])
        vec.append([
            jnp.sum(rate_low.astype(f32), axis=0, keepdims=True),
            jnp.sum(inlet_low.astype(f32), axis=0, keepdims=True),
            decay_row,
        ])
    rim = r.cgrad.at[pl.ds(count, RIM)]
    net.send(r.cgrad.at[pl.ds(0, RIM)], rim, (net.s_to[n_seq - 1], c), net.sems("rimback"), s > 0)

    @pl.when(s == n_seq - 1)
    def _():
        r.cgrad[pl.ds(count, RIM), :] = jnp.zeros((RIM, wide), bf)

    net.send(r.gates.at[:, :, :, 1 - x], r.gates_x, net.beside, net.sems("gatesx"))
    weight_grad(1, r.upg, r.full)

    @pl.when(s < n_seq - 1)
    def _():
        net.recv(rim, net.sems("rimback"))

    vectors = []
    for b in range(slots):
        cols = pl.ds(b * bw, bw)
        grad = r.cgrad[:, cols].astype(f32)
        own = grad[:count]
        recur = r.recur[:, cols].astype(f32)
        total = jnp.zeros((count, bw), f32)
        tap_rows = []
        for k in range(n_taps):
            tap_rows.append(jnp.sum(own * recur[RIM - k : RIM - k + count] * docs.valid(k), axis=0, keepdims=True))
            total = total + r.taps[k, b : b + 1, :] * grad[k : k + count] * ahead_docs.valid(k)[k : k + count]
        r.own[2, :, cols] = total.astype(bf)
        vectors.append(stack_rows(tap_rows + [jnp.sum(own, axis=0, keepdims=True)] + vec[b]))
    gather_start(2)
    gather_start(1)

    def norm_tile(i, _):
        cols = pl.ds(pl.multiple_of(i * 256, 256), 256)
        value = contract_last(r.own[1], r.gelu_w[cols, :]) + contract_last(r.own[2], r.recur_w[cols, :])
        for cc in range(n_ch):
            r.part[cc % 2, cc // 2, :, cols] = value[cc * rows : (cc + 1) * rows]
        return 0

    lax.fori_loop(0, d // 256, norm_tile, 0)
    norm_grad = net.ch_sum(r.part, r.mid, r.ylow, r.yfar, "norm")
    to_stream, mix_part = norm_back(values, r.mix_gain[...][None, :], norm_grad)
    r.sgrad[...] = middle_grad + to_stream
    r.late[n_z] = jnp.concatenate(vectors + [pack_gain(mix_part)], axis=1)
    net.send(r.early.at[n_z], r.pair.at[0], net.beside, net.sems("pair", 0, 2))
    net.send(r.late.at[n_z], r.pair.at[1], net.beside, net.sems("pair", 1, 2))
    net.recv(r.gates_x, net.sems("gatesx"))

    def gate_add(i, _):
        for a in range(2):
            for b in range(slots):
                value = r.gates[a, b, i, x].astype(f32) + r.gates_x[a, b, i].astype(f32)
                r.gates[a, b, i, x] = value.astype(bf)
        return 0

    lax.fori_loop(0, n_z, gate_add, 0)
    for k in range(1, n_z):
        to = net.z_of(k)
        net.send(r.gates.at[:, :, to, x], r.gates_z.at[k], net.dev(to, x, y, core), net.sems("gatesz", k, n_z))
    for at in (3, 2, 1, 0):
        outs.third(at)
    for a in (0, 1):
        left_pass(a)
    for a, ref in enumerate((r.early, r.late)):
        net.recv(r.pair.at[a], net.sems("pair", a, 2))
        ref[z] = ref[n_z] + r.pair[a]
        for k in range(1, n_z):
            to = net.z_of(k)
            net.send(ref.at[z], ref.at[z], net.dev(to, x, y, core), net.sems(("vec", a), k, n_z))
    for at in (1, 2, 3):
        for a in (0, 2, 1):
            gather_arrive(a, at)
    for at in (3, 2, 1):
        outs.fourth(at)
    out_sum = outs.fourth(0)
    for a in (0, 1):
        left_done(a)
    for a, ref in enumerate((r.early, r.late)):
        for k in range(1, n_z):
            net.recv(ref.at[(z + k) % n_z], net.sems(("vec", a), k, n_z))
    early, late = r.early[0], r.late[0]
    for q in range(1, n_z):
        early, late = early + r.early[q], late + r.late[q]
    r.shared[c] = jnp.concatenate([early, late[:, wide:]], axis=1)
    net.ch_gather_start(lambda cc: r.shared.at[cc], "shared")
    piece = bw // n_seq
    for b in range(slots):
        part = jnp.zeros((8, piece), f32)
        for q in range(n_seq):
            at = b * bw + q * piece
            part = jnp.where(s == q, late[:, at : at + piece], part)
        r.small[b] = part
    for k in range(1, n_z):
        net.recv(r.gates_z.at[k], net.sems("gatesz", k, n_z))
    for a in range(2):
        for b in range(slots):
            total = r.gates[a, b, z, x].astype(f32)
            for k in range(1, n_z):
                total = total + r.gates_z[k, a, b].astype(f32)
            r.gate_out[a, b] = total
    net.ch_gather_finish(lambda cc: r.shared.at[cc], "shared")
    gains = r.shared[0, :, wide:]
    for cc in range(1, n_ch):
        gains = gains + r.shared[cc, :, wide:]
    for cc in range(n_ch):
        r.finals[:, cc * wide : (cc + 1) * wide] = r.shared[cc, 0 : r.finals.shape[0], 0:wide]
    half = gains.shape[1] // 2
    for a in range(2):
        for i in range(half // 128):
            r.gains[a, i * 8 : (i + 1) * 8, :] = gains[:, a * half + i * 128 : a * half + (i + 1) * 128]
    r.mixed[...] = (middle + outs.total(out_sum)).astype(bf)
    for a in (2, 0, 1):
        weight_grad_done(a)
    for a in (0, 2, 1):
        gather_done(a)
    for copy in local:
        copy.wait()
    net.drain()


def finish_kernel(names, *refs):
    r = types.SimpleNamespace(**dict(zip(names, refs)))

    def left(a):
        value = r.left[a]
        return value.reshape(value.shape[0] * value.shape[1] * value.shape[2], value.shape[3])

    r.out_wg[...] = contract_first(r.gathered[0], left(1))
    r.gelu_wg[...] = contract_first(left(0), r.gathered[1])
    r.recur_wg[...] = contract_first(left(0), r.gathered[2])
    for a, ref in enumerate((r.gate_wg, r.up_wg)):
        for i in range(ref.shape[1] // 256):
            ref[:, i * 256 : (i + 1) * 256] = r.dw[a, i * 256 : (i + 1) * 256, :].T.astype(jnp.float32)
    r.down_wg[...] = r.dw[2].astype(jnp.float32)
    r.finals_o[...] = r.finals[...]
    r.mixed_o[...] = r.mixed[...]
    r.sgrad_o[...] = r.sgrad[...]
    r.ffn_o[...] = r.gains[0]
    r.mix_o[...] = r.gains[1]
    r.rate_o[...] = r.gate_out[0]
    r.inlet_o[...] = r.gate_out[1]
    n_taps = r.taps_o.shape[0]
    for b in range(r.small.shape[0]):
        for k in range(n_taps):
            r.taps_o[k, b : b + 1, :] = r.small[b, k : k + 1, :]
        for k, ref in enumerate((r.bias_o, r.rateb_o, r.inletb_o, r.decay_o)):
            ref[b : b + 1, :] = r.small[b, n_taps + k : n_taps + k + 1, :]


def gathered_body(
    stream, cotangent, mix_gain, gelu_weight, recur_weight, conv_taps, conv_bias, rate_weight, rate_bias, inlet_weight,
    inlet_bias, decay_param, init_states, out_weight, ffn_gain, gate_weight, up_weight, down_weight, doc_lengths, block_counts,
):
    n_seq, n_ch = lax.axis_size("seq"), lax.axis_size("ch")
    rows, d = stream.shape
    slots, bw = conv_bias.shape
    width, hidden = gate_weight.shape
    sl = hidden // n_seq
    n_z = n_seq // 2
    count, wide, tokens = rows * n_ch, slots * bw, rows * n_ch * n_seq
    piece = bw // n_seq
    n_taps, n_docs = conv_taps.shape[0], doc_lengths.shape[0]
    bf, f32 = jnp.bfloat16, jnp.float32
    vmem = pl.BlockSpec(memory_space=pltpu.VMEM)
    smem = pl.BlockSpec(memory_space=pltpu.SMEM)
    anywhere = pl.BlockSpec(memory_space=pl.ANY)
    inputs = dict(
        stream=stream, cot=cotangent, mix_gain=mix_gain, gelu_w=gelu_weight, recur_w=recur_weight, taps=conv_taps,
        bias=conv_bias, rate_w=rate_weight, rate_b=rate_bias, inlet_w=inlet_weight, inlet_b=inlet_bias, decay=decay_param,
        init=init_states, out_w=out_weight, ffn_gain=ffn_gain, gate_w=gate_weight, up_w=up_weight, down=down_weight,
        lengths=doc_lengths, counts=block_counts,
    )
    places = dict(lengths=smem, counts=smem, down=anywhere)
    outputs = dict(
        gathered=((3, tokens, wide), bf), left=((2, n_seq, n_ch, rows, width), bf), dw=((3, hidden, width), bf),
        finals=((n_docs, wide * n_ch), f32), mixed=((rows, d), bf), sgrad=((rows, d), f32), gains=((2, d // 128, 128), f32),
        gate_out=((2, slots, piece, bw), f32), small=((slots, 8, piece), f32),
    )
    out_places = dict(gathered=anywhere, dw=anywhere)
    packed = wide + d // 8
    scratch = dict(
        mix=((RIM + count, d), bf), full=((tokens, d), bf), cfull=((tokens, d), bf), turned=((2, hidden, width), bf),
        wt=((3, sl, d), bf), dwl=((3, sl, d), bf), value=((tokens, sl), f32), slope=((tokens, sl), f32),
        hid=((tokens, sl), bf), gat=((tokens, sl), bf), upg=((tokens, sl), bf),
        gelu=((count, wide), f32), recur=((RIM + count, wide), bf), conv=((count, wide), bf), rate_pre=((count, wide), f32),
        inlet_pre=((count, wide), f32), scan_a=((count, wide), f32), scan_b=((count, wide), f32), state=((count, wide), f32),
        own=((3, count, wide), bf), cgrad=((count + RIM, wide), bf), branch=((n_ch, rows, d), bf),
        summary=((n_seq, 8, bw), f32), summary_back=((n_seq, 8, bw), f32),
        part=((2, 2, rows, d), f32), mid=((2, rows, d), f32), ylow=((rows, d), bf), yfar=((rows, d), bf), middle=((rows, d), f32),
        npart=((n_z, 2, 4, rows, d), bf), nsib=((n_z, 4, rows, d), bf), nfar=((n_z, 2, rows // 2, d), bf),
        nside=((n_z, 2, rows, d), bf), nalong=((n_z, rows, d), bf),
        opart=((n_z, 2, 4, rows, d), bf), osib=((n_z, 4, rows, d), bf), ofar=((n_z, 2, rows // 2, d), bf),
        oside=((n_z, 2, rows, d), bf), oalong=((n_z, rows, d), bf),
        gates=((2, slots, n_z, 2, piece, bw), bf), gates_x=((2, slots, n_z, piece, bw), bf), gates_z=((n_z, 2, slots, piece, bw), bf),
        early=((n_z + 1, 8, packed), f32), late=((n_z + 1, 8, packed), f32), pair=((2, 8, packed), f32),
        shared=((n_ch, 8, packed + d // 8), f32),
    )
    dma = pltpu.SemaphoreType.DMA((N_SEMS,))
    results = pl.pallas_call(
        functools.partial(
            block_kernel, (n_seq, n_ch, rows, d, slots, bw, width, sl),
            list(inputs) + list(outputs) + list(scratch) + ["send_sems", "recv_sems"],
        ),
        out_shape=[jax.ShapeDtypeStruct(*what) for what in outputs.values()],
        in_specs=[places.get(name, vmem) for name in inputs],
        out_specs=[out_places.get(name, vmem) for name in outputs],
        scratch_shapes=[pltpu.VMEM(*what) for what in scratch.values()] + [dma, dma],
        compiler_params=pltpu.CompilerParams(collective_id=1, has_side_effects=True, vmem_limit_bytes=VMEM_BYTES),
    )(*inputs.values())
    vector = ((slots, piece), f32)
    ends = dict(
        finals_o=((n_docs, wide * n_ch), f32), mixed_o=((rows, d), bf), sgrad_o=((rows, d), f32), mix_o=((d // 128, 128), f32),
        gelu_wg=((width, wide), f32), recur_wg=((width, wide), f32), taps_o=((n_taps, slots, piece), f32), bias_o=vector,
        rate_o=((slots, piece, bw), f32), rateb_o=vector, inlet_o=((slots, piece, bw), f32), inletb_o=vector, decay_o=vector,
        out_wg=((wide, width), f32), ffn_o=((d // 128, 128), f32), gate_wg=((width, hidden), f32), up_wg=((width, hidden), f32),
        down_wg=((hidden, width), f32),
    )
    last = pl.pallas_call(
        functools.partial(finish_kernel, list(outputs) + list(ends)),
        out_shape=[jax.ShapeDtypeStruct(*what) for what in ends.values()],
        in_specs=[vmem] * len(outputs),
        out_specs=[vmem] * len(ends),
        compiler_params=pltpu.CompilerParams(vmem_limit_bytes=VMEM_BYTES),
    )(*results)
    named = dict(zip(ends, last))
    named["mix_o"], named["ffn_o"] = named["mix_o"].reshape(d), named["ffn_o"].reshape(d)
    return tuple(named.values())


def solution(mesh):
    in_specs = (
        P(("seq", "ch"), None),
        P(("seq", "ch"), None),
        P(),
        P(None, "ch"),
        P(None, "ch"),
        P(None, "ch", None),
        P("ch", None),
        P("ch", None, None),
        P("ch", None),
        P("ch", None, None),
        P("ch", None),
        P("ch", None),
        P(None, "ch"),
        P("ch", None),
        P(),
        P("seq", "ch"),
        P("seq", "ch"),
        P("ch", "seq"),
        P(),
        P("ch"),
    )
    out_specs = (
        P(),
        P(("seq", "ch"), None),
        P(("seq", "ch"), None),
        P(),
        P("seq", "ch"),
        P("seq", "ch"),
        P(None, "ch", "seq"),
        P("ch", "seq"),
        P("ch", "seq", None),
        P("ch", "seq"),
        P("ch", "seq", None),
        P("ch", "seq"),
        P("ch", "seq"),
        P("ch", "seq"),
        P(),
        P("seq", "ch"),
        P("seq", "ch"),
        P("ch", "seq"),
    )
    return jax.shard_map(gathered_body if mesh.shape['seq'] == 8 else body, mesh=mesh, in_specs=in_specs, out_specs=out_specs, check_vma=False)
```

```python
import functools
import math
import types

import jax
import jax.numpy as jnp
from jax import lax
from jax.experimental import pallas as pl
from jax.experimental.pallas import tpu as pltpu
from jax.sharding import PartitionSpec as P

EPS = 1e-06
HIGH = lax.Precision.HIGHEST
MESH = pl.DeviceIdType.MESH
SEQ = "seq"
CH = "ch"
K1 = 0.7978845608028654
K2 = 0.044715
VMEM_BYTES = 63 * 2**20
TILE = 1024
SEND_SEMS = 96
RECV_SEMS = 128
LOCAL_SEMS = 46


def passed_along(shard, axis, by):
    length = lax.axis_size(axis)
    pairs = [(i, i + by) for i in range(length) if 0 <= i + by < length]
    return lax.ppermute(shard, axis, pairs)


def entering_2(shard, axis, combine, identity, reverse):
    length, here = (lax.axis_size(axis), lax.axis_index(axis))
    everything = jax.tree.map(lambda part: lax.all_gather(part, axis), shard)
    start = jax.tree.map(
        lambda part, zero: jnp.broadcast_to(jnp.asarray(zero, part.dtype), part.shape),
        shard,
        identity,
    )

    def turn(k, before):
        at = length - 1 - k if reverse else k
        reached = at > here if reverse else at < here
        new = combine(before, jax.tree.map(lambda part: part[at], everything))
        return jax.tree.map(lambda a, b: jnp.where(reached, a, b), new, before)

    return lax.fori_loop(0, length, turn, start)


def normalize(values, gain):
    return values * lax.rsqrt(jnp.mean(values * values, axis=-1, keepdims=True) + EPS) * gain


def smooth(values):
    return jax.nn.gelu(values, approximate=True)


def affine(earlier, later):
    return (earlier[0] * later[0], later[0] * earlier[1] + later[1])


def doc_view(lengths, first, count):
    ends = jnp.cumsum(lengths)
    starts = ends - lengths
    position = first + jnp.arange(count, dtype=jnp.int32)
    owner = (position[:, None] >= starts[None, :]) & (position[:, None] < ends[None, :])
    start_of = jnp.sum(jnp.where(owner, starts[None, :], 0), axis=1)
    offset = position - start_of
    opening = (owner & (offset[:, None] == 0)).astype(jnp.float32)
    closing = (owner & (position[:, None] == ends[None, :] - 1)).astype(jnp.float32)
    return (offset, opening, closing)


def coefficients(rate_pre, inlet_pre, conv_value, decay, init_rows, keep):
    rate = jax.nn.sigmoid(rate_pre)
    inlet = jax.nn.sigmoid(inlet_pre)
    log_decay = -8.0 * rate * jax.nn.softplus(decay)
    factor = jnp.exp(log_decay)
    scale = jnp.sqrt(-jnp.expm1(2.0 * log_decay))
    carry_factor = keep * factor
    source = scale * inlet * conv_value + (1.0 - keep) * factor * init_rows
    return (carry_factor, source)


def spread(values):
    return lax.all_gather(values, CH, axis=0, tiled=True)


def collect(terms):
    return lax.psum_scatter(terms, CH, scatter_dimension=0, tiled=True)


def contract_last(left, right):
    return lax.dot_general(
        left, right, (((1,), (1,)), ((), ())), preferred_element_type=jnp.float32
    )


def contract_first(left, right):
    return lax.dot_general(
        left, right, (((0,), (0,)), ((), ())), preferred_element_type=jnp.float32
    )


def body(
    stream,
    cotangent,
    mix_gain,
    gelu_weight,
    recur_weight,
    conv_taps,
    conv_bias,
    rate_weight,
    rate_bias,
    inlet_weight,
    inlet_bias,
    decay_param,
    init_states,
    out_weight,
    ffn_gain,
    gate_weight,
    up_weight,
    down_weight,
    doc_lengths,
    block_counts,
):
    slot_count = rate_weight.shape[0]
    block_width = rate_weight.shape[1]
    local_width = slot_count * block_width
    taps = conv_taps.shape[0]
    token_count = stream.shape[0] * lax.axis_size(CH)
    hidden_width = gate_weight.shape[1]
    base = lax.axis_index(SEQ) * token_count
    offset_all, opening, closing = doc_view(doc_lengths, base, token_count + taps - 1)
    offset = offset_all[:token_count]
    opening = opening[:token_count]
    closing = closing[:token_count]
    keep = (offset > 0).astype(jnp.float32)[:, None]
    slot_live = (jnp.arange(slot_count, dtype=jnp.int32) < block_counts[0]).astype(jnp.float32)
    live = jnp.repeat(slot_live, block_width)[None, :]
    taps_flat = conv_taps.reshape(taps, local_width)
    decay_flat = decay_param.reshape(1, local_width)
    stream_float = stream.astype(jnp.float32)
    mix_low = normalize(stream_float, mix_gain).astype(jnp.bfloat16)
    mix_full = spread(mix_low)
    gelu_pre = jnp.dot(mix_full, gelu_weight, preferred_element_type=jnp.float32)
    recur_low = jnp.dot(mix_full, recur_weight, preferred_element_type=jnp.float32).astype(
        jnp.bfloat16
    )
    rim = passed_along(recur_low[token_count - taps + 1 :], SEQ, 1)
    extended = jnp.concatenate([rim, recur_low], axis=0).astype(jnp.float32)
    conv_pre = conv_bias.reshape(1, local_width)
    for tap_index in range(taps):
        valid = (offset >= tap_index).astype(jnp.float32)[:, None]
        lead = taps - 1 - tap_index
        conv_pre = (
            conv_pre + taps_flat[tap_index][None, :] * extended[lead : lead + token_count] * valid
        )
    conv_low = conv_pre.astype(jnp.bfloat16)
    conv_value = conv_low.astype(jnp.float32)
    grouped = conv_low.reshape(token_count, slot_count, block_width)
    rate_pre = (
        jnp.einsum("rsi,sio->rso", grouped, rate_weight, preferred_element_type=jnp.float32)
        + rate_bias[None]
    ).reshape(token_count, local_width)
    inlet_pre = (
        jnp.einsum("rsi,sio->rso", grouped, inlet_weight, preferred_element_type=jnp.float32)
        + inlet_bias[None]
    ).reshape(token_count, local_width)
    init_rows = jnp.dot(opening, init_states, precision=HIGH)
    carry_factor, source = coefficients(
        rate_pre, inlet_pre, conv_value, decay_flat, init_rows, keep
    )
    cumulative, local_state = lax.associative_scan(affine, (carry_factor, source), axis=0)
    summary = (cumulative[-1], local_state[-1])
    entering = entering_2(
        summary, SEQ, affine, (jnp.ones_like(summary[0]), jnp.zeros_like(summary[1])), False
    )
    state_in = entering[1]
    state = local_state + cumulative * state_in[None, :]
    gelu_value = smooth(gelu_pre)
    product_low = (gelu_value * state * live).astype(jnp.bfloat16)
    branch = collect(jnp.dot(product_low, out_weight, preferred_element_type=jnp.float32))
    middle = stream_float + branch
    ffn_low = normalize(middle, ffn_gain).astype(jnp.bfloat16)
    ffn_full = spread(ffn_low)
    stacked = jnp.concatenate([gate_weight, up_weight], axis=1)
    columns = ffn_full
    gate_up = jnp.dot(
        columns,
        lax.all_gather(stacked, SEQ, axis=0, tiled=True),
        preferred_element_type=jnp.float32,
    )
    gate = gate_up[:, :hidden_width]
    upward = gate_up[:, hidden_width:]
    hidden = (smooth(gate) * upward).astype(jnp.bfloat16)
    ffn_terms = jnp.dot(
        hidden,
        lax.all_gather(down_weight, SEQ, axis=1, tiled=True),
        preferred_element_type=jnp.float32,
    )
    mixed_out = (middle + collect(ffn_terms)).astype(jnp.bfloat16)
    out_grad_full = spread(cotangent)
    columns = out_grad_full
    hidden_grad = contract_last(columns, lax.all_gather(down_weight, SEQ, axis=1, tiled=True))
    down_weight_grad = contract_first(hidden, out_grad_full)
    unused, pair_pull = jax.vjp(lambda left, right: smooth(left) * right, gate, upward)
    gate_grad, up_grad = pair_pull(hidden_grad)
    pair_low = jnp.concatenate([gate_grad, up_grad], axis=1).astype(jnp.bfloat16)
    pair_weight_grad = contract_first(ffn_full, pair_low)
    norm_ffn_part = contract_last(pair_low, lax.all_gather(stacked, SEQ, axis=0, tiled=True))
    norm_ffn_grad = collect(norm_ffn_part)
    unused, ffn_norm_pull = jax.vjp(normalize, middle, ffn_gain)
    middle_norm_grad, ffn_gain_part = ffn_norm_pull(norm_ffn_grad)
    middle_grad = cotangent.astype(jnp.float32) + middle_norm_grad
    branch_full = spread(middle_grad.astype(jnp.bfloat16))
    out_weight_grad = contract_first(product_low, branch_full)
    product_grad = contract_last(branch_full, out_weight)
    state_grad = product_grad * gelu_value * live
    unused, gelu_pull = jax.vjp(smooth, gelu_pre)
    gelu_low = gelu_pull(product_grad * state * live)[0].astype(jnp.bfloat16)
    following = jnp.concatenate([carry_factor[1:], jnp.ones_like(carry_factor[:1])], axis=0)
    cum_back, adjoint_local = lax.associative_scan(
        affine, (jnp.flip(following, 0), jnp.flip(state_grad, 0)), axis=0
    )
    cum_back = jnp.flip(cum_back, 0)
    adjoint_local = jnp.flip(adjoint_local, 0)
    summary_back = (carry_factor[0] * cum_back[0], carry_factor[0] * adjoint_local[0])
    arriving = entering_2(
        summary_back,
        SEQ,
        affine,
        (jnp.ones_like(summary_back[0]), jnp.zeros_like(summary_back[1])),
        True,
    )
    adjoint_in = arriving[1]
    adjoint = adjoint_local + cum_back * adjoint_in[None, :]
    previous_state = jnp.concatenate([state_in[None, :], state[:-1]], axis=0)

    def local_coefficients(rate_value, inlet_value, conv_part, decay_value):
        return coefficients(rate_value, inlet_value, conv_part, decay_value, init_rows, keep)

    unused, coefficient_pull = jax.vjp(
        local_coefficients, rate_pre, inlet_pre, conv_value, decay_flat
    )
    rate_grad, inlet_grad, conv_direct, decay_part = coefficient_pull(
        (adjoint * previous_state, adjoint)
    )
    rate_low = rate_grad.astype(jnp.bfloat16).reshape(token_count, slot_count, block_width)
    inlet_low = inlet_grad.astype(jnp.bfloat16).reshape(token_count, slot_count, block_width)
    rate_weight_grad = jnp.einsum(
        "rsi,rso->sio", grouped, rate_low, preferred_element_type=jnp.float32
    )
    inlet_weight_grad = jnp.einsum(
        "rsi,rso->sio", grouped, inlet_low, preferred_element_type=jnp.float32
    )
    rate_bias_grad = jnp.sum(rate_low.astype(jnp.float32), axis=0)
    inlet_bias_grad = jnp.sum(inlet_low.astype(jnp.float32), axis=0)
    conv_back = jnp.einsum(
        "rso,sio->rsi", rate_low, rate_weight, preferred_element_type=jnp.float32
    )
    conv_back = conv_back + jnp.einsum(
        "rso,sio->rsi", inlet_low, inlet_weight, preferred_element_type=jnp.float32
    )
    conv_low_grad = (conv_direct + conv_back.reshape(token_count, local_width)).astype(jnp.bfloat16)
    rim_back = passed_along(conv_low_grad[: taps - 1], SEQ, -1)
    ahead = jnp.concatenate([conv_low_grad, rim_back], axis=0).astype(jnp.float32)
    own_grad = ahead[:token_count]
    recur_grad = jnp.zeros((token_count, local_width), jnp.float32)
    tap_grads = []
    for tap_index in range(taps):
        lead = taps - 1 - tap_index
        valid_here = (offset >= tap_index).astype(jnp.float32)[:, None]
        tap_grads.append(
            jnp.sum(own_grad * extended[lead : lead + token_count] * valid_here, axis=0)
        )
        valid_ahead = (offset_all[tap_index : tap_index + token_count] >= tap_index).astype(
            jnp.float32
        )[:, None]
        recur_grad = (
            recur_grad
            + taps_flat[tap_index][None, :]
            * ahead[tap_index : tap_index + token_count]
            * valid_ahead
        )
    conv_taps_grad = jnp.stack(tap_grads, axis=0).reshape(taps, slot_count, block_width)
    conv_bias_grad = jnp.sum(own_grad, axis=0).reshape(slot_count, block_width)
    recur_low_grad = recur_grad.astype(jnp.bfloat16)
    gelu_weight_grad = contract_first(mix_full, gelu_low)
    recur_weight_grad = contract_first(mix_full, recur_low_grad)
    norm_mix_part = contract_last(gelu_low, gelu_weight) + contract_last(
        recur_low_grad, recur_weight
    )
    norm_mix_grad = collect(norm_mix_part)
    unused, mix_norm_pull = jax.vjp(normalize, stream_float, mix_gain)
    stream_norm_grad, mix_gain_part = mix_norm_pull(norm_mix_grad)
    stream_grad = middle_grad + stream_norm_grad
    finals_local = lax.dot_general(closing, state * live, (((0,), (0,)), ((), ())), precision=HIGH)
    finals_wide = jnp.zeros((finals_local.shape[0], local_width * lax.axis_size(CH)), jnp.float32)
    finals_wide = lax.dynamic_update_slice(
        finals_wide, finals_local, (jnp.int32(0), lax.axis_index(CH) * local_width)
    )
    final_states, mix_gain_grad, ffn_gain_grad = lax.psum(
        (finals_wide, mix_gain_part, ffn_gain_part), (SEQ, CH)
    )
    summed = (
        lax.psum_scatter(gelu_weight_grad, SEQ, scatter_dimension=0, tiled=True),
        lax.psum_scatter(recur_weight_grad, SEQ, scatter_dimension=0, tiled=True),
        lax.psum_scatter(conv_taps_grad, SEQ, scatter_dimension=2, tiled=True),
        lax.psum_scatter(conv_bias_grad, SEQ, scatter_dimension=1, tiled=True),
        lax.psum_scatter(rate_weight_grad, SEQ, scatter_dimension=1, tiled=True),
        lax.psum_scatter(rate_bias_grad, SEQ, scatter_dimension=1, tiled=True),
        lax.psum_scatter(inlet_weight_grad, SEQ, scatter_dimension=1, tiled=True),
        lax.psum_scatter(inlet_bias_grad, SEQ, scatter_dimension=1, tiled=True),
        lax.psum_scatter(
            decay_part.reshape(slot_count, block_width), SEQ, scatter_dimension=1, tiled=True
        ),
        lax.psum_scatter(out_weight_grad, SEQ, scatter_dimension=1, tiled=True),
        lax.psum_scatter(
            pair_weight_grad[:, :hidden_width], SEQ, scatter_dimension=0, tiled=True
        ),
        lax.psum_scatter(
            pair_weight_grad[:, hidden_width:], SEQ, scatter_dimension=0, tiled=True
        ),
        lax.psum_scatter(down_weight_grad, SEQ, scatter_dimension=1, tiled=True),
    )
    return (
        final_states,
        mixed_out,
        stream_grad,
        mix_gain_grad,
        summed[0],
        summed[1],
        summed[2],
        summed[3],
        summed[4],
        summed[5],
        summed[6],
        summed[7],
        summed[8],
        summed[9],
        ffn_gain_grad,
        summed[10],
        summed[11],
        summed[12],
    )


class Net:
    def __init__(self, n_seq, n_ch, rows, send_sems, recv_sems, local_sems):
        self.n_seq, self.n_ch, self.rows = n_seq, n_ch, rows
        self.n_z = n_seq // 2
        self.send_sems, self.recv_sems, self.local_sems = send_sems, recv_sems, local_sems
        self.tags, self.used, self.sent, self.locals = {}, 0, [], 0
        self.s, self.c = lax.axis_index(SEQ), lax.axis_index(CH)
        s, c, n_z = self.s, self.c, self.n_z
        self.z, self.x, self.y, self.core = s // 2, s % 2, c // 2, c % 2
        x, y = self.x, self.y
        self.s_to = [(s + k) % n_seq for k in range(n_seq)]
        self.s_from = [(s + n_seq - k) % n_seq for k in range(n_seq)]
        self.sibling = self.dev(self.z, x, y, 1 - self.core)
        self.across = self.dev(self.z, x, 1 - y, self.core)
        self.beside = self.dev(self.z, 1 - x, y, self.core)
        self.above = self.dev((self.z + 1) % n_z, x, y, self.core)
        self.below = self.dev((self.z + n_z - 1) % n_z, x, y, self.core)

    def nearest(self):
        order = [self.z * 2 + 1 - self.x]
        for at in range(1, self.n_z):
            there = self.z_of(self.slot(at))
            order += [there * 2 + self.x, there * 2 + 1 - self.x]
        return order

    def dev(self, z, x, y, core):
        return (z * 2 + x, y * 2 + core)

    def block(self, z, x, y, core):
        rows = self.rows
        return pl.multiple_of(((z * 2 + x) * self.n_ch + y * 2 + core) * rows, rows)

    def z_of(self, slot):
        return (self.z + self.n_z - slot) % self.n_z

    def slot(self, at):
        if at == 0:
            return 0
        n_z, z = self.n_z, self.z
        low, high = (n_z - 1 - z) // (n_z - 1), z // (n_z - 1)
        inner = (at + 1) // 2 if at % 2 else n_z - at // 2
        return low * (n_z - at) + high * at + (1 - low - high) * inner

    def greet(self, peers):
        barrier = pltpu.get_barrier_semaphore()
        for peer in peers:
            pl.semaphore_signal(barrier, inc=1, device_id=peer, device_id_type=MESH)

    def meet(self, peers):
        pl.semaphore_wait(pltpu.get_barrier_semaphore(), len(peers))

    def sem(self, tag, at=0, size=1):
        if tag not in self.tags:
            self.tags[tag] = self.used
            self.used += size
        return self.recv_sems.at[self.tags[tag] + at]

    def send(self, src, dst, to, sem, when=None):
        size = self.send_sems.shape[0]
        if len(self.sent) >= size:
            self.sent_wait(len(self.sent) - size)
        copy = pltpu.make_async_remote_copy(
            src_ref=src, dst_ref=dst, send_sem=self.send_sems.at[len(self.sent) % size], recv_sem=sem,
            device_id=to, device_id_type=MESH,
        )
        if when is None:
            copy.start()
        else:
            @pl.when(when)
            def _():
                copy.start()
        self.sent.append((copy, when))

    def sent_wait(self, at):
        if self.sent[at] is None:
            return
        copy, when = self.sent[at]
        self.sent[at] = None
        if when is None:
            copy.wait_send()
        else:
            @pl.when(when)
            def _():
                copy.wait_send()

    def recv(self, view, sem):
        pltpu.make_async_remote_copy(
            src_ref=view, dst_ref=view, send_sem=self.send_sems.at[0], recv_sem=sem,
            device_id=(self.s, self.c), device_id_type=MESH,
        ).wait_recv()

    def local(self, src, dst):
        copy = pltpu.make_async_copy(src, dst, self.local_sems.at[self.locals])
        self.locals += 1
        copy.start()
        return copy

    def drain(self):
        for at in range(len(self.sent)):
            self.sent_wait(at)

    def ch_gather_start(self, view_of, tag):
        mine = view_of(self.c)
        self.send(mine, mine, self.across, self.sem((tag, "y")))
        self.send(mine, mine, self.sibling, self.sem((tag, "core")))

    def ch_gather_finish(self, view_of, tag):
        y, core = self.y, self.core
        theirs = view_of((1 - y) * 2 + core)
        self.recv(theirs, self.sem((tag, "y")))
        self.send(theirs, theirs, self.sibling, self.sem((tag, "fwd")))
        self.recv(view_of(y * 2 + 1 - core), self.sem((tag, "core")))
        self.recv(view_of((1 - y) * 2 + 1 - core), self.sem((tag, "fwd")))

    def ch_sum(self, part, mid, low, far, tag):
        y, core = self.y, self.core
        first = len(self.sent)
        self.send(part.at[1 - core], mid, self.sibling, self.sem((tag, "core")))
        self.recv(mid, self.sem((tag, "core")))
        low[...] = (part[core, 1 - y] + mid[1 - y]).astype(jnp.bfloat16)
        self.send(low, far, self.across, self.sem((tag, "y")))
        total = part[core, y] + mid[y]
        self.recv(far, self.sem((tag, "y")))
        self.sent_wait(first)
        self.sent_wait(first + 1)
        return total + far[...].astype(jnp.float32)

    def chain_start(self, mine, target, tag):
        n_z, z = self.n_z, self.z
        self.send(mine, target, self.above, self.sem((tag, "z"), 1, n_z), z < n_z - 1)
        self.send(mine, target, self.below, self.sem((tag, "z"), n_z - 1, n_z), z > 0)

    def chain_arrive(self, view, slot, tag):
        n_z, z = self.n_z, self.z
        self.recv(view, self.sem((tag, "z"), slot, n_z))
        self.send(view, view, self.above, self.sem((tag, "z"), (slot + 1) % n_z, n_z), (z >= slot) & (z < n_z - 1))
        self.send(view, view, self.below, self.sem((tag, "z"), (slot + n_z - 1) % n_z, n_z), (z < slot) & (z > 0))


class Spread:
    def __init__(self, net, ref, tag):
        self.net, self.ref, self.tag = net, ref, tag

    def view(self, slot, x, y, core):
        net = self.net
        return self.ref.at[pl.ds(net.block(net.z_of(slot), x, y, core), net.rows)]

    def sem(self, what, slot):
        return self.net.sem((self.tag, what), slot, self.net.n_z)

    def start(self):
        net = self.net
        mine = self.view(0, net.x, net.y, net.core)
        net.chain_start(mine, mine, self.tag)
        self.plane(0)

    def plane(self, slot):
        net = self.net
        view = self.view(slot, net.x, net.y, net.core)
        net.send(view, view, net.beside, self.sem("x", slot))
        net.send(view, view, net.across, self.sem("y", slot))
        net.send(view, view, net.sibling, self.sem("s", slot))

    def arrive(self, slot):
        net = self.net
        net.chain_arrive(self.view(slot, net.x, net.y, net.core), slot, self.tag)
        self.plane(slot)

    def relay(self, slot):
        net = self.net
        view = self.view(slot, 1 - net.x, net.y, net.core)
        net.recv(view, self.sem("x", slot))
        net.send(view, view, net.across, self.sem("d", slot))
        net.send(view, view, net.sibling, self.sem("s", slot))

    def relay_far(self, slot):
        net = self.net
        for what, x in (("y", net.x), ("d", 1 - net.x)):
            view = self.view(slot, x, 1 - net.y, net.core)
            net.recv(view, self.sem(what, slot))
            net.send(view, view, net.sibling, self.sem("s", slot))

    def done(self, slot):
        net = self.net
        at = net.block(net.z_of(slot), 0, 0, 0)
        net.recv(self.ref.at[pl.ds(at, 4 * net.rows)], self.sem("s", slot))


class Collect:
    def __init__(self, net, part, sib, far, side, along, tag):
        self.net, self.part, self.sib, self.far, self.side, self.along, self.tag = net, part, sib, far, side, along, tag

    def sem(self, what, at):
        return self.net.sem((self.tag, what), at, self.net.n_z)

    def first(self, at):
        net = self.net
        net.send(self.part.at[at, 1 - net.core], self.sib.at[at], net.sibling, self.sem("s", at))

    def second(self, at):
        net = self.net
        net.recv(self.sib.at[at], self.sem("s", at))
        core, part, sib = net.core, self.part, self.sib
        for first in (1 - net.y, net.y):
            for x in range(2):
                value = part[at, core, first, x].astype(jnp.float32) + sib[at, first, x].astype(jnp.float32)
                part[at, core, first, x] = value.astype(jnp.bfloat16)
            if first is not net.y:
                net.send(part.at[at, core, first], self.far.at[at], net.across, self.sem("f", at))

    def third(self, at):
        net, part, far = self.net, self.part, self.far
        net.recv(far.at[at], self.sem("f", at))
        there = 1 - net.x
        value = part[at, net.core, net.y, there].astype(jnp.float32) + far[at, there].astype(jnp.float32)
        part[at, net.core, net.y, there] = value.astype(jnp.bfloat16)
        net.send(part.at[at, net.core, net.y, there], self.side.at[at], net.beside, self.sem("p", at))

    def plane_total(self, at):
        net = self.net
        net.recv(self.side.at[at], self.sem("p", at))
        total = self.part[at, net.core, net.y, net.x].astype(jnp.float32)
        return total + self.far[at, net.x].astype(jnp.float32) + self.side[at].astype(jnp.float32)

    def fourth(self, at):
        net, part = self.net, self.part
        total = self.plane_total(at)
        if at == 0:
            return total
        slot = net.slot(at)
        part[at, net.core, net.y, net.x] = total.astype(jnp.bfloat16)
        net.send(
            part.at[at, net.core, net.y, net.x], self.along.at[slot],
            net.dev(net.z_of(slot), net.x, net.y, net.core), net.sem((self.tag, "z")),
        )
        return None

    def total(self, own):
        net = self.net
        net.recv(self.along.at[pl.ds(1, net.n_z - 1)], net.sem((self.tag, "z")))
        for slot in range(1, net.n_z):
            own = own + self.along[slot].astype(jnp.float32)
        return own


class CollectEven(Collect):
    def second(self, at):
        net = self.net
        net.recv(self.sib.at[at], self.sem("s", at))
        core, part, sib = net.core, self.part, self.sib
        half = net.rows // 2
        for y in (1 - net.y, net.y):
            for x in (1 - net.x, net.x):
                value = part[at, core, y, x].astype(jnp.float32) + sib[at, y, x].astype(jnp.float32)
                part[at, core, y, x] = value.astype(jnp.bfloat16)
                if y is not net.y and x is not net.x:
                    diagonal = part.at[at, core, y, x]
                    net.send(diagonal.at[pl.ds(0, half)], self.far.at[at, 0], net.beside, self.sem("f0", at))
                    net.send(diagonal.at[pl.ds(half, half)], self.far.at[at, 1], net.across, self.sem("f1", at))

    def third(self, at):
        net, part, far = self.net, self.part, self.far
        half = net.rows // 2
        for which, y, x, first, to in (
            (0, 1 - net.y, net.x, 0, net.across), (1, net.y, 1 - net.x, half, net.beside),
        ):
            net.recv(far.at[at, which], self.sem(f"f{which}", at))
            rows = pl.ds(first, half)
            value = part[at, net.core, y, x, rows, :].astype(jnp.float32) + far[at, which].astype(jnp.float32)
            part[at, net.core, y, x, rows, :] = value.astype(jnp.bfloat16)
            net.send(part.at[at, net.core, y, x], self.side.at[at, which], to, self.sem("p", at))

    def plane_total(self, at):
        net = self.net
        net.recv(self.side.at[at], self.sem("p", at))
        total = self.part[at, net.core, net.y, net.x].astype(jnp.float32)
        return total + self.side[at, 0].astype(jnp.float32) + self.side[at, 1].astype(jnp.float32)


def stack_rows(rows):
    return jnp.concatenate(rows, axis=0)


def smooth_pair(v):
    t = jnp.tanh(K1 * (v + K2 * v * v * v))
    value = 0.5 * v * (1.0 + t)
    slope = 0.5 * (1.0 + t) + 0.5 * v * (1.0 - t * t) * K1 * (1.0 + 3.0 * K2 * v * v)
    return value, slope


def sigmoid(v):
    return 1.0 / (1.0 + jnp.exp(-v))


def softplus_exact(d):
    u = jnp.exp(-jnp.abs(d))
    r = u / (2.0 + u)
    q = r * r
    series = 1.0 / 15.0
    for k in (13, 11, 9, 7, 5, 3, 1):
        series = series * q + 1.0 / k
    return jnp.maximum(d, 0.0) + 2.0 * r * series


def minus_expm1(v):
    series = 1.0 / 362880.0
    for k in (40320.0, 5040.0, 720.0, 120.0, 24.0, 6.0, 2.0, 1.0):
        series = series * v + 1.0 / k
    return jnp.where(v > -0.5, -v * series, 1.0 - jnp.exp(v))


class Docs:
    def __init__(self, lengths, first, count, before=0):
        position = first - before + lax.broadcasted_iota(jnp.int32, (count, 1), 0)
        self.opening, self.closing = [], []
        start_of = jnp.zeros((count, 1), jnp.int32)
        start = jnp.int32(0)
        for e in range(lengths.shape[0]):
            end = start + lengths[e]
            owner = (position >= start) & (position < end)
            start_of = jnp.where(owner, start, start_of)
            self.opening.append((position == start).astype(jnp.float32))
            self.closing.append((position == end - 1).astype(jnp.float32))
            start = end
        self.offset = position - start_of
        self.keep = (self.offset > 0).astype(jnp.float32)

    def valid(self, k):
        return (self.offset >= k).astype(jnp.float32)


def prefix(a, b, count):
    row = lax.broadcasted_iota(jnp.int32, a.shape, 0)
    k = 1
    while k < count:
        inside = row >= k
        a_far = jnp.where(inside, pltpu.roll(a, k, 0), 1.0)
        b_far = jnp.where(inside, pltpu.roll(b, k, 0), 0.0)
        b = a * b_far + b
        a = a * a_far
        k *= 2
    return a, b


def suffix(a, b, count):
    row = lax.broadcasted_iota(jnp.int32, a.shape, 0)
    k = 1
    while k < count:
        inside = row < count - k
        a_far = jnp.where(inside, pltpu.roll(a, count - k, 0), 1.0)
        b_far = jnp.where(inside, pltpu.roll(b, count - k, 0), 0.0)
        b = a * b_far + b
        a = a * a_far
        k *= 2
    return a, b


def coefficient_parts(rate_pre, inlet_pre, decay):
    rate = sigmoid(rate_pre)
    inlet = sigmoid(inlet_pre)
    sp = softplus_exact(decay)
    log_decay = -8.0 * rate * sp
    factor = jnp.exp(log_decay)
    scale = jnp.sqrt(minus_expm1(2.0 * log_decay))
    return rate, inlet, sp, log_decay, factor, scale


def opening_rows(docs, init):
    total = docs.opening[0] * init[0:1]
    for e in range(1, len(docs.opening)):
        total = total + docs.opening[e] * init[e : e + 1]
    return total


def pack_gain(row):
    tiles = [row[:, i * 128 : (i + 1) * 128] for i in range(row.shape[1] // 128)]
    return jnp.concatenate([stack_rows(tiles[i : i + 8]) for i in range(0, len(tiles), 8)], axis=1)


def norm_back(values, gain, grad):
    r = lax.rsqrt(jnp.mean(values * values, axis=-1, keepdims=True) + EPS)
    u = grad * gain
    to_values = r * u - values * (r * r * r) * jnp.mean(u * values, axis=-1, keepdims=True)
    to_gain = jnp.sum(grad * values * r, axis=0, keepdims=True)
    return to_values, to_gain


def unit(size):
    row = lax.broadcasted_iota(jnp.int32, (size, size), 0)
    column = lax.broadcasted_iota(jnp.int32, (size, size), 1)
    return jnp.where(row == column, 1.0, 0.0).astype(jnp.bfloat16)


RIM = 16


def block_kernel(sizes, names, *refs):
    n_seq, n_ch, rows, d, slots, bw, width, sl = sizes
    r = types.SimpleNamespace(**dict(zip(names, refs)))
    bf, f32 = jnp.bfloat16, jnp.float32
    net = Net(n_seq, n_ch, rows, r.send_sems, r.recv_sems, r.local_sems)
    s, c, x, y, z, core, n_z = net.s, net.c, net.x, net.y, net.z, net.core, net.n_z
    count, wide, tokens = rows * n_ch, slots * bw, rows * n_ch * n_seq
    n_taps = r.taps_v.shape[1]
    mine = net.block(z, x, y, core)
    seq_peers = [(net.s_to[k], c) for k in range(1, n_seq)]
    rim_peers = [(net.s_to[k], (c + i) % n_ch) for k in (1, n_seq - 1) for i in range(1, n_ch)]
    peers = seq_peers + rim_peers + [net.sibling, net.across]
    net.greet(peers)
    loads = {}
    cuts = dict(gelu_w=4, recur_w=4, out_w=4)

    def load_halves(name, dst):
        src, size = getattr(r, name), dst.shape[2]
        loads[name] = [net.local(src.at[:, pl.ds(i * size, size)], dst.at[i]) for i in range(2)]

    def load(name, n):
        src, dst = getattr(r, name), getattr(r, name + "_v")
        if n == 1:
            loads[name] = [net.local(src, dst)]
            return
        size = src.shape[0] // n
        loads[name] = [
            net.local(src.at[pl.ds(i * size, size)], dst.at[pl.ds(i * size, size)])
            for i in range(n)
        ]

    def loaded(name):
        for copy in loads.pop(name):
            copy.wait()

    load("stream", 1)
    load("mix_gain", 1)
    load_halves("gate_w", r.give)
    load("cot", 1)
    load_halves("up_w", r.take)
    for name in ("gelu_w", "recur_w", "taps", "bias", "rate_w", "rate_b",
                 "inlet_w", "inlet_b", "decay", "init", "out_w", "ffn_gain"):
        load(name, cuts.get(name, 1))

    own_cols = pl.ds(pl.multiple_of(s * width, width), width)
    own_count = pl.ds(pl.multiple_of(s * count, count), count)
    own_slice = pl.ds(pl.multiple_of(s * sl, sl), sl)
    local = []

    loaded("stream")
    loaded("mix_gain")
    values = r.stream_v[...].astype(f32)
    scale = lax.rsqrt(jnp.mean(values * values, axis=-1, keepdims=True) + EPS)
    mix_rows = pl.ds(pl.multiple_of(RIM + c * rows, 16), rows)
    r.mix[mix_rows, :] = (values * scale * r.mix_gain_v[...][None, :]).astype(bf)

    loaded("cot")
    r.cfull[pl.ds(mine, rows), :] = r.cot_v[...]

    def turn(a, src):
        half = src.shape[2]
        for i in range(2 * half // 256):
            at = i * 256 % half
            r.turned[a, i * 256 : (i + 1) * 256, :] = contract_first(
                src[i * 256 // half, :, at : at + 256], unit(src.shape[1])
            ).astype(bf)

    loaded("gate_w")
    turn(0, r.give)
    loaded("up_w")
    turn(1, r.take)
    net.meet(peers)

    def mix_of(cc):
        return r.mix.at[pl.ds(pl.multiple_of(RIM + cc * rows, 16), rows)]

    last, first = r.mix.at[pl.ds(count, RIM)], r.mix.at[pl.ds(0, RIM)]
    net.ch_gather_start(mix_of, "mix")
    for i in range(n_ch):
        net.send(last, first, (net.s_to[1], i), net.sem("rim"), (c == n_ch - 1) & (s < n_seq - 1))

    @pl.when(s == 0)
    def _():
        r.mix[pl.ds(0, RIM), :] = jnp.zeros((RIM, d), bf)

    cots = Spread(net, r.cfull, "cot")
    lows = Spread(net, r.full, "low")
    cots.start()

    pair_width = 2 * width

    def pair_cols(to):
        return pl.ds(pl.multiple_of(to * pair_width, pair_width), pair_width)

    def left_start(a, src):
        r.left[a, z, c] = src[:, pair_cols(z)]
        for at in range(1, n_z):
            to = net.z_of(net.slot(at))
            net.send(src.at[:, pair_cols(to)], r.left.at[a, z, c], net.dev(to, x, y, core), net.sem(("left", a)))

    def left_pass(a):
        net.recv(r.left.at[a, pl.ds(0, n_z - 1), c], net.sem(("left", a)))
        net.ch_gather_start(lambda cc: r.left.at[a, :, cc], ("leftch", a))

    def left_done(a):
        net.ch_gather_finish(lambda cc: r.left.at[a, :, cc], ("leftch", a))

    left_start(0, r.mix.at[mix_rows])

    others = net.nearest()

    def weight_start(a, which=None):
        src = r.turned.at[a] if a < 2 else r.down
        which = others if which is None else which
        for to in which:
            net.send(
                src.at[pl.ds(pl.multiple_of(to * sl, sl), sl)], r.wt.at[a, :, own_cols], (to, c), net.sem(("w", a)),
            )
        if which[-1] is others[-1]:
            local.append(net.local(src.at[own_slice], r.wt.at[a, :, own_cols]))

    def weight_done(a):
        net.recv(r.wt.at[a, :, pl.ds(0, (n_seq - 1) * width)], net.sem(("w", a)))
        local.pop(0).wait()

    weight_start(0, others[:2])
    for name in [name for name in loads if name != "out_w"]:
        loaded(name)

    net.ch_gather_finish(mix_of, "mix")
    cots.arrive(net.slot(1))
    for i in range(n_ch):
        @pl.when((s > 0) & (c == i))
        def _(i=i):
            net.recv(first, net.sem("rim"))

    docs = Docs(r.lengths, s * count, count)
    keep = docs.keep
    ends_a, ends_b = [], []
    for b in range(slots):
        cols = pl.ds(b * bw, bw)
        rowsof = r.mix[...]
        r.gelu[:, cols] = jnp.dot(rowsof[RIM:], r.gelu_w_v[:, cols], preferred_element_type=f32)
        recur = jnp.dot(rowsof, r.recur_w_v[:, cols], preferred_element_type=f32).astype(bf)
        r.recur[:, cols] = recur
        recur = recur.astype(f32)
        conv_pre = r.bias_v[b : b + 1, :]
        for k in range(n_taps):
            conv_pre = conv_pre + r.taps_v[b, k : k + 1, :] * recur[RIM - k : RIM - k + count] * docs.valid(k)
        conv_low = conv_pre.astype(bf)
        r.conv[:, cols] = conv_low
        rate_pre = jnp.dot(conv_low, r.rate_w_v[b], preferred_element_type=f32) + r.rate_b_v[b : b + 1, :]
        inlet_pre = jnp.dot(conv_low, r.inlet_w_v[b], preferred_element_type=f32) + r.inlet_b_v[b : b + 1, :]
        r.rate_pre[:, cols] = rate_pre
        r.inlet_pre[:, cols] = inlet_pre
        rate, inlet, sp, log_decay, factor, scale = coefficient_parts(rate_pre, inlet_pre, r.decay_v[b : b + 1, :])
        source = scale * inlet * conv_low.astype(f32) + (1.0 - keep) * factor * opening_rows(docs, r.init_v[:, cols])
        total, part = prefix(keep * factor, source, count)
        r.scan_a[:, cols] = total
        r.scan_b[:, cols] = part
        ends_a.append(total[count - 1 : count])
        ends_b.append(part[count - 1 : count])

    def exchange(summary, pieces, tag):
        summary[s] = stack_rows(pieces + [jnp.zeros((8 - 2 * slots, bw), f32)])
        for k in range(1, n_seq):
            net.send(summary.at[s], summary.at[s], (net.s_to[k], c), net.sem(tag))

    def exchanged(summary, tag):
        net.recv(summary.at[pl.ds(0, n_seq - 1)], net.sem(tag))

    exchange(r.summary, ends_a + ends_b, "sum")
    cots.arrive(net.slot(2))
    cots.relay(0)
    weight_start(0, others[2:])
    loaded("out_w")
    exchanged(r.summary, "sum")
    enter = jnp.zeros((slots, bw), f32)
    for q in range(n_seq - 1):
        after = r.summary[q, 0:slots] * enter + r.summary[q, slots : 2 * slots]
        enter = jnp.where(s > q, after, enter)
    finals = []
    for b in range(slots):
        cols = pl.ds(b * bw, bw)
        live = jnp.where(r.counts[0] > b, 1.0, 0.0)
        state = r.scan_b[:, cols] + r.scan_a[:, cols] * enter[b : b + 1]
        r.state[:, cols] = state
        value, _ = smooth_pair(r.gelu[:, cols])
        r.gath[0, z, :, cols] = (value * state * live).astype(bf)
        ends = [jnp.sum(mark * state, axis=0, keepdims=True) * live for mark in docs.closing]
        finals.append(stack_rows(ends + [jnp.zeros((8 - len(ends), bw), f32)]))

    def branch_tile(i, _):
        cols = pl.ds(pl.multiple_of(i * TILE, TILE), TILE)
        value = jnp.dot(r.gath[0, z], r.out_w_v[:, cols], preferred_element_type=f32)
        for cc in range(n_ch):
            r.part[cc % 2, cc // 2, :, cols] = value[cc * rows : (cc + 1) * rows]
        return 0

    lax.fori_loop(0, d // TILE, branch_tile, 0)
    middle = values + net.ch_sum(r.part, r.mid, r.ylow, r.yfar, "branch")
    scale = lax.rsqrt(jnp.mean(middle * middle, axis=-1, keepdims=True) + EPS)
    r.full[pl.ds(mine, rows), :] = (middle * scale * r.ffn_gain_v[...][None, :]).astype(bf)
    r.middle[...] = middle

    def gather_start(a):
        net.chain_start(r.gath.at[a, z], r.gath.at[a, z], ("g", a))

    def gather_arrive(a, at):
        slot = net.slot(at)
        net.chain_arrive(r.gath.at[a, net.z_of(slot)], slot, ("g", a))

    def gather_product(a):
        right = r.gath[a].reshape(n_z * count, wide)
        for which, there in ((0, 1 - x), (1, x)):
            half = r.left[1 if a == 0 else 0, :, :, :, pl.ds(pl.multiple_of(there * width, width), width)]
            half = half.reshape(n_z * count, width)
            value = contract_first(right, half) if a == 0 else contract_first(half, right)
            if which == 0:
                ref = r.give_out if a == 0 else r.give.at[a - 1]
                ref[...] = value.astype(bf)
                net.send(ref, r.take_out if a == 0 else r.take.at[a - 1], net.beside, net.sem(("take", a)))
            elif a == 0:
                r.keep_out_v[...] = value
                local.append(net.local(r.keep_out_v, r.keep_out))
            else:
                r.keep_v[a - 1] = value
                local.append(net.local(r.keep_v.at[a - 1], r.keep.at[a - 1]))

    def gather_done(a):
        ref = r.take_out if a == 0 else r.take.at[a - 1]
        net.recv(ref, net.sem(("take", a)))
        local.append(net.local(ref, r.took_out if a == 0 else r.took.at[a - 1]))

    lows.start()
    weight_start(1, others[:2])
    cots.relay(net.slot(1))
    lows.relay(0)
    lows.arrive(net.slot(1))
    weight_start(1, others[2:4])
    cots.relay(net.slot(2))
    lows.arrive(net.slot(2))
    cots.arrive(net.slot(3))
    weight_start(1, others[4:])
    lows.relay_far(0)
    lows.relay(net.slot(1))
    lows.relay(net.slot(2))
    lows.arrive(net.slot(3))
    weight_start(2)
    gather_start(0)
    group = n_ch * 2 * rows

    def chunk(at):
        return pl.ds(pl.multiple_of(net.z_of(net.slot(at)) * group, group), group)

    weight_done(0)
    weight_done(1)

    def forward(at):
        lows.done(net.slot(at))
        here = chunk(at)
        gate = contract_last(r.full[here, :], r.wt[0])
        up = contract_last(r.full[here, :], r.wt[1])
        value, slope = smooth_pair(gate)
        r.value[here, :] = value
        r.slope[here, :] = up * slope
        r.hid[here, :] = (value * up).astype(bf)

    lows.relay_far(net.slot(1))
    forward(0)
    lows.relay_far(net.slot(2))
    lows.relay(net.slot(3))
    forward(1)
    cots.relay(net.slot(3))
    forward(2)
    lows.relay_far(net.slot(3))
    for at in range(n_z):
        cots.relay_far(net.slot(at))
    forward(3)
    for at in range(n_z):
        cots.done(net.slot(at))

    def weight_grad(a, left, right):
        def tile(i, _):
            cols = pl.ds(pl.multiple_of(i * TILE, TILE), TILE)
            r.dwl[a, :, cols] = contract_first(left[...], right[:, cols]).astype(bf)
            return 0

        lax.fori_loop(0, d // TILE, tile, 0)

    def weight_grad_send(a, which=None):
        which = others if which is None else which
        for to in which:
            cols = pl.ds(pl.multiple_of(to * width, width), width)
            net.send(r.dwl.at[a, :, cols], r.dw.at[a, own_slice], (to, c), net.sem(("dw", a)))
        if which[-1] is others[-1]:
            local.append(net.local(r.dwl.at[a, :, own_cols], r.dw.at[a, own_slice]))

    def weight_grad_done(a):
        net.recv(r.dw.at[a, pl.ds(0, (n_seq - 1) * sl)], net.sem(("dw", a)))

    weight_grad(2, r.hid, r.cfull)
    weight_done(2)
    weight_grad_send(2)

    def spread_out(ref, at, value, cols):
        value = value.astype(bf)
        for xx in range(2):
            for yy in range(2):
                for cc in range(2):
                    row = (xx * 4 + yy * 2 + cc) * rows
                    ref[at, cc, yy, xx, :, cols] = value[row : row + rows]

    def backward(at):
        here = chunk(at)
        grad = contract_last(r.cfull[here, :], r.wt[2])
        r.gat[here, :] = (grad * r.slope[here, :]).astype(bf)
        r.upg[here, :] = (grad * r.value[here, :]).astype(bf)

        def tile(i, _):
            cols = pl.ds(pl.multiple_of(i * TILE, TILE), TILE)
            value = jnp.dot(r.gat[here, :], r.wt[0, :, cols], preferred_element_type=f32)
            value = value + jnp.dot(r.upg[here, :], r.wt[1, :, cols], preferred_element_type=f32)
            spread_out(r.npart, at, value, cols)
            return 0

        lax.fori_loop(0, d // TILE, tile, 0)

    def output(at):
        here = chunk(at)

        def tile(i, _):
            cols = pl.ds(pl.multiple_of(i * TILE, TILE), TILE)
            value = jnp.dot(r.hid[here, :], r.wt[2, :, cols], preferred_element_type=f32)
            spread_out(r.opart, at, value, cols)
            return 0

        lax.fori_loop(0, d // TILE, tile, 0)

    norms = CollectEven(net, r.npart, r.nsib, r.nfar, r.nside, r.nalong, "norm")
    outs = Collect(net, r.opart, r.osib, r.ofar, r.oside, r.oalong, "out")
    backward(3)
    norms.first(3)
    backward(2)
    norms.first(2)
    norms.second(3)
    backward(1)
    norms.first(1)
    norms.second(2)
    norms.third(3)
    backward(0)
    norms.first(0)
    norms.second(1)
    norms.third(2)
    norms.fourth(3)
    norms.second(0)
    output(3)
    output(2)
    norms.third(1)
    norms.fourth(2)
    output(1)
    output(0)
    norms.third(0)
    norms.fourth(1)
    for at in (3, 2, 1, 0):
        outs.first(at)
    gather_arrive(0, 1)
    weight_grad(0, r.gat, r.full)
    weight_grad(1, r.upg, r.full)
    own_norm = norms.fourth(0)
    left_pass(0)
    gather_arrive(0, 2)
    nfg = norms.total(own_norm)

    to_middle, ffn_part = norm_back(middle, r.ffn_gain_v[...][None, :], nfg)
    middle_grad = r.cot_v[...].astype(f32) + to_middle
    r.branch[c] = middle_grad.astype(bf)
    net.ch_gather_start(lambda cc: r.branch.at[cc], "bgrad")
    left_start(1, r.branch.at[c])
    weight_grad_send(0, others[:3])
    for at in (3, 2, 1, 0):
        outs.second(at)
    r.early[n_z] = jnp.concatenate(finals + [pack_gain(ffn_part)], axis=1)
    net.send(r.early.at[n_z], r.pair.at[0], net.beside, net.sem("pair", 0, 2))
    net.ch_gather_finish(lambda cc: r.branch.at[cc], "bgrad")

    ahead_docs = Docs(r.lengths, s * count, count + RIM)
    row = lax.broadcasted_iota(jnp.int32, (count, bw), 0)
    heads_a, heads_b = [], []
    for b in range(slots):
        cols = pl.ds(b * bw, bw)
        live = jnp.where(r.counts[0] > b, 1.0, 0.0)
        product_grad = contract_last(r.branch[...].reshape(count, d), r.out_w_v[b * bw : (b + 1) * bw, :])
        value, slope = smooth_pair(r.gelu[:, cols])
        r.gath[1, z, :, cols] = (product_grad * r.state[:, cols] * live * slope).astype(bf)
        rate, inlet, sp, log_decay, factor, scale = coefficient_parts(r.rate_pre[:, cols], r.inlet_pre[:, cols], r.decay_v[b : b + 1, :])
        carry = keep * factor
        following = jnp.where(row < count - 1, pltpu.roll(carry, count - 1, 0), 1.0)
        total, part = suffix(following, product_grad * value * live, count)
        r.scan_a[:, cols] = total
        r.scan_b[:, cols] = part
        heads_a.append(carry[0:1] * total[0:1])
        heads_b.append(carry[0:1] * part[0:1])
    exchange(r.summary_back, heads_a + heads_b, "sumback")

    gather_start(1)
    gather_arrive(0, 3)
    weight_grad_send(0, others[3:4])
    exchanged(r.summary_back, "sumback")

    def pair_sum(a, ref):
        net.recv(r.pair.at[a], net.sem("pair", a, 2))
        ref[z] = ref[n_z] + r.pair[a]
        for k in range(1, n_z):
            to = net.z_of(k)
            net.send(ref.at[z], ref.at[z], net.dev(to, x, y, core), net.sem(("vec", a)))

    pair_sum(0, r.early)
    enter_back = jnp.zeros((slots, bw), f32)
    for q in range(n_seq - 1, 0, -1):
        after = r.summary_back[q, 0:slots] * enter_back + r.summary_back[q, slots : 2 * slots]
        enter_back = jnp.where(s < q, after, enter_back)
    vec = []
    for b in range(slots):
        cols = pl.ds(b * bw, bw)
        adjoint = r.scan_b[:, cols] + r.scan_a[:, cols] * enter_back[b : b + 1]
        previous = jnp.where(row > 0, pltpu.roll(r.state[:, cols], 1, 0), enter[b : b + 1])
        decay = r.decay_v[b : b + 1, :]
        rate, inlet, sp, log_decay, factor, scale = coefficient_parts(r.rate_pre[:, cols], r.inlet_pre[:, cols], decay)
        conv_low = r.conv[:, cols]
        conv = conv_low.astype(f32)
        init_rows = opening_rows(docs, r.init_v[:, cols])
        log_grad = adjoint * (
            factor * (keep * previous + (1.0 - keep) * init_rows) - inlet * conv * jnp.exp(2.0 * log_decay) / scale
        )
        rate_low = (log_grad * (-8.0 * sp) * rate * (1.0 - rate)).astype(bf)
        direct = adjoint * scale
        inlet_low = (direct * conv * inlet * (1.0 - inlet)).astype(bf)
        decay_row = jnp.sum(log_grad * (-8.0 * rate), axis=0, keepdims=True) * sigmoid(decay)
        back = direct * inlet + contract_last(rate_low, r.rate_w_v[b]) + contract_last(inlet_low, r.inlet_w_v[b])
        r.cgrad[0:count, cols] = back.astype(bf)
        for a, low in enumerate((rate_low, inlet_low)):
            part = contract_first(conv_low, low).astype(bf)
            r.gates[a, b] = part.reshape(r.gates.shape[2:])
        vec.append([
            jnp.sum(rate_low.astype(f32), axis=0, keepdims=True),
            jnp.sum(inlet_low.astype(f32), axis=0, keepdims=True),
            decay_row,
        ])
    rim = r.cgrad.at[pl.ds(count, RIM)]
    net.send(r.cgrad.at[pl.ds(0, RIM)], rim, (net.s_to[n_seq - 1], c), net.sem("rimback"), s > 0)

    @pl.when(s == n_seq - 1)
    def _():
        r.cgrad[pl.ds(count, RIM), :] = jnp.zeros((RIM, wide), bf)

    net.send(r.gates.at[:, :, :, 1 - x], r.gates_x, net.beside, net.sem("gatesx"))
    gather_arrive(1, 1)
    weight_grad_send(0, others[4:])

    @pl.when(s < n_seq - 1)
    def _():
        net.recv(rim, net.sem("rimback"))

    vectors = []
    for b in range(slots):
        cols = pl.ds(b * bw, bw)
        grad = r.cgrad[:, cols].astype(f32)
        own = grad[:count]
        recur = r.recur[:, cols].astype(f32)
        total = jnp.zeros((count, bw), f32)
        tap_rows = []
        for k in range(n_taps):
            tap_rows.append(jnp.sum(own * recur[RIM - k : RIM - k + count] * docs.valid(k), axis=0, keepdims=True))
            total = total + r.taps_v[b, k : k + 1, :] * grad[k : k + count] * ahead_docs.valid(k)[k : k + count]
        r.gath[2, z, :, cols] = total.astype(bf)
        vectors.append(stack_rows(tap_rows + [jnp.sum(own, axis=0, keepdims=True)] + vec[b]))
    gather_start(2)
    for at in (3, 2, 1, 0):
        outs.third(at)

    def norm_tile(i, _):
        cols = pl.ds(pl.multiple_of(i * TILE, TILE), TILE)
        value = contract_last(r.gath[1, z], r.gelu_w_v[cols, :]) + contract_last(r.gath[2, z], r.recur_w_v[cols, :])
        for cc in range(n_ch):
            r.part[cc % 2, cc // 2, :, cols] = value[cc * rows : (cc + 1) * rows]
        return 0

    lax.fori_loop(0, d // TILE, norm_tile, 0)
    gather_arrive(1, 2)
    left_pass(1)
    left_done(0)
    norm_grad = net.ch_sum(r.part, r.mid, r.ylow, r.yfar, "norm")
    to_stream, mix_part = norm_back(values, r.mix_gain_v[...][None, :], norm_grad)
    r.sgrad_v[...] = middle_grad + to_stream
    r.late[n_z] = jnp.concatenate(vectors + [pack_gain(mix_part)], axis=1)
    net.send(r.late.at[n_z], r.pair.at[1], net.beside, net.sem("pair", 1, 2))
    net.recv(r.gates_x, net.sem("gatesx"))

    def gate_add(i, _):
        for a in range(2):
            for b in range(slots):
                value = r.gates[a, b, i, x].astype(f32) + r.gates_x[a, b, i].astype(f32)
                r.gates[a, b, i, x] = value.astype(bf)
        return 0

    lax.fori_loop(0, n_z, gate_add, 0)
    gather_arrive(2, 1)
    weight_grad_send(1, others[:3])
    for k in range(1, n_z):
        to = net.z_of(k)
        net.send(r.gates.at[:, :, to, x], r.gates_z.at[k], net.dev(to, x, y, core), net.sem("gatesz"))
    pair_sum(1, r.late)
    left_done(1)
    gather_product(0)
    gather_arrive(1, 3)
    gather_arrive(2, 2)
    for at in (3, 2, 1):
        outs.fourth(at)
    out_sum = outs.fourth(0)
    weight_grad_send(1, others[3:])
    gather_product(1)
    gather_arrive(2, 3)
    gather_product(2)
    for a, ref in enumerate((r.early, r.late)):
        net.recv(ref.at[pl.ds(0, n_z - 1)], net.sem(("vec", a)))
    early, late = r.early[0], r.late[0]
    for q in range(1, n_z):
        early, late = early + r.early[q], late + r.late[q]
    r.shared[c] = jnp.concatenate([early, late[:, wide:]], axis=1)
    net.ch_gather_start(lambda cc: r.shared.at[cc], "shared")
    piece = bw // n_seq
    for b in range(slots):
        part = jnp.zeros((8, piece), f32)
        for q in range(n_seq):
            at = b * bw + q * piece
            part = jnp.where(s == q, late[:, at : at + piece], part)
        r.small_v[b] = part
    net.recv(r.gates_z.at[pl.ds(1, n_z - 1)], net.sem("gatesz"))
    for a in range(2):
        for b in range(slots):
            total = r.gates[a, b, z, x].astype(f32)
            for k in range(1, n_z):
                total = total + r.gates_z[k, a, b].astype(f32)
            r.gate_out_v[a, b] = total
    net.ch_gather_finish(lambda cc: r.shared.at[cc], "shared")
    gains = r.shared[0, :, wide:]
    for cc in range(1, n_ch):
        gains = gains + r.shared[cc, :, wide:]
    for cc in range(n_ch):
        r.finals_v[:, cc * wide : (cc + 1) * wide] = r.shared[cc, 0 : r.finals_v.shape[0], 0:wide]
    half = gains.shape[1] // 2
    for a in range(2):
        for i in range(half // 128):
            r.gains_v[a, i * 8 : (i + 1) * 8, :] = gains[:, a * half + i * 128 : a * half + (i + 1) * 128]
    r.mixed_v[...] = (middle + outs.total(out_sum)).astype(bf)
    for a in (2, 0, 1):
        weight_grad_done(a)
    for a in range(3):
        gather_done(a)
    for name in ("finals", "mixed", "sgrad", "gains", "gate_out", "small"):
        local.append(net.local(getattr(r, name + "_v"), getattr(r, name)))
    for copy in local:
        copy.wait()
    net.drain()


def finish_kernel(names, *refs):
    r = types.SimpleNamespace(**dict(zip(names, refs)))
    f32 = jnp.float32
    used = []

    def sem():
        used.append(0)
        return r.sems.at[len(used) - 1]

    def copy(src, dst):
        start = pltpu.make_async_copy(src, dst, sem())
        start.start()
        return start

    incoming = {}
    for name, index in (("dw", 2), ("dw", 0), ("dw", 1), ("keep", 0), ("took", 0), ("keep", 1), ("took", 1)):
        incoming[name, index] = copy(getattr(r, name).at[index], getattr(r, name + "_v").at[index])
    for name in ("keep_out", "took_out", "gains", "gate_out", "small", "finals", "mixed", "sgrad"):
        incoming[name] = copy(getattr(r, name), getattr(r, name + "_v"))
    leaving = []

    def leave(name):
        leaving.append(copy(getattr(r, name + "_v"), getattr(r, name)))

    incoming["dw", 2].wait()
    r.down_wg_v[...] = r.dw_v[2].astype(f32)
    leave("down_wg")
    for a, name in enumerate(("gate_wg", "up_wg")):
        incoming["dw", a].wait()
        ref = getattr(r, name + "_v")
        for i in range(ref.shape[1] // 256):
            ref[:, i * 256 : (i + 1) * 256] = contract_first(r.dw_v[a, i * 256 : (i + 1) * 256, :], unit(256))
        leave(name)
    for a, name in enumerate(("gelu_wg", "recur_wg")):
        incoming["keep", a].wait()
        incoming["took", a].wait()
        getattr(r, name + "_v")[...] = r.keep_v[a] + r.took_v[a].astype(f32)
        leave(name)
    for name in ("keep_out", "took_out", "gains", "gate_out", "small", "finals", "mixed", "sgrad"):
        incoming[name].wait()
    r.out_wg_v[...] = r.keep_out_v[...] + r.took_out_v[...].astype(f32)
    leave("out_wg")
    leaving += [
        copy(r.finals_v, r.finals_o), copy(r.mixed_v, r.mixed_o), copy(r.sgrad_v, r.sgrad_o),
        copy(r.gains_v.at[0], r.ffn_o), copy(r.gains_v.at[1], r.mix_o), copy(r.gate_out_v.at[0], r.rate_o),
        copy(r.gate_out_v.at[1], r.inlet_o),
    ]
    n_taps = r.taps_o_v.shape[1]
    for b in range(r.small_v.shape[0]):
        for k in range(n_taps):
            r.taps_o_v[b, k : k + 1, :] = r.small_v[b, k : k + 1, :]
        for k, name in enumerate(("bias_o", "rateb_o", "inletb_o", "decay_o")):
            getattr(r, name + "_v")[b : b + 1, :] = r.small_v[b, n_taps + k : n_taps + k + 1, :]
    for name in ("taps_o", "bias_o", "rateb_o", "inletb_o", "decay_o"):
        leave(name)
    for start in leaving:
        start.wait()


def gathered_body(
    stream, cotangent, mix_gain, gelu_weight, recur_weight, conv_taps, conv_bias, rate_weight, rate_bias, inlet_weight,
    inlet_bias, decay_param, init_states, out_weight, ffn_gain, gate_weight, up_weight, down_weight, doc_lengths, block_counts,
):
    n_seq, n_ch = lax.axis_size(SEQ), lax.axis_size(CH)
    rows, d = stream.shape
    slots, bw = conv_bias.shape
    width, hidden = gate_weight.shape
    sl = hidden // n_seq
    n_z = n_seq // 2
    count, wide, tokens = rows * n_ch, slots * bw, rows * n_ch * n_seq
    piece = bw // n_seq
    n_taps, n_docs = conv_taps.shape[0], doc_lengths.shape[0]
    bf, f32 = jnp.bfloat16, jnp.float32
    vmem = pl.BlockSpec(memory_space=pltpu.VMEM)
    smem = pl.BlockSpec(memory_space=pltpu.SMEM)
    anywhere = pl.BlockSpec(memory_space=pl.ANY)
    inputs = dict(
        stream=stream, cot=cotangent, mix_gain=mix_gain, gelu_w=gelu_weight, recur_w=recur_weight, taps=conv_taps.transpose(1, 0, 2),
        bias=conv_bias, rate_w=rate_weight, rate_b=rate_bias, inlet_w=inlet_weight, inlet_b=inlet_bias, decay=decay_param,
        init=init_states, out_w=out_weight, ffn_gain=ffn_gain, gate_w=gate_weight, up_w=up_weight, down=down_weight,
        lengths=doc_lengths, counts=block_counts,
    )
    places = dict(lengths=smem, counts=smem)
    staged = [name for name in inputs if name not in ("lengths", "counts", "gate_w", "up_w", "down")]
    outputs = dict(
        keep=((2, width, wide), f32), keep_out=((wide, width), f32), took=((2, width, wide), bf), took_out=((wide, width), bf),
        dw=((3, hidden, width), bf),
        finals=((n_docs, wide * n_ch), f32), mixed=((rows, d), bf), sgrad=((rows, d), f32), gains=((2, d // 128, 128), f32),
        gate_out=((2, slots, piece, bw), f32), small=((slots, 8, piece), f32),
    )
    packed = wide + d // 8
    scratch = dict(
        mix=((RIM + count, d), bf), full=((tokens, d), bf), cfull=((tokens, d), bf), turned=((2, hidden, width), bf),
        wt=((3, sl, d), bf), dwl=((3, sl, d), bf), value=((tokens, sl), f32), slope=((tokens, sl), f32),
        hid=((tokens, sl), bf), gat=((tokens, sl), bf), upg=((tokens, sl), bf),
        gelu=((count, wide), f32), recur=((RIM + count, wide), bf), conv=((count, wide), bf), rate_pre=((count, wide), f32),
        inlet_pre=((count, wide), f32), scan_a=((count, wide), f32), scan_b=((count, wide), f32), state=((count, wide), f32),
        gath=((3, n_z, count, wide), bf), left=((2, n_z, n_ch, rows, 2 * width), bf), give=((2, width, wide), bf),
        give_out=((wide, width), bf), take=((2, width, wide), bf), take_out=((wide, width), bf), cgrad=((count + RIM, wide), bf), branch=((n_ch, rows, d), bf),
        summary=((n_seq, 8, bw), f32), summary_back=((n_seq, 8, bw), f32),
        part=((2, 2, rows, d), f32), mid=((2, rows, d), f32), ylow=((rows, d), bf), yfar=((rows, d), bf), middle=((rows, d), f32),
        npart=((n_z, 2, 2, 2, rows, d), bf), nsib=((n_z, 2, 2, rows, d), bf), nfar=((n_z, 2, rows // 2, d), bf),
        nside=((n_z, 2, rows, d), bf), nalong=((n_z, rows, d), bf),
        opart=((n_z, 2, 2, 2, rows, d), bf), osib=((n_z, 2, 2, rows, d), bf), ofar=((n_z, 2, rows, d), bf),
        oside=((n_z, rows, d), bf), oalong=((n_z, rows, d), bf),
        gates=((2, slots, n_z, 2, piece, bw), bf), gates_x=((2, slots, n_z, piece, bw), bf), gates_z=((n_z, 2, slots, piece, bw), bf),
        early=((n_z + 1, 8, packed), f32), late=((n_z + 1, 8, packed), f32), pair=((2, 8, packed), f32),
        shared=((n_ch, 8, packed + d // 8), f32),
    )
    scratch.update({name + "_v": (inputs[name].shape, inputs[name].dtype) for name in staged})
    scratch.update({name + "_v": what for name, what in outputs.items() if name not in ("took", "took_out", "dw")})
    dma = pltpu.SemaphoreType.DMA
    results = pl.pallas_call(
        functools.partial(
            block_kernel, (n_seq, n_ch, rows, d, slots, bw, width, sl),
            list(inputs) + list(outputs) + list(scratch) + ["send_sems", "recv_sems", "local_sems"],
        ),
        out_shape=[jax.ShapeDtypeStruct(*what) for what in outputs.values()],
        in_specs=[places.get(name, anywhere) for name in inputs],
        out_specs=[anywhere] * len(outputs),
        scratch_shapes=[pltpu.VMEM(*what) for what in scratch.values()] + [dma((SEND_SEMS,)), dma((RECV_SEMS,)), dma((LOCAL_SEMS,))],
        compiler_params=pltpu.CompilerParams(collective_id=1, has_side_effects=True, vmem_limit_bytes=VMEM_BYTES),
    )(*inputs.values())
    vector = ((slots, piece), f32)
    ends = dict(
        finals_o=((n_docs, wide * n_ch), f32), mixed_o=((rows, d), bf), sgrad_o=((rows, d), f32), mix_o=((d // 128, 128), f32),
        gelu_wg=((width, wide), f32), recur_wg=((width, wide), f32), taps_o=((slots, n_taps, piece), f32), bias_o=vector,
        rate_o=((slots, piece, bw), f32), rateb_o=vector, inlet_o=((slots, piece, bw), f32), inletb_o=vector, decay_o=vector,
        out_wg=((wide, width), f32), ffn_o=((d // 128, 128), f32), gate_wg=((width, hidden), f32), up_wg=((width, hidden), f32),
        down_wg=((hidden, width), f32),
    )
    direct = ("finals_o", "mixed_o", "sgrad_o", "ffn_o", "mix_o", "rate_o", "inlet_o")
    kept = {name + "_v": outputs[name] for name in outputs}
    kept.update({name + "_v": what for name, what in ends.items() if name not in direct})
    last = pl.pallas_call(
        functools.partial(finish_kernel, list(outputs) + list(ends) + list(kept) + ["sems"]),
        out_shape=[jax.ShapeDtypeStruct(*what) for what in ends.values()],
        in_specs=[anywhere] * len(outputs),
        out_specs=[anywhere] * len(ends),
        scratch_shapes=[pltpu.VMEM(*what) for what in kept.values()] + [pltpu.SemaphoreType.DMA((40,))],
        compiler_params=pltpu.CompilerParams(vmem_limit_bytes=VMEM_BYTES),
    )(*results)
    named = dict(zip(ends, last))
    named["taps_o"] = named["taps_o"].transpose(1, 0, 2)
    named["mix_o"], named["ffn_o"] = named["mix_o"].reshape(d), named["ffn_o"].reshape(d)
    return tuple(named.values())


def solution(mesh):
    in_specs = (
        P((SEQ, CH), None),
        P((SEQ, CH), None),
        P(),
        P(None, CH),
        P(None, CH),
        P(None, CH, None),
        P(CH, None),
        P(CH, None, None),
        P(CH, None),
        P(CH, None, None),
        P(CH, None),
        P(CH, None),
        P(None, CH),
        P(CH, None),
        P(),
        P(SEQ, CH),
        P(SEQ, CH),
        P(CH, SEQ),
        P(),
        P(CH),
    )
    out_specs = (
        P(),
        P((SEQ, CH), None),
        P((SEQ, CH), None),
        P(),
        P(SEQ, CH),
        P(SEQ, CH),
        P(None, CH, SEQ),
        P(CH, SEQ),
        P(CH, SEQ, None),
        P(CH, SEQ),
        P(CH, SEQ, None),
        P(CH, SEQ),
        P(CH, SEQ),
        P(CH, SEQ),
        P(),
        P(SEQ, CH),
        P(SEQ, CH),
        P(CH, SEQ),
    )
    return jax.shard_map(gathered_body if mesh.shape[SEQ] == 8 else body, mesh=mesh, in_specs=in_specs, out_specs=out_specs, check_vma=False)
```

```python
import functools
import math
import types

import jax
import jax.numpy as jnp
from jax import lax
from jax.experimental import pallas as pl
from jax.experimental.pallas import tpu as pltpu
from jax.sharding import PartitionSpec as P

EPS = 1e-06
HIGH = lax.Precision.HIGHEST
MESH = pl.DeviceIdType.MESH
SEQ = "seq"
CH = "ch"
K1 = 0.7978845608028654
K2 = 0.044715
VMEM_BYTES = 63 * 2**20
TILE = 1024
SEND_SEMS = 96
RECV_SEMS = 140
LOCAL_SEMS = 46


def passed_along(shard, axis, by):
    length = lax.axis_size(axis)
    pairs = [(i, i + by) for i in range(length) if 0 <= i + by < length]
    return lax.ppermute(shard, axis, pairs)


def entering_2(shard, axis, combine, identity, reverse):
    length, here = (lax.axis_size(axis), lax.axis_index(axis))
    everything = jax.tree.map(lambda part: lax.all_gather(part, axis), shard)
    start = jax.tree.map(
        lambda part, zero: jnp.broadcast_to(jnp.asarray(zero, part.dtype), part.shape),
        shard,
        identity,
    )

    def turn(k, before):
        at = length - 1 - k if reverse else k
        reached = at > here if reverse else at < here
        new = combine(before, jax.tree.map(lambda part: part[at], everything))
        return jax.tree.map(lambda a, b: jnp.where(reached, a, b), new, before)

    return lax.fori_loop(0, length, turn, start)


def normalize(values, gain):
    return values * lax.rsqrt(jnp.mean(values * values, axis=-1, keepdims=True) + EPS) * gain


def smooth(values):
    return jax.nn.gelu(values, approximate=True)


def affine(earlier, later):
    return (earlier[0] * later[0], later[0] * earlier[1] + later[1])


def doc_view(lengths, first, count):
    ends = jnp.cumsum(lengths)
    starts = ends - lengths
    position = first + jnp.arange(count, dtype=jnp.int32)
    owner = (position[:, None] >= starts[None, :]) & (position[:, None] < ends[None, :])
    start_of = jnp.sum(jnp.where(owner, starts[None, :], 0), axis=1)
    offset = position - start_of
    opening = (owner & (offset[:, None] == 0)).astype(jnp.float32)
    closing = (owner & (position[:, None] == ends[None, :] - 1)).astype(jnp.float32)
    return (offset, opening, closing)


def coefficients(rate_pre, inlet_pre, conv_value, decay, init_rows, keep):
    rate = jax.nn.sigmoid(rate_pre)
    inlet = jax.nn.sigmoid(inlet_pre)
    log_decay = -8.0 * rate * jax.nn.softplus(decay)
    factor = jnp.exp(log_decay)
    scale = jnp.sqrt(-jnp.expm1(2.0 * log_decay))
    carry_factor = keep * factor
    source = scale * inlet * conv_value + (1.0 - keep) * factor * init_rows
    return (carry_factor, source)


def spread(values):
    return lax.all_gather(values, CH, axis=0, tiled=True)


def collect(terms):
    return lax.psum_scatter(terms, CH, scatter_dimension=0, tiled=True)


def contract_last(left, right):
    return lax.dot_general(
        left, right, (((1,), (1,)), ((), ())), preferred_element_type=jnp.float32
    )


def contract_first(left, right):
    return lax.dot_general(
        left, right, (((0,), (0,)), ((), ())), preferred_element_type=jnp.float32
    )


def body(
    stream,
    cotangent,
    mix_gain,
    gelu_weight,
    recur_weight,
    conv_taps,
    conv_bias,
    rate_weight,
    rate_bias,
    inlet_weight,
    inlet_bias,
    decay_param,
    init_states,
    out_weight,
    ffn_gain,
    gate_weight,
    up_weight,
    down_weight,
    doc_lengths,
    block_counts,
):
    slot_count = rate_weight.shape[0]
    block_width = rate_weight.shape[1]
    local_width = slot_count * block_width
    taps = conv_taps.shape[0]
    token_count = stream.shape[0] * lax.axis_size(CH)
    hidden_width = gate_weight.shape[1]
    base = lax.axis_index(SEQ) * token_count
    offset_all, opening, closing = doc_view(doc_lengths, base, token_count + taps - 1)
    offset = offset_all[:token_count]
    opening = opening[:token_count]
    closing = closing[:token_count]
    keep = (offset > 0).astype(jnp.float32)[:, None]
    slot_live = (jnp.arange(slot_count, dtype=jnp.int32) < block_counts[0]).astype(jnp.float32)
    live = jnp.repeat(slot_live, block_width)[None, :]
    taps_flat = conv_taps.reshape(taps, local_width)
    decay_flat = decay_param.reshape(1, local_width)
    stream_float = stream.astype(jnp.float32)
    mix_low = normalize(stream_float, mix_gain).astype(jnp.bfloat16)
    mix_full = spread(mix_low)
    gelu_pre = jnp.dot(mix_full, gelu_weight, preferred_element_type=jnp.float32)
    recur_low = jnp.dot(mix_full, recur_weight, preferred_element_type=jnp.float32).astype(
        jnp.bfloat16
    )
    rim = passed_along(recur_low[token_count - taps + 1 :], SEQ, 1)
    extended = jnp.concatenate([rim, recur_low], axis=0).astype(jnp.float32)
    conv_pre = conv_bias.reshape(1, local_width)
    for tap_index in range(taps):
        valid = (offset >= tap_index).astype(jnp.float32)[:, None]
        lead = taps - 1 - tap_index
        conv_pre = (
            conv_pre + taps_flat[tap_index][None, :] * extended[lead : lead + token_count] * valid
        )
    conv_low = conv_pre.astype(jnp.bfloat16)
    conv_value = conv_low.astype(jnp.float32)
    grouped = conv_low.reshape(token_count, slot_count, block_width)
    rate_pre = (
        jnp.einsum("rsi,sio->rso", grouped, rate_weight, preferred_element_type=jnp.float32)
        + rate_bias[None]
    ).reshape(token_count, local_width)
    inlet_pre = (
        jnp.einsum("rsi,sio->rso", grouped, inlet_weight, preferred_element_type=jnp.float32)
        + inlet_bias[None]
    ).reshape(token_count, local_width)
    init_rows = jnp.dot(opening, init_states, precision=HIGH)
    carry_factor, source = coefficients(
        rate_pre, inlet_pre, conv_value, decay_flat, init_rows, keep
    )
    cumulative, local_state = lax.associative_scan(affine, (carry_factor, source), axis=0)
    summary = (cumulative[-1], local_state[-1])
    entering = entering_2(
        summary, SEQ, affine, (jnp.ones_like(summary[0]), jnp.zeros_like(summary[1])), False
    )
    state_in = entering[1]
    state = local_state + cumulative * state_in[None, :]
    gelu_value = smooth(gelu_pre)
    product_low = (gelu_value * state * live).astype(jnp.bfloat16)
    branch = collect(jnp.dot(product_low, out_weight, preferred_element_type=jnp.float32))
    middle = stream_float + branch
    ffn_low = normalize(middle, ffn_gain).astype(jnp.bfloat16)
    ffn_full = spread(ffn_low)
    stacked = jnp.concatenate([gate_weight, up_weight], axis=1)
    columns = ffn_full
    gate_up = jnp.dot(
        columns,
        lax.all_gather(stacked, SEQ, axis=0, tiled=True),
        preferred_element_type=jnp.float32,
    )
    gate = gate_up[:, :hidden_width]
    upward = gate_up[:, hidden_width:]
    hidden = (smooth(gate) * upward).astype(jnp.bfloat16)
    ffn_terms = jnp.dot(
        hidden,
        lax.all_gather(down_weight, SEQ, axis=1, tiled=True),
        preferred_element_type=jnp.float32,
    )
    mixed_out = (middle + collect(ffn_terms)).astype(jnp.bfloat16)
    out_grad_full = spread(cotangent)
    columns = out_grad_full
    hidden_grad = contract_last(columns, lax.all_gather(down_weight, SEQ, axis=1, tiled=True))
    down_weight_grad = contract_first(hidden, out_grad_full)
    unused, pair_pull = jax.vjp(lambda left, right: smooth(left) * right, gate, upward)
    gate_grad, up_grad = pair_pull(hidden_grad)
    pair_low = jnp.concatenate([gate_grad, up_grad], axis=1).astype(jnp.bfloat16)
    pair_weight_grad = contract_first(ffn_full, pair_low)
    norm_ffn_part = contract_last(pair_low, lax.all_gather(stacked, SEQ, axis=0, tiled=True))
    norm_ffn_grad = collect(norm_ffn_part)
    unused, ffn_norm_pull = jax.vjp(normalize, middle, ffn_gain)
    middle_norm_grad, ffn_gain_part = ffn_norm_pull(norm_ffn_grad)
    middle_grad = cotangent.astype(jnp.float32) + middle_norm_grad
    branch_full = spread(middle_grad.astype(jnp.bfloat16))
    out_weight_grad = contract_first(product_low, branch_full)
    product_grad = contract_last(branch_full, out_weight)
    state_grad = product_grad * gelu_value * live
    unused, gelu_pull = jax.vjp(smooth, gelu_pre)
    gelu_low = gelu_pull(product_grad * state * live)[0].astype(jnp.bfloat16)
    following = jnp.concatenate([carry_factor[1:], jnp.ones_like(carry_factor[:1])], axis=0)
    cum_back, adjoint_local = lax.associative_scan(
        affine, (jnp.flip(following, 0), jnp.flip(state_grad, 0)), axis=0
    )
    cum_back = jnp.flip(cum_back, 0)
    adjoint_local = jnp.flip(adjoint_local, 0)
    summary_back = (carry_factor[0] * cum_back[0], carry_factor[0] * adjoint_local[0])
    arriving = entering_2(
        summary_back,
        SEQ,
        affine,
        (jnp.ones_like(summary_back[0]), jnp.zeros_like(summary_back[1])),
        True,
    )
    adjoint_in = arriving[1]
    adjoint = adjoint_local + cum_back * adjoint_in[None, :]
    previous_state = jnp.concatenate([state_in[None, :], state[:-1]], axis=0)

    def local_coefficients(rate_value, inlet_value, conv_part, decay_value):
        return coefficients(rate_value, inlet_value, conv_part, decay_value, init_rows, keep)

    unused, coefficient_pull = jax.vjp(
        local_coefficients, rate_pre, inlet_pre, conv_value, decay_flat
    )
    rate_grad, inlet_grad, conv_direct, decay_part = coefficient_pull(
        (adjoint * previous_state, adjoint)
    )
    rate_low = rate_grad.astype(jnp.bfloat16).reshape(token_count, slot_count, block_width)
    inlet_low = inlet_grad.astype(jnp.bfloat16).reshape(token_count, slot_count, block_width)
    rate_weight_grad = jnp.einsum(
        "rsi,rso->sio", grouped, rate_low, preferred_element_type=jnp.float32
    )
    inlet_weight_grad = jnp.einsum(
        "rsi,rso->sio", grouped, inlet_low, preferred_element_type=jnp.float32
    )
    rate_bias_grad = jnp.sum(rate_low.astype(jnp.float32), axis=0)
    inlet_bias_grad = jnp.sum(inlet_low.astype(jnp.float32), axis=0)
    conv_back = jnp.einsum(
        "rso,sio->rsi", rate_low, rate_weight, preferred_element_type=jnp.float32
    )
    conv_back = conv_back + jnp.einsum(
        "rso,sio->rsi", inlet_low, inlet_weight, preferred_element_type=jnp.float32
    )
    conv_low_grad = (conv_direct + conv_back.reshape(token_count, local_width)).astype(jnp.bfloat16)
    rim_back = passed_along(conv_low_grad[: taps - 1], SEQ, -1)
    ahead = jnp.concatenate([conv_low_grad, rim_back], axis=0).astype(jnp.float32)
    own_grad = ahead[:token_count]
    recur_grad = jnp.zeros((token_count, local_width), jnp.float32)
    tap_grads = []
    for tap_index in range(taps):
        lead = taps - 1 - tap_index
        valid_here = (offset >= tap_index).astype(jnp.float32)[:, None]
        tap_grads.append(
            jnp.sum(own_grad * extended[lead : lead + token_count] * valid_here, axis=0)
        )
        valid_ahead = (offset_all[tap_index : tap_index + token_count] >= tap_index).astype(
            jnp.float32
        )[:, None]
        recur_grad = (
            recur_grad
            + taps_flat[tap_index][None, :]
            * ahead[tap_index : tap_index + token_count]
            * valid_ahead
        )
    conv_taps_grad = jnp.stack(tap_grads, axis=0).reshape(taps, slot_count, block_width)
    conv_bias_grad = jnp.sum(own_grad, axis=0).reshape(slot_count, block_width)
    recur_low_grad = recur_grad.astype(jnp.bfloat16)
    gelu_weight_grad = contract_first(mix_full, gelu_low)
    recur_weight_grad = contract_first(mix_full, recur_low_grad)
    norm_mix_part = contract_last(gelu_low, gelu_weight) + contract_last(
        recur_low_grad, recur_weight
    )
    norm_mix_grad = collect(norm_mix_part)
    unused, mix_norm_pull = jax.vjp(normalize, stream_float, mix_gain)
    stream_norm_grad, mix_gain_part = mix_norm_pull(norm_mix_grad)
    stream_grad = middle_grad + stream_norm_grad
    finals_local = lax.dot_general(closing, state * live, (((0,), (0,)), ((), ())), precision=HIGH)
    finals_wide = jnp.zeros((finals_local.shape[0], local_width * lax.axis_size(CH)), jnp.float32)
    finals_wide = lax.dynamic_update_slice(
        finals_wide, finals_local, (jnp.int32(0), lax.axis_index(CH) * local_width)
    )
    final_states, mix_gain_grad, ffn_gain_grad = lax.psum(
        (finals_wide, mix_gain_part, ffn_gain_part), (SEQ, CH)
    )
    summed = (
        lax.psum_scatter(gelu_weight_grad, SEQ, scatter_dimension=0, tiled=True),
        lax.psum_scatter(recur_weight_grad, SEQ, scatter_dimension=0, tiled=True),
        lax.psum_scatter(conv_taps_grad, SEQ, scatter_dimension=2, tiled=True),
        lax.psum_scatter(conv_bias_grad, SEQ, scatter_dimension=1, tiled=True),
        lax.psum_scatter(rate_weight_grad, SEQ, scatter_dimension=1, tiled=True),
        lax.psum_scatter(rate_bias_grad, SEQ, scatter_dimension=1, tiled=True),
        lax.psum_scatter(inlet_weight_grad, SEQ, scatter_dimension=1, tiled=True),
        lax.psum_scatter(inlet_bias_grad, SEQ, scatter_dimension=1, tiled=True),
        lax.psum_scatter(
            decay_part.reshape(slot_count, block_width), SEQ, scatter_dimension=1, tiled=True
        ),
        lax.psum_scatter(out_weight_grad, SEQ, scatter_dimension=1, tiled=True),
        lax.psum_scatter(
            pair_weight_grad[:, :hidden_width], SEQ, scatter_dimension=0, tiled=True
        ),
        lax.psum_scatter(
            pair_weight_grad[:, hidden_width:], SEQ, scatter_dimension=0, tiled=True
        ),
        lax.psum_scatter(down_weight_grad, SEQ, scatter_dimension=1, tiled=True),
    )
    return (
        final_states,
        mixed_out,
        stream_grad,
        mix_gain_grad,
        summed[0],
        summed[1],
        summed[2],
        summed[3],
        summed[4],
        summed[5],
        summed[6],
        summed[7],
        summed[8],
        summed[9],
        ffn_gain_grad,
        summed[10],
        summed[11],
        summed[12],
    )


class Net:
    def __init__(self, n_seq, n_ch, rows, send_sems, recv_sems, local_sems):
        self.n_seq, self.n_ch, self.rows = n_seq, n_ch, rows
        self.n_z = n_seq // 2
        self.send_sems, self.recv_sems, self.local_sems = send_sems, recv_sems, local_sems
        self.tags, self.used, self.sent, self.locals = {}, 0, [], 0
        self.s, self.c = lax.axis_index(SEQ), lax.axis_index(CH)
        s, c, n_z = self.s, self.c, self.n_z
        self.z, self.x, self.y, self.core = s // 2, s % 2, c // 2, c % 2
        x, y = self.x, self.y
        self.s_to = [(s + k) % n_seq for k in range(n_seq)]
        self.s_from = [(s + n_seq - k) % n_seq for k in range(n_seq)]
        self.sibling = self.dev(self.z, x, y, 1 - self.core)
        self.across = self.dev(self.z, x, 1 - y, self.core)
        self.beside = self.dev(self.z, 1 - x, y, self.core)
        self.above = self.dev((self.z + 1) % n_z, x, y, self.core)
        self.below = self.dev((self.z + n_z - 1) % n_z, x, y, self.core)

    def nearest(self):
        order = [self.z * 2 + 1 - self.x]
        for at in range(1, self.n_z):
            there = self.z_of(self.slot(at))
            order += [there * 2 + self.x, there * 2 + 1 - self.x]
        return order

    def dev(self, z, x, y, core):
        return (z * 2 + x, y * 2 + core)

    def block(self, z, x, y, core):
        rows = self.rows
        return pl.multiple_of(((z * 2 + x) * self.n_ch + y * 2 + core) * rows, rows)

    def z_of(self, slot):
        return (self.z + self.n_z - slot) % self.n_z

    def slot(self, at):
        if at == 0:
            return 0
        n_z, z = self.n_z, self.z
        low, high = (n_z - 1 - z) // (n_z - 1), z // (n_z - 1)
        inner = (at + 1) // 2 if at % 2 else n_z - at // 2
        return low * (n_z - at) + high * at + (1 - low - high) * inner

    def greet(self, peers):
        barrier = pltpu.get_barrier_semaphore()
        for peer in peers:
            pl.semaphore_signal(barrier, inc=1, device_id=peer, device_id_type=MESH)

    def meet(self, peers):
        pl.semaphore_wait(pltpu.get_barrier_semaphore(), len(peers))

    def sem(self, tag, at=0, size=1):
        if tag not in self.tags:
            self.tags[tag] = self.used
            self.used += size
        return self.recv_sems.at[self.tags[tag] + at]

    def send(self, src, dst, to, sem, when=None):
        size = self.send_sems.shape[0]
        if len(self.sent) >= size:
            self.sent_wait(len(self.sent) - size)
        copy = pltpu.make_async_remote_copy(
            src_ref=src, dst_ref=dst, send_sem=self.send_sems.at[len(self.sent) % size], recv_sem=sem,
            device_id=to, device_id_type=MESH,
        )
        if when is None:
            copy.start()
        else:
            @pl.when(when)
            def _():
                copy.start()
        self.sent.append((copy, when))

    def sent_wait(self, at):
        if self.sent[at] is None:
            return
        copy, when = self.sent[at]
        self.sent[at] = None
        if when is None:
            copy.wait_send()
        else:
            @pl.when(when)
            def _():
                copy.wait_send()

    def recv(self, view, sem):
        pltpu.make_async_remote_copy(
            src_ref=view, dst_ref=view, send_sem=self.send_sems.at[0], recv_sem=sem,
            device_id=(self.s, self.c), device_id_type=MESH,
        ).wait_recv()

    def local(self, src, dst):
        copy = pltpu.make_async_copy(src, dst, self.local_sems.at[self.locals])
        self.locals += 1
        copy.start()
        return copy

    def drain(self):
        for at in range(len(self.sent)):
            self.sent_wait(at)

    def ch_gather_start(self, view_of, tag):
        mine = view_of(self.c)
        self.send(mine, mine, self.across, self.sem((tag, "y")))
        self.send(mine, mine, self.sibling, self.sem((tag, "core")))

    def ch_gather_finish(self, view_of, tag):
        y, core = self.y, self.core
        theirs = view_of((1 - y) * 2 + core)
        self.recv(theirs, self.sem((tag, "y")))
        self.send(theirs, theirs, self.sibling, self.sem((tag, "fwd")))
        self.recv(view_of(y * 2 + 1 - core), self.sem((tag, "core")))
        self.recv(view_of((1 - y) * 2 + 1 - core), self.sem((tag, "fwd")))

    def ch_sum(self, part, mid, low, far, tag):
        y, core = self.y, self.core
        first = len(self.sent)
        self.send(part.at[1 - core], mid, self.sibling, self.sem((tag, "core")))
        self.recv(mid, self.sem((tag, "core")))
        low[...] = (part[core, 1 - y] + mid[1 - y]).astype(jnp.bfloat16)
        self.send(low, far, self.across, self.sem((tag, "y")))
        total = part[core, y] + mid[y]
        self.recv(far, self.sem((tag, "y")))
        self.sent_wait(first)
        self.sent_wait(first + 1)
        return total + far[...].astype(jnp.float32)

    def chain_start(self, mine, target, tag):
        n_z, z = self.n_z, self.z
        self.send(mine, target, self.above, self.sem((tag, "z"), 1, n_z), z < n_z - 1)
        self.send(mine, target, self.below, self.sem((tag, "z"), n_z - 1, n_z), z > 0)

    def chain_arrive(self, view, slot, tag):
        n_z, z = self.n_z, self.z
        self.recv(view, self.sem((tag, "z"), slot, n_z))
        self.send(view, view, self.above, self.sem((tag, "z"), (slot + 1) % n_z, n_z), (z >= slot) & (z < n_z - 1))
        self.send(view, view, self.below, self.sem((tag, "z"), (slot + n_z - 1) % n_z, n_z), (z < slot) & (z > 0))


    def chain_sum(self, k, term, lands, add, tag):
        n_z, z = self.n_z, self.z
        for way, to, goes, comes in ((1, self.above, z + k < n_z, z > 0), (n_z - 1, self.below, z >= k, z < n_z - 1)):
            land, name = lands[way > 1], (tag, way > 1)
            mine = term((z + way * k) % n_z)
            if k < n_z - 1:
                @pl.when(goes & comes)
                def _():
                    self.recv(land.at[k], self.sem(name, k, n_z - 1))
                    add(mine, land.at[k])

            self.send(mine, land.at[k - 1], to, self.sem(name, k - 1, n_z - 1), goes)

    def chain_sum_last(self, lands, add, total, tag):
        n_z, z = self.n_z, self.z
        for side, comes in ((0, z > 0), (1, z < n_z - 1)):
            @pl.when(comes)
            def _(side=side):
                self.recv(lands[side].at[0], self.sem((tag, side > 0), 0, n_z - 1))
                add(total, lands[side].at[0])

    def arrival(self, slot):
        n_z, z = self.n_z, self.z
        low, high = (n_z - 1 - z) // (n_z - 1), z // (n_z - 1)
        far = slot // (n_z // 2 + 1)
        inner = (1 - far) * (2 * slot - 1) + far * 2 * (n_z - slot)
        return (low * (n_z - slot) + high * slot + (1 - low - high) * inner + n_z) % n_z


def add_into(mine, more):
    mine[...] = (mine[...].astype(jnp.float32) + more[...].astype(jnp.float32)).astype(mine.dtype)


class Spread:
    def __init__(self, net, ref, tag):
        self.net, self.ref, self.tag = net, ref, tag

    def view(self, slot, x, y, core):
        net = self.net
        return self.ref.at[pl.ds(net.block(net.z_of(slot), x, y, core), net.rows)]

    def sem(self, what, slot):
        return self.net.sem((self.tag, what), slot, self.net.n_z)

    def start(self):
        net = self.net
        mine = self.view(0, net.x, net.y, net.core)
        net.chain_start(mine, mine, self.tag)
        self.plane(0)

    def plane(self, slot):
        net = self.net
        view = self.view(slot, net.x, net.y, net.core)
        net.send(view, view, net.beside, self.sem("x", slot))
        net.send(view, view, net.across, self.sem("y", slot))
        net.send(view, view, net.sibling, self.sem("s", slot))

    def arrive(self, slot):
        net = self.net
        net.chain_arrive(self.view(slot, net.x, net.y, net.core), slot, self.tag)
        self.plane(slot)

    def relay(self, slot):
        net = self.net
        view = self.view(slot, 1 - net.x, net.y, net.core)
        net.recv(view, self.sem("x", slot))
        net.send(view, view, net.across, self.sem("d", slot))
        net.send(view, view, net.sibling, self.sem("s", slot))

    def relay_far(self, slot):
        net = self.net
        for what, x in (("y", net.x), ("d", 1 - net.x)):
            view = self.view(slot, x, 1 - net.y, net.core)
            net.recv(view, self.sem(what, slot))
            net.send(view, view, net.sibling, self.sem("s", slot))

    def done(self, slot):
        net = self.net
        at = net.block(net.z_of(slot), 0, 0, 0)
        net.recv(self.ref.at[pl.ds(at, 4 * net.rows)], self.sem("s", slot))


class Collect:
    def __init__(self, net, part, sib, far, side, tag):
        self.net, self.part, self.sib, self.far, self.side, self.tag = net, part, sib, far, side, tag

    def sem(self, what, at):
        return self.net.sem((self.tag, what), at, self.net.n_z)

    def first(self, at):
        net = self.net
        net.send(self.part.at[at, 1 - net.core], self.sib.at[at], net.sibling, self.sem("s", at))

    def second(self, at):
        net = self.net
        net.recv(self.sib.at[at], self.sem("s", at))
        core, part, sib = net.core, self.part, self.sib
        for first in (1 - net.y, net.y):
            for x in range(2):
                value = part[at, core, first, x].astype(jnp.float32) + sib[at, first, x].astype(jnp.float32)
                part[at, core, first, x] = value.astype(jnp.bfloat16)
            if first is not net.y:
                net.send(part.at[at, core, first], self.far.at[at], net.across, self.sem("f", at))

    def third(self, at):
        net, part, far = self.net, self.part, self.far
        net.recv(far.at[at], self.sem("f", at))
        there = 1 - net.x
        value = part[at, net.core, net.y, there].astype(jnp.float32) + far[at, there].astype(jnp.float32)
        part[at, net.core, net.y, there] = value.astype(jnp.bfloat16)
        net.send(part.at[at, net.core, net.y, there], self.side.at[at], net.beside, self.sem("p", at))

    def plane_total(self, at):
        net = self.net
        net.recv(self.side.at[at], self.sem("p", at))
        total = self.part[at, net.core, net.y, net.x].astype(jnp.float32)
        return total + self.far[at, net.x].astype(jnp.float32) + self.side[at].astype(jnp.float32)

    def fourth(self, at):
        net, part = self.net, self.part
        total = self.plane_total(at)
        if at == 0:
            return total
        part[at, net.core, net.y, net.x] = total.astype(jnp.bfloat16)
        return None

    def term(self, there):
        net = self.net
        at = net.arrival((net.z + net.n_z - there) % net.n_z)
        return self.part.at[at, net.core, net.y, net.x]


class CollectEven(Collect):
    def second(self, at):
        net = self.net
        net.recv(self.sib.at[at], self.sem("s", at))
        core, part, sib = net.core, self.part, self.sib
        half = net.rows // 2
        for y in (1 - net.y, net.y):
            for x in (1 - net.x, net.x):
                value = part[at, core, y, x].astype(jnp.float32) + sib[at, y, x].astype(jnp.float32)
                part[at, core, y, x] = value.astype(jnp.bfloat16)
                if y is not net.y and x is not net.x:
                    diagonal = part.at[at, core, y, x]
                    net.send(diagonal.at[pl.ds(0, half)], self.far.at[at, 0], net.beside, self.sem("f0", at))
                    net.send(diagonal.at[pl.ds(half, half)], self.far.at[at, 1], net.across, self.sem("f1", at))

    def third(self, at):
        net, part, far = self.net, self.part, self.far
        half = net.rows // 2
        for which, y, x, first, to in (
            (0, 1 - net.y, net.x, 0, net.across), (1, net.y, 1 - net.x, half, net.beside),
        ):
            net.recv(far.at[at, which], self.sem(f"f{which}", at))
            rows = pl.ds(first, half)
            value = part[at, net.core, y, x, rows, :].astype(jnp.float32) + far[at, which].astype(jnp.float32)
            part[at, net.core, y, x, rows, :] = value.astype(jnp.bfloat16)
            net.send(part.at[at, net.core, y, x], self.side.at[at, which], to, self.sem("p", at))

    def plane_total(self, at):
        net = self.net
        net.recv(self.side.at[at], self.sem("p", at))
        total = self.part[at, net.core, net.y, net.x].astype(jnp.float32)
        return total + self.side[at, 0].astype(jnp.float32) + self.side[at, 1].astype(jnp.float32)


def stack_rows(rows):
    return jnp.concatenate(rows, axis=0)


def smooth_pair(v):
    t = jnp.tanh(K1 * (v + K2 * v * v * v))
    value = 0.5 * v * (1.0 + t)
    slope = 0.5 * (1.0 + t) + 0.5 * v * (1.0 - t * t) * K1 * (1.0 + 3.0 * K2 * v * v)
    return value, slope


def sigmoid(v):
    return 1.0 / (1.0 + jnp.exp(-v))


def softplus_exact(d):
    u = jnp.exp(-jnp.abs(d))
    r = u / (2.0 + u)
    q = r * r
    series = 1.0 / 15.0
    for k in (13, 11, 9, 7, 5, 3, 1):
        series = series * q + 1.0 / k
    return jnp.maximum(d, 0.0) + 2.0 * r * series


def minus_expm1(v):
    series = 1.0 / 362880.0
    for k in (40320.0, 5040.0, 720.0, 120.0, 24.0, 6.0, 2.0, 1.0):
        series = series * v + 1.0 / k
    return jnp.where(v > -0.5, -v * series, 1.0 - jnp.exp(v))


class Docs:
    def __init__(self, lengths, first, count, before=0):
        position = first - before + lax.broadcasted_iota(jnp.int32, (count, 1), 0)
        self.opening, self.closing = [], []
        start_of = jnp.zeros((count, 1), jnp.int32)
        start = jnp.int32(0)
        for e in range(lengths.shape[0]):
            end = start + lengths[e]
            owner = (position >= start) & (position < end)
            start_of = jnp.where(owner, start, start_of)
            self.opening.append((position == start).astype(jnp.float32))
            self.closing.append((position == end - 1).astype(jnp.float32))
            start = end
        self.offset = position - start_of
        self.keep = (self.offset > 0).astype(jnp.float32)

    def valid(self, k):
        return (self.offset >= k).astype(jnp.float32)


def prefix(a, b, count):
    row = lax.broadcasted_iota(jnp.int32, a.shape, 0)
    k = 1
    while k < count:
        inside = row >= k
        a_far = jnp.where(inside, pltpu.roll(a, k, 0), 1.0)
        b_far = jnp.where(inside, pltpu.roll(b, k, 0), 0.0)
        b = a * b_far + b
        a = a * a_far
        k *= 2
    return a, b


def suffix(a, b, count):
    row = lax.broadcasted_iota(jnp.int32, a.shape, 0)
    k = 1
    while k < count:
        inside = row < count - k
        a_far = jnp.where(inside, pltpu.roll(a, count - k, 0), 1.0)
        b_far = jnp.where(inside, pltpu.roll(b, count - k, 0), 0.0)
        b = a * b_far + b
        a = a * a_far
        k *= 2
    return a, b


def coefficient_parts(rate_pre, inlet_pre, decay):
    rate = sigmoid(rate_pre)
    inlet = sigmoid(inlet_pre)
    sp = softplus_exact(decay)
    log_decay = -8.0 * rate * sp
    factor = jnp.exp(log_decay)
    scale = jnp.sqrt(minus_expm1(2.0 * log_decay))
    return rate, inlet, sp, log_decay, factor, scale


def opening_rows(docs, init):
    total = docs.opening[0] * init[0:1]
    for e in range(1, len(docs.opening)):
        total = total + docs.opening[e] * init[e : e + 1]
    return total


def pack_gain(row):
    tiles = [row[:, i * 128 : (i + 1) * 128] for i in range(row.shape[1] // 128)]
    return jnp.concatenate([stack_rows(tiles[i : i + 8]) for i in range(0, len(tiles), 8)], axis=1)


def norm_back(values, gain, grad):
    r = lax.rsqrt(jnp.mean(values * values, axis=-1, keepdims=True) + EPS)
    u = grad * gain
    to_values = r * u - values * (r * r * r) * jnp.mean(u * values, axis=-1, keepdims=True)
    to_gain = jnp.sum(grad * values * r, axis=0, keepdims=True)
    return to_values, to_gain


def unit(size):
    row = lax.broadcasted_iota(jnp.int32, (size, size), 0)
    column = lax.broadcasted_iota(jnp.int32, (size, size), 1)
    return jnp.where(row == column, 1.0, 0.0).astype(jnp.bfloat16)


RIM = 16


def block_kernel(sizes, names, *refs):
    n_seq, n_ch, rows, d, slots, bw, width, sl = sizes
    r = types.SimpleNamespace(**dict(zip(names, refs)))
    bf, f32 = jnp.bfloat16, jnp.float32
    net = Net(n_seq, n_ch, rows, r.send_sems, r.recv_sems, r.local_sems)
    s, c, x, y, z, core, n_z = net.s, net.c, net.x, net.y, net.z, net.core, net.n_z
    count, wide, tokens = rows * n_ch, slots * bw, rows * n_ch * n_seq
    n_taps = r.taps_v.shape[1]
    mine = net.block(z, x, y, core)
    seq_peers = [(net.s_to[k], c) for k in range(1, n_seq)]
    rim_peers = [(net.s_to[k], (c + i) % n_ch) for k in (1, n_seq - 1) for i in range(1, n_ch)]
    peers = seq_peers + rim_peers + [net.sibling, net.across]
    net.greet(peers)
    loads = {}
    cuts = dict(gelu_w=4, recur_w=4, out_w=4)

    def load_halves(name, dst):
        src, size = getattr(r, name), dst.shape[2]
        loads[name] = [net.local(src.at[:, pl.ds(i * size, size)], dst.at[i]) for i in range(2)]

    def load(name, n):
        src, dst = getattr(r, name), getattr(r, name + "_v")
        if n == 1:
            loads[name] = [net.local(src, dst)]
            return
        size = src.shape[0] // n
        loads[name] = [
            net.local(src.at[pl.ds(i * size, size)], dst.at[pl.ds(i * size, size)])
            for i in range(n)
        ]

    def loaded(name):
        for copy in loads.pop(name):
            copy.wait()

    load("stream", 1)
    load("mix_gain", 1)
    load_halves("gate_w", r.give)
    load("cot", 1)
    load_halves("up_w", r.take)
    for name in ("gelu_w", "recur_w", "taps", "bias", "rate_w", "rate_b",
                 "inlet_w", "inlet_b", "decay", "init", "out_w", "ffn_gain"):
        load(name, cuts.get(name, 1))

    own_cols = pl.ds(pl.multiple_of(s * width, width), width)
    own_count = pl.ds(pl.multiple_of(s * count, count), count)
    own_slice = pl.ds(pl.multiple_of(s * sl, sl), sl)
    local = []

    loaded("stream")
    loaded("mix_gain")
    values = r.stream_v[...].astype(f32)
    scale = lax.rsqrt(jnp.mean(values * values, axis=-1, keepdims=True) + EPS)
    mix_rows = pl.ds(pl.multiple_of(RIM + c * rows, 16), rows)
    r.mix[mix_rows, :] = (values * scale * r.mix_gain_v[...][None, :]).astype(bf)

    loaded("cot")
    r.cfull[pl.ds(mine, rows), :] = r.cot_v[...]

    def turn(a, src):
        half = src.shape[2]
        for i in range(2 * half // 256):
            at = i * 256 % half
            r.turned[a, i * 256 : (i + 1) * 256, :] = contract_first(
                src[i * 256 // half, :, at : at + 256], unit(src.shape[1])
            ).astype(bf)

    loaded("gate_w")
    turn(0, r.give)
    loaded("up_w")
    turn(1, r.take)
    net.meet(peers)

    def mix_of(cc):
        return r.mix.at[pl.ds(pl.multiple_of(RIM + cc * rows, 16), rows)]

    last, first = r.mix.at[pl.ds(count, RIM)], r.mix.at[pl.ds(0, RIM)]
    net.ch_gather_start(mix_of, "mix")
    for i in range(n_ch):
        net.send(last, first, (net.s_to[1], i), net.sem("rim"), (c == n_ch - 1) & (s < n_seq - 1))

    @pl.when(s == 0)
    def _():
        r.mix[pl.ds(0, RIM), :] = jnp.zeros((RIM, d), bf)

    cots = Spread(net, r.cfull, "cot")
    lows = Spread(net, r.full, "low")
    cots.start()

    pair_width = 2 * width

    def pair_cols(to):
        return pl.ds(pl.multiple_of(to * pair_width, pair_width), pair_width)

    def left_start(a, src):
        r.left[a, z, c] = src[:, pair_cols(z)]
        for at in range(1, n_z):
            to = net.z_of(net.slot(at))
            net.send(src.at[:, pair_cols(to)], r.left.at[a, z, c], net.dev(to, x, y, core), net.sem(("left", a)))

    def left_pass(a):
        net.recv(r.left.at[a, pl.ds(0, n_z - 1), c], net.sem(("left", a)))
        net.ch_gather_start(lambda cc: r.left.at[a, :, cc], ("leftch", a))

    def left_done(a):
        net.ch_gather_finish(lambda cc: r.left.at[a, :, cc], ("leftch", a))

    left_start(0, r.mix.at[mix_rows])

    others = net.nearest()

    def weight_start(a, which=None):
        src = r.turned.at[a] if a < 2 else r.down
        which = others if which is None else which
        for to in which:
            net.send(
                src.at[pl.ds(pl.multiple_of(to * sl, sl), sl)], r.wt.at[a, :, own_cols], (to, c), net.sem(("w", a)),
            )
        if which[-1] is others[-1]:
            local.append(net.local(src.at[own_slice], r.wt.at[a, :, own_cols]))

    def weight_done(a):
        net.recv(r.wt.at[a, :, pl.ds(0, (n_seq - 1) * width)], net.sem(("w", a)))
        local.pop(0).wait()

    weight_start(0, others[:2])
    for name in [name for name in loads if name != "out_w"]:
        loaded(name)

    net.ch_gather_finish(mix_of, "mix")
    cots.arrive(net.slot(1))
    for i in range(n_ch):
        @pl.when((s > 0) & (c == i))
        def _(i=i):
            net.recv(first, net.sem("rim"))

    docs = Docs(r.lengths, s * count, count)
    keep = docs.keep
    ends_a, ends_b = [], []
    for b in range(slots):
        cols = pl.ds(b * bw, bw)
        rowsof = r.mix[...]
        r.gelu[:, cols] = jnp.dot(rowsof[RIM:], r.gelu_w_v[:, cols], preferred_element_type=f32)
        recur = jnp.dot(rowsof, r.recur_w_v[:, cols], preferred_element_type=f32).astype(bf)
        r.recur[:, cols] = recur
        recur = recur.astype(f32)
        conv_pre = r.bias_v[b : b + 1, :]
        for k in range(n_taps):
            conv_pre = conv_pre + r.taps_v[b, k : k + 1, :] * recur[RIM - k : RIM - k + count] * docs.valid(k)
        conv_low = conv_pre.astype(bf)
        r.conv[:, cols] = conv_low
        rate_pre = jnp.dot(conv_low, r.rate_w_v[b], preferred_element_type=f32) + r.rate_b_v[b : b + 1, :]
        inlet_pre = jnp.dot(conv_low, r.inlet_w_v[b], preferred_element_type=f32) + r.inlet_b_v[b : b + 1, :]
        r.rate_pre[:, cols] = rate_pre
        r.inlet_pre[:, cols] = inlet_pre
        rate, inlet, sp, log_decay, factor, scale = coefficient_parts(rate_pre, inlet_pre, r.decay_v[b : b + 1, :])
        source = scale * inlet * conv_low.astype(f32) + (1.0 - keep) * factor * opening_rows(docs, r.init_v[:, cols])
        total, part = prefix(keep * factor, source, count)
        r.scan_a[:, cols] = total
        r.scan_b[:, cols] = part
        ends_a.append(total[count - 1 : count])
        ends_b.append(part[count - 1 : count])

    def exchange(summary, pieces, tag):
        summary[s] = stack_rows(pieces + [jnp.zeros((8 - 2 * slots, bw), f32)])
        for k in range(1, n_seq):
            net.send(summary.at[s], summary.at[s], (net.s_to[k], c), net.sem(tag))

    def exchanged(summary, tag):
        net.recv(summary.at[pl.ds(0, n_seq - 1)], net.sem(tag))

    exchange(r.summary, ends_a + ends_b, "sum")
    weight_start(0, others[2:])
    cots.relay(0)
    cots.arrive(net.slot(2))
    loaded("out_w")
    exchanged(r.summary, "sum")
    enter = jnp.zeros((slots, bw), f32)
    for q in range(n_seq - 1):
        after = r.summary[q, 0:slots] * enter + r.summary[q, slots : 2 * slots]
        enter = jnp.where(s > q, after, enter)
    finals = []
    for b in range(slots):
        cols = pl.ds(b * bw, bw)
        live = jnp.where(r.counts[0] > b, 1.0, 0.0)
        state = r.scan_b[:, cols] + r.scan_a[:, cols] * enter[b : b + 1]
        r.state[:, cols] = state
        value, _ = smooth_pair(r.gelu[:, cols])
        r.gath[0, z, :, cols] = (value * state * live).astype(bf)
        ends = [jnp.sum(mark * state, axis=0, keepdims=True) * live for mark in docs.closing]
        finals.append(stack_rows(ends + [jnp.zeros((8 - len(ends), bw), f32)]))

    def branch_tile(i, _):
        cols = pl.ds(pl.multiple_of(i * TILE, TILE), TILE)
        value = jnp.dot(r.gath[0, z], r.out_w_v[:, cols], preferred_element_type=f32)
        for cc in range(n_ch):
            r.part[cc % 2, cc // 2, :, cols] = value[cc * rows : (cc + 1) * rows]
        return 0

    lax.fori_loop(0, d // TILE, branch_tile, 0)
    middle = r.stream_v[...].astype(f32) + net.ch_sum(r.part, r.mid, r.ylow, r.yfar, "branch")
    scale = lax.rsqrt(jnp.mean(middle * middle, axis=-1, keepdims=True) + EPS)
    r.full[pl.ds(mine, rows), :] = (middle * scale * r.ffn_gain_v[...][None, :]).astype(bf)
    r.middle[...] = middle

    def gather_start(a):
        net.chain_start(r.gath.at[a, z], r.gath.at[a, z], ("g", a))

    def gather_arrive(a, at):
        slot = net.slot(at)
        net.chain_arrive(r.gath.at[a, net.z_of(slot)], slot, ("g", a))

    def gather_product(a):
        right = r.gath[a].reshape(n_z * count, wide)
        for which, there in ((0, 1 - x), (1, x)):
            half = r.left[1 if a == 0 else 0, :, :, :, pl.ds(pl.multiple_of(there * width, width), width)]
            half = half.reshape(n_z * count, width)
            value = contract_first(right, half) if a == 0 else contract_first(half, right)
            if which == 0:
                ref = r.give_out if a == 0 else r.give.at[a - 1]
                ref[...] = value.astype(bf)
                net.send(ref, r.take_out if a == 0 else r.take.at[a - 1], net.beside, net.sem(("take", a)))
            elif a == 0:
                r.keep_out_v[...] = value
                local.append(net.local(r.keep_out_v, r.keep_out))
            else:
                r.keep_v[a - 1] = value
                local.append(net.local(r.keep_v.at[a - 1], r.keep.at[a - 1]))

    def gather_done(a):
        ref = r.take_out if a == 0 else r.take.at[a - 1]
        net.recv(ref, net.sem(("take", a)))
        local.append(net.local(ref, r.took_out if a == 0 else r.took.at[a - 1]))

    lows.start()
    weight_start(1, others[:2])
    cots.relay(net.slot(1))
    lows.relay(0)
    lows.arrive(net.slot(1))
    weight_start(1, others[2:4])
    cots.relay(net.slot(2))
    lows.arrive(net.slot(2))
    cots.arrive(net.slot(3))
    weight_start(1, others[4:])
    lows.relay_far(0)
    lows.relay(net.slot(1))
    lows.relay(net.slot(2))
    lows.arrive(net.slot(3))
    weight_start(2)
    gather_start(0)
    group = n_ch * 2 * rows

    def chunk(at):
        return pl.ds(pl.multiple_of(net.z_of(net.slot(at)) * group, group), group)

    weight_done(0)
    weight_done(1)

    def forward(at):
        lows.done(net.slot(at))
        here = chunk(at)
        gate = contract_last(r.full[here, :], r.wt[0])
        up = contract_last(r.full[here, :], r.wt[1])
        value, slope = smooth_pair(gate)
        r.value[here, :] = value
        r.slope[here, :] = up * slope
        r.hid[here, :] = (value * up).astype(bf)

    lows.relay_far(net.slot(1))
    forward(0)
    lows.relay_far(net.slot(2))
    lows.relay(net.slot(3))
    forward(1)
    cots.relay(net.slot(3))
    forward(2)
    lows.relay_far(net.slot(3))
    for at in range(n_z):
        cots.relay_far(net.slot(at))
    forward(3)
    for at in range(n_z):
        cots.done(net.slot(at))

    def weight_grad(a, left, right):
        def tile(i, _):
            cols = pl.ds(pl.multiple_of(i * TILE, TILE), TILE)
            r.dwl[a, :, cols] = contract_first(left[...], right[:, cols]).astype(bf)
            return 0

        lax.fori_loop(0, d // TILE, tile, 0)

    def weight_grad_send(a, which=None):
        which = others if which is None else which
        for to in which:
            cols = pl.ds(pl.multiple_of(to * width, width), width)
            net.send(r.dwl.at[a, :, cols], r.dw.at[a, own_slice], (to, c), net.sem(("dw", a)))
        if which[-1] is others[-1]:
            local.append(net.local(r.dwl.at[a, :, own_cols], r.dw.at[a, own_slice]))

    def weight_grad_done(a):
        net.recv(r.dw.at[a, pl.ds(0, (n_seq - 1) * sl)], net.sem(("dw", a)))

    weight_grad(2, r.hid, r.cfull)
    weight_done(2)
    weight_grad_send(2)

    def spread_out(ref, at, value, cols):
        value = value.astype(bf)
        for xx in range(2):
            for yy in range(2):
                for cc in range(2):
                    row = (xx * 4 + yy * 2 + cc) * rows
                    ref[at, cc, yy, xx, :, cols] = value[row : row + rows]

    def backward(at):
        here = chunk(at)
        grad = contract_last(r.cfull[here, :], r.wt[2])
        r.gat[here, :] = (grad * r.slope[here, :]).astype(bf)
        r.upg[here, :] = (grad * r.value[here, :]).astype(bf)

        def tile(i, _):
            cols = pl.ds(pl.multiple_of(i * TILE, TILE), TILE)
            value = jnp.dot(r.gat[here, :], r.wt[0, :, cols], preferred_element_type=f32)
            value = value + jnp.dot(r.upg[here, :], r.wt[1, :, cols], preferred_element_type=f32)
            spread_out(r.npart, at, value, cols)
            return 0

        lax.fori_loop(0, d // TILE, tile, 0)

    def output(at):
        here = chunk(at)

        def tile(i, _):
            cols = pl.ds(pl.multiple_of(i * TILE, TILE), TILE)
            value = jnp.dot(r.hid[here, :], r.wt[2, :, cols], preferred_element_type=f32)
            spread_out(r.opart, at, value, cols)
            return 0

        lax.fori_loop(0, d // TILE, tile, 0)

    def norm_step(k):
        net.chain_sum(k, norms.term, (r.oup, r.odown), add_into, 2)

    def out_step(k):
        net.chain_sum(k, outs.term, (r.oup, r.odown), add_into, 0)

    norms = CollectEven(net, r.npart, r.nsib, r.nfar, r.nside, "norm")
    outs = Collect(net, r.opart, r.osib, r.ofar, r.oside, "out")
    backward(3)
    norms.first(3)
    backward(2)
    norms.first(2)
    norms.second(3)
    backward(1)
    norms.first(1)
    norms.second(2)
    norms.third(3)
    backward(0)
    norms.first(0)
    norms.second(1)
    norms.third(2)
    norms.fourth(3)
    norm_step(3)
    norms.second(0)
    output(3)
    output(2)
    norms.third(1)
    norms.fourth(2)
    norm_step(2)
    output(1)
    output(0)
    norms.third(0)
    norms.fourth(1)
    norm_step(1)
    for at in (3, 2, 1, 0):
        outs.first(at)
    gather_arrive(0, 1)
    weight_grad(0, r.gat, r.full)
    weight_grad(1, r.upg, r.full)
    r.sgrad_v[...] = norms.fourth(0)
    left_pass(0)
    gather_arrive(0, 2)
    net.chain_sum_last((r.oup, r.odown), add_into, r.sgrad_v, 2)
    nfg = r.sgrad_v[...]

    to_middle, ffn_part = norm_back(r.middle[...], r.ffn_gain_v[...][None, :], nfg)
    middle_grad = r.cot_v[...].astype(f32) + to_middle
    r.sgrad_v[...] = middle_grad
    r.branch[c] = middle_grad.astype(bf)
    net.ch_gather_start(lambda cc: r.branch.at[cc], "bgrad")
    left_start(1, r.branch.at[c])
    weight_grad_send(0, others[:3])
    for at in (3, 2, 1, 0):
        outs.second(at)
    r.early[n_z] = jnp.concatenate(finals + [pack_gain(ffn_part)], axis=1)
    net.send(r.early.at[n_z], r.pair.at[0], net.beside, net.sem("pair", 0, 2))
    net.ch_gather_finish(lambda cc: r.branch.at[cc], "bgrad")

    ahead_docs = Docs(r.lengths, s * count, count + RIM)
    row = lax.broadcasted_iota(jnp.int32, (count, bw), 0)
    heads_a, heads_b = [], []
    for b in range(slots):
        cols = pl.ds(b * bw, bw)
        live = jnp.where(r.counts[0] > b, 1.0, 0.0)
        product_grad = contract_last(r.branch[...].reshape(count, d), r.out_w_v[b * bw : (b + 1) * bw, :])
        value, slope = smooth_pair(r.gelu[:, cols])
        r.gath[1, z, :, cols] = (product_grad * r.state[:, cols] * live * slope).astype(bf)
        rate, inlet, sp, log_decay, factor, scale = coefficient_parts(r.rate_pre[:, cols], r.inlet_pre[:, cols], r.decay_v[b : b + 1, :])
        carry = keep * factor
        following = jnp.where(row < count - 1, pltpu.roll(carry, count - 1, 0), 1.0)
        total, part = suffix(following, product_grad * value * live, count)
        r.scan_a[:, cols] = total
        r.scan_b[:, cols] = part
        heads_a.append(carry[0:1] * total[0:1])
        heads_b.append(carry[0:1] * part[0:1])
    exchange(r.summary_back, heads_a + heads_b, "sumback")

    gather_start(1)
    gather_arrive(0, 3)
    weight_grad_send(0, others[3:4])
    exchanged(r.summary_back, "sumback")

    def pair_sum(a, ref):
        net.recv(r.pair.at[a], net.sem("pair", a, 2))
        ref[z] = ref[n_z] + r.pair[a]
        for k in range(1, n_z):
            to = net.z_of(k)
            net.send(ref.at[z], ref.at[z], net.dev(to, x, y, core), net.sem(("vec", a)))

    pair_sum(0, r.early)
    enter_back = jnp.zeros((slots, bw), f32)
    for q in range(n_seq - 1, 0, -1):
        after = r.summary_back[q, 0:slots] * enter_back + r.summary_back[q, slots : 2 * slots]
        enter_back = jnp.where(s < q, after, enter_back)
    vec = []
    for b in range(slots):
        cols = pl.ds(b * bw, bw)
        adjoint = r.scan_b[:, cols] + r.scan_a[:, cols] * enter_back[b : b + 1]
        previous = jnp.where(row > 0, pltpu.roll(r.state[:, cols], 1, 0), enter[b : b + 1])
        decay = r.decay_v[b : b + 1, :]
        rate, inlet, sp, log_decay, factor, scale = coefficient_parts(r.rate_pre[:, cols], r.inlet_pre[:, cols], decay)
        conv_low = r.conv[:, cols]
        conv = conv_low.astype(f32)
        init_rows = opening_rows(docs, r.init_v[:, cols])
        log_grad = adjoint * (
            factor * (keep * previous + (1.0 - keep) * init_rows) - inlet * conv * jnp.exp(2.0 * log_decay) / scale
        )
        rate_low = (log_grad * (-8.0 * sp) * rate * (1.0 - rate)).astype(bf)
        direct = adjoint * scale
        inlet_low = (direct * conv * inlet * (1.0 - inlet)).astype(bf)
        decay_row = jnp.sum(log_grad * (-8.0 * rate), axis=0, keepdims=True) * sigmoid(decay)
        back = direct * inlet + contract_last(rate_low, r.rate_w_v[b]) + contract_last(inlet_low, r.inlet_w_v[b])
        r.cgrad[0:count, cols] = back.astype(bf)
        for a, low in enumerate((rate_low, inlet_low)):
            part = contract_first(conv_low, low).astype(bf)
            r.gates[a, b] = part.reshape(r.gates.shape[2:])
        vec.append([
            jnp.sum(rate_low.astype(f32), axis=0, keepdims=True),
            jnp.sum(inlet_low.astype(f32), axis=0, keepdims=True),
            decay_row,
        ])
    rim = r.cgrad.at[pl.ds(count, RIM)]
    net.send(r.cgrad.at[pl.ds(0, RIM)], rim, (net.s_to[n_seq - 1], c), net.sem("rimback"), s > 0)

    @pl.when(s == n_seq - 1)
    def _():
        r.cgrad[pl.ds(count, RIM), :] = jnp.zeros((RIM, wide), bf)

    net.send(r.gates.at[:, :, :, 1 - x], r.gates_x, net.beside, net.sem("gatesx"))
    gather_arrive(1, 1)
    weight_grad_send(0, others[4:])

    @pl.when(s < n_seq - 1)
    def _():
        net.recv(rim, net.sem("rimback"))

    vectors = []
    for b in range(slots):
        cols = pl.ds(b * bw, bw)
        grad = r.cgrad[:, cols].astype(f32)
        own = grad[:count]
        recur = r.recur[:, cols].astype(f32)
        total = jnp.zeros((count, bw), f32)
        tap_rows = []
        for k in range(n_taps):
            tap_rows.append(jnp.sum(own * recur[RIM - k : RIM - k + count] * docs.valid(k), axis=0, keepdims=True))
            total = total + r.taps_v[b, k : k + 1, :] * grad[k : k + count] * ahead_docs.valid(k)[k : k + count]
        r.gath[2, z, :, cols] = total.astype(bf)
        vectors.append(stack_rows(tap_rows + [jnp.sum(own, axis=0, keepdims=True)] + vec[b]))
    gather_start(2)
    for at in (3, 2, 1, 0):
        outs.third(at)

    def norm_tile(i, _):
        cols = pl.ds(pl.multiple_of(i * TILE, TILE), TILE)
        value = contract_last(r.gath[1, z], r.gelu_w_v[cols, :]) + contract_last(r.gath[2, z], r.recur_w_v[cols, :])
        for cc in range(n_ch):
            r.part[cc % 2, cc // 2, :, cols] = value[cc * rows : (cc + 1) * rows]
        return 0

    lax.fori_loop(0, d // TILE, norm_tile, 0)
    gather_arrive(1, 2)
    left_pass(1)
    left_done(0)
    norm_grad = net.ch_sum(r.part, r.mid, r.ylow, r.yfar, "norm")
    to_stream, mix_part = norm_back(r.stream_v[...].astype(f32), r.mix_gain_v[...][None, :], norm_grad)
    r.sgrad_v[...] += to_stream
    r.late[n_z] = jnp.concatenate(vectors + [pack_gain(mix_part)], axis=1)
    net.send(r.late.at[n_z], r.pair.at[1], net.beside, net.sem("pair", 1, 2))
    net.recv(r.gates_x, net.sem("gatesx"))

    def gate_step(k):
        net.chain_sum(k, lambda there: r.gates.at[:, :, there, x], (r.gates_up, r.gates_down), add_into, 1)

    def gate_add(i, _):
        for a in range(2):
            for b in range(slots):
                value = r.gates[a, b, i, x].astype(f32) + r.gates_x[a, b, i].astype(f32)
                r.gates[a, b, i, x] = value.astype(bf)
        return 0

    lax.fori_loop(0, n_z, gate_add, 0)
    gather_arrive(2, 1)
    weight_grad_send(1, others[:3])
    gate_step(3)
    pair_sum(1, r.late)
    left_done(1)
    gather_product(0)
    gather_arrive(1, 3)
    gather_arrive(2, 2)
    for at in (3, 2, 1):
        outs.fourth(at)
    r.middle[...] += outs.fourth(0)
    out_step(3)
    gate_step(2)
    weight_grad_send(1, others[3:5])
    gather_product(1)
    out_step(2)
    gate_step(1)
    weight_grad_send(1, others[5:])
    gather_arrive(2, 3)
    out_step(1)
    gather_product(2)
    for a, ref in enumerate((r.early, r.late)):
        net.recv(ref.at[pl.ds(0, n_z - 1)], net.sem(("vec", a)))
    early, late = r.early[0], r.late[0]
    for q in range(1, n_z):
        early, late = early + r.early[q], late + r.late[q]
    r.shared[c] = jnp.concatenate([early, late[:, wide:]], axis=1)
    net.ch_gather_start(lambda cc: r.shared.at[cc], "shared")
    piece = bw // n_seq
    for b in range(slots):
        part = jnp.zeros((8, piece), f32)
        for q in range(n_seq):
            at = b * bw + q * piece
            part = jnp.where(s == q, late[:, at : at + piece], part)
        r.small_v[b] = part
    r.gate_out_v[...] = r.gates[:, :, z, x].astype(f32)
    net.chain_sum_last((r.gates_up, r.gates_down), add_into, r.gate_out_v, 1)
    net.ch_gather_finish(lambda cc: r.shared.at[cc], "shared")
    gains = r.shared[0, :, wide:]
    for cc in range(1, n_ch):
        gains = gains + r.shared[cc, :, wide:]
    for cc in range(n_ch):
        r.finals_v[:, cc * wide : (cc + 1) * wide] = r.shared[cc, 0 : r.finals_v.shape[0], 0:wide]
    half = gains.shape[1] // 2
    for a in range(2):
        for i in range(half // 128):
            r.gains_v[a, i * 8 : (i + 1) * 8, :] = gains[:, a * half + i * 128 : a * half + (i + 1) * 128]
    net.chain_sum_last((r.oup, r.odown), add_into, r.middle, 0)
    r.mixed_v[...] = r.middle[...].astype(bf)
    for a in (2, 0, 1):
        weight_grad_done(a)
    for a in range(3):
        gather_done(a)
    for name in ("finals", "mixed", "sgrad", "gains", "gate_out", "small"):
        local.append(net.local(getattr(r, name + "_v"), getattr(r, name)))
    for copy in local:
        copy.wait()
    net.drain()


def finish_kernel(names, *refs):
    r = types.SimpleNamespace(**dict(zip(names, refs)))
    f32 = jnp.float32
    used = []

    def sem():
        used.append(0)
        return r.sems.at[len(used) - 1]

    def copy(src, dst):
        start = pltpu.make_async_copy(src, dst, sem())
        start.start()
        return start

    incoming = {}
    for name, index in (("dw", 2), ("dw", 0), ("dw", 1), ("keep", 0), ("took", 0), ("keep", 1), ("took", 1)):
        incoming[name, index] = copy(getattr(r, name).at[index], getattr(r, name + "_v").at[index])
    for name in ("keep_out", "took_out", "gains", "gate_out", "small", "finals", "mixed", "sgrad"):
        incoming[name] = copy(getattr(r, name), getattr(r, name + "_v"))
    leaving = []

    def leave(name):
        leaving.append(copy(getattr(r, name + "_v"), getattr(r, name)))

    incoming["dw", 2].wait()
    r.down_wg_v[...] = r.dw_v[2].astype(f32)
    leave("down_wg")
    for a, name in enumerate(("gate_wg", "up_wg")):
        incoming["dw", a].wait()
        ref = getattr(r, name + "_v")
        for i in range(ref.shape[1] // 256):
            ref[:, i * 256 : (i + 1) * 256] = contract_first(r.dw_v[a, i * 256 : (i + 1) * 256, :], unit(256))
        leave(name)
    for a, name in enumerate(("gelu_wg", "recur_wg")):
        incoming["keep", a].wait()
        incoming["took", a].wait()
        getattr(r, name + "_v")[...] = r.keep_v[a] + r.took_v[a].astype(f32)
        leave(name)
    for name in ("keep_out", "took_out", "gains", "gate_out", "small", "finals", "mixed", "sgrad"):
        incoming[name].wait()
    r.out_wg_v[...] = r.keep_out_v[...] + r.took_out_v[...].astype(f32)
    leave("out_wg")
    leaving += [
        copy(r.finals_v, r.finals_o), copy(r.mixed_v, r.mixed_o), copy(r.sgrad_v, r.sgrad_o),
        copy(r.gains_v.at[0], r.ffn_o), copy(r.gains_v.at[1], r.mix_o), copy(r.gate_out_v.at[0], r.rate_o),
        copy(r.gate_out_v.at[1], r.inlet_o),
    ]
    n_taps = r.taps_o_v.shape[1]
    for b in range(r.small_v.shape[0]):
        for k in range(n_taps):
            r.taps_o_v[b, k : k + 1, :] = r.small_v[b, k : k + 1, :]
        for k, name in enumerate(("bias_o", "rateb_o", "inletb_o", "decay_o")):
            getattr(r, name + "_v")[b : b + 1, :] = r.small_v[b, n_taps + k : n_taps + k + 1, :]
    for name in ("taps_o", "bias_o", "rateb_o", "inletb_o", "decay_o"):
        leave(name)
    for start in leaving:
        start.wait()


def gathered_body(
    stream, cotangent, mix_gain, gelu_weight, recur_weight, conv_taps, conv_bias, rate_weight, rate_bias, inlet_weight,
    inlet_bias, decay_param, init_states, out_weight, ffn_gain, gate_weight, up_weight, down_weight, doc_lengths, block_counts,
):
    n_seq, n_ch = lax.axis_size(SEQ), lax.axis_size(CH)
    rows, d = stream.shape
    slots, bw = conv_bias.shape
    width, hidden = gate_weight.shape
    sl = hidden // n_seq
    n_z = n_seq // 2
    count, wide, tokens = rows * n_ch, slots * bw, rows * n_ch * n_seq
    piece = bw // n_seq
    n_taps, n_docs = conv_taps.shape[0], doc_lengths.shape[0]
    bf, f32 = jnp.bfloat16, jnp.float32
    vmem = pl.BlockSpec(memory_space=pltpu.VMEM)
    smem = pl.BlockSpec(memory_space=pltpu.SMEM)
    anywhere = pl.BlockSpec(memory_space=pl.ANY)
    inputs = dict(
        stream=stream, cot=cotangent, mix_gain=mix_gain, gelu_w=gelu_weight, recur_w=recur_weight, taps=conv_taps.transpose(1, 0, 2),
        bias=conv_bias, rate_w=rate_weight, rate_b=rate_bias, inlet_w=inlet_weight, inlet_b=inlet_bias, decay=decay_param,
        init=init_states, out_w=out_weight, ffn_gain=ffn_gain, gate_w=gate_weight, up_w=up_weight, down=down_weight,
        lengths=doc_lengths, counts=block_counts,
    )
    places = dict(lengths=smem, counts=smem)
    staged = [name for name in inputs if name not in ("lengths", "counts", "gate_w", "up_w", "down")]
    outputs = dict(
        keep=((2, width, wide), f32), keep_out=((wide, width), f32), took=((2, width, wide), bf), took_out=((wide, width), bf),
        dw=((3, hidden, width), bf),
        finals=((n_docs, wide * n_ch), f32), mixed=((rows, d), bf), sgrad=((rows, d), f32), gains=((2, d // 128, 128), f32),
        gate_out=((2, slots, piece, bw), f32), small=((slots, 8, piece), f32),
    )
    packed = wide + d // 8
    scratch = dict(
        mix=((RIM + count, d), bf), full=((tokens, d), bf), cfull=((tokens, d), bf), turned=((2, hidden, width), bf),
        wt=((3, sl, d), bf), dwl=((3, sl, d), bf), value=((tokens, sl), f32), slope=((tokens, sl), f32),
        hid=((tokens, sl), bf), gat=((tokens, sl), bf), upg=((tokens, sl), bf),
        gelu=((count, wide), f32), recur=((RIM + count, wide), bf), conv=((count, wide), bf), rate_pre=((count, wide), f32),
        inlet_pre=((count, wide), f32), scan_a=((count, wide), f32), scan_b=((count, wide), f32), state=((count, wide), f32),
        gath=((3, n_z, count, wide), bf), left=((2, n_z, n_ch, rows, 2 * width), bf), give=((2, width, wide), bf),
        give_out=((wide, width), bf), take=((2, width, wide), bf), take_out=((wide, width), bf), cgrad=((count + RIM, wide), bf), branch=((n_ch, rows, d), bf),
        summary=((n_seq, 8, bw), f32), summary_back=((n_seq, 8, bw), f32),
        part=((2, 2, rows, d), f32), mid=((2, rows, d), f32), ylow=((rows, d), bf), yfar=((rows, d), bf), middle=((rows, d), f32),
        npart=((n_z, 2, 2, 2, rows, d), bf), nsib=((n_z, 2, 2, rows, d), bf), nfar=((n_z, 2, rows // 2, d), bf),
        nside=((n_z, 2, rows, d), bf),
        opart=((n_z, 2, 2, 2, rows, d), bf), osib=((n_z, 2, 2, rows, d), bf), ofar=((n_z, 2, rows, d), bf),
        oside=((n_z, rows, d), bf), oup=((n_z - 1, rows, d), bf), odown=((n_z - 1, rows, d), bf),
        gates=((2, slots, n_z, 2, piece, bw), bf), gates_x=((2, slots, n_z, piece, bw), bf), gates_up=((n_z - 1, 2, slots, piece, bw), bf), gates_down=((n_z - 1, 2, slots, piece, bw), bf),
        early=((n_z + 1, 8, packed), f32), late=((n_z + 1, 8, packed), f32), pair=((2, 8, packed), f32),
        shared=((n_ch, 8, packed + d // 8), f32),
    )
    scratch.update({name + "_v": (inputs[name].shape, inputs[name].dtype) for name in staged})
    scratch.update({name + "_v": what for name, what in outputs.items() if name not in ("took", "took_out", "dw")})
    dma = pltpu.SemaphoreType.DMA
    results = pl.pallas_call(
        functools.partial(
            block_kernel, (n_seq, n_ch, rows, d, slots, bw, width, sl),
            list(inputs) + list(outputs) + list(scratch) + ["send_sems", "recv_sems", "local_sems"],
        ),
        out_shape=[jax.ShapeDtypeStruct(*what) for what in outputs.values()],
        in_specs=[places.get(name, anywhere) for name in inputs],
        out_specs=[anywhere] * len(outputs),
        scratch_shapes=[pltpu.VMEM(*what) for what in scratch.values()] + [dma((SEND_SEMS,)), dma((RECV_SEMS,)), dma((LOCAL_SEMS,))],
        compiler_params=pltpu.CompilerParams(collective_id=1, has_side_effects=True, vmem_limit_bytes=VMEM_BYTES),
    )(*inputs.values())
    vector = ((slots, piece), f32)
    ends = dict(
        finals_o=((n_docs, wide * n_ch), f32), mixed_o=((rows, d), bf), sgrad_o=((rows, d), f32), mix_o=((d // 128, 128), f32),
        gelu_wg=((width, wide), f32), recur_wg=((width, wide), f32), taps_o=((slots, n_taps, piece), f32), bias_o=vector,
        rate_o=((slots, piece, bw), f32), rateb_o=vector, inlet_o=((slots, piece, bw), f32), inletb_o=vector, decay_o=vector,
        out_wg=((wide, width), f32), ffn_o=((d // 128, 128), f32), gate_wg=((width, hidden), f32), up_wg=((width, hidden), f32),
        down_wg=((hidden, width), f32),
    )
    direct = ("finals_o", "mixed_o", "sgrad_o", "ffn_o", "mix_o", "rate_o", "inlet_o")
    kept = {name + "_v": outputs[name] for name in outputs}
    kept.update({name + "_v": what for name, what in ends.items() if name not in direct})
    last = pl.pallas_call(
        functools.partial(finish_kernel, list(outputs) + list(ends) + list(kept) + ["sems"]),
        out_shape=[jax.ShapeDtypeStruct(*what) for what in ends.values()],
        in_specs=[anywhere] * len(outputs),
        out_specs=[anywhere] * len(ends),
        scratch_shapes=[pltpu.VMEM(*what) for what in kept.values()] + [pltpu.SemaphoreType.DMA((40,))],
        compiler_params=pltpu.CompilerParams(vmem_limit_bytes=VMEM_BYTES),
    )(*results)
    named = dict(zip(ends, last))
    named["taps_o"] = named["taps_o"].transpose(1, 0, 2)
    named["mix_o"], named["ffn_o"] = named["mix_o"].reshape(d), named["ffn_o"].reshape(d)
    return tuple(named.values())


def solution(mesh):
    in_specs = (
        P((SEQ, CH), None),
        P((SEQ, CH), None),
        P(),
        P(None, CH),
        P(None, CH),
        P(None, CH, None),
        P(CH, None),
        P(CH, None, None),
        P(CH, None),
        P(CH, None, None),
        P(CH, None),
        P(CH, None),
        P(None, CH),
        P(CH, None),
        P(),
        P(SEQ, CH),
        P(SEQ, CH),
        P(CH, SEQ),
        P(),
        P(CH),
    )
    out_specs = (
        P(),
        P((SEQ, CH), None),
        P((SEQ, CH), None),
        P(),
        P(SEQ, CH),
        P(SEQ, CH),
        P(None, CH, SEQ),
        P(CH, SEQ),
        P(CH, SEQ, None),
        P(CH, SEQ),
        P(CH, SEQ, None),
        P(CH, SEQ),
        P(CH, SEQ),
        P(CH, SEQ),
        P(),
        P(SEQ, CH),
        P(SEQ, CH),
        P(CH, SEQ),
    )
    return jax.shard_map(gathered_body if mesh.shape[SEQ] == 8 else body, mesh=mesh, in_specs=in_specs, out_specs=out_specs, check_vma=False)
```

```python
import functools
import math
import types

import jax
import jax.numpy as jnp
from jax import lax
from jax.experimental import pallas as pl
from jax.experimental.pallas import tpu as pltpu
from jax.sharding import PartitionSpec as P

EPS = 1e-06
HIGH = lax.Precision.HIGHEST
MESH = pl.DeviceIdType.MESH
SEQ = "seq"
CH = "ch"
K1 = 0.7978845608028654
K2 = 0.044715
VMEM_BYTES = 63 * 2**20
TILE = 1024
SEND_SEMS = 96
RECV_SEMS = 140
LOCAL_SEMS = 46


def passed_along(shard, axis, by):
    length = lax.axis_size(axis)
    pairs = [(i, i + by) for i in range(length) if 0 <= i + by < length]
    return lax.ppermute(shard, axis, pairs)


def entering_2(shard, axis, combine, identity, reverse):
    length, here = (lax.axis_size(axis), lax.axis_index(axis))
    everything = jax.tree.map(lambda part: lax.all_gather(part, axis), shard)
    start = jax.tree.map(
        lambda part, zero: jnp.broadcast_to(jnp.asarray(zero, part.dtype), part.shape),
        shard,
        identity,
    )

    def turn(k, before):
        at = length - 1 - k if reverse else k
        reached = at > here if reverse else at < here
        new = combine(before, jax.tree.map(lambda part: part[at], everything))
        return jax.tree.map(lambda a, b: jnp.where(reached, a, b), new, before)

    return lax.fori_loop(0, length, turn, start)


def normalize(values, gain):
    return values * lax.rsqrt(jnp.mean(values * values, axis=-1, keepdims=True) + EPS) * gain


def smooth(values):
    return jax.nn.gelu(values, approximate=True)


def affine(earlier, later):
    return (earlier[0] * later[0], later[0] * earlier[1] + later[1])


def doc_view(lengths, first, count):
    ends = jnp.cumsum(lengths)
    starts = ends - lengths
    position = first + jnp.arange(count, dtype=jnp.int32)
    owner = (position[:, None] >= starts[None, :]) & (position[:, None] < ends[None, :])
    start_of = jnp.sum(jnp.where(owner, starts[None, :], 0), axis=1)
    offset = position - start_of
    opening = (owner & (offset[:, None] == 0)).astype(jnp.float32)
    closing = (owner & (position[:, None] == ends[None, :] - 1)).astype(jnp.float32)
    return (offset, opening, closing)


def coefficients(rate_pre, inlet_pre, conv_value, decay, init_rows, keep):
    rate = jax.nn.sigmoid(rate_pre)
    inlet = jax.nn.sigmoid(inlet_pre)
    log_decay = -8.0 * rate * jax.nn.softplus(decay)
    factor = jnp.exp(log_decay)
    scale = jnp.sqrt(-jnp.expm1(2.0 * log_decay))
    carry_factor = keep * factor
    source = scale * inlet * conv_value + (1.0 - keep) * factor * init_rows
    return (carry_factor, source)


def spread(values):
    return lax.all_gather(values, CH, axis=0, tiled=True)


def collect(terms):
    return lax.psum_scatter(terms, CH, scatter_dimension=0, tiled=True)


def contract_last(left, right):
    return lax.dot_general(
        left, right, (((1,), (1,)), ((), ())), preferred_element_type=jnp.float32
    )


def contract_first(left, right):
    return lax.dot_general(
        left, right, (((0,), (0,)), ((), ())), preferred_element_type=jnp.float32
    )


def body(
    stream,
    cotangent,
    mix_gain,
    gelu_weight,
    recur_weight,
    conv_taps,
    conv_bias,
    rate_weight,
    rate_bias,
    inlet_weight,
    inlet_bias,
    decay_param,
    init_states,
    out_weight,
    ffn_gain,
    gate_weight,
    up_weight,
    down_weight,
    doc_lengths,
    block_counts,
):
    slot_count = rate_weight.shape[0]
    block_width = rate_weight.shape[1]
    local_width = slot_count * block_width
    taps = conv_taps.shape[0]
    token_count = stream.shape[0] * lax.axis_size(CH)
    hidden_width = gate_weight.shape[1]
    base = lax.axis_index(SEQ) * token_count
    offset_all, opening, closing = doc_view(doc_lengths, base, token_count + taps - 1)
    offset = offset_all[:token_count]
    opening = opening[:token_count]
    closing = closing[:token_count]
    keep = (offset > 0).astype(jnp.float32)[:, None]
    slot_live = (jnp.arange(slot_count, dtype=jnp.int32) < block_counts[0]).astype(jnp.float32)
    live = jnp.repeat(slot_live, block_width)[None, :]
    taps_flat = conv_taps.reshape(taps, local_width)
    decay_flat = decay_param.reshape(1, local_width)
    stream_float = stream.astype(jnp.float32)
    mix_low = normalize(stream_float, mix_gain).astype(jnp.bfloat16)
    mix_full = spread(mix_low)
    gelu_pre = jnp.dot(mix_full, gelu_weight, preferred_element_type=jnp.float32)
    recur_low = jnp.dot(mix_full, recur_weight, preferred_element_type=jnp.float32).astype(
        jnp.bfloat16
    )
    rim = passed_along(recur_low[token_count - taps + 1 :], SEQ, 1)
    extended = jnp.concatenate([rim, recur_low], axis=0).astype(jnp.float32)
    conv_pre = conv_bias.reshape(1, local_width)
    for tap_index in range(taps):
        valid = (offset >= tap_index).astype(jnp.float32)[:, None]
        lead = taps - 1 - tap_index
        conv_pre = (
            conv_pre + taps_flat[tap_index][None, :] * extended[lead : lead + token_count] * valid
        )
    conv_low = conv_pre.astype(jnp.bfloat16)
    conv_value = conv_low.astype(jnp.float32)
    grouped = conv_low.reshape(token_count, slot_count, block_width)
    rate_pre = (
        jnp.einsum("rsi,sio->rso", grouped, rate_weight, preferred_element_type=jnp.float32)
        + rate_bias[None]
    ).reshape(token_count, local_width)
    inlet_pre = (
        jnp.einsum("rsi,sio->rso", grouped, inlet_weight, preferred_element_type=jnp.float32)
        + inlet_bias[None]
    ).reshape(token_count, local_width)
    init_rows = jnp.dot(opening, init_states, precision=HIGH)
    carry_factor, source = coefficients(
        rate_pre, inlet_pre, conv_value, decay_flat, init_rows, keep
    )
    cumulative, local_state = lax.associative_scan(affine, (carry_factor, source), axis=0)
    summary = (cumulative[-1], local_state[-1])
    entering = entering_2(
        summary, SEQ, affine, (jnp.ones_like(summary[0]), jnp.zeros_like(summary[1])), False
    )
    state_in = entering[1]
    state = local_state + cumulative * state_in[None, :]
    gelu_value = smooth(gelu_pre)
    product_low = (gelu_value * state * live).astype(jnp.bfloat16)
    branch = collect(jnp.dot(product_low, out_weight, preferred_element_type=jnp.float32))
    middle = stream_float + branch
    ffn_low = normalize(middle, ffn_gain).astype(jnp.bfloat16)
    ffn_full = spread(ffn_low)
    stacked = jnp.concatenate([gate_weight, up_weight], axis=1)
    columns = ffn_full
    gate_up = jnp.dot(
        columns,
        lax.all_gather(stacked, SEQ, axis=0, tiled=True),
        preferred_element_type=jnp.float32,
    )
    gate = gate_up[:, :hidden_width]
    upward = gate_up[:, hidden_width:]
    hidden = (smooth(gate) * upward).astype(jnp.bfloat16)
    ffn_terms = jnp.dot(
        hidden,
        lax.all_gather(down_weight, SEQ, axis=1, tiled=True),
        preferred_element_type=jnp.float32,
    )
    mixed_out = (middle + collect(ffn_terms)).astype(jnp.bfloat16)
    out_grad_full = spread(cotangent)
    columns = out_grad_full
    hidden_grad = contract_last(columns, lax.all_gather(down_weight, SEQ, axis=1, tiled=True))
    down_weight_grad = contract_first(hidden, out_grad_full)
    unused, pair_pull = jax.vjp(lambda left, right: smooth(left) * right, gate, upward)
    gate_grad, up_grad = pair_pull(hidden_grad)
    pair_low = jnp.concatenate([gate_grad, up_grad], axis=1).astype(jnp.bfloat16)
    pair_weight_grad = contract_first(ffn_full, pair_low)
    norm_ffn_part = contract_last(pair_low, lax.all_gather(stacked, SEQ, axis=0, tiled=True))
    norm_ffn_grad = collect(norm_ffn_part)
    unused, ffn_norm_pull = jax.vjp(normalize, middle, ffn_gain)
    middle_norm_grad, ffn_gain_part = ffn_norm_pull(norm_ffn_grad)
    middle_grad = cotangent.astype(jnp.float32) + middle_norm_grad
    branch_full = spread(middle_grad.astype(jnp.bfloat16))
    out_weight_grad = contract_first(product_low, branch_full)
    product_grad = contract_last(branch_full, out_weight)
    state_grad = product_grad * gelu_value * live
    unused, gelu_pull = jax.vjp(smooth, gelu_pre)
    gelu_low = gelu_pull(product_grad * state * live)[0].astype(jnp.bfloat16)
    following = jnp.concatenate([carry_factor[1:], jnp.ones_like(carry_factor[:1])], axis=0)
    cum_back, adjoint_local = lax.associative_scan(
        affine, (jnp.flip(following, 0), jnp.flip(state_grad, 0)), axis=0
    )
    cum_back = jnp.flip(cum_back, 0)
    adjoint_local = jnp.flip(adjoint_local, 0)
    summary_back = (carry_factor[0] * cum_back[0], carry_factor[0] * adjoint_local[0])
    arriving = entering_2(
        summary_back,
        SEQ,
        affine,
        (jnp.ones_like(summary_back[0]), jnp.zeros_like(summary_back[1])),
        True,
    )
    adjoint_in = arriving[1]
    adjoint = adjoint_local + cum_back * adjoint_in[None, :]
    previous_state = jnp.concatenate([state_in[None, :], state[:-1]], axis=0)

    def local_coefficients(rate_value, inlet_value, conv_part, decay_value):
        return coefficients(rate_value, inlet_value, conv_part, decay_value, init_rows, keep)

    unused, coefficient_pull = jax.vjp(
        local_coefficients, rate_pre, inlet_pre, conv_value, decay_flat
    )
    rate_grad, inlet_grad, conv_direct, decay_part = coefficient_pull(
        (adjoint * previous_state, adjoint)
    )
    rate_low = rate_grad.astype(jnp.bfloat16).reshape(token_count, slot_count, block_width)
    inlet_low = inlet_grad.astype(jnp.bfloat16).reshape(token_count, slot_count, block_width)
    rate_weight_grad = jnp.einsum(
        "rsi,rso->sio", grouped, rate_low, preferred_element_type=jnp.float32
    )
    inlet_weight_grad = jnp.einsum(
        "rsi,rso->sio", grouped, inlet_low, preferred_element_type=jnp.float32
    )
    rate_bias_grad = jnp.sum(rate_low.astype(jnp.float32), axis=0)
    inlet_bias_grad = jnp.sum(inlet_low.astype(jnp.float32), axis=0)
    conv_back = jnp.einsum(
        "rso,sio->rsi", rate_low, rate_weight, preferred_element_type=jnp.float32
    )
    conv_back = conv_back + jnp.einsum(
        "rso,sio->rsi", inlet_low, inlet_weight, preferred_element_type=jnp.float32
    )
    conv_low_grad = (conv_direct + conv_back.reshape(token_count, local_width)).astype(jnp.bfloat16)
    rim_back = passed_along(conv_low_grad[: taps - 1], SEQ, -1)
    ahead = jnp.concatenate([conv_low_grad, rim_back], axis=0).astype(jnp.float32)
    own_grad = ahead[:token_count]
    recur_grad = jnp.zeros((token_count, local_width), jnp.float32)
    tap_grads = []
    for tap_index in range(taps):
        lead = taps - 1 - tap_index
        valid_here = (offset >= tap_index).astype(jnp.float32)[:, None]
        tap_grads.append(
            jnp.sum(own_grad * extended[lead : lead + token_count] * valid_here, axis=0)
        )
        valid_ahead = (offset_all[tap_index : tap_index + token_count] >= tap_index).astype(
            jnp.float32
        )[:, None]
        recur_grad = (
            recur_grad
            + taps_flat[tap_index][None, :]
            * ahead[tap_index : tap_index + token_count]
            * valid_ahead
        )
    conv_taps_grad = jnp.stack(tap_grads, axis=0).reshape(taps, slot_count, block_width)
    conv_bias_grad = jnp.sum(own_grad, axis=0).reshape(slot_count, block_width)
    recur_low_grad = recur_grad.astype(jnp.bfloat16)
    gelu_weight_grad = contract_first(mix_full, gelu_low)
    recur_weight_grad = contract_first(mix_full, recur_low_grad)
    norm_mix_part = contract_last(gelu_low, gelu_weight) + contract_last(
        recur_low_grad, recur_weight
    )
    norm_mix_grad = collect(norm_mix_part)
    unused, mix_norm_pull = jax.vjp(normalize, stream_float, mix_gain)
    stream_norm_grad, mix_gain_part = mix_norm_pull(norm_mix_grad)
    stream_grad = middle_grad + stream_norm_grad
    finals_local = lax.dot_general(closing, state * live, (((0,), (0,)), ((), ())), precision=HIGH)
    finals_wide = jnp.zeros((finals_local.shape[0], local_width * lax.axis_size(CH)), jnp.float32)
    finals_wide = lax.dynamic_update_slice(
        finals_wide, finals_local, (jnp.int32(0), lax.axis_index(CH) * local_width)
    )
    final_states, mix_gain_grad, ffn_gain_grad = lax.psum(
        (finals_wide, mix_gain_part, ffn_gain_part), (SEQ, CH)
    )
    summed = (
        lax.psum_scatter(gelu_weight_grad, SEQ, scatter_dimension=0, tiled=True),
        lax.psum_scatter(recur_weight_grad, SEQ, scatter_dimension=0, tiled=True),
        lax.psum_scatter(conv_taps_grad, SEQ, scatter_dimension=2, tiled=True),
        lax.psum_scatter(conv_bias_grad, SEQ, scatter_dimension=1, tiled=True),
        lax.psum_scatter(rate_weight_grad, SEQ, scatter_dimension=1, tiled=True),
        lax.psum_scatter(rate_bias_grad, SEQ, scatter_dimension=1, tiled=True),
        lax.psum_scatter(inlet_weight_grad, SEQ, scatter_dimension=1, tiled=True),
        lax.psum_scatter(inlet_bias_grad, SEQ, scatter_dimension=1, tiled=True),
        lax.psum_scatter(
            decay_part.reshape(slot_count, block_width), SEQ, scatter_dimension=1, tiled=True
        ),
        lax.psum_scatter(out_weight_grad, SEQ, scatter_dimension=1, tiled=True),
        lax.psum_scatter(
            pair_weight_grad[:, :hidden_width], SEQ, scatter_dimension=0, tiled=True
        ),
        lax.psum_scatter(
            pair_weight_grad[:, hidden_width:], SEQ, scatter_dimension=0, tiled=True
        ),
        lax.psum_scatter(down_weight_grad, SEQ, scatter_dimension=1, tiled=True),
    )
    return (
        final_states,
        mixed_out,
        stream_grad,
        mix_gain_grad,
        summed[0],
        summed[1],
        summed[2],
        summed[3],
        summed[4],
        summed[5],
        summed[6],
        summed[7],
        summed[8],
        summed[9],
        ffn_gain_grad,
        summed[10],
        summed[11],
        summed[12],
    )


class Net:
    def __init__(self, n_seq, n_ch, rows, send_sems, recv_sems, local_sems):
        self.n_seq, self.n_ch, self.rows = n_seq, n_ch, rows
        self.n_z = n_seq // 2
        self.send_sems, self.recv_sems, self.local_sems = send_sems, recv_sems, local_sems
        self.tags, self.used, self.sent, self.locals = {}, 0, [], 0
        self.s, self.c = lax.axis_index(SEQ), lax.axis_index(CH)
        s, c, n_z = self.s, self.c, self.n_z
        self.z, self.x, self.y, self.core = s // 2, s % 2, c // 2, c % 2
        x, y = self.x, self.y
        self.s_to = [(s + k) % n_seq for k in range(n_seq)]
        self.s_from = [(s + n_seq - k) % n_seq for k in range(n_seq)]
        self.sibling = self.dev(self.z, x, y, 1 - self.core)
        self.across = self.dev(self.z, x, 1 - y, self.core)
        self.beside = self.dev(self.z, 1 - x, y, self.core)
        self.above = self.dev((self.z + 1) % n_z, x, y, self.core)
        self.below = self.dev((self.z + n_z - 1) % n_z, x, y, self.core)

    def nearest(self):
        order = [self.z * 2 + 1 - self.x]
        for at in range(1, self.n_z):
            there = self.z_of(self.slot(at))
            order += [there * 2 + self.x, there * 2 + 1 - self.x]
        return order

    def dev(self, z, x, y, core):
        return (z * 2 + x, y * 2 + core)

    def block(self, z, x, y, core):
        rows = self.rows
        return pl.multiple_of(((z * 2 + x) * self.n_ch + y * 2 + core) * rows, rows)

    def z_of(self, slot):
        return (self.z + self.n_z - slot) % self.n_z

    def slot(self, at):
        if at == 0:
            return 0
        n_z, z = self.n_z, self.z
        low, high = (n_z - 1 - z) // (n_z - 1), z // (n_z - 1)
        inner = (at + 1) // 2 if at % 2 else n_z - at // 2
        return low * (n_z - at) + high * at + (1 - low - high) * inner

    def greet(self, peers):
        barrier = pltpu.get_barrier_semaphore()
        for peer in peers:
            pl.semaphore_signal(barrier, inc=1, device_id=peer, device_id_type=MESH)

    def meet(self, peers):
        pl.semaphore_wait(pltpu.get_barrier_semaphore(), len(peers))

    def sem(self, tag, at=0, size=1):
        if tag not in self.tags:
            self.tags[tag] = self.used
            self.used += size
        return self.recv_sems.at[self.tags[tag] + at]

    def send(self, src, dst, to, sem, when=None):
        size = self.send_sems.shape[0]
        if len(self.sent) >= size:
            self.sent_wait(len(self.sent) - size)
        copy = pltpu.make_async_remote_copy(
            src_ref=src, dst_ref=dst, send_sem=self.send_sems.at[len(self.sent) % size], recv_sem=sem,
            device_id=to, device_id_type=MESH,
        )
        if when is None:
            copy.start()
        else:
            @pl.when(when)
            def _():
                copy.start()
        self.sent.append((copy, when))

    def sent_wait(self, at):
        if self.sent[at] is None:
            return
        copy, when = self.sent[at]
        self.sent[at] = None
        if when is None:
            copy.wait_send()
        else:
            @pl.when(when)
            def _():
                copy.wait_send()

    def recv(self, view, sem):
        pltpu.make_async_remote_copy(
            src_ref=view, dst_ref=view, send_sem=self.send_sems.at[0], recv_sem=sem,
            device_id=(self.s, self.c), device_id_type=MESH,
        ).wait_recv()

    def local(self, src, dst):
        copy = pltpu.make_async_copy(src, dst, self.local_sems.at[self.locals])
        self.locals += 1
        copy.start()
        return copy

    def drain(self):
        for at in range(len(self.sent)):
            self.sent_wait(at)

    def ch_gather_start(self, view_of, tag):
        mine = view_of(self.c)
        self.send(mine, mine, self.across, self.sem((tag, "y")))
        self.send(mine, mine, self.sibling, self.sem((tag, "core")))

    def ch_gather_finish(self, view_of, tag):
        y, core = self.y, self.core
        theirs = view_of((1 - y) * 2 + core)
        self.recv(theirs, self.sem((tag, "y")))
        self.send(theirs, theirs, self.sibling, self.sem((tag, "fwd")))
        self.recv(view_of(y * 2 + 1 - core), self.sem((tag, "core")))
        self.recv(view_of((1 - y) * 2 + 1 - core), self.sem((tag, "fwd")))

    def ch_sum(self, part, mid, low, far, tag):
        y, core = self.y, self.core
        first = len(self.sent)
        self.send(part.at[1 - core], mid, self.sibling, self.sem((tag, "core")))
        self.recv(mid, self.sem((tag, "core")))
        low[...] = (part[core, 1 - y] + mid[1 - y]).astype(jnp.bfloat16)
        self.send(low, far, self.across, self.sem((tag, "y")))
        total = part[core, y] + mid[y]
        self.recv(far, self.sem((tag, "y")))
        self.sent_wait(first)
        self.sent_wait(first + 1)
        return total + far[...].astype(jnp.float32)

    def chain_start(self, mine, target, tag):
        n_z, z = self.n_z, self.z
        self.send(mine, target, self.above, self.sem((tag, "z"), 1, n_z), z < n_z - 1)
        self.send(mine, target, self.below, self.sem((tag, "z"), n_z - 1, n_z), z > 0)

    def chain_arrive(self, view, slot, tag):
        n_z, z = self.n_z, self.z
        self.recv(view, self.sem((tag, "z"), slot, n_z))
        self.send(view, view, self.above, self.sem((tag, "z"), (slot + 1) % n_z, n_z), (z >= slot) & (z < n_z - 1))
        self.send(view, view, self.below, self.sem((tag, "z"), (slot + n_z - 1) % n_z, n_z), (z < slot) & (z > 0))


    def chain_sum(self, k, term, lands, add, tag):
        n_z, z = self.n_z, self.z
        for way, to, goes, comes in ((1, self.above, z + k < n_z, z > 0), (n_z - 1, self.below, z >= k, z < n_z - 1)):
            land, name = lands[way > 1], (tag, way > 1)
            mine = term((z + way * k) % n_z)
            if k < n_z - 1:
                @pl.when(goes & comes)
                def _():
                    self.recv(land.at[k], self.sem(name, k, n_z - 1))
                    add(mine, land.at[k])

            self.send(mine, land.at[k - 1], to, self.sem(name, k - 1, n_z - 1), goes)

    def chain_sum_last(self, lands, add, total, tag):
        n_z, z = self.n_z, self.z
        for side, comes in ((0, z > 0), (1, z < n_z - 1)):
            @pl.when(comes)
            def _(side=side):
                self.recv(lands[side].at[0], self.sem((tag, side > 0), 0, n_z - 1))
                add(total, lands[side].at[0])

    def arrival(self, slot):
        n_z, z = self.n_z, self.z
        low, high = (n_z - 1 - z) // (n_z - 1), z // (n_z - 1)
        far = slot // (n_z // 2 + 1)
        inner = (1 - far) * (2 * slot - 1) + far * 2 * (n_z - slot)
        return (low * (n_z - slot) + high * slot + (1 - low - high) * inner + n_z) % n_z


def add_into(mine, more):
    mine[...] = (mine[...].astype(jnp.float32) + more[...].astype(jnp.float32)).astype(mine.dtype)


class Spread:
    def __init__(self, net, ref, tag):
        self.net, self.ref, self.tag = net, ref, tag

    def view(self, slot, x, y, core):
        net = self.net
        return self.ref.at[pl.ds(net.block(net.z_of(slot), x, y, core), net.rows)]

    def sem(self, what, slot):
        return self.net.sem((self.tag, what), slot, self.net.n_z)

    def start(self):
        net = self.net
        mine = self.view(0, net.x, net.y, net.core)
        net.chain_start(mine, mine, self.tag)
        self.plane(0)

    def plane(self, slot):
        net = self.net
        view = self.view(slot, net.x, net.y, net.core)
        net.send(view, view, net.beside, self.sem("x", slot))
        net.send(view, view, net.across, self.sem("y", slot))
        net.send(view, view, net.sibling, self.sem("s", slot))

    def arrive(self, slot):
        net = self.net
        net.chain_arrive(self.view(slot, net.x, net.y, net.core), slot, self.tag)
        self.plane(slot)

    def relay(self, slot):
        net = self.net
        view = self.view(slot, 1 - net.x, net.y, net.core)
        net.recv(view, self.sem("x", slot))
        net.send(view, view, net.across, self.sem("d", slot))
        net.send(view, view, net.sibling, self.sem("s", slot))

    def relay_far(self, slot):
        net = self.net
        for what, x in (("y", net.x), ("d", 1 - net.x)):
            view = self.view(slot, x, 1 - net.y, net.core)
            net.recv(view, self.sem(what, slot))
            net.send(view, view, net.sibling, self.sem("s", slot))

    def done(self, slot):
        net = self.net
        at = net.block(net.z_of(slot), 0, 0, 0)
        net.recv(self.ref.at[pl.ds(at, 4 * net.rows)], self.sem("s", slot))


class Collect:
    def __init__(self, net, part, sib, far, side, tag):
        self.net, self.part, self.sib, self.far, self.side, self.tag = net, part, sib, far, side, tag

    def sem(self, what, at):
        return self.net.sem((self.tag, what), at, self.net.n_z)

    def first(self, at):
        net = self.net
        net.send(self.part.at[at, 1 - net.core], self.sib.at[at], net.sibling, self.sem("s", at))

    def second(self, at):
        net = self.net
        net.recv(self.sib.at[at], self.sem("s", at))
        core, part, sib = net.core, self.part, self.sib
        for first in (1 - net.y, net.y):
            for x in range(2):
                value = part[at, core, first, x].astype(jnp.float32) + sib[at, first, x].astype(jnp.float32)
                part[at, core, first, x] = value.astype(jnp.bfloat16)
            if first is not net.y:
                net.send(part.at[at, core, first], self.far.at[at], net.across, self.sem("f", at))

    def third(self, at):
        net, part, far = self.net, self.part, self.far
        net.recv(far.at[at], self.sem("f", at))
        there = 1 - net.x
        value = part[at, net.core, net.y, there].astype(jnp.float32) + far[at, there].astype(jnp.float32)
        part[at, net.core, net.y, there] = value.astype(jnp.bfloat16)
        net.send(part.at[at, net.core, net.y, there], self.side.at[at], net.beside, self.sem("p", at))

    def plane_total(self, at):
        net = self.net
        net.recv(self.side.at[at], self.sem("p", at))
        total = self.part[at, net.core, net.y, net.x].astype(jnp.float32)
        return total + self.far[at, net.x].astype(jnp.float32) + self.side[at].astype(jnp.float32)

    def fourth(self, at):
        net, part = self.net, self.part
        total = self.plane_total(at)
        if at == 0:
            return total
        part[at, net.core, net.y, net.x] = total.astype(jnp.bfloat16)
        return None

    def term(self, there):
        net = self.net
        at = net.arrival((net.z + net.n_z - there) % net.n_z)
        return self.part.at[at, net.core, net.y, net.x]


class CollectEven(Collect):
    def second(self, at):
        net = self.net
        net.recv(self.sib.at[at], self.sem("s", at))
        core, part, sib = net.core, self.part, self.sib
        half = net.rows // 2
        for y in (1 - net.y, net.y):
            for x in (1 - net.x, net.x):
                value = part[at, core, y, x].astype(jnp.float32) + sib[at, y, x].astype(jnp.float32)
                part[at, core, y, x] = value.astype(jnp.bfloat16)
                if y is not net.y and x is not net.x:
                    diagonal = part.at[at, core, y, x]
                    net.send(diagonal.at[pl.ds(0, half)], self.far.at[at, 0], net.beside, self.sem("f0", at))
                    net.send(diagonal.at[pl.ds(half, half)], self.far.at[at, 1], net.across, self.sem("f1", at))

    def third(self, at):
        net, part, far = self.net, self.part, self.far
        half = net.rows // 2
        for which, y, x, first, to in (
            (0, 1 - net.y, net.x, 0, net.across), (1, net.y, 1 - net.x, half, net.beside),
        ):
            net.recv(far.at[at, which], self.sem(f"f{which}", at))
            rows = pl.ds(first, half)
            value = part[at, net.core, y, x, rows, :].astype(jnp.float32) + far[at, which].astype(jnp.float32)
            part[at, net.core, y, x, rows, :] = value.astype(jnp.bfloat16)
            net.send(part.at[at, net.core, y, x], self.side.at[at, which], to, self.sem("p", at))

    def plane_total(self, at):
        net = self.net
        net.recv(self.side.at[at], self.sem("p", at))
        total = self.part[at, net.core, net.y, net.x].astype(jnp.float32)
        return total + self.side[at, 0].astype(jnp.float32) + self.side[at, 1].astype(jnp.float32)


def stack_rows(rows):
    return jnp.concatenate(rows, axis=0)


def smooth_pair(v):
    t = jnp.tanh(K1 * (v + K2 * v * v * v))
    value = 0.5 * v * (1.0 + t)
    slope = 0.5 * (1.0 + t) + 0.5 * v * (1.0 - t * t) * K1 * (1.0 + 3.0 * K2 * v * v)
    return value, slope


def sigmoid(v):
    return 1.0 / (1.0 + jnp.exp(-v))


def softplus_exact(d):
    u = jnp.exp(-jnp.abs(d))
    r = u / (2.0 + u)
    q = r * r
    series = 1.0 / 15.0
    for k in (13, 11, 9, 7, 5, 3, 1):
        series = series * q + 1.0 / k
    return jnp.maximum(d, 0.0) + 2.0 * r * series


def minus_expm1(v):
    series = 1.0 / 362880.0
    for k in (40320.0, 5040.0, 720.0, 120.0, 24.0, 6.0, 2.0, 1.0):
        series = series * v + 1.0 / k
    return jnp.where(v > -0.5, -v * series, 1.0 - jnp.exp(v))


class Docs:
    def __init__(self, lengths, first, count, before=0):
        position = first - before + lax.broadcasted_iota(jnp.int32, (count, 1), 0)
        self.opening, self.closing = [], []
        start_of = jnp.zeros((count, 1), jnp.int32)
        start = jnp.int32(0)
        for e in range(lengths.shape[0]):
            end = start + lengths[e]
            owner = (position >= start) & (position < end)
            start_of = jnp.where(owner, start, start_of)
            self.opening.append((position == start).astype(jnp.float32))
            self.closing.append((position == end - 1).astype(jnp.float32))
            start = end
        self.offset = position - start_of
        self.keep = (self.offset > 0).astype(jnp.float32)

    def valid(self, k):
        return (self.offset >= k).astype(jnp.float32)


def prefix(a, b, count):
    row = lax.broadcasted_iota(jnp.int32, a.shape, 0)
    k = 1
    while k < count:
        inside = row >= k
        a_far = jnp.where(inside, pltpu.roll(a, k, 0), 1.0)
        b_far = jnp.where(inside, pltpu.roll(b, k, 0), 0.0)
        b = a * b_far + b
        a = a * a_far
        k *= 2
    return a, b


def suffix(a, b, count):
    row = lax.broadcasted_iota(jnp.int32, a.shape, 0)
    k = 1
    while k < count:
        inside = row < count - k
        a_far = jnp.where(inside, pltpu.roll(a, count - k, 0), 1.0)
        b_far = jnp.where(inside, pltpu.roll(b, count - k, 0), 0.0)
        b = a * b_far + b
        a = a * a_far
        k *= 2
    return a, b


def coefficient_parts(rate_pre, inlet_pre, decay):
    rate = sigmoid(rate_pre)
    inlet = sigmoid(inlet_pre)
    sp = softplus_exact(decay)
    log_decay = -8.0 * rate * sp
    factor = jnp.exp(log_decay)
    scale = jnp.sqrt(minus_expm1(2.0 * log_decay))
    return rate, inlet, sp, log_decay, factor, scale


def opening_rows(docs, init):
    total = docs.opening[0] * init[0:1]
    for e in range(1, len(docs.opening)):
        total = total + docs.opening[e] * init[e : e + 1]
    return total


def pack_gain(row):
    tiles = [row[:, i * 128 : (i + 1) * 128] for i in range(row.shape[1] // 128)]
    return jnp.concatenate([stack_rows(tiles[i : i + 8]) for i in range(0, len(tiles), 8)], axis=1)


def norm_back(values, gain, grad):
    r = lax.rsqrt(jnp.mean(values * values, axis=-1, keepdims=True) + EPS)
    u = grad * gain
    to_values = r * u - values * (r * r * r) * jnp.mean(u * values, axis=-1, keepdims=True)
    to_gain = jnp.sum(grad * values * r, axis=0, keepdims=True)
    return to_values, to_gain


def unit(size):
    row = lax.broadcasted_iota(jnp.int32, (size, size), 0)
    column = lax.broadcasted_iota(jnp.int32, (size, size), 1)
    return jnp.where(row == column, 1.0, 0.0).astype(jnp.bfloat16)


RIM = 16


def block_kernel(sizes, names, *refs):
    n_seq, n_ch, rows, d, slots, bw, width, sl = sizes
    r = types.SimpleNamespace(**dict(zip(names, refs)))
    bf, f32 = jnp.bfloat16, jnp.float32
    net = Net(n_seq, n_ch, rows, r.send_sems, r.recv_sems, r.local_sems)
    s, c, x, y, z, core, n_z = net.s, net.c, net.x, net.y, net.z, net.core, net.n_z
    count, wide, tokens = rows * n_ch, slots * bw, rows * n_ch * n_seq
    n_taps = r.taps_v.shape[1]
    mine = net.block(z, x, y, core)
    seq_peers = [(net.s_to[k], c) for k in range(1, n_seq)]
    rim_peers = [(net.s_to[k], (c + i) % n_ch) for k in (1, n_seq - 1) for i in range(1, n_ch)]
    peers = seq_peers + rim_peers + [net.sibling, net.across]
    net.greet(peers)
    loads = {}
    cuts = dict(gelu_w=4, recur_w=4, out_w=4)

    def load_halves(name, dst):
        src, size = getattr(r, name), dst.shape[2]
        loads[name] = [net.local(src.at[:, pl.ds(i * size, size)], dst.at[i]) for i in range(2)]

    def load(name, n):
        src, dst = getattr(r, name), getattr(r, name + "_v")
        if n == 1:
            loads[name] = [net.local(src, dst)]
            return
        size = src.shape[0] // n
        loads[name] = [
            net.local(src.at[pl.ds(i * size, size)], dst.at[pl.ds(i * size, size)])
            for i in range(n)
        ]

    def loaded(name):
        for copy in loads.pop(name):
            copy.wait()

    load("stream", 1)
    load("mix_gain", 1)
    load_halves("gate_w", r.give)
    load("cot", 1)
    load_halves("up_w", r.take)
    for name in ("gelu_w", "recur_w", "taps", "bias", "rate_w", "rate_b",
                 "inlet_w", "inlet_b", "decay", "init", "out_w", "ffn_gain"):
        load(name, cuts.get(name, 1))

    own_cols = pl.ds(pl.multiple_of(s * width, width), width)
    own_count = pl.ds(pl.multiple_of(s * count, count), count)
    own_slice = pl.ds(pl.multiple_of(s * sl, sl), sl)
    local = []

    loaded("stream")
    loaded("mix_gain")
    values = r.stream_v[...].astype(f32)
    scale = lax.rsqrt(jnp.mean(values * values, axis=-1, keepdims=True) + EPS)
    mix_rows = pl.ds(pl.multiple_of(RIM + c * rows, 16), rows)
    r.mix[mix_rows, :] = (values * scale * r.mix_gain_v[...][None, :]).astype(bf)

    loaded("cot")
    r.cfull[pl.ds(mine, rows), :] = r.cot_v[...]

    def turn(a, src):
        half = src.shape[2]
        for i in range(2 * half // 256):
            at = i * 256 % half
            r.turned[a, i * 256 : (i + 1) * 256, :] = contract_first(
                src[i * 256 // half, :, at : at + 256], unit(src.shape[1])
            ).astype(bf)

    net.meet(peers)

    def mix_of(cc):
        return r.mix.at[pl.ds(pl.multiple_of(RIM + cc * rows, 16), rows)]

    last, first = r.mix.at[pl.ds(count, RIM)], r.mix.at[pl.ds(0, RIM)]
    net.ch_gather_start(mix_of, "mix")
    for i in range(n_ch):
        net.send(last, first, (net.s_to[1], i), net.sem("rim"), (c == n_ch - 1) & (s < n_seq - 1))

    @pl.when(s == 0)
    def _():
        r.mix[pl.ds(0, RIM), :] = jnp.zeros((RIM, d), bf)

    cots = Spread(net, r.cfull, "cot")
    lows = Spread(net, r.full, "low")
    cots.start()

    pair_width = 2 * width

    def pair_cols(to):
        return pl.ds(pl.multiple_of(to * pair_width, pair_width), pair_width)

    def left_start(a, src):
        r.left[a, z, c] = src[:, pair_cols(z)]
        for at in range(1, n_z):
            to = net.z_of(net.slot(at))
            net.send(src.at[:, pair_cols(to)], r.left.at[a, z, c], net.dev(to, x, y, core), net.sem(("left", a)))

    def left_pass(a):
        net.recv(r.left.at[a, pl.ds(0, n_z - 1), c], net.sem(("left", a)))
        net.ch_gather_start(lambda cc: r.left.at[a, :, cc], ("leftch", a))

    def left_done(a):
        net.ch_gather_finish(lambda cc: r.left.at[a, :, cc], ("leftch", a))

    left_start(0, r.mix.at[mix_rows])

    others = net.nearest()

    def weight_start(a, which=None):
        src = r.turned.at[a] if a < 2 else r.down
        which = others if which is None else which
        for to in which:
            net.send(
                src.at[pl.ds(pl.multiple_of(to * sl, sl), sl)], r.wt.at[a, :, own_cols], (to, c), net.sem(("w", a)),
            )
        if which[-1] is others[-1]:
            local.append(net.local(src.at[own_slice], r.wt.at[a, :, own_cols]))

    def weight_done(a):
        net.recv(r.wt.at[a, :, pl.ds(0, (n_seq - 1) * width)], net.sem(("w", a)))
        local.pop(0).wait()

    loaded("gate_w")
    turn(0, r.give)
    loaded("up_w")
    turn(1, r.take)
    weight_start(0, others[:2])
    for name in [name for name in loads if name != "out_w"]:
        loaded(name)

    net.ch_gather_finish(mix_of, "mix")
    cots.arrive(net.slot(1))
    for i in range(n_ch):
        @pl.when((s > 0) & (c == i))
        def _(i=i):
            net.recv(first, net.sem("rim"))

    docs = Docs(r.lengths, s * count, count)
    keep = docs.keep
    ends_a, ends_b = [], []
    for b in range(slots):
        cols = pl.ds(b * bw, bw)
        rowsof = r.mix[...]
        r.gelu[:, cols] = jnp.dot(rowsof[RIM:], r.gelu_w_v[:, cols], preferred_element_type=f32)
        recur = jnp.dot(rowsof, r.recur_w_v[:, cols], preferred_element_type=f32).astype(bf)
        r.recur[:, cols] = recur
        recur = recur.astype(f32)
        conv_pre = r.bias_v[b : b + 1, :]
        for k in range(n_taps):
            conv_pre = conv_pre + r.taps_v[b, k : k + 1, :] * recur[RIM - k : RIM - k + count] * docs.valid(k)
        conv_low = conv_pre.astype(bf)
        r.conv[:, cols] = conv_low
        rate_pre = jnp.dot(conv_low, r.rate_w_v[b], preferred_element_type=f32) + r.rate_b_v[b : b + 1, :]
        inlet_pre = jnp.dot(conv_low, r.inlet_w_v[b], preferred_element_type=f32) + r.inlet_b_v[b : b + 1, :]
        r.rate_pre[:, cols] = rate_pre
        r.inlet_pre[:, cols] = inlet_pre
        rate, inlet, sp, log_decay, factor, scale = coefficient_parts(rate_pre, inlet_pre, r.decay_v[b : b + 1, :])
        source = scale * inlet * conv_low.astype(f32) + (1.0 - keep) * factor * opening_rows(docs, r.init_v[:, cols])
        total, part = prefix(keep * factor, source, count)
        r.scan_a[:, cols] = total
        r.scan_b[:, cols] = part
        ends_a.append(total[count - 1 : count])
        ends_b.append(part[count - 1 : count])

    def exchange(summary, pieces, tag):
        summary[s] = stack_rows(pieces + [jnp.zeros((8 - 2 * slots, bw), f32)])
        for k in range(1, n_seq):
            net.send(summary.at[s], summary.at[s], (net.s_to[k], c), net.sem(tag))

    def exchanged(summary, tag):
        net.recv(summary.at[pl.ds(0, n_seq - 1)], net.sem(tag))

    exchange(r.summary, ends_a + ends_b, "sum")
    weight_start(0, others[2:])
    cots.relay(0)
    cots.arrive(net.slot(2))
    loaded("out_w")
    exchanged(r.summary, "sum")
    enter = jnp.zeros((slots, bw), f32)
    for q in range(n_seq - 1):
        after = r.summary[q, 0:slots] * enter + r.summary[q, slots : 2 * slots]
        enter = jnp.where(s > q, after, enter)
    finals = []
    for b in range(slots):
        cols = pl.ds(b * bw, bw)
        live = jnp.where(r.counts[0] > b, 1.0, 0.0)
        state = r.scan_b[:, cols] + r.scan_a[:, cols] * enter[b : b + 1]
        r.state[:, cols] = state
        value, _ = smooth_pair(r.gelu[:, cols])
        r.gath[0, z, :, cols] = (value * state * live).astype(bf)
        ends = [jnp.sum(mark * state, axis=0, keepdims=True) * live for mark in docs.closing]
        finals.append(stack_rows(ends + [jnp.zeros((8 - len(ends), bw), f32)]))

    def branch_tile(i, _):
        cols = pl.ds(pl.multiple_of(i * TILE, TILE), TILE)
        value = jnp.dot(r.gath[0, z], r.out_w_v[:, cols], preferred_element_type=f32)
        for cc in range(n_ch):
            r.part[cc % 2, cc // 2, :, cols] = value[cc * rows : (cc + 1) * rows]
        return 0

    lax.fori_loop(0, d // TILE, branch_tile, 0)
    middle = r.stream_v[...].astype(f32) + net.ch_sum(r.part, r.mid, r.ylow, r.yfar, "branch")
    scale = lax.rsqrt(jnp.mean(middle * middle, axis=-1, keepdims=True) + EPS)
    r.full[pl.ds(mine, rows), :] = (middle * scale * r.ffn_gain_v[...][None, :]).astype(bf)
    r.middle[...] = middle

    def gather_start(a):
        net.chain_start(r.gath.at[a, z], r.gath.at[a, z], ("g", a))

    def gather_arrive(a, at):
        slot = net.slot(at)
        net.chain_arrive(r.gath.at[a, net.z_of(slot)], slot, ("g", a))

    def gather_product(a):
        right = r.gath[a].reshape(n_z * count, wide)
        for which, there in ((0, 1 - x), (1, x)):
            half = r.left[1 if a == 0 else 0, :, :, :, pl.ds(pl.multiple_of(there * width, width), width)]
            half = half.reshape(n_z * count, width)
            value = contract_first(right, half) if a == 0 else contract_first(half, right)
            if which == 0:
                ref = r.give_out if a == 0 else r.give.at[a - 1]
                ref[...] = value.astype(bf)
                net.send(ref, r.took_out if a == 0 else r.took.at[a - 1], net.beside, net.sem(("take", a)))
            elif a == 0:
                r.keep_out_v[...] = value
                local.append(net.local(r.keep_out_v, r.keep_out))
            else:
                r.keep_v[a - 1] = value
                local.append(net.local(r.keep_v.at[a - 1], r.keep.at[a - 1]))

    def gather_done(a):
        net.recv(r.took_out if a == 0 else r.took.at[a - 1], net.sem(("take", a)))

    lows.start()
    weight_start(1, others[:2])
    cots.relay(net.slot(1))
    lows.relay(0)
    lows.arrive(net.slot(1))
    weight_start(1, others[2:4])
    cots.relay(net.slot(2))
    lows.arrive(net.slot(2))
    cots.arrive(net.slot(3))
    weight_start(1, others[4:])
    lows.relay_far(0)
    lows.relay(net.slot(1))
    lows.relay(net.slot(2))
    lows.arrive(net.slot(3))
    weight_start(2)
    gather_start(0)
    group = n_ch * 2 * rows

    def chunk(at):
        return pl.ds(pl.multiple_of(net.z_of(net.slot(at)) * group, group), group)

    weight_done(0)
    weight_done(1)

    def forward(at):
        lows.done(net.slot(at))
        here = chunk(at)
        gate = contract_last(r.full[here, :], r.wt[0])
        up = contract_last(r.full[here, :], r.wt[1])
        value, slope = smooth_pair(gate)
        r.value[here, :] = value
        r.slope[here, :] = up * slope
        r.hid[here, :] = (value * up).astype(bf)

    lows.relay_far(net.slot(1))
    forward(0)
    lows.relay_far(net.slot(2))
    lows.relay(net.slot(3))
    forward(1)
    cots.relay(net.slot(3))
    forward(2)
    lows.relay_far(net.slot(3))
    for at in range(n_z):
        cots.relay_far(net.slot(at))
    forward(3)
    for at in range(n_z):
        cots.done(net.slot(at))

    def weight_grad(a, left, right):
        def tile(i, _):
            cols = pl.ds(pl.multiple_of(i * TILE, TILE), TILE)
            r.dwl[a, :, cols] = contract_first(left[...], right[:, cols]).astype(bf)
            return 0

        lax.fori_loop(0, d // TILE, tile, 0)

    def weight_grad_send(a, which=None):
        which = others if which is None else which
        for to in which:
            cols = pl.ds(pl.multiple_of(to * width, width), width)
            net.send(r.dwl.at[a, :, cols], r.dw.at[a, own_slice], (to, c), net.sem(("dw", a)))
        if which[-1] is others[-1]:
            local.append(net.local(r.dwl.at[a, :, own_cols], r.dw.at[a, own_slice]))

    def weight_grad_done(a):
        net.recv(r.dw.at[a, pl.ds(0, (n_seq - 1) * sl)], net.sem(("dw", a)))

    weight_grad(2, r.hid, r.cfull)
    weight_done(2)
    weight_grad_send(2)

    def spread_out(ref, at, value, cols):
        value = value.astype(bf)
        for xx in range(2):
            for yy in range(2):
                for cc in range(2):
                    row = (xx * 4 + yy * 2 + cc) * rows
                    ref[at, cc, yy, xx, :, cols] = value[row : row + rows]

    def backward(at):
        here = chunk(at)
        grad = contract_last(r.cfull[here, :], r.wt[2])
        r.gat[here, :] = (grad * r.slope[here, :]).astype(bf)
        r.upg[here, :] = (grad * r.value[here, :]).astype(bf)

        def tile(i, _):
            cols = pl.ds(pl.multiple_of(i * TILE, TILE), TILE)
            value = jnp.dot(r.gat[here, :], r.wt[0, :, cols], preferred_element_type=f32)
            value = value + jnp.dot(r.upg[here, :], r.wt[1, :, cols], preferred_element_type=f32)
            spread_out(r.npart, at, value, cols)
            return 0

        lax.fori_loop(0, d // TILE, tile, 0)

    def output(at):
        here = chunk(at)

        def tile(i, _):
            cols = pl.ds(pl.multiple_of(i * TILE, TILE), TILE)
            value = jnp.dot(r.hid[here, :], r.wt[2, :, cols], preferred_element_type=f32)
            spread_out(r.opart, at, value, cols)
            return 0

        lax.fori_loop(0, d // TILE, tile, 0)

    def norm_step(k):
        net.chain_sum(k, norms.term, (r.oup, r.odown), add_into, 2)

    def out_step(k):
        net.chain_sum(k, outs.term, (r.oup, r.odown), add_into, 0)

    norms = CollectEven(net, r.npart, r.nsib, r.nfar, r.nside, "norm")
    outs = Collect(net, r.opart, r.osib, r.ofar, r.oside, "out")
    backward(3)
    norms.first(3)
    backward(2)
    norms.first(2)
    norms.second(3)
    backward(1)
    norms.first(1)
    norms.second(2)
    norms.third(3)
    backward(0)
    norms.first(0)
    norms.second(1)
    norms.third(2)
    norms.fourth(3)
    norm_step(3)
    norms.second(0)
    output(3)
    output(2)
    norms.third(1)
    norms.fourth(2)
    norm_step(2)
    output(1)
    output(0)
    norms.third(0)
    norms.fourth(1)
    norm_step(1)
    for at in (3, 2, 1, 0):
        outs.first(at)
    gather_arrive(0, 1)
    weight_grad(0, r.gat, r.full)
    weight_grad(1, r.upg, r.full)
    r.sgrad_v[...] = norms.fourth(0)
    left_pass(0)
    gather_arrive(0, 2)
    net.chain_sum_last((r.oup, r.odown), add_into, r.sgrad_v, 2)
    nfg = r.sgrad_v[...]

    to_middle, ffn_part = norm_back(r.middle[...], r.ffn_gain_v[...][None, :], nfg)
    middle_grad = r.cot_v[...].astype(f32) + to_middle
    r.sgrad_v[...] = middle_grad
    r.branch[c] = middle_grad.astype(bf)
    net.ch_gather_start(lambda cc: r.branch.at[cc], "bgrad")
    left_start(1, r.branch.at[c])
    weight_grad_send(0, others[:3])
    for at in (3, 2, 1, 0):
        outs.second(at)
    n_docs = r.finals_v.shape[0]
    spare = jnp.concatenate([ffn_part, jnp.zeros((1, (8 - n_docs) * wide - d), f32)], axis=1)
    spare = [spare[:, i * wide : (i + 1) * wide] for i in range(8 - n_docs)]
    r.early[n_z] = stack_rows([jnp.concatenate(finals, axis=1)[:n_docs]] + spare)
    net.send(r.early.at[n_z], r.early_pair, net.beside, net.sem("pair", 0, 2))
    net.ch_gather_finish(lambda cc: r.branch.at[cc], "bgrad")

    ahead_docs = Docs(r.lengths, s * count, count + RIM)
    row = lax.broadcasted_iota(jnp.int32, (count, bw), 0)
    heads_a, heads_b = [], []
    for b in range(slots):
        cols = pl.ds(b * bw, bw)
        live = jnp.where(r.counts[0] > b, 1.0, 0.0)
        product_grad = contract_last(r.branch[...].reshape(count, d), r.out_w_v[b * bw : (b + 1) * bw, :])
        value, slope = smooth_pair(r.gelu[:, cols])
        r.gath[1, z, :, cols] = (product_grad * r.state[:, cols] * live * slope).astype(bf)
        rate, inlet, sp, log_decay, factor, scale = coefficient_parts(r.rate_pre[:, cols], r.inlet_pre[:, cols], r.decay_v[b : b + 1, :])
        carry = keep * factor
        following = jnp.where(row < count - 1, pltpu.roll(carry, count - 1, 0), 1.0)
        total, part = suffix(following, product_grad * value * live, count)
        r.scan_a[:, cols] = total
        r.scan_b[:, cols] = part
        heads_a.append(carry[0:1] * total[0:1])
        heads_b.append(carry[0:1] * part[0:1])
    exchange(r.summary_back, heads_a + heads_b, "sumback")

    gather_start(1)
    gather_arrive(0, 3)
    weight_grad_send(0, others[3:4])
    exchanged(r.summary_back, "sumback")

    net.recv(r.early_pair, net.sem("pair", 0, 2))
    r.early[z] = r.early[n_z] + r.early_pair[...]
    for k in range(1, n_z):
        to = net.z_of(k)
        net.send(r.early.at[z], r.early.at[z], net.dev(to, x, y, core), net.sem(("vec", 0)))
    enter_back = jnp.zeros((slots, bw), f32)
    for q in range(n_seq - 1, 0, -1):
        after = r.summary_back[q, 0:slots] * enter_back + r.summary_back[q, slots : 2 * slots]
        enter_back = jnp.where(s < q, after, enter_back)
    vec = []
    for b in range(slots):
        cols = pl.ds(b * bw, bw)
        adjoint = r.scan_b[:, cols] + r.scan_a[:, cols] * enter_back[b : b + 1]
        previous = jnp.where(row > 0, pltpu.roll(r.state[:, cols], 1, 0), enter[b : b + 1])
        decay = r.decay_v[b : b + 1, :]
        rate, inlet, sp, log_decay, factor, scale = coefficient_parts(r.rate_pre[:, cols], r.inlet_pre[:, cols], decay)
        conv_low = r.conv[:, cols]
        conv = conv_low.astype(f32)
        init_rows = opening_rows(docs, r.init_v[:, cols])
        log_grad = adjoint * (
            factor * (keep * previous + (1.0 - keep) * init_rows) - inlet * conv * jnp.exp(2.0 * log_decay) / scale
        )
        rate_low = (log_grad * (-8.0 * sp) * rate * (1.0 - rate)).astype(bf)
        direct = adjoint * scale
        inlet_low = (direct * conv * inlet * (1.0 - inlet)).astype(bf)
        decay_row = jnp.sum(log_grad * (-8.0 * rate), axis=0, keepdims=True) * sigmoid(decay)
        back = direct * inlet + contract_last(rate_low, r.rate_w_v[b]) + contract_last(inlet_low, r.inlet_w_v[b])
        r.cgrad[0:count, cols] = back.astype(bf)
        for a, low in enumerate((rate_low, inlet_low)):
            part = contract_first(conv_low, low).astype(bf)
            r.gates[a, b] = part.reshape(r.gates.shape[2:])
        vec.append([
            jnp.sum(rate_low.astype(f32), axis=0, keepdims=True),
            jnp.sum(inlet_low.astype(f32), axis=0, keepdims=True),
            decay_row,
        ])
    rim = r.cgrad.at[pl.ds(count, RIM)]
    net.send(r.cgrad.at[pl.ds(0, RIM)], rim, (net.s_to[n_seq - 1], c), net.sem("rimback"), s > 0)

    @pl.when(s == n_seq - 1)
    def _():
        r.cgrad[pl.ds(count, RIM), :] = jnp.zeros((RIM, wide), bf)

    net.send(r.gates.at[:, :, :, 1 - x], r.gates_x, net.beside, net.sem("gatesx"))
    gather_arrive(1, 1)
    weight_grad_send(0, others[4:])

    @pl.when(s < n_seq - 1)
    def _():
        net.recv(rim, net.sem("rimback"))

    vectors = []
    for b in range(slots):
        cols = pl.ds(b * bw, bw)
        grad = r.cgrad[:, cols].astype(f32)
        own = grad[:count]
        recur = r.recur[:, cols].astype(f32)
        total = jnp.zeros((count, bw), f32)
        tap_rows = []
        for k in range(n_taps):
            tap_rows.append(jnp.sum(own * recur[RIM - k : RIM - k + count] * docs.valid(k), axis=0, keepdims=True))
            total = total + r.taps_v[b, k : k + 1, :] * grad[k : k + count] * ahead_docs.valid(k)[k : k + count]
        r.gath[2, z, :, cols] = total.astype(bf)
        vectors.append(stack_rows(tap_rows + [jnp.sum(own, axis=0, keepdims=True)] + vec[b]))
    gather_start(2)
    for at in (3, 2, 1, 0):
        outs.third(at)

    def norm_tile(i, _):
        cols = pl.ds(pl.multiple_of(i * TILE, TILE), TILE)
        value = contract_last(r.gath[1, z], r.gelu_w_v[cols, :]) + contract_last(r.gath[2, z], r.recur_w_v[cols, :])
        for cc in range(n_ch):
            r.part[cc % 2, cc // 2, :, cols] = value[cc * rows : (cc + 1) * rows]
        return 0

    lax.fori_loop(0, d // TILE, norm_tile, 0)
    gather_arrive(1, 2)
    left_pass(1)
    left_done(0)
    norm_grad = net.ch_sum(r.part, r.mid, r.ylow, r.yfar, "norm")
    to_stream, mix_part = norm_back(r.stream_v[...].astype(f32), r.mix_gain_v[...][None, :], norm_grad)
    r.sgrad_v[...] += to_stream
    local.append(net.local(r.sgrad_v, r.sgrad))
    r.late[...] = jnp.concatenate(vectors + [pack_gain(mix_part)], axis=1)
    net.send(r.late, r.late_pair, net.beside, net.sem("pair", 1, 2))
    net.recv(r.gates_x, net.sem("gatesx"))

    def gate_step(k):
        net.chain_sum(k, lambda there: r.gates.at[:, :, there, x], (r.gates_up, r.gates_down), add_into, 1)

    def gate_add(i, _):
        for a in range(2):
            for b in range(slots):
                value = r.gates[a, b, i, x].astype(f32) + r.gates_x[a, b, i].astype(f32)
                r.gates[a, b, i, x] = value.astype(bf)
        return 0

    lax.fori_loop(0, n_z, gate_add, 0)
    gather_arrive(2, 1)
    weight_grad_send(1, others[:3])
    gate_step(3)
    net.recv(r.late_pair, net.sem("pair", 1, 2))
    late = r.late[...] + r.late_pair[...]
    piece = bw // n_seq
    gap = jnp.zeros((8, r.late_out.shape[2] - (late.shape[1] - wide) - 2 * slots * piece), f32)
    for q in range(n_z):
        cuts_at = [b * bw + 2 * q * piece for b in range(slots)]
        r.late_out[q] = jnp.concatenate([late[:, at : at + 2 * piece] for at in cuts_at] + [gap, late[:, wide:]], axis=1)
    r.late_in[z] = r.late_out[z]
    for k in range(1, n_z):
        to = net.z_of(k)
        net.send(r.late_out.at[to], r.late_in.at[z], net.dev(to, x, y, core), net.sem(("vec", 1)))
    left_done(1)
    gather_product(0)
    gather_arrive(1, 3)
    gather_arrive(2, 2)
    for at in (3, 2, 1):
        outs.fourth(at)
    r.middle[...] += outs.fourth(0)
    out_step(3)
    gate_step(2)
    weight_grad_send(1, others[3:5])
    gather_product(1)
    out_step(2)
    gate_step(1)
    weight_grad_send(1, others[5:])
    for a, ref in enumerate((r.early, r.late_in)):
        net.recv(ref.at[pl.ds(0, n_z - 1)], net.sem(("vec", a)))
    early, late = r.early[0], r.late_in[0]
    for q in range(1, n_z):
        early, late = early + r.early[q], late + r.late_in[q]
    r.shared[c] = jnp.concatenate([early, late[:, late.shape[1] - d // 8 :]], axis=1)
    net.ch_gather_start(lambda cc: r.shared.at[cc], "shared")
    for b in range(slots):
        at = 2 * b * piece
        r.small_v[b] = jnp.where(x == 0, late[:, at : at + piece], late[:, at + piece : at + 2 * piece])
    local.append(net.local(r.small_v, r.small))
    gather_arrive(2, 3)
    out_step(1)
    gather_product(2)
    r.gate_out_v[...] = r.gates[:, :, z, x].astype(f32)
    net.chain_sum_last((r.gates_up, r.gates_down), add_into, r.gate_out_v, 1)
    local.append(net.local(r.gate_out_v, r.gate_out))
    net.ch_gather_finish(lambda cc: r.shared.at[cc], "shared")
    total = r.shared[0]
    for cc in range(1, n_ch):
        total = total + r.shared[cc]
    for cc in range(n_ch):
        r.finals_v[:, cc * wide : (cc + 1) * wide] = r.shared[cc, 0:n_docs, 0:wide]
    local.append(net.local(r.finals_v, r.finals))
    for i in range(d // 128):
        at, line = i * 128 % wide, n_docs + i * 128 // wide
        r.gains_v[0, i : i + 1, :] = total[line : line + 1, at : at + 128]
    for i in range(d // 1024):
        r.gains_v[1, i * 8 : (i + 1) * 8, :] = total[:, wide + i * 128 : wide + (i + 1) * 128]
    local.append(net.local(r.gains_v, r.gains))
    net.chain_sum_last((r.oup, r.odown), add_into, r.middle, 0)
    r.mixed_v[...] = r.middle[...].astype(bf)
    local.append(net.local(r.mixed_v, r.mixed))
    for a in (2, 0, 1):
        weight_grad_done(a)
    for a in range(3):
        gather_done(a)
    for copy in local:
        copy.wait()
    net.drain()


def finish_kernel(names, *refs):
    r = types.SimpleNamespace(**dict(zip(names, refs)))
    f32 = jnp.float32
    used = []

    def sem():
        used.append(0)
        return r.sems.at[len(used) - 1]

    def copy(src, dst):
        start = pltpu.make_async_copy(src, dst, sem())
        start.start()
        return start

    incoming = {}
    for name, index in (("dw", 0), ("dw", 1), ("dw", 2), ("keep", 0), ("took", 0), ("keep", 1), ("took", 1)):
        incoming[name, index] = copy(getattr(r, name).at[index], getattr(r, name + "_v").at[index])
    for name in ("keep_out", "took_out", "gains", "gate_out", "small", "finals", "mixed", "sgrad"):
        incoming[name] = copy(getattr(r, name), getattr(r, name + "_v"))
    leaving = []

    def leave(name):
        leaving.append(copy(getattr(r, name + "_v"), getattr(r, name)))

    for a, name in enumerate(("gate_wg", "up_wg")):
        incoming["dw", a].wait()
        ref = getattr(r, name + "_v")
        for i in range(ref.shape[1] // 256):
            ref[:, i * 256 : (i + 1) * 256] = contract_first(r.dw_v[a, i * 256 : (i + 1) * 256, :], unit(256))
        leave(name)
    incoming["dw", 2].wait()
    r.down_wg_v[...] = r.dw_v[2].astype(f32)
    leave("down_wg")
    for a, name in enumerate(("gelu_wg", "recur_wg")):
        incoming["keep", a].wait()
        incoming["took", a].wait()
        getattr(r, name + "_v")[...] = r.keep_v[a] + r.took_v[a].astype(f32)
        leave(name)
    for name in ("keep_out", "took_out", "gains", "gate_out", "small", "finals", "mixed", "sgrad"):
        incoming[name].wait()
    r.out_wg_v[...] = r.keep_out_v[...] + r.took_out_v[...].astype(f32)
    leave("out_wg")
    leaving += [
        copy(r.finals_v, r.finals_o), copy(r.mixed_v, r.mixed_o), copy(r.sgrad_v, r.sgrad_o),
        copy(r.gains_v.at[0], r.ffn_o), copy(r.gains_v.at[1], r.mix_o), copy(r.gate_out_v.at[0], r.rate_o),
        copy(r.gate_out_v.at[1], r.inlet_o),
    ]
    n_taps = r.taps_o_v.shape[1]
    for b in range(r.small_v.shape[0]):
        for k in range(n_taps):
            r.taps_o_v[b, k : k + 1, :] = r.small_v[b, k : k + 1, :]
        for k, name in enumerate(("bias_o", "rateb_o", "inletb_o", "decay_o")):
            getattr(r, name + "_v")[b : b + 1, :] = r.small_v[b, n_taps + k : n_taps + k + 1, :]
    for name in ("taps_o", "bias_o", "rateb_o", "inletb_o", "decay_o"):
        leave(name)
    for start in leaving:
        start.wait()


def gathered_body(
    stream, cotangent, mix_gain, gelu_weight, recur_weight, conv_taps, conv_bias, rate_weight, rate_bias, inlet_weight,
    inlet_bias, decay_param, init_states, out_weight, ffn_gain, gate_weight, up_weight, down_weight, doc_lengths, block_counts,
):
    n_seq, n_ch = lax.axis_size(SEQ), lax.axis_size(CH)
    rows, d = stream.shape
    slots, bw = conv_bias.shape
    width, hidden = gate_weight.shape
    sl = hidden // n_seq
    n_z = n_seq // 2
    count, wide, tokens = rows * n_ch, slots * bw, rows * n_ch * n_seq
    piece = bw // n_seq
    n_taps, n_docs = conv_taps.shape[0], doc_lengths.shape[0]
    bf, f32 = jnp.bfloat16, jnp.float32
    vmem = pl.BlockSpec(memory_space=pltpu.VMEM)
    smem = pl.BlockSpec(memory_space=pltpu.SMEM)
    anywhere = pl.BlockSpec(memory_space=pl.ANY)
    inputs = dict(
        stream=stream, cot=cotangent, mix_gain=mix_gain, gelu_w=gelu_weight, recur_w=recur_weight, taps=conv_taps.transpose(1, 0, 2),
        bias=conv_bias, rate_w=rate_weight, rate_b=rate_bias, inlet_w=inlet_weight, inlet_b=inlet_bias, decay=decay_param,
        init=init_states, out_w=out_weight, ffn_gain=ffn_gain, gate_w=gate_weight, up_w=up_weight, down=down_weight,
        lengths=doc_lengths, counts=block_counts,
    )
    places = dict(lengths=smem, counts=smem)
    staged = [name for name in inputs if name not in ("lengths", "counts", "gate_w", "up_w", "down")]
    outputs = dict(
        keep=((2, width, wide), f32), keep_out=((wide, width), f32), took=((2, width, wide), bf), took_out=((wide, width), bf),
        dw=((3, hidden, width), bf),
        finals=((n_docs, wide * n_ch), f32), mixed=((rows, d), bf), sgrad=((rows, d), f32), gains=((2, d // 128, 128), f32),
        gate_out=((2, slots, piece, bw), f32), small=((slots, 8, piece), f32),
    )
    packed = wide + d // 8
    scratch = dict(
        mix=((RIM + count, d), bf), full=((tokens, d), bf), cfull=((tokens, d), bf), turned=((2, hidden, width), bf),
        wt=((3, sl, d), bf), dwl=((3, sl, d), bf), value=((tokens, sl), f32), slope=((tokens, sl), f32),
        hid=((tokens, sl), bf), gat=((tokens, sl), bf), upg=((tokens, sl), bf),
        gelu=((count, wide), f32), recur=((RIM + count, wide), bf), conv=((count, wide), bf), rate_pre=((count, wide), f32),
        inlet_pre=((count, wide), f32), scan_a=((count, wide), f32), scan_b=((count, wide), f32), state=((count, wide), f32),
        gath=((3, n_z, count, wide), bf), left=((2, n_z, n_ch, rows, 2 * width), bf), give=((2, width, wide), bf),
        give_out=((wide, width), bf), take=((2, width, wide), bf), cgrad=((count + RIM, wide), bf), branch=((n_ch, rows, d), bf),
        summary=((n_seq, 8, bw), f32), summary_back=((n_seq, 8, bw), f32),
        part=((2, 2, rows, d), f32), mid=((2, rows, d), f32), ylow=((rows, d), bf), yfar=((rows, d), bf), middle=((rows, d), f32),
        npart=((n_z, 2, 2, 2, rows, d), bf), nsib=((n_z, 2, 2, rows, d), bf), nfar=((n_z, 2, rows // 2, d), bf),
        nside=((n_z, 2, rows, d), bf),
        opart=((n_z, 2, 2, 2, rows, d), bf), osib=((n_z, 2, 2, rows, d), bf), ofar=((n_z, 2, rows, d), bf),
        oside=((n_z, rows, d), bf), oup=((n_z - 1, rows, d), bf), odown=((n_z - 1, rows, d), bf),
        gates=((2, slots, n_z, 2, piece, bw), bf), gates_x=((2, slots, n_z, piece, bw), bf), gates_up=((n_z - 1, 2, slots, piece, bw), bf), gates_down=((n_z - 1, 2, slots, piece, bw), bf),
        early=((n_z + 1, 8, wide), f32), early_pair=((8, wide), f32), late=((8, packed), f32), late_pair=((8, packed), f32),
        late_out=((n_z, 8, 2 * d // 8), f32), late_in=((n_z, 8, 2 * d // 8), f32),
        shared=((n_ch, 8, packed), f32),
    )
    scratch.update({name + "_v": (inputs[name].shape, inputs[name].dtype) for name in staged})
    scratch.update({name + "_v": what for name, what in outputs.items() if name not in ("took", "took_out", "dw")})
    dma = pltpu.SemaphoreType.DMA
    results = pl.pallas_call(
        functools.partial(
            block_kernel, (n_seq, n_ch, rows, d, slots, bw, width, sl),
            list(inputs) + list(outputs) + list(scratch) + ["send_sems", "recv_sems", "local_sems"],
        ),
        out_shape=[jax.ShapeDtypeStruct(*what) for what in outputs.values()],
        in_specs=[places.get(name, anywhere) for name in inputs],
        out_specs=[anywhere] * len(outputs),
        scratch_shapes=[pltpu.VMEM(*what) for what in scratch.values()] + [dma((SEND_SEMS,)), dma((RECV_SEMS,)), dma((LOCAL_SEMS,))],
        compiler_params=pltpu.CompilerParams(collective_id=1, has_side_effects=True, vmem_limit_bytes=VMEM_BYTES),
    )(*inputs.values())
    vector = ((slots, piece), f32)
    ends = dict(
        finals_o=((n_docs, wide * n_ch), f32), mixed_o=((rows, d), bf), sgrad_o=((rows, d), f32), mix_o=((d // 128, 128), f32),
        gelu_wg=((width, wide), f32), recur_wg=((width, wide), f32), taps_o=((slots, n_taps, piece), f32), bias_o=vector,
        rate_o=((slots, piece, bw), f32), rateb_o=vector, inlet_o=((slots, piece, bw), f32), inletb_o=vector, decay_o=vector,
        out_wg=((wide, width), f32), ffn_o=((d // 128, 128), f32), gate_wg=((width, hidden), f32), up_wg=((width, hidden), f32),
        down_wg=((hidden, width), f32),
    )
    direct = ("finals_o", "mixed_o", "sgrad_o", "ffn_o", "mix_o", "rate_o", "inlet_o")
    kept = {name + "_v": outputs[name] for name in outputs}
    kept.update({name + "_v": what for name, what in ends.items() if name not in direct})
    last = pl.pallas_call(
        functools.partial(finish_kernel, list(outputs) + list(ends) + list(kept) + ["sems"]),
        out_shape=[jax.ShapeDtypeStruct(*what) for what in ends.values()],
        in_specs=[anywhere] * len(outputs),
        out_specs=[anywhere] * len(ends),
        scratch_shapes=[pltpu.VMEM(*what) for what in kept.values()] + [pltpu.SemaphoreType.DMA((40,))],
        compiler_params=pltpu.CompilerParams(vmem_limit_bytes=VMEM_BYTES),
    )(*results)
    named = dict(zip(ends, last))
    named["taps_o"] = named["taps_o"].transpose(1, 0, 2)
    named["mix_o"], named["ffn_o"] = named["mix_o"].reshape(d), named["ffn_o"].reshape(d)
    return tuple(named.values())


def solution(mesh):
    in_specs = (
        P((SEQ, CH), None),
        P((SEQ, CH), None),
        P(),
        P(None, CH),
        P(None, CH),
        P(None, CH, None),
        P(CH, None),
        P(CH, None, None),
        P(CH, None),
        P(CH, None, None),
        P(CH, None),
        P(CH, None),
        P(None, CH),
        P(CH, None),
        P(),
        P(SEQ, CH),
        P(SEQ, CH),
        P(CH, SEQ),
        P(),
        P(CH),
    )
    out_specs = (
        P(),
        P((SEQ, CH), None),
        P((SEQ, CH), None),
        P(),
        P(SEQ, CH),
        P(SEQ, CH),
        P(None, CH, SEQ),
        P(CH, SEQ),
        P(CH, SEQ, None),
        P(CH, SEQ),
        P(CH, SEQ, None),
        P(CH, SEQ),
        P(CH, SEQ),
        P(CH, SEQ),
        P(),
        P(SEQ, CH),
        P(SEQ, CH),
        P(CH, SEQ),
    )
    return jax.shard_map(gathered_body if mesh.shape[SEQ] == 8 else body, mesh=mesh, in_specs=in_specs, out_specs=out_specs, check_vma=False)
```

```python
import functools
import math
import types

import jax
import jax.numpy as jnp
from jax import lax
from jax.experimental import pallas as pl
from jax.experimental.pallas import tpu as pltpu
from jax.sharding import PartitionSpec as P

EPS = 1e-06
HIGH = lax.Precision.HIGHEST
MESH = pl.DeviceIdType.MESH
SEQ = "seq"
CH = "ch"
K1 = 0.7978845608028654
K2 = 0.044715
VMEM_BYTES = 63 * 2**20
TILE = 1024
SEND_SEMS = 96
RECV_SEMS = 140
LOCAL_SEMS = 46


def passed_along(shard, axis, by):
    length = lax.axis_size(axis)
    pairs = [(i, i + by) for i in range(length) if 0 <= i + by < length]
    return lax.ppermute(shard, axis, pairs)


def entering_2(shard, axis, combine, identity, reverse):
    length, here = (lax.axis_size(axis), lax.axis_index(axis))
    everything = jax.tree.map(lambda part: lax.all_gather(part, axis), shard)
    start = jax.tree.map(
        lambda part, zero: jnp.broadcast_to(jnp.asarray(zero, part.dtype), part.shape),
        shard,
        identity,
    )

    def turn(k, before):
        at = length - 1 - k if reverse else k
        reached = at > here if reverse else at < here
        new = combine(before, jax.tree.map(lambda part: part[at], everything))
        return jax.tree.map(lambda a, b: jnp.where(reached, a, b), new, before)

    return lax.fori_loop(0, length, turn, start)


def normalize(values, gain):
    return values * lax.rsqrt(jnp.mean(values * values, axis=-1, keepdims=True) + EPS) * gain


def smooth(values):
    return jax.nn.gelu(values, approximate=True)


def affine(earlier, later):
    return (earlier[0] * later[0], later[0] * earlier[1] + later[1])


def doc_view(lengths, first, count):
    ends = jnp.cumsum(lengths)
    starts = ends - lengths
    position = first + jnp.arange(count, dtype=jnp.int32)
    owner = (position[:, None] >= starts[None, :]) & (position[:, None] < ends[None, :])
    start_of = jnp.sum(jnp.where(owner, starts[None, :], 0), axis=1)
    offset = position - start_of
    opening = (owner & (offset[:, None] == 0)).astype(jnp.float32)
    closing = (owner & (position[:, None] == ends[None, :] - 1)).astype(jnp.float32)
    return (offset, opening, closing)


def coefficients(rate_pre, inlet_pre, conv_value, decay, init_rows, keep):
    rate = jax.nn.sigmoid(rate_pre)
    inlet = jax.nn.sigmoid(inlet_pre)
    log_decay = -8.0 * rate * jax.nn.softplus(decay)
    factor = jnp.exp(log_decay)
    scale = jnp.sqrt(-jnp.expm1(2.0 * log_decay))
    carry_factor = keep * factor
    source = scale * inlet * conv_value + (1.0 - keep) * factor * init_rows
    return (carry_factor, source)


def spread(values):
    return lax.all_gather(values, CH, axis=0, tiled=True)


def collect(terms):
    return lax.psum_scatter(terms, CH, scatter_dimension=0, tiled=True)


def contract_last(left, right):
    return lax.dot_general(
        left, right, (((1,), (1,)), ((), ())), preferred_element_type=jnp.float32
    )


def contract_first(left, right):
    return lax.dot_general(
        left, right, (((0,), (0,)), ((), ())), preferred_element_type=jnp.float32
    )


def body(
    stream,
    cotangent,
    mix_gain,
    gelu_weight,
    recur_weight,
    conv_taps,
    conv_bias,
    rate_weight,
    rate_bias,
    inlet_weight,
    inlet_bias,
    decay_param,
    init_states,
    out_weight,
    ffn_gain,
    gate_weight,
    up_weight,
    down_weight,
    doc_lengths,
    block_counts,
):
    slot_count = rate_weight.shape[0]
    block_width = rate_weight.shape[1]
    local_width = slot_count * block_width
    taps = conv_taps.shape[0]
    token_count = stream.shape[0] * lax.axis_size(CH)
    hidden_width = gate_weight.shape[1]
    base = lax.axis_index(SEQ) * token_count
    offset_all, opening, closing = doc_view(doc_lengths, base, token_count + taps - 1)
    offset = offset_all[:token_count]
    opening = opening[:token_count]
    closing = closing[:token_count]
    keep = (offset > 0).astype(jnp.float32)[:, None]
    slot_live = (jnp.arange(slot_count, dtype=jnp.int32) < block_counts[0]).astype(jnp.float32)
    live = jnp.repeat(slot_live, block_width)[None, :]
    taps_flat = conv_taps.reshape(taps, local_width)
    decay_flat = decay_param.reshape(1, local_width)
    stream_float = stream.astype(jnp.float32)
    mix_low = normalize(stream_float, mix_gain).astype(jnp.bfloat16)
    mix_full = spread(mix_low)
    gelu_pre = jnp.dot(mix_full, gelu_weight, preferred_element_type=jnp.float32)
    recur_low = jnp.dot(mix_full, recur_weight, preferred_element_type=jnp.float32).astype(
        jnp.bfloat16
    )
    rim = passed_along(recur_low[token_count - taps + 1 :], SEQ, 1)
    extended = jnp.concatenate([rim, recur_low], axis=0).astype(jnp.float32)
    conv_pre = conv_bias.reshape(1, local_width)
    for tap_index in range(taps):
        valid = (offset >= tap_index).astype(jnp.float32)[:, None]
        lead = taps - 1 - tap_index
        conv_pre = (
            conv_pre + taps_flat[tap_index][None, :] * extended[lead : lead + token_count] * valid
        )
    conv_low = conv_pre.astype(jnp.bfloat16)
    conv_value = conv_low.astype(jnp.float32)
    grouped = conv_low.reshape(token_count, slot_count, block_width)
    rate_pre = (
        jnp.einsum("rsi,sio->rso", grouped, rate_weight, preferred_element_type=jnp.float32)
        + rate_bias[None]
    ).reshape(token_count, local_width)
    inlet_pre = (
        jnp.einsum("rsi,sio->rso", grouped, inlet_weight, preferred_element_type=jnp.float32)
        + inlet_bias[None]
    ).reshape(token_count, local_width)
    init_rows = jnp.dot(opening, init_states, precision=HIGH)
    carry_factor, source = coefficients(
        rate_pre, inlet_pre, conv_value, decay_flat, init_rows, keep
    )
    cumulative, local_state = lax.associative_scan(affine, (carry_factor, source), axis=0)
    summary = (cumulative[-1], local_state[-1])
    entering = entering_2(
        summary, SEQ, affine, (jnp.ones_like(summary[0]), jnp.zeros_like(summary[1])), False
    )
    state_in = entering[1]
    state = local_state + cumulative * state_in[None, :]
    gelu_value = smooth(gelu_pre)
    product_low = (gelu_value * state * live).astype(jnp.bfloat16)
    branch = collect(jnp.dot(product_low, out_weight, preferred_element_type=jnp.float32))
    middle = stream_float + branch
    ffn_low = normalize(middle, ffn_gain).astype(jnp.bfloat16)
    ffn_full = spread(ffn_low)
    stacked = jnp.concatenate([gate_weight, up_weight], axis=1)
    columns = ffn_full
    gate_up = jnp.dot(
        columns,
        lax.all_gather(stacked, SEQ, axis=0, tiled=True),
        preferred_element_type=jnp.float32,
    )
    gate = gate_up[:, :hidden_width]
    upward = gate_up[:, hidden_width:]
    hidden = (smooth(gate) * upward).astype(jnp.bfloat16)
    ffn_terms = jnp.dot(
        hidden,
        lax.all_gather(down_weight, SEQ, axis=1, tiled=True),
        preferred_element_type=jnp.float32,
    )
    mixed_out = (middle + collect(ffn_terms)).astype(jnp.bfloat16)
    out_grad_full = spread(cotangent)
    columns = out_grad_full
    hidden_grad = contract_last(columns, lax.all_gather(down_weight, SEQ, axis=1, tiled=True))
    down_weight_grad = contract_first(hidden, out_grad_full)
    unused, pair_pull = jax.vjp(lambda left, right: smooth(left) * right, gate, upward)
    gate_grad, up_grad = pair_pull(hidden_grad)
    pair_low = jnp.concatenate([gate_grad, up_grad], axis=1).astype(jnp.bfloat16)
    pair_weight_grad = contract_first(ffn_full, pair_low)
    norm_ffn_part = contract_last(pair_low, lax.all_gather(stacked, SEQ, axis=0, tiled=True))
    norm_ffn_grad = collect(norm_ffn_part)
    unused, ffn_norm_pull = jax.vjp(normalize, middle, ffn_gain)
    middle_norm_grad, ffn_gain_part = ffn_norm_pull(norm_ffn_grad)
    middle_grad = cotangent.astype(jnp.float32) + middle_norm_grad
    branch_full = spread(middle_grad.astype(jnp.bfloat16))
    out_weight_grad = contract_first(product_low, branch_full)
    product_grad = contract_last(branch_full, out_weight)
    state_grad = product_grad * gelu_value * live
    unused, gelu_pull = jax.vjp(smooth, gelu_pre)
    gelu_low = gelu_pull(product_grad * state * live)[0].astype(jnp.bfloat16)
    following = jnp.concatenate([carry_factor[1:], jnp.ones_like(carry_factor[:1])], axis=0)
    cum_back, adjoint_local = lax.associative_scan(
        affine, (jnp.flip(following, 0), jnp.flip(state_grad, 0)), axis=0
    )
    cum_back = jnp.flip(cum_back, 0)
    adjoint_local = jnp.flip(adjoint_local, 0)
    summary_back = (carry_factor[0] * cum_back[0], carry_factor[0] * adjoint_local[0])
    arriving = entering_2(
        summary_back,
        SEQ,
        affine,
        (jnp.ones_like(summary_back[0]), jnp.zeros_like(summary_back[1])),
        True,
    )
    adjoint_in = arriving[1]
    adjoint = adjoint_local + cum_back * adjoint_in[None, :]
    previous_state = jnp.concatenate([state_in[None, :], state[:-1]], axis=0)

    def local_coefficients(rate_value, inlet_value, conv_part, decay_value):
        return coefficients(rate_value, inlet_value, conv_part, decay_value, init_rows, keep)

    unused, coefficient_pull = jax.vjp(
        local_coefficients, rate_pre, inlet_pre, conv_value, decay_flat
    )
    rate_grad, inlet_grad, conv_direct, decay_part = coefficient_pull(
        (adjoint * previous_state, adjoint)
    )
    rate_low = rate_grad.astype(jnp.bfloat16).reshape(token_count, slot_count, block_width)
    inlet_low = inlet_grad.astype(jnp.bfloat16).reshape(token_count, slot_count, block_width)
    rate_weight_grad = jnp.einsum(
        "rsi,rso->sio", grouped, rate_low, preferred_element_type=jnp.float32
    )
    inlet_weight_grad = jnp.einsum(
        "rsi,rso->sio", grouped, inlet_low, preferred_element_type=jnp.float32
    )
    rate_bias_grad = jnp.sum(rate_low.astype(jnp.float32), axis=0)
    inlet_bias_grad = jnp.sum(inlet_low.astype(jnp.float32), axis=0)
    conv_back = jnp.einsum(
        "rso,sio->rsi", rate_low, rate_weight, preferred_element_type=jnp.float32
    )
    conv_back = conv_back + jnp.einsum(
        "rso,sio->rsi", inlet_low, inlet_weight, preferred_element_type=jnp.float32
    )
    conv_low_grad = (conv_direct + conv_back.reshape(token_count, local_width)).astype(jnp.bfloat16)
    rim_back = passed_along(conv_low_grad[: taps - 1], SEQ, -1)
    ahead = jnp.concatenate([conv_low_grad, rim_back], axis=0).astype(jnp.float32)
    own_grad = ahead[:token_count]
    recur_grad = jnp.zeros((token_count, local_width), jnp.float32)
    tap_grads = []
    for tap_index in range(taps):
        lead = taps - 1 - tap_index
        valid_here = (offset >= tap_index).astype(jnp.float32)[:, None]
        tap_grads.append(
            jnp.sum(own_grad * extended[lead : lead + token_count] * valid_here, axis=0)
        )
        valid_ahead = (offset_all[tap_index : tap_index + token_count] >= tap_index).astype(
            jnp.float32
        )[:, None]
        recur_grad = (
            recur_grad
            + taps_flat[tap_index][None, :]
            * ahead[tap_index : tap_index + token_count]
            * valid_ahead
        )
    conv_taps_grad = jnp.stack(tap_grads, axis=0).reshape(taps, slot_count, block_width)
    conv_bias_grad = jnp.sum(own_grad, axis=0).reshape(slot_count, block_width)
    recur_low_grad = recur_grad.astype(jnp.bfloat16)
    gelu_weight_grad = contract_first(mix_full, gelu_low)
    recur_weight_grad = contract_first(mix_full, recur_low_grad)
    norm_mix_part = contract_last(gelu_low, gelu_weight) + contract_last(
        recur_low_grad, recur_weight
    )
    norm_mix_grad = collect(norm_mix_part)
    unused, mix_norm_pull = jax.vjp(normalize, stream_float, mix_gain)
    stream_norm_grad, mix_gain_part = mix_norm_pull(norm_mix_grad)
    stream_grad = middle_grad + stream_norm_grad
    finals_local = lax.dot_general(closing, state * live, (((0,), (0,)), ((), ())), precision=HIGH)
    finals_wide = jnp.zeros((finals_local.shape[0], local_width * lax.axis_size(CH)), jnp.float32)
    finals_wide = lax.dynamic_update_slice(
        finals_wide, finals_local, (jnp.int32(0), lax.axis_index(CH) * local_width)
    )
    final_states, mix_gain_grad, ffn_gain_grad = lax.psum(
        (finals_wide, mix_gain_part, ffn_gain_part), (SEQ, CH)
    )
    summed = (
        lax.psum_scatter(gelu_weight_grad, SEQ, scatter_dimension=0, tiled=True),
        lax.psum_scatter(recur_weight_grad, SEQ, scatter_dimension=0, tiled=True),
        lax.psum_scatter(conv_taps_grad, SEQ, scatter_dimension=2, tiled=True),
        lax.psum_scatter(conv_bias_grad, SEQ, scatter_dimension=1, tiled=True),
        lax.psum_scatter(rate_weight_grad, SEQ, scatter_dimension=1, tiled=True),
        lax.psum_scatter(rate_bias_grad, SEQ, scatter_dimension=1, tiled=True),
        lax.psum_scatter(inlet_weight_grad, SEQ, scatter_dimension=1, tiled=True),
        lax.psum_scatter(inlet_bias_grad, SEQ, scatter_dimension=1, tiled=True),
        lax.psum_scatter(
            decay_part.reshape(slot_count, block_width), SEQ, scatter_dimension=1, tiled=True
        ),
        lax.psum_scatter(out_weight_grad, SEQ, scatter_dimension=1, tiled=True),
        lax.psum_scatter(
            pair_weight_grad[:, :hidden_width], SEQ, scatter_dimension=0, tiled=True
        ),
        lax.psum_scatter(
            pair_weight_grad[:, hidden_width:], SEQ, scatter_dimension=0, tiled=True
        ),
        lax.psum_scatter(down_weight_grad, SEQ, scatter_dimension=1, tiled=True),
    )
    return (
        final_states,
        mixed_out,
        stream_grad,
        mix_gain_grad,
        summed[0],
        summed[1],
        summed[2],
        summed[3],
        summed[4],
        summed[5],
        summed[6],
        summed[7],
        summed[8],
        summed[9],
        ffn_gain_grad,
        summed[10],
        summed[11],
        summed[12],
    )


class Net:
    def __init__(self, n_seq, n_ch, rows, send_sems, recv_sems, local_sems):
        self.n_seq, self.n_ch, self.rows = n_seq, n_ch, rows
        self.n_z = n_seq // 2
        self.send_sems, self.recv_sems, self.local_sems = send_sems, recv_sems, local_sems
        self.tags, self.used, self.sent, self.locals = {}, 0, [], 0
        self.s, self.c = lax.axis_index(SEQ), lax.axis_index(CH)
        s, c, n_z = self.s, self.c, self.n_z
        self.z, self.x, self.y, self.core = s // 2, s % 2, c // 2, c % 2
        x, y = self.x, self.y
        self.s_to = [(s + k) % n_seq for k in range(n_seq)]
        self.s_from = [(s + n_seq - k) % n_seq for k in range(n_seq)]
        self.sibling = self.dev(self.z, x, y, 1 - self.core)
        self.across = self.dev(self.z, x, 1 - y, self.core)
        self.beside = self.dev(self.z, 1 - x, y, self.core)
        self.above = self.dev((self.z + 1) % n_z, x, y, self.core)
        self.below = self.dev((self.z + n_z - 1) % n_z, x, y, self.core)

    def nearest(self):
        order = [self.z * 2 + 1 - self.x]
        for at in range(1, self.n_z):
            there = self.z_of(self.slot(at))
            order += [there * 2 + self.x, there * 2 + 1 - self.x]
        return order

    def dev(self, z, x, y, core):
        return (z * 2 + x, y * 2 + core)

    def block(self, z, x, y, core):
        rows = self.rows
        return pl.multiple_of(((z * 2 + x) * self.n_ch + y * 2 + core) * rows, rows)

    def z_of(self, slot):
        return (self.z + self.n_z - slot) % self.n_z

    def slot(self, at):
        if at == 0:
            return 0
        n_z, z = self.n_z, self.z
        low, high = (n_z - 1 - z) // (n_z - 1), z // (n_z - 1)
        inner = (at + 1) // 2 if at % 2 else n_z - at // 2
        return low * (n_z - at) + high * at + (1 - low - high) * inner

    def greet(self, peers):
        barrier = pltpu.get_barrier_semaphore()
        for peer in peers:
            pl.semaphore_signal(barrier, inc=1, device_id=peer, device_id_type=MESH)

    def meet(self, peers):
        pl.semaphore_wait(pltpu.get_barrier_semaphore(), len(peers))

    def sem(self, tag, at=0, size=1):
        if tag not in self.tags:
            self.tags[tag] = self.used
            self.used += size
        return self.recv_sems.at[self.tags[tag] + at]

    def send(self, src, dst, to, sem, when=None):
        size = self.send_sems.shape[0]
        if len(self.sent) >= size:
            self.sent_wait(len(self.sent) - size)
        copy = pltpu.make_async_remote_copy(
            src_ref=src, dst_ref=dst, send_sem=self.send_sems.at[len(self.sent) % size], recv_sem=sem,
            device_id=to, device_id_type=MESH,
        )
        if when is None:
            copy.start()
        else:
            @pl.when(when)
            def _():
                copy.start()
        self.sent.append((copy, when))

    def sent_wait(self, at):
        if self.sent[at] is None:
            return
        copy, when = self.sent[at]
        self.sent[at] = None
        if when is None:
            copy.wait_send()
        else:
            @pl.when(when)
            def _():
                copy.wait_send()

    def recv(self, view, sem):
        pltpu.make_async_remote_copy(
            src_ref=view, dst_ref=view, send_sem=self.send_sems.at[0], recv_sem=sem,
            device_id=(self.s, self.c), device_id_type=MESH,
        ).wait_recv()

    def local(self, src, dst):
        copy = pltpu.make_async_copy(src, dst, self.local_sems.at[self.locals])
        self.locals += 1
        copy.start()
        return copy

    def drain(self):
        for at in range(len(self.sent)):
            self.sent_wait(at)

    def ch_gather_start(self, view_of, tag):
        mine = view_of(self.c)
        self.send(mine, mine, self.across, self.sem((tag, "y")))
        self.send(mine, mine, self.sibling, self.sem((tag, "core")))

    def ch_gather_finish(self, view_of, tag):
        y, core = self.y, self.core
        theirs = view_of((1 - y) * 2 + core)
        self.recv(theirs, self.sem((tag, "y")))
        self.send(theirs, theirs, self.sibling, self.sem((tag, "fwd")))
        self.recv(view_of(y * 2 + 1 - core), self.sem((tag, "core")))
        self.recv(view_of((1 - y) * 2 + 1 - core), self.sem((tag, "fwd")))

    def ch_sum(self, part, mid, low, far, tag):
        y, core = self.y, self.core
        first = len(self.sent)
        self.send(part.at[1 - core], mid, self.sibling, self.sem((tag, "core")))
        self.recv(mid, self.sem((tag, "core")))
        low[...] = (part[core, 1 - y] + mid[1 - y]).astype(jnp.bfloat16)
        self.send(low, far, self.across, self.sem((tag, "y")))
        total = part[core, y] + mid[y]
        self.recv(far, self.sem((tag, "y")))
        self.sent_wait(first)
        self.sent_wait(first + 1)
        return total + far[...].astype(jnp.float32)

    def chain_start(self, mine, target, tag):
        n_z, z = self.n_z, self.z
        self.send(mine, target, self.above, self.sem((tag, "z"), 1, n_z), z < n_z - 1)
        self.send(mine, target, self.below, self.sem((tag, "z"), n_z - 1, n_z), z > 0)

    def chain_arrive(self, view, slot, tag):
        n_z, z = self.n_z, self.z
        self.recv(view, self.sem((tag, "z"), slot, n_z))
        self.send(view, view, self.above, self.sem((tag, "z"), (slot + 1) % n_z, n_z), (z >= slot) & (z < n_z - 1))
        self.send(view, view, self.below, self.sem((tag, "z"), (slot + n_z - 1) % n_z, n_z), (z < slot) & (z > 0))


    def chain_sum(self, k, term, lands, add, tag):
        n_z, z = self.n_z, self.z
        for way, to, goes, comes in ((1, self.above, z + k < n_z, z > 0), (n_z - 1, self.below, z >= k, z < n_z - 1)):
            land, name = lands[way > 1], (tag, way > 1)
            mine = term((z + way * k) % n_z)
            if k < n_z - 1:
                @pl.when(goes & comes)
                def _():
                    self.recv(land.at[k], self.sem(name, k, n_z - 1))
                    add(mine, land.at[k])

            self.send(mine, land.at[k - 1], to, self.sem(name, k - 1, n_z - 1), goes)

    def chain_sum_last(self, lands, add, total, tag):
        n_z, z = self.n_z, self.z
        for side, comes in ((0, z > 0), (1, z < n_z - 1)):
            @pl.when(comes)
            def _(side=side):
                self.recv(lands[side].at[0], self.sem((tag, side > 0), 0, n_z - 1))
                add(total, lands[side].at[0])

    def arrival(self, slot):
        n_z, z = self.n_z, self.z
        low, high = (n_z - 1 - z) // (n_z - 1), z // (n_z - 1)
        far = slot // (n_z // 2 + 1)
        inner = (1 - far) * (2 * slot - 1) + far * 2 * (n_z - slot)
        return (low * (n_z - slot) + high * slot + (1 - low - high) * inner + n_z) % n_z


def add_into(mine, more):
    mine[...] = (mine[...].astype(jnp.float32) + more[...].astype(jnp.float32)).astype(mine.dtype)


class Spread:
    def __init__(self, net, ref, tag):
        self.net, self.ref, self.tag = net, ref, tag

    def view(self, slot, x, y, core):
        net = self.net
        return self.ref.at[pl.ds(net.block(net.z_of(slot), x, y, core), net.rows)]

    def sem(self, what, slot):
        return self.net.sem((self.tag, what), slot, self.net.n_z)

    def start(self):
        net = self.net
        mine = self.view(0, net.x, net.y, net.core)
        net.chain_start(mine, mine, self.tag)
        self.plane(0)

    def plane(self, slot):
        net = self.net
        view = self.view(slot, net.x, net.y, net.core)
        net.send(view, view, net.beside, self.sem("x", slot))
        net.send(view, view, net.across, self.sem("y", slot))
        net.send(view, view, net.sibling, self.sem("s", slot))

    def arrive(self, slot):
        net = self.net
        net.chain_arrive(self.view(slot, net.x, net.y, net.core), slot, self.tag)
        self.plane(slot)

    def relay(self, slot):
        net = self.net
        view = self.view(slot, 1 - net.x, net.y, net.core)
        net.recv(view, self.sem("x", slot))
        net.send(view, view, net.across, self.sem("d", slot))
        net.send(view, view, net.sibling, self.sem("s", slot))

    def relay_far(self, slot):
        net = self.net
        for what, x in (("y", net.x), ("d", 1 - net.x)):
            view = self.view(slot, x, 1 - net.y, net.core)
            net.recv(view, self.sem(what, slot))
            net.send(view, view, net.sibling, self.sem("s", slot))

    def done(self, slot):
        net = self.net
        at = net.block(net.z_of(slot), 0, 0, 0)
        net.recv(self.ref.at[pl.ds(at, 4 * net.rows)], self.sem("s", slot))


class Collect:
    def __init__(self, net, part, sib, far, side, tag):
        self.net, self.part, self.sib, self.far, self.side, self.tag = net, part, sib, far, side, tag

    def sem(self, what, at):
        return self.net.sem((self.tag, what), at, self.net.n_z)

    def first(self, at):
        net = self.net
        net.send(self.part.at[at, 1 - net.core], self.sib.at[at], net.sibling, self.sem("s", at))

    def second(self, at):
        net = self.net
        net.recv(self.sib.at[at], self.sem("s", at))
        core, part, sib = net.core, self.part, self.sib
        for first in (1 - net.y, net.y):
            for x in range(2):
                value = part[at, core, first, x].astype(jnp.float32) + sib[at, first, x].astype(jnp.float32)
                part[at, core, first, x] = value.astype(jnp.bfloat16)
            if first is not net.y:
                net.send(part.at[at, core, first], self.far.at[at], net.across, self.sem("f", at))

    def third(self, at):
        net, part, far = self.net, self.part, self.far
        net.recv(far.at[at], self.sem("f", at))
        there = 1 - net.x
        value = part[at, net.core, net.y, there].astype(jnp.float32) + far[at, there].astype(jnp.float32)
        part[at, net.core, net.y, there] = value.astype(jnp.bfloat16)
        net.send(part.at[at, net.core, net.y, there], self.side.at[at], net.beside, self.sem("p", at))

    def plane_total(self, at):
        net = self.net
        net.recv(self.side.at[at], self.sem("p", at))
        total = self.part[at, net.core, net.y, net.x].astype(jnp.float32)
        return total + self.far[at, net.x].astype(jnp.float32) + self.side[at].astype(jnp.float32)

    def fourth(self, at):
        net, part = self.net, self.part
        total = self.plane_total(at)
        if at == 0:
            return total
        part[at, net.core, net.y, net.x] = total.astype(jnp.bfloat16)
        return None

    def term(self, there):
        net = self.net
        at = net.arrival((net.z + net.n_z - there) % net.n_z)
        return self.part.at[at, net.core, net.y, net.x]


class CollectEven(Collect):
    def second(self, at):
        net = self.net
        net.recv(self.sib.at[at], self.sem("s", at))
        core, part, sib = net.core, self.part, self.sib
        half = net.rows // 2
        for y in (1 - net.y, net.y):
            for x in (1 - net.x, net.x):
                value = part[at, core, y, x].astype(jnp.float32) + sib[at, y, x].astype(jnp.float32)
                part[at, core, y, x] = value.astype(jnp.bfloat16)
                if y is not net.y and x is not net.x:
                    diagonal = part.at[at, core, y, x]
                    net.send(diagonal.at[pl.ds(0, half)], self.far.at[at, 0], net.beside, self.sem("f0", at))
                    net.send(diagonal.at[pl.ds(half, half)], self.far.at[at, 1], net.across, self.sem("f1", at))

    def third(self, at):
        net, part, far = self.net, self.part, self.far
        half = net.rows // 2
        for which, y, x, first, to in (
            (0, 1 - net.y, net.x, 0, net.across), (1, net.y, 1 - net.x, half, net.beside),
        ):
            net.recv(far.at[at, which], self.sem(f"f{which}", at))
            rows = pl.ds(first, half)
            value = part[at, net.core, y, x, rows, :].astype(jnp.float32) + far[at, which].astype(jnp.float32)
            part[at, net.core, y, x, rows, :] = value.astype(jnp.bfloat16)
            net.send(part.at[at, net.core, y, x], self.side.at[at, which], to, self.sem("p", at))

    def plane_total(self, at):
        net = self.net
        net.recv(self.side.at[at], self.sem("p", at))
        total = self.part[at, net.core, net.y, net.x].astype(jnp.float32)
        return total + self.side[at, 0].astype(jnp.float32) + self.side[at, 1].astype(jnp.float32)


def stack_rows(rows):
    return jnp.concatenate(rows, axis=0)


def smooth_pair(v):
    t = jnp.tanh(K1 * (v + K2 * v * v * v))
    value = 0.5 * v * (1.0 + t)
    slope = 0.5 * (1.0 + t) + 0.5 * v * (1.0 - t * t) * K1 * (1.0 + 3.0 * K2 * v * v)
    return value, slope


def sigmoid(v):
    return 1.0 / (1.0 + jnp.exp(-v))


def softplus_exact(d):
    u = jnp.exp(-jnp.abs(d))
    r = u / (2.0 + u)
    q = r * r
    series = 1.0 / 15.0
    for k in (13, 11, 9, 7, 5, 3, 1):
        series = series * q + 1.0 / k
    return jnp.maximum(d, 0.0) + 2.0 * r * series


def minus_expm1(v):
    series = 1.0 / 362880.0
    for k in (40320.0, 5040.0, 720.0, 120.0, 24.0, 6.0, 2.0, 1.0):
        series = series * v + 1.0 / k
    return jnp.where(v > -0.5, -v * series, 1.0 - jnp.exp(v))


class Docs:
    def __init__(self, lengths, first, count, before=0):
        position = first - before + lax.broadcasted_iota(jnp.int32, (count, 1), 0)
        self.opening, self.closing = [], []
        start_of = jnp.zeros((count, 1), jnp.int32)
        start = jnp.int32(0)
        for e in range(lengths.shape[0]):
            end = start + lengths[e]
            owner = (position >= start) & (position < end)
            start_of = jnp.where(owner, start, start_of)
            self.opening.append((position == start).astype(jnp.float32))
            self.closing.append((position == end - 1).astype(jnp.float32))
            start = end
        self.offset = position - start_of
        self.keep = (self.offset > 0).astype(jnp.float32)

    def valid(self, k):
        return (self.offset >= k).astype(jnp.float32)


def prefix(a, b, count):
    row = lax.broadcasted_iota(jnp.int32, a.shape, 0)
    k = 1
    while k < count:
        inside = row >= k
        a_far = jnp.where(inside, pltpu.roll(a, k, 0), 1.0)
        b_far = jnp.where(inside, pltpu.roll(b, k, 0), 0.0)
        b = a * b_far + b
        a = a * a_far
        k *= 2
    return a, b


def suffix(a, b, count):
    row = lax.broadcasted_iota(jnp.int32, a.shape, 0)
    k = 1
    while k < count:
        inside = row < count - k
        a_far = jnp.where(inside, pltpu.roll(a, count - k, 0), 1.0)
        b_far = jnp.where(inside, pltpu.roll(b, count - k, 0), 0.0)
        b = a * b_far + b
        a = a * a_far
        k *= 2
    return a, b


def coefficient_parts(rate_pre, inlet_pre, decay):
    rate = sigmoid(rate_pre)
    inlet = sigmoid(inlet_pre)
    sp = softplus_exact(decay)
    log_decay = -8.0 * rate * sp
    factor = jnp.exp(log_decay)
    scale = jnp.sqrt(minus_expm1(2.0 * log_decay))
    return rate, inlet, sp, log_decay, factor, scale


def opening_rows(docs, init):
    total = docs.opening[0] * init[0:1]
    for e in range(1, len(docs.opening)):
        total = total + docs.opening[e] * init[e : e + 1]
    return total


def pack_gain(row):
    tiles = [row[:, i * 128 : (i + 1) * 128] for i in range(row.shape[1] // 128)]
    return jnp.concatenate([stack_rows(tiles[i : i + 8]) for i in range(0, len(tiles), 8)], axis=1)


def norm_back(values, gain, grad):
    r = lax.rsqrt(jnp.mean(values * values, axis=-1, keepdims=True) + EPS)
    u = grad * gain
    to_values = r * u - values * (r * r * r) * jnp.mean(u * values, axis=-1, keepdims=True)
    to_gain = jnp.sum(grad * values * r, axis=0, keepdims=True)
    return to_values, to_gain


def unit(size):
    row = lax.broadcasted_iota(jnp.int32, (size, size), 0)
    column = lax.broadcasted_iota(jnp.int32, (size, size), 1)
    return jnp.where(row == column, 1.0, 0.0).astype(jnp.bfloat16)


RIM = 16


def block_kernel(sizes, names, *refs):
    n_seq, n_ch, rows, d, slots, bw, width, sl = sizes
    r = types.SimpleNamespace(**dict(zip(names, refs)))
    bf, f32 = jnp.bfloat16, jnp.float32
    net = Net(n_seq, n_ch, rows, r.send_sems, r.recv_sems, r.local_sems)
    s, c, x, y, z, core, n_z = net.s, net.c, net.x, net.y, net.z, net.core, net.n_z
    count, wide, tokens = rows * n_ch, slots * bw, rows * n_ch * n_seq
    n_taps = r.taps_v.shape[1]
    mine = net.block(z, x, y, core)
    seq_peers = [(net.s_to[k], c) for k in range(1, n_seq)]
    rim_peers = [(net.s_to[k], (c + i) % n_ch) for k in (1, n_seq - 1) for i in range(1, n_ch)]
    peers = seq_peers + rim_peers + [net.sibling, net.across]
    net.greet(peers)
    loads = {}
    cuts = dict(gelu_w=4, recur_w=4, out_w=4)

    def load_halves(name, dst):
        src, size = getattr(r, name), dst.shape[2]
        loads[name] = [net.local(src.at[:, pl.ds(i * size, size)], dst.at[i]) for i in range(2)]

    def load(name, n):
        src, dst = getattr(r, name), getattr(r, name + "_v")
        if n == 1:
            loads[name] = [net.local(src, dst)]
            return
        size = src.shape[0] // n
        loads[name] = [
            net.local(src.at[pl.ds(i * size, size)], dst.at[pl.ds(i * size, size)])
            for i in range(n)
        ]

    def loaded(name):
        for copy in loads.pop(name):
            copy.wait()

    load("stream", 1)
    load("mix_gain", 1)
    load_halves("gate_w", r.give)
    load("cot", 1)
    load_halves("up_w", r.take)
    for name in ("gelu_w", "recur_w", "taps", "bias", "rate_w", "rate_b",
                 "inlet_w", "inlet_b", "decay", "init", "out_w", "ffn_gain"):
        load(name, cuts.get(name, 1))

    own_cols = pl.ds(pl.multiple_of(s * width, width), width)
    own_count = pl.ds(pl.multiple_of(s * count, count), count)
    own_slice = pl.ds(pl.multiple_of(s * sl, sl), sl)
    local = []

    loaded("stream")
    loaded("mix_gain")
    values = r.stream_v[...].astype(f32)
    scale = lax.rsqrt(jnp.mean(values * values, axis=-1, keepdims=True) + EPS)
    mix_rows = pl.ds(pl.multiple_of(RIM + c * rows, 16), rows)
    r.mix[mix_rows, :] = (values * scale * r.mix_gain_v[...][None, :]).astype(bf)

    loaded("cot")
    r.cfull[pl.ds(mine, rows), :] = r.cot_v[...]

    def turn(a, src):
        half = src.shape[2]
        for i in range(2 * half // 256):
            at = i * 256 % half
            r.turned[a, i * 256 : (i + 1) * 256, :] = contract_first(
                src[i * 256 // half, :, at : at + 256], unit(src.shape[1])
            ).astype(bf)

    net.meet(peers)

    def mix_of(cc):
        return r.mix.at[pl.ds(pl.multiple_of(RIM + cc * rows, 16), rows)]

    last, first = r.mix.at[pl.ds(count, RIM)], r.mix.at[pl.ds(0, RIM)]
    net.ch_gather_start(mix_of, "mix")
    for i in range(n_ch):
        net.send(last, first, (net.s_to[1], i), net.sem("rim"), (c == n_ch - 1) & (s < n_seq - 1))

    @pl.when(s == 0)
    def _():
        r.mix[pl.ds(0, RIM), :] = jnp.zeros((RIM, d), bf)

    cots = Spread(net, r.cfull, "cot")
    lows = Spread(net, r.full, "low")
    cots.start()

    pair_width = 2 * width

    def pair_cols(to):
        return pl.ds(pl.multiple_of(to * pair_width, pair_width), pair_width)

    def left_start(a, src):
        r.left[a, z, c] = src[:, pair_cols(z)]
        for at in range(1, n_z):
            to = net.z_of(net.slot(at))
            net.send(src.at[:, pair_cols(to)], r.left.at[a, z, c], net.dev(to, x, y, core), net.sem(("left", a)))

    def left_pass(a):
        net.recv(r.left.at[a, pl.ds(0, n_z - 1), c], net.sem(("left", a)))
        net.ch_gather_start(lambda cc: r.left.at[a, :, cc], ("leftch", a))

    def left_done(a):
        net.ch_gather_finish(lambda cc: r.left.at[a, :, cc], ("leftch", a))

    left_start(0, r.mix.at[mix_rows])

    others = net.nearest()

    def weight_start(a, which=None):
        src = r.turned.at[a] if a < 2 else r.down
        which = others if which is None else which
        for to in which:
            net.send(
                src.at[pl.ds(pl.multiple_of(to * sl, sl), sl)], r.wt.at[a, :, own_cols], (to, c), net.sem(("w", a)),
            )
        if which[-1] is others[-1]:
            local.append(net.local(src.at[own_slice], r.wt.at[a, :, own_cols]))

    def weight_done(a):
        net.recv(r.wt.at[a, :, pl.ds(0, (n_seq - 1) * width)], net.sem(("w", a)))
        local.pop(0).wait()

    loaded("gate_w")
    turn(0, r.give)
    loaded("up_w")
    turn(1, r.take)
    weight_start(0, others[:2])
    for name in [name for name in loads if name != "out_w"]:
        loaded(name)

    net.ch_gather_finish(mix_of, "mix")
    cots.arrive(net.slot(1))
    for i in range(n_ch):
        @pl.when((s > 0) & (c == i))
        def _(i=i):
            net.recv(first, net.sem("rim"))

    docs = Docs(r.lengths, s * count, count)
    keep = docs.keep
    ends_a, ends_b = [], []
    for b in range(slots):
        cols = pl.ds(b * bw, bw)
        rowsof = r.mix[...]
        r.gelu[:, cols] = jnp.dot(rowsof[RIM:], r.gelu_w_v[:, cols], preferred_element_type=f32)
        recur = jnp.dot(rowsof, r.recur_w_v[:, cols], preferred_element_type=f32).astype(bf)
        r.recur[:, cols] = recur
        recur = recur.astype(f32)
        conv_pre = r.bias_v[b : b + 1, :]
        for k in range(n_taps):
            conv_pre = conv_pre + r.taps_v[b, k : k + 1, :] * recur[RIM - k : RIM - k + count] * docs.valid(k)
        conv_low = conv_pre.astype(bf)
        r.conv[:, cols] = conv_low
        rate_pre = jnp.dot(conv_low, r.rate_w_v[b], preferred_element_type=f32) + r.rate_b_v[b : b + 1, :]
        inlet_pre = jnp.dot(conv_low, r.inlet_w_v[b], preferred_element_type=f32) + r.inlet_b_v[b : b + 1, :]
        r.rate_pre[:, cols] = rate_pre
        r.inlet_pre[:, cols] = inlet_pre
        rate, inlet, sp, log_decay, factor, scale = coefficient_parts(rate_pre, inlet_pre, r.decay_v[b : b + 1, :])
        source = scale * inlet * conv_low.astype(f32) + (1.0 - keep) * factor * opening_rows(docs, r.init_v[:, cols])
        total, part = prefix(keep * factor, source, count)
        r.scan_a[:, cols] = total
        r.scan_b[:, cols] = part
        ends_a.append(total[count - 1 : count])
        ends_b.append(part[count - 1 : count])

    def exchange(summary, pieces, tag):
        summary[s] = stack_rows(pieces + [jnp.zeros((8 - 2 * slots, bw), f32)])
        for k in range(1, n_seq):
            net.send(summary.at[s], summary.at[s], (net.s_to[k], c), net.sem(tag))

    def exchanged(summary, tag):
        net.recv(summary.at[pl.ds(0, n_seq - 1)], net.sem(tag))

    exchange(r.summary, ends_a + ends_b, "sum")
    weight_start(0, others[2:])
    cots.relay(0)
    cots.arrive(net.slot(2))
    loaded("out_w")
    exchanged(r.summary, "sum")
    enter = jnp.zeros((slots, bw), f32)
    for q in range(n_seq - 1):
        after = r.summary[q, 0:slots] * enter + r.summary[q, slots : 2 * slots]
        enter = jnp.where(s > q, after, enter)
    finals = []
    for b in range(slots):
        cols = pl.ds(b * bw, bw)
        live = jnp.where(r.counts[0] > b, 1.0, 0.0)
        state = r.scan_b[:, cols] + r.scan_a[:, cols] * enter[b : b + 1]
        r.state[:, cols] = state
        value, _ = smooth_pair(r.gelu[:, cols])
        r.gath[0, z, :, cols] = (value * state * live).astype(bf)
        ends = [jnp.sum(mark * state, axis=0, keepdims=True) * live for mark in docs.closing]
        finals.append(stack_rows(ends + [jnp.zeros((8 - len(ends), bw), f32)]))

    def branch_tile(i, _):
        cols = pl.ds(pl.multiple_of(i * TILE, TILE), TILE)
        value = jnp.dot(r.gath[0, z], r.out_w_v[:, cols], preferred_element_type=f32)
        for cc in range(n_ch):
            r.part[cc % 2, cc // 2, :, cols] = value[cc * rows : (cc + 1) * rows]
        return 0

    lax.fori_loop(0, d // TILE, branch_tile, 0)
    middle = r.stream_v[...].astype(f32) + net.ch_sum(r.part, r.mid, r.ylow, r.yfar, "branch")
    scale = lax.rsqrt(jnp.mean(middle * middle, axis=-1, keepdims=True) + EPS)
    r.full[pl.ds(mine, rows), :] = (middle * scale * r.ffn_gain_v[...][None, :]).astype(bf)
    r.middle[...] = middle

    def gather_start(a):
        net.chain_start(r.gath.at[a, z], r.gath.at[a, z], ("g", a))

    def gather_arrive(a, at):
        slot = net.slot(at)
        net.chain_arrive(r.gath.at[a, net.z_of(slot)], slot, ("g", a))

    def gather_product(a):
        right = r.gath[a].reshape(n_z * count, wide)
        for which, there in ((0, 1 - x), (1, x)):
            half = r.left[1 if a == 0 else 0, :, :, :, pl.ds(pl.multiple_of(there * width, width), width)]
            half = half.reshape(n_z * count, width)
            value = contract_first(right, half) if a == 0 else contract_first(half, right)
            if which == 0:
                ref = r.give_out if a == 0 else r.give.at[a - 1]
                ref[...] = value.astype(bf)
                net.send(ref, r.took_out if a == 0 else r.took.at[a - 1], net.beside, net.sem(("take", a)))
            elif a == 0:
                r.keep_out_v[...] = value
                local.append(net.local(r.keep_out_v, r.keep_out))
            else:
                r.keep_v[a - 1] = value
                local.append(net.local(r.keep_v.at[a - 1], r.keep.at[a - 1]))

    def gather_done(a):
        net.recv(r.took_out if a == 0 else r.took.at[a - 1], net.sem(("take", a)))

    lows.start()
    weight_start(1, others[:2])
    cots.relay(net.slot(1))
    lows.relay(0)
    lows.arrive(net.slot(1))
    weight_start(1, others[2:4])
    cots.relay(net.slot(2))
    lows.arrive(net.slot(2))
    cots.arrive(net.slot(3))
    weight_start(1, others[4:])
    lows.relay_far(0)
    lows.relay(net.slot(1))
    lows.relay(net.slot(2))
    lows.arrive(net.slot(3))
    weight_start(2)
    gather_start(0)
    group = n_ch * 2 * rows

    def chunk(at):
        return pl.ds(pl.multiple_of(net.z_of(net.slot(at)) * group, group), group)

    weight_done(0)
    weight_done(1)

    def forward(at):
        lows.done(net.slot(at))
        here = chunk(at)
        gate = contract_last(r.full[here, :], r.wt[0])
        up = contract_last(r.full[here, :], r.wt[1])
        value, slope = smooth_pair(gate)
        r.value[here, :] = value
        r.slope[here, :] = up * slope
        r.hid[here, :] = (value * up).astype(bf)

    lows.relay_far(net.slot(1))
    forward(0)
    lows.relay_far(net.slot(2))
    lows.relay(net.slot(3))
    forward(1)
    cots.relay(net.slot(3))
    forward(2)
    lows.relay_far(net.slot(3))
    for at in range(n_z):
        cots.relay_far(net.slot(at))
    forward(3)
    for at in range(n_z):
        cots.done(net.slot(at))

    def weight_grad(a, left, right):
        def tile(i, _):
            cols = pl.ds(pl.multiple_of(i * TILE, TILE), TILE)
            r.dwl[a, :, cols] = contract_first(left[...], right[:, cols]).astype(bf)
            return 0

        lax.fori_loop(0, d // TILE, tile, 0)

    def weight_grad_send(a, which=None):
        which = others if which is None else which
        for to in which:
            cols = pl.ds(pl.multiple_of(to * width, width), width)
            net.send(r.dwl.at[a, :, cols], r.dw.at[a, own_slice], (to, c), net.sem(("dw", a)))
        if which[-1] is others[-1]:
            local.append(net.local(r.dwl.at[a, :, own_cols], r.dw.at[a, own_slice]))

    def weight_grad_done(a):
        net.recv(r.dw.at[a, pl.ds(0, (n_seq - 1) * sl)], net.sem(("dw", a)))

    weight_grad(2, r.hid, r.cfull)
    weight_done(2)
    weight_grad_send(2)

    def spread_out(ref, at, value, cols):
        value = value.astype(bf)
        for xx in range(2):
            for yy in range(2):
                for cc in range(2):
                    row = (xx * 4 + yy * 2 + cc) * rows
                    ref[at, cc, yy, xx, :, cols] = value[row : row + rows]

    def backward(at):
        here = chunk(at)
        grad = contract_last(r.cfull[here, :], r.wt[2])
        r.gat[here, :] = (grad * r.slope[here, :]).astype(bf)
        r.upg[here, :] = (grad * r.value[here, :]).astype(bf)

        def tile(i, _):
            cols = pl.ds(pl.multiple_of(i * TILE, TILE), TILE)
            value = jnp.dot(r.gat[here, :], r.wt[0, :, cols], preferred_element_type=f32)
            value = value + jnp.dot(r.upg[here, :], r.wt[1, :, cols], preferred_element_type=f32)
            spread_out(r.npart, at, value, cols)
            return 0

        lax.fori_loop(0, d // TILE, tile, 0)

    def output(at):
        here = chunk(at)

        def tile(i, _):
            cols = pl.ds(pl.multiple_of(i * TILE, TILE), TILE)
            value = jnp.dot(r.hid[here, :], r.wt[2, :, cols], preferred_element_type=f32)
            spread_out(r.opart, at, value, cols)
            return 0

        lax.fori_loop(0, d // TILE, tile, 0)

    def norm_step(k):
        net.chain_sum(k, norms.term, (r.oup, r.odown), add_into, 2)

    def out_step(k):
        net.chain_sum(k, outs.term, (r.oup, r.odown), add_into, 0)

    norms = CollectEven(net, r.npart, r.nsib, r.nfar, r.nside, "norm")
    outs = Collect(net, r.opart, r.osib, r.ofar, r.oside, "out")
    backward(3)
    norms.first(3)
    backward(2)
    norms.first(2)
    norms.second(3)
    backward(1)
    norms.first(1)
    norms.second(2)
    norms.third(3)
    backward(0)
    norms.first(0)
    norms.second(1)
    norms.third(2)
    norms.fourth(3)
    norm_step(3)
    norms.second(0)
    output(3)
    output(2)
    norms.third(1)
    norms.fourth(2)
    norm_step(2)
    output(1)
    output(0)
    norms.third(0)
    norms.fourth(1)
    norm_step(1)
    for at in (3, 2, 1, 0):
        outs.first(at)
    gather_arrive(0, 1)
    weight_grad(0, r.gat, r.full)
    weight_grad(1, r.upg, r.full)
    r.sgrad_v[...] = norms.fourth(0)
    left_pass(0)
    gather_arrive(0, 2)
    net.chain_sum_last((r.oup, r.odown), add_into, r.sgrad_v, 2)
    nfg = r.sgrad_v[...]

    to_middle, ffn_part = norm_back(r.middle[...], r.ffn_gain_v[...][None, :], nfg)
    middle_grad = r.cot_v[...].astype(f32) + to_middle
    r.sgrad_v[...] = middle_grad
    r.branch[c] = middle_grad.astype(bf)
    net.ch_gather_start(lambda cc: r.branch.at[cc], "bgrad")
    left_start(1, r.branch.at[c])
    weight_grad_send(0, others[:3])
    for at in (3, 2, 1, 0):
        outs.second(at)
    n_docs = r.finals_v.shape[0]
    spare = jnp.concatenate([ffn_part, jnp.zeros((1, (8 - n_docs) * wide - d), f32)], axis=1)
    spare = [spare[:, i * wide : (i + 1) * wide] for i in range(8 - n_docs)]
    r.early[n_z] = stack_rows([jnp.concatenate(finals, axis=1)[:n_docs]] + spare)
    net.send(r.early.at[n_z], r.early_pair, net.beside, net.sem("pair", 0, 2))
    net.ch_gather_finish(lambda cc: r.branch.at[cc], "bgrad")

    ahead_docs = Docs(r.lengths, s * count, count + RIM)
    row = lax.broadcasted_iota(jnp.int32, (count, bw), 0)
    heads_a, heads_b = [], []
    for b in range(slots):
        cols = pl.ds(b * bw, bw)
        live = jnp.where(r.counts[0] > b, 1.0, 0.0)
        product_grad = contract_last(r.branch[...].reshape(count, d), r.out_w_v[b * bw : (b + 1) * bw, :])
        value, slope = smooth_pair(r.gelu[:, cols])
        r.gath[1, z, :, cols] = (product_grad * r.state[:, cols] * live * slope).astype(bf)
        rate, inlet, sp, log_decay, factor, scale = coefficient_parts(r.rate_pre[:, cols], r.inlet_pre[:, cols], r.decay_v[b : b + 1, :])
        carry = keep * factor
        following = jnp.where(row < count - 1, pltpu.roll(carry, count - 1, 0), 1.0)
        total, part = suffix(following, product_grad * value * live, count)
        r.scan_a[:, cols] = total
        r.scan_b[:, cols] = part
        heads_a.append(carry[0:1] * total[0:1])
        heads_b.append(carry[0:1] * part[0:1])
    exchange(r.summary_back, heads_a + heads_b, "sumback")

    gather_start(1)
    gather_arrive(0, 3)
    weight_grad_send(0, others[3:4])
    exchanged(r.summary_back, "sumback")

    net.recv(r.early_pair, net.sem("pair", 0, 2))
    r.early[z] = r.early[n_z] + r.early_pair[...]
    for k in range(1, n_z):
        to = net.z_of(k)
        net.send(r.early.at[z], r.early.at[z], net.dev(to, x, y, core), net.sem(("vec", 0)))
    enter_back = jnp.zeros((slots, bw), f32)
    for q in range(n_seq - 1, 0, -1):
        after = r.summary_back[q, 0:slots] * enter_back + r.summary_back[q, slots : 2 * slots]
        enter_back = jnp.where(s < q, after, enter_back)
    vec = []
    for b in range(slots):
        cols = pl.ds(b * bw, bw)
        adjoint = r.scan_b[:, cols] + r.scan_a[:, cols] * enter_back[b : b + 1]
        previous = jnp.where(row > 0, pltpu.roll(r.state[:, cols], 1, 0), enter[b : b + 1])
        decay = r.decay_v[b : b + 1, :]
        rate, inlet, sp, log_decay, factor, scale = coefficient_parts(r.rate_pre[:, cols], r.inlet_pre[:, cols], decay)
        conv_low = r.conv[:, cols]
        conv = conv_low.astype(f32)
        init_rows = opening_rows(docs, r.init_v[:, cols])
        log_grad = adjoint * (
            factor * (keep * previous + (1.0 - keep) * init_rows) - inlet * conv * jnp.exp(2.0 * log_decay) / scale
        )
        rate_low = (log_grad * (-8.0 * sp) * rate * (1.0 - rate)).astype(bf)
        direct = adjoint * scale
        inlet_low = (direct * conv * inlet * (1.0 - inlet)).astype(bf)
        decay_row = jnp.sum(log_grad * (-8.0 * rate), axis=0, keepdims=True) * sigmoid(decay)
        back = direct * inlet + contract_last(rate_low, r.rate_w_v[b]) + contract_last(inlet_low, r.inlet_w_v[b])
        r.cgrad[0:count, cols] = back.astype(bf)
        for a, low in enumerate((rate_low, inlet_low)):
            part = contract_first(conv_low, low).astype(bf)
            r.gates[a, b] = part.reshape(r.gates.shape[2:])
        vec.append([
            jnp.sum(rate_low.astype(f32), axis=0, keepdims=True),
            jnp.sum(inlet_low.astype(f32), axis=0, keepdims=True),
            decay_row,
        ])
    rim = r.cgrad.at[pl.ds(count, RIM)]
    net.send(r.cgrad.at[pl.ds(0, RIM)], rim, (net.s_to[n_seq - 1], c), net.sem("rimback"), s > 0)

    @pl.when(s == n_seq - 1)
    def _():
        r.cgrad[pl.ds(count, RIM), :] = jnp.zeros((RIM, wide), bf)

    net.send(r.gates.at[:, :, :, 1 - x], r.gates_x, net.beside, net.sem("gatesx"))
    gather_arrive(1, 1)
    weight_grad_send(0, others[4:])

    @pl.when(s < n_seq - 1)
    def _():
        net.recv(rim, net.sem("rimback"))

    vectors = []
    for b in range(slots):
        cols = pl.ds(b * bw, bw)
        grad = r.cgrad[:, cols].astype(f32)
        own = grad[:count]
        recur = r.recur[:, cols].astype(f32)
        total = jnp.zeros((count, bw), f32)
        tap_rows = []
        for k in range(n_taps):
            tap_rows.append(jnp.sum(own * recur[RIM - k : RIM - k + count] * docs.valid(k), axis=0, keepdims=True))
            total = total + r.taps_v[b, k : k + 1, :] * grad[k : k + count] * ahead_docs.valid(k)[k : k + count]
        r.gath[2, z, :, cols] = total.astype(bf)
        vectors.append(stack_rows(tap_rows + [jnp.sum(own, axis=0, keepdims=True)] + vec[b]))
    gather_start(2)
    for at in (3, 2, 1, 0):
        outs.third(at)

    def norm_tile(i, _):
        cols = pl.ds(pl.multiple_of(i * TILE, TILE), TILE)
        value = contract_last(r.gath[1, z], r.gelu_w_v[cols, :]) + contract_last(r.gath[2, z], r.recur_w_v[cols, :])
        for cc in range(n_ch):
            r.part[cc % 2, cc // 2, :, cols] = value[cc * rows : (cc + 1) * rows]
        return 0

    lax.fori_loop(0, d // TILE, norm_tile, 0)
    gather_arrive(1, 2)
    left_pass(1)
    left_done(0)
    norm_grad = net.ch_sum(r.part, r.mid, r.ylow, r.yfar, "norm")
    to_stream, mix_part = norm_back(r.stream_v[...].astype(f32), r.mix_gain_v[...][None, :], norm_grad)
    r.sgrad_v[...] += to_stream
    local.append(net.local(r.sgrad_v, r.sgrad))
    r.late[...] = jnp.concatenate(vectors + [pack_gain(mix_part)], axis=1)
    net.send(r.late, r.late_pair, net.beside, net.sem("pair", 1, 2))
    net.recv(r.gates_x, net.sem("gatesx"))

    def gate_step(k):
        net.chain_sum(k, lambda there: r.gates.at[:, :, there, x], (r.gates_up, r.gates_down), add_into, 1)

    def gate_add(i, _):
        for a in range(2):
            for b in range(slots):
                value = r.gates[a, b, i, x].astype(f32) + r.gates_x[a, b, i].astype(f32)
                r.gates[a, b, i, x] = value.astype(bf)
        return 0

    lax.fori_loop(0, n_z, gate_add, 0)
    gather_arrive(2, 1)
    weight_grad_send(1, others[:3])
    gate_step(3)
    net.recv(r.late_pair, net.sem("pair", 1, 2))
    late = r.late[...] + r.late_pair[...]
    piece = bw // n_seq
    gap = jnp.zeros((8, r.late_out.shape[2] - (late.shape[1] - wide) - 2 * slots * piece), f32)
    for q in range(n_z):
        cuts_at = [b * bw + 2 * q * piece for b in range(slots)]
        r.late_out[q] = jnp.concatenate([late[:, at : at + 2 * piece] for at in cuts_at] + [gap, late[:, wide:]], axis=1)
    r.late_in[z] = r.late_out[z]
    for k in range(1, n_z):
        to = net.z_of(k)
        net.send(r.late_out.at[to], r.late_in.at[z], net.dev(to, x, y, core), net.sem(("vec", 1)))
    left_done(1)
    gather_product(0)
    gather_arrive(1, 3)
    gather_arrive(2, 2)
    for at in (3, 2, 1):
        outs.fourth(at)
    r.middle[...] += outs.fourth(0)
    out_step(3)
    gate_step(2)
    weight_grad_send(1, others[3:5])
    gather_product(1)
    out_step(2)
    gate_step(1)
    weight_grad_send(1, others[5:])
    for a, ref in enumerate((r.early, r.late_in)):
        net.recv(ref.at[pl.ds(0, n_z - 1)], net.sem(("vec", a)))
    early, late = r.early[0], r.late_in[0]
    for q in range(1, n_z):
        early, late = early + r.early[q], late + r.late_in[q]
    r.shared[c] = jnp.concatenate([early, late[:, late.shape[1] - d // 8 :]], axis=1)
    net.ch_gather_start(lambda cc: r.shared.at[cc], "shared")
    for b in range(slots):
        at = 2 * b * piece
        r.small_v[b] = jnp.where(x == 0, late[:, at : at + piece], late[:, at + piece : at + 2 * piece])
    local.append(net.local(r.small_v, r.small))
    gather_arrive(2, 3)
    out_step(1)
    gather_product(2)
    r.gate_out_v[...] = r.gates[:, :, z, x].astype(f32)
    net.chain_sum_last((r.gates_up, r.gates_down), add_into, r.gate_out_v, 1)
    local.append(net.local(r.gate_out_v, r.gate_out))
    net.ch_gather_finish(lambda cc: r.shared.at[cc], "shared")
    total = r.shared[0]
    for cc in range(1, n_ch):
        total = total + r.shared[cc]
    for cc in range(n_ch):
        r.finals_v[:, cc * wide : (cc + 1) * wide] = r.shared[cc, 0:n_docs, 0:wide]
    local.append(net.local(r.finals_v, r.finals))
    for i in range(d // 128):
        at, line = i * 128 % wide, n_docs + i * 128 // wide
        r.gains_v[0, i : i + 1, :] = total[line : line + 1, at : at + 128]
    for i in range(d // 1024):
        r.gains_v[1, i * 8 : (i + 1) * 8, :] = total[:, wide + i * 128 : wide + (i + 1) * 128]
    local.append(net.local(r.gains_v, r.gains))
    net.chain_sum_last((r.oup, r.odown), add_into, r.middle, 0)
    r.mixed_v[...] = r.middle[...].astype(bf)
    local.append(net.local(r.mixed_v, r.mixed))
    for a in (2, 0, 1):
        weight_grad_done(a)
    for a in range(3):
        gather_done(a)
    for copy in local:
        copy.wait()
    net.drain()


def finish_kernel(names, *refs):
    r = types.SimpleNamespace(**dict(zip(names, refs)))
    f32 = jnp.float32
    used = []

    def sem():
        used.append(0)
        return r.sems.at[len(used) - 1]

    def copy(src, dst):
        start = pltpu.make_async_copy(src, dst, sem())
        start.start()
        return start

    incoming, halves = {}, {}
    for a in range(2):
        size = r.dw.shape[1] // 2
        for half in range(2):
            at = pl.ds(half * size, size)
            halves[a, half] = copy(r.dw.at[a, at], r.dw_v.at[a, at])
    for name, index in (("dw", 2), ("keep", 0), ("took", 0), ("keep", 1), ("took", 1)):
        incoming[name, index] = copy(getattr(r, name).at[index], getattr(r, name + "_v").at[index])
    for name in ("keep_out", "took_out", "gains", "gate_out", "small", "finals", "mixed", "sgrad"):
        incoming[name] = copy(getattr(r, name), getattr(r, name + "_v"))
    leaving = []

    def leave(name):
        leaving.append(copy(getattr(r, name + "_v"), getattr(r, name)))

    for a, name in enumerate(("gate_wg", "up_wg")):
        ref, out = getattr(r, name + "_v"), getattr(r, name)
        size = ref.shape[1] // 2
        for half in range(2):
            halves[a, half].wait()
            for i in range(half * size // 256, (half + 1) * size // 256):
                ref[:, i * 256 : (i + 1) * 256] = contract_first(r.dw_v[a, i * 256 : (i + 1) * 256, :], unit(256))
            cols = pl.ds(half * size, size)
            leaving.append(copy(ref.at[:, cols], out.at[:, cols]))
    incoming["dw", 2].wait()
    r.down_wg_v[...] = r.dw_v[2].astype(f32)
    leave("down_wg")
    for a, name in enumerate(("gelu_wg", "recur_wg")):
        incoming["keep", a].wait()
        incoming["took", a].wait()
        getattr(r, name + "_v")[...] = r.keep_v[a] + r.took_v[a].astype(f32)
        leave(name)
    for name in ("keep_out", "took_out", "gains", "gate_out", "small", "finals", "mixed", "sgrad"):
        incoming[name].wait()
    r.out_wg_v[...] = r.keep_out_v[...] + r.took_out_v[...].astype(f32)
    leave("out_wg")
    leaving += [
        copy(r.finals_v, r.finals_o), copy(r.mixed_v, r.mixed_o), copy(r.sgrad_v, r.sgrad_o),
        copy(r.gains_v.at[0], r.ffn_o), copy(r.gains_v.at[1], r.mix_o), copy(r.gate_out_v.at[0], r.rate_o),
        copy(r.gate_out_v.at[1], r.inlet_o),
    ]
    n_taps = r.taps_o_v.shape[1]
    for b in range(r.small_v.shape[0]):
        for k in range(n_taps):
            r.taps_o_v[b, k : k + 1, :] = r.small_v[b, k : k + 1, :]
        for k, name in enumerate(("bias_o", "rateb_o", "inletb_o", "decay_o")):
            getattr(r, name + "_v")[b : b + 1, :] = r.small_v[b, n_taps + k : n_taps + k + 1, :]
    for name in ("taps_o", "bias_o", "rateb_o", "inletb_o", "decay_o"):
        leave(name)
    for start in leaving:
        start.wait()


def gathered_body(
    stream, cotangent, mix_gain, gelu_weight, recur_weight, conv_taps, conv_bias, rate_weight, rate_bias, inlet_weight,
    inlet_bias, decay_param, init_states, out_weight, ffn_gain, gate_weight, up_weight, down_weight, doc_lengths, block_counts,
):
    n_seq, n_ch = lax.axis_size(SEQ), lax.axis_size(CH)
    rows, d = stream.shape
    slots, bw = conv_bias.shape
    width, hidden = gate_weight.shape
    sl = hidden // n_seq
    n_z = n_seq // 2
    count, wide, tokens = rows * n_ch, slots * bw, rows * n_ch * n_seq
    piece = bw // n_seq
    n_taps, n_docs = conv_taps.shape[0], doc_lengths.shape[0]
    bf, f32 = jnp.bfloat16, jnp.float32
    vmem = pl.BlockSpec(memory_space=pltpu.VMEM)
    smem = pl.BlockSpec(memory_space=pltpu.SMEM)
    anywhere = pl.BlockSpec(memory_space=pl.ANY)
    inputs = dict(
        stream=stream, cot=cotangent, mix_gain=mix_gain, gelu_w=gelu_weight, recur_w=recur_weight, taps=conv_taps.transpose(1, 0, 2),
        bias=conv_bias, rate_w=rate_weight, rate_b=rate_bias, inlet_w=inlet_weight, inlet_b=inlet_bias, decay=decay_param,
        init=init_states, out_w=out_weight, ffn_gain=ffn_gain, gate_w=gate_weight, up_w=up_weight, down=down_weight,
        lengths=doc_lengths, counts=block_counts,
    )
    places = dict(lengths=smem, counts=smem)
    staged = [name for name in inputs if name not in ("lengths", "counts", "gate_w", "up_w", "down")]
    outputs = dict(
        keep=((2, width, wide), f32), keep_out=((wide, width), f32), took=((2, width, wide), bf), took_out=((wide, width), bf),
        dw=((3, hidden, width), bf),
        finals=((n_docs, wide * n_ch), f32), mixed=((rows, d), bf), sgrad=((rows, d), f32), gains=((2, d // 128, 128), f32),
        gate_out=((2, slots, piece, bw), f32), small=((slots, 8, piece), f32),
    )
    packed = wide + d // 8
    scratch = dict(
        mix=((RIM + count, d), bf), full=((tokens, d), bf), cfull=((tokens, d), bf), turned=((2, hidden, width), bf),
        wt=((3, sl, d), bf), dwl=((3, sl, d), bf), value=((tokens, sl), f32), slope=((tokens, sl), f32),
        hid=((tokens, sl), bf), gat=((tokens, sl), bf), upg=((tokens, sl), bf),
        gelu=((count, wide), f32), recur=((RIM + count, wide), bf), conv=((count, wide), bf), rate_pre=((count, wide), f32),
        inlet_pre=((count, wide), f32), scan_a=((count, wide), f32), scan_b=((count, wide), f32), state=((count, wide), f32),
        gath=((3, n_z, count, wide), bf), left=((2, n_z, n_ch, rows, 2 * width), bf), give=((2, width, wide), bf),
        give_out=((wide, width), bf), take=((2, width, wide), bf), cgrad=((count + RIM, wide), bf), branch=((n_ch, rows, d), bf),
        summary=((n_seq, 8, bw), f32), summary_back=((n_seq, 8, bw), f32),
        part=((2, 2, rows, d), f32), mid=((2, rows, d), f32), ylow=((rows, d), bf), yfar=((rows, d), bf), middle=((rows, d), f32),
        npart=((n_z, 2, 2, 2, rows, d), bf), nsib=((n_z, 2, 2, rows, d), bf), nfar=((n_z, 2, rows // 2, d), bf),
        nside=((n_z, 2, rows, d), bf),
        opart=((n_z, 2, 2, 2, rows, d), bf), osib=((n_z, 2, 2, rows, d), bf), ofar=((n_z, 2, rows, d), bf),
        oside=((n_z, rows, d), bf), oup=((n_z - 1, rows, d), bf), odown=((n_z - 1, rows, d), bf),
        gates=((2, slots, n_z, 2, piece, bw), bf), gates_x=((2, slots, n_z, piece, bw), bf), gates_up=((n_z - 1, 2, slots, piece, bw), bf), gates_down=((n_z - 1, 2, slots, piece, bw), bf),
        early=((n_z + 1, 8, wide), f32), early_pair=((8, wide), f32), late=((8, packed), f32), late_pair=((8, packed), f32),
        late_out=((n_z, 8, 2 * d // 8), f32), late_in=((n_z, 8, 2 * d // 8), f32),
        shared=((n_ch, 8, packed), f32),
    )
    scratch.update({name + "_v": (inputs[name].shape, inputs[name].dtype) for name in staged})
    scratch.update({name + "_v": what for name, what in outputs.items() if name not in ("took", "took_out", "dw")})
    dma = pltpu.SemaphoreType.DMA
    results = pl.pallas_call(
        functools.partial(
            block_kernel, (n_seq, n_ch, rows, d, slots, bw, width, sl),
            list(inputs) + list(outputs) + list(scratch) + ["send_sems", "recv_sems", "local_sems"],
        ),
        out_shape=[jax.ShapeDtypeStruct(*what) for what in outputs.values()],
        in_specs=[places.get(name, anywhere) for name in inputs],
        out_specs=[anywhere] * len(outputs),
        scratch_shapes=[pltpu.VMEM(*what) for what in scratch.values()] + [dma((SEND_SEMS,)), dma((RECV_SEMS,)), dma((LOCAL_SEMS,))],
        compiler_params=pltpu.CompilerParams(collective_id=1, has_side_effects=True, vmem_limit_bytes=VMEM_BYTES),
    )(*inputs.values())
    vector = ((slots, piece), f32)
    ends = dict(
        finals_o=((n_docs, wide * n_ch), f32), mixed_o=((rows, d), bf), sgrad_o=((rows, d), f32), mix_o=((d // 128, 128), f32),
        gelu_wg=((width, wide), f32), recur_wg=((width, wide), f32), taps_o=((slots, n_taps, piece), f32), bias_o=vector,
        rate_o=((slots, piece, bw), f32), rateb_o=vector, inlet_o=((slots, piece, bw), f32), inletb_o=vector, decay_o=vector,
        out_wg=((wide, width), f32), ffn_o=((d // 128, 128), f32), gate_wg=((width, hidden), f32), up_wg=((width, hidden), f32),
        down_wg=((hidden, width), f32),
    )
    direct = ("finals_o", "mixed_o", "sgrad_o", "ffn_o", "mix_o", "rate_o", "inlet_o")
    kept = {name + "_v": outputs[name] for name in outputs}
    kept.update({name + "_v": what for name, what in ends.items() if name not in direct})
    last = pl.pallas_call(
        functools.partial(finish_kernel, list(outputs) + list(ends) + list(kept) + ["sems"]),
        out_shape=[jax.ShapeDtypeStruct(*what) for what in ends.values()],
        in_specs=[anywhere] * len(outputs),
        out_specs=[anywhere] * len(ends),
        scratch_shapes=[pltpu.VMEM(*what) for what in kept.values()] + [pltpu.SemaphoreType.DMA((40,))],
        compiler_params=pltpu.CompilerParams(vmem_limit_bytes=VMEM_BYTES),
    )(*results)
    named = dict(zip(ends, last))
    named["taps_o"] = named["taps_o"].transpose(1, 0, 2)
    named["mix_o"], named["ffn_o"] = named["mix_o"].reshape(d), named["ffn_o"].reshape(d)
    return tuple(named.values())


def solution(mesh):
    in_specs = (
        P((SEQ, CH), None),
        P((SEQ, CH), None),
        P(),
        P(None, CH),
        P(None, CH),
        P(None, CH, None),
        P(CH, None),
        P(CH, None, None),
        P(CH, None),
        P(CH, None, None),
        P(CH, None),
        P(CH, None),
        P(None, CH),
        P(CH, None),
        P(),
        P(SEQ, CH),
        P(SEQ, CH),
        P(CH, SEQ),
        P(),
        P(CH),
    )
    out_specs = (
        P(),
        P((SEQ, CH), None),
        P((SEQ, CH), None),
        P(),
        P(SEQ, CH),
        P(SEQ, CH),
        P(None, CH, SEQ),
        P(CH, SEQ),
        P(CH, SEQ, None),
        P(CH, SEQ),
        P(CH, SEQ, None),
        P(CH, SEQ),
        P(CH, SEQ),
        P(CH, SEQ),
        P(),
        P(SEQ, CH),
        P(SEQ, CH),
        P(CH, SEQ),
    )
    return jax.shard_map(gathered_body if mesh.shape[SEQ] == 8 else body, mesh=mesh, in_specs=in_specs, out_specs=out_specs, check_vma=False)
```
